128 devices in a mesh: seq: 16 (over x, z), head: 8 (over y, core).
Axes of the slice: x: 4, y: 4, z: 4, core: 2. Of those that a mesh axis runs over, the one named last changes fastest.
Arguments:
- inputs: bfloat16 [8192, 2048], P('seq'), may hold values from -6 to 6
- gain_mix: float32 [2048], replicated, may hold values from 0.5 to 1.5
- feat_query: bfloat16 [2048, 256], P(None, 'head'), may hold values from -0.25 to 0.25
- feat_key: bfloat16 [2048, 256], P(None, 'head'), may hold values from -0.25 to 0.25
- win_query: bfloat16 [2048, 2048], P(None, 'head'), may hold values from -0.125 to 0.125
- win_key: bfloat16 [2048, 2048], P(None, 'head'), may hold values from -0.125 to 0.125
- value_proj: bfloat16 [2048, 2048], P(None, 'head'), may hold values from -0.125 to 0.125
- out_proj: bfloat16 [2048, 2048], P('head'), may hold values from -0.5 to 0.5
- gain_ffn: float32 [2048], replicated, may hold values from 0.5 to 1.5
- gate_proj: bfloat16 [2048, 5632], P(None, 'head'), may hold values from -0.125 to 0.125
- up_proj: bfloat16 [2048, 5632], P(None, 'head'), may hold values from -0.125 to 0.125
- down_proj: bfloat16 [5632, 2048], P('head'), may hold values from -0.078125 to 0.078125
- document_starts: int32 [1, 4], replicated, may hold values from 1 to 8191, as said below
- cotangent: bfloat16 [8192, 2048], P('seq'), may hold values from -6 to 6
Outputs:
- output: bfloat16 [8192, 2048], P('seq')
- grad_x: float32 [8192, 2048], P('seq')
- grad_gain_mix: float32 [2048], P('seq')
- grad_feat_query: float32 [2048, 256], P('seq', 'head')
- grad_feat_key: float32 [2048, 256], P('seq', 'head')
- grad_win_query: float32 [2048, 2048], P('seq', 'head')
- grad_win_key: float32 [2048, 2048], P('seq', 'head')
- grad_value_proj: float32 [2048, 2048], P('seq', 'head')
- grad_out_proj: float32 [2048, 2048], P('head', 'seq')
- grad_gain_ffn: float32 [2048], P('seq')
- grad_gate_proj: float32 [2048, 5632], P('seq', 'head')
- grad_up_proj: float32 [2048, 5632], P('seq', 'head')
- grad_down_proj: float32 [5632, 2048], P('head', 'seq')
The draws below stay inside these ranges and needn't reach their ends.
Inputs may be any that keep to these rules, and one draw needn't show every extreme that they name: `document_starts`: each row's entries are strictly increasing positions within the row; the first two lie in 1 to 511, the third in the last 512 positions of the row but not the first of them, the fourth after it. Position 0 of every row begins a document.
All inputs are finite; a program needn't handle non-finite values.
Results may differ from the reference program's by a relative error of at most 0.02.
Values may be sent and summed in bfloat16 or wider, within the bound.
No kernel may reach another device: no remote copies, remote signals or barrier semaphores. Data moves between devices by JAX's collectives and lax.ppermute only.
A program may use at most 192 MiB of HBM per device.

```python
import math
import jax
import jax.numpy as jnp
from jax import lax

D = 2048
HEAD_TOTAL = 16
F = 16
VALUE_WIDTH = 128
FF = 5632
WIN = 64
BLOCK_TOKENS = 512
SPAN = 16
FEATURE_COUNT = 273
ROW_LENGTH = 8192
PACKED_ROWS = 1
TOKENS = 8192


def starts_of_row(row_key):
    random_subkeys = jax.random.split(row_key, 4)
    block_halfway = BLOCK_TOKENS // 2
    final_block_index = ROW_LENGTH - BLOCK_TOKENS
    first_start = jax.random.randint(random_subkeys[0], (), 1, block_halfway)
    second_start = jax.random.randint(random_subkeys[1], (), block_halfway, BLOCK_TOKENS)
    third_start = jax.random.randint(random_subkeys[2], (), final_block_index + 1, final_block_index + block_halfway)
    fourth_begin_index = jax.random.randint(random_subkeys[3], (), final_block_index + block_halfway, ROW_LENGTH)
    return jnp.stack([first_start, second_start, third_start, fourth_begin_index]).astype(jnp.int32)


def draw_document_starts(key, part):
    key = jax.random.fold_in(key, 7)
    row_keys = jax.random.split(key, PACKED_ROWS)
    return jax.vmap(starts_of_row)(row_keys).astype(jnp.int32)


def block_scale(own_key, extent, pieces, smallest, high):
    def one(position, blocks):
        steps = jax.random.uniform(jax.random.fold_in(jax.random.fold_in(own_key, 6), position), (blocks,), jnp.float32, smallest / len(pieces), high / len(pieces))
        return jnp.repeat(jnp.exp(steps), extent[position] // blocks).reshape((-1,) + (1,) * (len(extent) - position - 1))

    level = one(*pieces[0])
    for cut in pieces[1:]:
        level = level * one(*cut)
    return level


def gaussian(own_key, dims, spread, most, shards=(), held_as=jnp.bfloat16):
    loudness = block_scale(own_key, dims, shards, -0.22, 0.18) if shards else 1.0
    array = jax.random.normal(own_key, dims, jnp.float32) * spread * loudness
    return jnp.minimum(jnp.maximum(array, -most), most).astype(held_as)


def setup_inputs(seed: int = 0) -> dict:
    keys = jax.random.split(jax.random.key(seed), 15)
    inputs = gaussian(keys[0], (TOKENS, D), 1.0, 6.0, ((0, 16),))
    gain_mix = jnp.clip(1.0 + 0.1 * jax.random.normal(keys[1], (D,), jnp.float32), 0.5, 1.5)
    feat_query = gaussian(keys[2], (D, HEAD_TOTAL * F), (D // 4) ** -0.5, 0.25, ((1, 8),))
    feat_key = gaussian(keys[3], (D, HEAD_TOTAL * F), (D // 4) ** -0.5, 0.25, ((1, 8),))
    win_query = gaussian(keys[4], (D, HEAD_TOTAL * VALUE_WIDTH), D ** -0.5, 0.125, ((1, 8),))
    win_key = gaussian(keys[5], (D, HEAD_TOTAL * VALUE_WIDTH), D ** -0.5, 0.125, ((1, 8),))
    value_proj = gaussian(keys[6], (D, HEAD_TOTAL * VALUE_WIDTH), D ** -0.5, 0.125, ((1, 8),))
    out_proj = gaussian(keys[7], (HEAD_TOTAL * VALUE_WIDTH, D), (HEAD_TOTAL * VALUE_WIDTH // 16) ** -0.5, 0.5, ((0, 8),))
    gain_ffn = jnp.clip(1.0 + 0.1 * jax.random.normal(keys[8], (D,), jnp.float32), 0.5, 1.5)
    gate_proj = gaussian(keys[9], (D, FF), D ** -0.5, 0.125, ((1, 8),))
    up_proj = gaussian(keys[10], (D, FF), D ** -0.5, 0.125, ((1, 8),))
    down_proj = gaussian(keys[11], (FF, D), FF ** -0.5, 0.078125, ((0, 8),))
    document_starts = draw_document_starts(jax.random.fold_in(keys[14], 71), 0)
    cotangent = gaussian(keys[13], (TOKENS, D), 1.0, 6.0, ((0, 16),))
    return {"inputs": inputs, "gain_mix": gain_mix, "feat_query": feat_query, "feat_key": feat_key, "win_query": win_query, "win_key": win_key, "value_proj": value_proj, "out_proj": out_proj, "gain_ffn": gain_ffn, "gate_proj": gate_proj, "up_proj": up_proj, "down_proj": down_proj, "document_starts": document_starts, "cotangent": cotangent}


@jax.custom_vjp
def low(v):
    return lax.optimization_barrier(v.astype(jnp.bfloat16)).astype(jnp.float32)

@jax.custom_vjp
def low_back(v):
    return v

def low_keep(v):
    return (low(v), None)

def low_pass(kept, grad):
    return (grad,)

def back_keep(v):
    return (v, None)

def back_low(kept, grad):
    return (low(grad),)
low.defvjp(low_keep, low_pass)
low_back.defvjp(back_keep, back_low)
EPS = 1e-05
HIGH = lax.Precision.HIGHEST

def high_dot(left_side, right_side):
    return jnp.dot(left_side, right_side, precision=HIGH)

def high_sum(form, left_side, right_side):
    return jnp.einsum(form, left_side, right_side, precision=HIGH)

def rms_norm(value_matrix, gain):
    return value_matrix * lax.rsqrt(lax.optimization_barrier(jnp.mean(value_matrix * value_matrix, axis=-1, keepdims=True)) + EPS) * gain

def segment_of(token_positions, starts):
    return lax.optimization_barrier(jnp.sum((token_positions[:, None] >= starts[None, :]).astype(jnp.int32), axis=-1))

def features(value_matrix):
    factor = F ** (-0.25)
    products = value_matrix[..., :, None] * value_matrix[..., None, :]
    constant = jnp.ones(value_matrix.shape[:-1] + (1,), value_matrix.dtype)
    return jnp.concatenate([constant, value_matrix * factor, products.reshape(value_matrix.shape[:-1] + (F * F,)) * (factor * factor / math.sqrt(2.0))], axis=-1)

def row_mixer(packed_tokens):
    query_features, key_features, value_matrix, window_queries, window_keys, starts = packed_tokens
    pad_keys = jnp.concatenate([jnp.zeros((WIN, HEAD_TOTAL, VALUE_WIDTH), window_keys.dtype), window_keys], axis=0)
    pad_values = jnp.concatenate([jnp.zeros((WIN, HEAD_TOTAL, VALUE_WIDTH), value_matrix.dtype), value_matrix], axis=0)
    token_positions = jnp.arange(ROW_LENGTH, dtype=jnp.int32)
    doc_ids = segment_of(token_positions, starts)
    factor = VALUE_WIDTH ** (-0.5)

    def block_step(carry, block_index):
        state, norm_sum = carry
        start = (block_index * BLOCK_TOKENS).astype(jnp.int32)
        q_rows = lax.dynamic_slice_in_dim(query_features, start, BLOCK_TOKENS, 0)
        k_rows = lax.dynamic_slice_in_dim(key_features, start, BLOCK_TOKENS, 0)
        v_rows = lax.dynamic_slice_in_dim(value_matrix, start, BLOCK_TOKENS, 0)
        qw_rows = lax.dynamic_slice_in_dim(window_queries, start, BLOCK_TOKENS, 0)
        row_pos = lax.dynamic_slice_in_dim(token_positions, start, BLOCK_TOKENS, 0)
        row_ids = lax.dynamic_slice_in_dim(doc_ids, start, BLOCK_TOKENS, 0)
        before_id = jnp.sum((starts <= start - 1).astype(jnp.int32))
        use_prefix = ((row_ids == before_id) & (start > 0)).astype(state.dtype)
        tail_mask = (row_ids == row_ids[BLOCK_TOKENS - 1]).astype(state.dtype)
        inside = jnp.sum(((starts >= start) & (starts < start + BLOCK_TOKENS)).astype(jnp.int32))
        keep_flag = jnp.where((inside > 0) | (start == 0), 0.0, 1.0).astype(state.dtype)
        num_inter = high_sum('chp,hpe->che', q_rows, low(state)) * use_prefix[:, None, None]
        den_inter = high_sum('chp,hp->ch', q_rows, norm_sum) * use_prefix[:, None]
        causal = (row_pos[:, None] >= row_pos[None, :]) & (row_ids[:, None] == row_ids[None, :])
        weights_lin = low_back(jnp.where(causal[None], high_sum('chp,dhp->hcd', q_rows, k_rows), 0.0))
        numerator = low_back(num_inter + high_sum('hcd,dhe->che', low(weights_lin), v_rows))
        denominator = den_inter + lax.optimization_barrier(jnp.sum(weights_lin, axis=-1)).T
        linear = numerator / denominator[:, :, None]
        key_pos = start - WIN + jnp.arange(BLOCK_TOKENS + WIN, dtype=jnp.int32)
        key_ids = segment_of(key_pos, starts)
        near = (key_pos[None, :] <= row_pos[:, None]) & (row_pos[:, None] - key_pos[None, :] < WIN) & (key_ids[None, :] == row_ids[:, None]) & (key_pos[None, :] >= 0)
        key_rows = lax.dynamic_slice_in_dim(pad_keys, start, BLOCK_TOKENS + WIN, 0)
        value_rows = lax.dynamic_slice_in_dim(pad_values, start, BLOCK_TOKENS + WIN, 0)
        logits = low_back(jnp.where(near[None], high_sum('che,khe->hck', qw_rows, key_rows) * factor, -1e+30))
        row_max = lax.optimization_barrier(jnp.max(logits, axis=-1, keepdims=True))
        weights_exp = jnp.exp(logits - row_max)
        probs = weights_exp / lax.optimization_barrier(jnp.sum(weights_exp, axis=-1, keepdims=True))
        window = high_sum('hck,khe->che', low(probs), value_rows)
        mixed = low(low_back(linear + window)).reshape(BLOCK_TOKENS, HEAD_TOTAL * VALUE_WIDTH)
        tail_values = v_rows * tail_mask[:, None, None]
        state_loc = low_back(high_sum('chp,che->hpe', k_rows, tail_values))
        norm_loc = lax.optimization_barrier(jnp.sum(k_rows * tail_mask[:, None, None], axis=0))
        return ((state * keep_flag + state_loc, norm_sum * keep_flag + norm_loc), mixed)
    initial = (jnp.zeros((HEAD_TOTAL, FEATURE_COUNT, VALUE_WIDTH), query_features.dtype), jnp.zeros((HEAD_TOTAL, FEATURE_COUNT), query_features.dtype))
    final_carry, mixer_block_outputs = lax.scan(jax.checkpoint(block_step), initial, jnp.arange(SPAN, dtype=jnp.int32))
    return mixer_block_outputs.reshape(ROW_LENGTH, HEAD_TOTAL * VALUE_WIDTH)

def forward(x_in, gain_mix, feat_query, feat_key, win_query, win_key, value_proj, out_proj, gain_ffn, gate_proj, up_proj, down_proj, document_starts):
    normed = low(rms_norm(x_in, gain_mix))
    query_features = low(features(low_back(high_dot(normed, feat_query)).reshape(TOKENS, HEAD_TOTAL, F)))
    key_features = low(features(low_back(high_dot(normed, feat_key)).reshape(TOKENS, HEAD_TOTAL, F)))
    value_matrix = low(low_back(high_dot(normed, value_proj))).reshape(TOKENS, HEAD_TOTAL, VALUE_WIDTH)
    window_queries = low(low_back(high_dot(normed, win_query))).reshape(TOKENS, HEAD_TOTAL, VALUE_WIDTH)
    window_keys = low(low_back(high_dot(normed, win_key))).reshape(TOKENS, HEAD_TOTAL, VALUE_WIDTH)
    packed_tokens = (query_features.reshape(PACKED_ROWS, ROW_LENGTH, HEAD_TOTAL, FEATURE_COUNT), key_features.reshape(PACKED_ROWS, ROW_LENGTH, HEAD_TOTAL, FEATURE_COUNT), value_matrix.reshape(PACKED_ROWS, ROW_LENGTH, HEAD_TOTAL, VALUE_WIDTH), window_queries.reshape(PACKED_ROWS, ROW_LENGTH, HEAD_TOTAL, VALUE_WIDTH), window_keys.reshape(PACKED_ROWS, ROW_LENGTH, HEAD_TOTAL, VALUE_WIDTH), document_starts)
    mixed = lax.map(row_mixer, packed_tokens).reshape(TOKENS, HEAD_TOTAL * VALUE_WIDTH)
    resid = x_in + low_back(high_dot(mixed, out_proj))
    normed_ffn = low(rms_norm(resid, gain_ffn))
    gate = low_back(high_dot(normed_ffn, gate_proj))
    up_value = low_back(high_dot(normed_ffn, up_proj))
    activation = low(jax.nn.silu(gate) * up_value)
    return resid + low_back(high_dot(activation, down_proj))

def reference(inputs, gain_mix, feat_query, feat_key, win_query, win_key, value_proj, out_proj, gain_ffn, gate_proj, up_proj, down_proj, document_starts, cotangent):
    floats = tuple((item.astype(jnp.float32) for item in (inputs, gain_mix, feat_query, feat_key, win_query, win_key, value_proj, out_proj, gain_ffn, gate_proj, up_proj, down_proj)))

    def wrapped(*arrays):
        return forward(*arrays, document_starts)
    result, pullback = jax.vjp(wrapped, *floats)
    grads = pullback(cotangent.astype(jnp.float32))
    return (result.astype(jnp.bfloat16), grads[0], grads[1], grads[2], grads[3], grads[4], grads[5], grads[6], grads[7], grads[8], grads[9], grads[10], grads[11])
```

```python
import math

import jax
import jax.numpy as jnp
from jax import lax
from jax.sharding import PartitionSpec as P

F = 16
VALUE_WIDTH = 128
WIN = 64


EPS = 1e-05


def along_y(distance):
    return [(i, (i + 2 * distance) % 8) for i in range(8)]


def sibling():
    return [(i, i ^ 1) for i in range(8)]


def along_x(distance):
    return [(i, (i + 4 * distance) % 16) for i in range(16)]


def along_z(distance):
    return [(4 * a + z, 4 * a + (z + distance) % 4) for a in range(4) for z in range(4)]


def pick(stack, index):
    return lax.dynamic_index_in_dim(stack, index, 0, keepdims=False)


def head_sum_scatter(part):
    me = lax.axis_index("head")
    y, core = me // 2, me % 2
    rows, width = part.shape
    halves = part.reshape(2, rows // 2, width)
    other = lax.ppermute(pick(halves, 1 - core).astype(jnp.bfloat16), "head", sibling())
    quarters = (pick(halves, core) + other.astype(jnp.float32)).astype(jnp.bfloat16)
    quarters = quarters.reshape(4, rows // 8, width)
    got = [
        lax.ppermute(pick(quarters, (y + d) % 4), "head", along_y(d)).astype(jnp.float32)
        for d in (1, 2, 3)
    ]
    return pick(quarters, y).astype(jnp.float32) + got[0] + got[1] + got[2]


def head_gather(own):
    me = lax.axis_index("head")
    y, core = me // 2, me % 2
    half = jnp.zeros((4,) + own.shape, own.dtype)
    half = lax.dynamic_update_index_in_dim(half, own, y, 0)
    for d in (1, 2, 3):
        got = lax.ppermute(own, "head", along_y(d))
        half = lax.dynamic_update_index_in_dim(half, got, (y + 4 - d) % 4, 0)
    other = lax.ppermute(half, "head", sibling())
    full = jnp.where(core == 0, jnp.stack([half, other]), jnp.stack([other, half]))
    return full.reshape((8 * own.shape[0],) + own.shape[1:])


def own_rows(block):
    me = lax.axis_index("head")
    y, core = me // 2, me % 2
    count = block.shape[0] // 8
    return lax.dynamic_slice_in_dim(block, core * 4 * count + y * count, count, 0)


def small_head_sum(part):
    total = part + lax.ppermute(part, "head", sibling())
    got = [lax.ppermute(total, "head", along_y(d)) for d in (1, 2, 3)]
    return total + got[0] + got[1] + got[2]


def low_pair(part):
    high = part.astype(jnp.bfloat16)
    return high, (part - high.astype(jnp.float32)).astype(jnp.bfloat16)


def pack_state(state, norm):
    heads, count, width = state.shape
    rows = -(-count // width)
    padded = jnp.pad(norm, ((0, 0), (0, rows * width - count))).reshape(heads, rows, width)
    high, rest = low_pair(padded)
    return jnp.concatenate([state.astype(jnp.bfloat16), high, rest], axis=1)


def unpack_state(packed, count):
    heads, _, width = packed.shape
    rows = -(-count // width)
    norm = packed[:, count : count + rows] + packed[:, count + rows :]
    return packed[:, :count], norm.reshape(heads, rows * width)[:, :count]


def exclusive_sum(state, norm, reverse):
    f32 = jnp.float32
    me = lax.axis_index("seq")
    xx, zz = me // 4, me % 4
    sign = -1 if reverse else 1
    place_x, place_z = (3 - xx, 3 - zz) if reverse else (xx, zz)
    own = pack_state(state, norm)
    before = jnp.zeros(own.shape, f32)
    for d in (1, 2, 3):
        got = lax.ppermute(own, "seq", along_x(sign * d)).astype(f32)
        before = before + jnp.where(place_x >= d, got, 0.0)
    with_own = before + own.astype(f32)
    total = before
    count = state.shape[1]
    low_before = pack_state(*unpack_state(before, count))
    low_with = pack_state(*unpack_state(with_own, count))
    for d in (1, 2, 3):
        sent = jnp.where(place_z + d < 4, low_with, low_before)
        total = total + lax.ppermute(sent, "seq", along_z(sign * d)).astype(f32)
    return unpack_state(total, count)


def shifted(block, axis, distance):
    devices = range(lax.axis_size(axis))
    route = [(i - distance, i) for i in devices if i - distance in devices]
    return lax.ppermute(block, axis, route)


def contract_rows(left_side, right_side):
    return lax.dot_general(
        left_side, right_side, (((0,), (0,)), ((), ())), preferred_element_type=jnp.float32
    )


def times_transposed(left_side, right_side):
    return lax.dot_general(
        left_side, right_side, (((1,), (1,)), ((), ())), preferred_element_type=jnp.float32
    )


def segment_of(token_positions, starts):
    return jnp.sum((token_positions[:, None] >= starts[None, :]).astype(jnp.int32), axis=-1)


def features(value_matrix):
    factor = F ** (-0.25)
    products = value_matrix[..., :, None] * value_matrix[..., None, :]
    constant = jnp.ones(value_matrix.shape[:-1] + (1,), jnp.float32)
    return jnp.concatenate(
        [
            constant,
            value_matrix * factor,
            products.reshape(value_matrix.shape[:-1] + (F * F,))
            * (factor * factor / math.sqrt(2.0)),
        ],
        axis=-1,
    )


def feature_grad(value_matrix, gradient):
    factor = F ** (-0.25)
    square = gradient[..., 1 + F :].reshape(value_matrix.shape + (F,))
    symmetric = square + jnp.swapaxes(square, -1, -2)
    return gradient[..., 1 : 1 + F] * factor + jnp.einsum(
        "chab,chb->cha", symmetric, value_matrix
    ) * (factor * factor / math.sqrt(2.0))


def norm_back(in_rows, inv_rms, gain, grad_normed):
    weighted = grad_normed * gain
    return inv_rms * weighted - in_rows * inv_rms**3 * jnp.mean(
        weighted * in_rows, axis=-1, keepdims=True
    )


def shards(
    inputs,
    gain_mix,
    feat_query,
    feat_key,
    win_query,
    win_key,
    value_proj,
    out_proj,
    gain_ffn,
    gate_proj,
    up_proj,
    down_proj,
    document_starts,
    cotangent,
):
    f32 = jnp.float32
    bf16 = jnp.bfloat16
    row_count = inputs.shape[0]
    head_count = value_proj.shape[1] // VALUE_WIDTH
    width = head_count * VALUE_WIDTH
    factor = VALUE_WIDTH ** (-0.5)
    in_row = lax.axis_index("seq")
    row_starts = document_starts[0]
    base_pos = in_row * row_count
    token_positions = base_pos + jnp.arange(row_count, dtype=jnp.int32)
    doc_ids = segment_of(token_positions, row_starts)
    before_id = segment_of((base_pos - 1).reshape(1), row_starts)[0]
    use_prefix = ((doc_ids == before_id) & (in_row > 0)).astype(f32)
    use_low = use_prefix[:, None, None].astype(bf16)
    tail_mask = (doc_ids == doc_ids[row_count - 1]).astype(f32)
    causal = (token_positions[:, None] >= token_positions[None, :]) & (
        doc_ids[:, None] == doc_ids[None, :]
    )
    key_pos = base_pos - WIN + jnp.arange(row_count + WIN, dtype=jnp.int32)
    key_ids = segment_of(key_pos, row_starts)
    near = (
        (key_pos[None, :] <= token_positions[:, None])
        & (token_positions[:, None] - key_pos[None, :] < WIN)
        & (key_ids[None, :] == doc_ids[:, None])
        & (key_pos[None, :] >= 0)
    )
    x_float = inputs.astype(f32)
    inv_mix = lax.rsqrt(jnp.mean(x_float * x_float, axis=-1, keepdims=True) + EPS)
    normed = (x_float * inv_mix * gain_mix).astype(bf16)
    q_raw = jnp.dot(normed, feat_query, preferred_element_type=f32).reshape(
        row_count, head_count, F
    )
    k_raw = jnp.dot(normed, feat_key, preferred_element_type=f32).reshape(row_count, head_count, F)
    query_features = features(q_raw).astype(bf16)
    key_features = features(k_raw).astype(bf16)
    value_matrix = jnp.dot(normed, value_proj, preferred_element_type=f32).astype(bf16)
    window_queries = jnp.dot(normed, win_query, preferred_element_type=f32).astype(bf16)
    window_keys = jnp.dot(normed, win_key, preferred_element_type=f32).astype(bf16)
    value_heads = value_matrix.reshape(row_count, head_count, VALUE_WIDTH)
    query_heads = window_queries.reshape(row_count, head_count, VALUE_WIDTH)
    tail_values = value_heads * tail_mask[:, None, None].astype(bf16)
    state_loc = jnp.einsum("chp,che->hpe", key_features, tail_values, preferred_element_type=f32)
    norm_loc = jnp.sum(key_features.astype(f32) * tail_mask[:, None, None], axis=0)
    state_pre, norm_pre = exclusive_sum(state_loc, norm_loc, False)
    state_low = state_pre.astype(bf16)
    q_float = query_features.astype(f32)
    num_inter = (
        jnp.einsum("chp,hpe->che", query_features, state_low, preferred_element_type=f32)
        * use_prefix[:, None, None]
    )
    den_inter = (
        jnp.einsum("chp,hp->ch", q_float, norm_pre, precision=lax.Precision.HIGHEST)
        * use_prefix[:, None]
    )
    weights_lin = jnp.where(
        causal[None],
        jnp.einsum("chp,dhp->hcd", query_features, key_features, preferred_element_type=f32),
        0.0,
    )
    weights_low = weights_lin.astype(bf16)
    numerator = num_inter + jnp.einsum(
        "hcd,dhe->che", weights_low, value_heads, preferred_element_type=f32
    )
    denominator = den_inter + jnp.sum(weights_lin, axis=-1).T
    linear = numerator / denominator[:, :, None]
    left_rows = shifted(
        jnp.stack([window_keys[row_count - WIN :], value_matrix[row_count - WIN :]]), "seq", 1
    )
    key_rows = jnp.concatenate([left_rows[0], window_keys], axis=0).reshape(
        row_count + WIN, head_count, VALUE_WIDTH
    )
    value_rows = jnp.concatenate([left_rows[1], value_matrix], axis=0).reshape(
        row_count + WIN, head_count, VALUE_WIDTH
    )
    logits = jnp.where(
        near[None],
        jnp.einsum("che,khe->hck", query_heads, key_rows, preferred_element_type=f32) * factor,
        -1e30,
    )
    row_max = jnp.max(logits, axis=-1, keepdims=True)
    weights_exp = jnp.exp(logits - row_max)
    probs = weights_exp / jnp.sum(weights_exp, axis=-1, keepdims=True)
    probs_low = probs.astype(bf16)
    window = jnp.einsum("hck,khe->che", probs_low, value_rows, preferred_element_type=f32)
    mixed = (linear + window).astype(bf16).reshape(row_count, width)
    resid = own_rows(x_float) + head_sum_scatter(
        jnp.dot(mixed, out_proj, preferred_element_type=f32)
    )
    inv_ffn = lax.rsqrt(jnp.mean(resid * resid, axis=-1, keepdims=True) + EPS)
    normed_ffn = head_gather((resid * inv_ffn * gain_ffn).astype(bf16))
    gate = jnp.dot(normed_ffn, gate_proj, preferred_element_type=f32)
    up_value = jnp.dot(normed_ffn, up_proj, preferred_element_type=f32)
    sigmoid_gate = jax.nn.sigmoid(gate)
    silu_gate = gate * sigmoid_gate
    activation = (silu_gate * up_value).astype(bf16)
    grad_low = cotangent
    grad_act = times_transposed(grad_low, down_proj)
    grad_gate = (grad_act * up_value * sigmoid_gate * (1.0 + gate * (1.0 - sigmoid_gate))).astype(
        bf16
    )
    grad_up = (grad_act * silu_gate).astype(bf16)
    grad_normed_ffn = head_sum_scatter(
        times_transposed(grad_gate, gate_proj) + times_transposed(grad_up, up_proj)
    )
    ffn_grads = jnp.concatenate(
        [
            contract_rows(normed_ffn, grad_gate),
            contract_rows(normed_ffn, grad_up),
            contract_rows(grad_low, activation),
        ],
        axis=1,
    ).astype(bf16)
    ffn_grads = lax.psum_scatter(ffn_grads, "seq", scatter_dimension=0, tiled=True).astype(f32)
    grad_gain_ffn = jnp.sum(grad_normed_ffn * resid * inv_ffn, axis=0)
    grad_resid = own_rows(cotangent).astype(f32) + norm_back(
        resid, inv_ffn, gain_ffn, grad_normed_ffn
    )
    grad_mix_low = head_gather(grad_resid.astype(bf16))
    ffn_out = head_sum_scatter(jnp.dot(activation, down_proj, preferred_element_type=f32))
    output = head_gather((resid + ffn_out).astype(bf16))
    grad_out_w = contract_rows(grad_mix_low, mixed)
    grad_mixed = (
        times_transposed(grad_mix_low, out_proj)
        .astype(bf16)
        .reshape(row_count, head_count, VALUE_WIDTH)
    )
    grad_probs = jnp.einsum("che,khe->hck", grad_mixed, value_rows, preferred_element_type=f32)
    grad_value_rows = jnp.einsum("hck,che->khe", probs_low, grad_mixed, preferred_element_type=f32)
    grad_logits = (
        probs * (grad_probs - jnp.sum(grad_probs * probs, axis=-1, keepdims=True))
    ).astype(bf16)
    grad_query_win = (
        jnp.einsum("hck,khe->che", grad_logits, key_rows, preferred_element_type=f32) * factor
    )
    grad_key_rows = (
        jnp.einsum("hck,che->khe", grad_logits, query_heads, preferred_element_type=f32) * factor
    )
    edge_grads = jnp.stack(
        [grad_key_rows[:WIN].reshape(WIN, width), grad_value_rows[:WIN].reshape(WIN, width)]
    )
    right_grads = shifted(edge_grads.astype(jnp.bfloat16), "seq", -1).astype(edge_grads.dtype)
    filler = jnp.zeros((row_count - WIN, width), f32)
    grad_float = grad_mixed.astype(f32)
    grad_num = (grad_float / denominator[:, :, None]).astype(bf16)
    grad_den = -jnp.sum(grad_float * linear, axis=-1) / denominator
    grad_weights = (
        jnp.einsum("che,dhe->hcd", grad_num, value_heads, preferred_element_type=f32)
        + grad_den.T[:, :, None]
    )
    grad_weights_low = jnp.where(causal[None], grad_weights, 0.0).astype(bf16)
    grad_num_use = grad_num * use_low
    grad_den_use = grad_den * use_prefix[:, None]
    grad_state = jnp.einsum(
        "chp,che->hpe", query_features, grad_num_use, preferred_element_type=f32
    )
    grad_norm = jnp.einsum("chp,ch->hp", q_float, grad_den_use, precision=lax.Precision.HIGHEST)
    later_state, later_norm = exclusive_sum(grad_state, grad_norm, True)
    later_low = later_state.astype(bf16)
    grad_q_feat = jnp.einsum(
        "hcd,dhp->chp", grad_weights_low, key_features, preferred_element_type=f32
    )
    grad_q_feat = grad_q_feat + jnp.einsum(
        "che,hpe->chp", grad_num_use, state_low, preferred_element_type=f32
    )
    grad_q_feat = grad_q_feat + grad_den_use[:, :, None] * norm_pre[None]
    grad_k_feat = jnp.einsum(
        "hcd,chp->dhp", grad_weights_low, query_features, preferred_element_type=f32
    )
    grad_k_feat = grad_k_feat + jnp.einsum(
        "che,hpe->chp", tail_values, later_low, preferred_element_type=f32
    )
    grad_k_feat = grad_k_feat + tail_mask[:, None, None] * later_norm[None]
    grad_value_lin = jnp.einsum("hcd,che->dhe", weights_low, grad_num, preferred_element_type=f32)
    grad_value_lin = (
        grad_value_lin
        + jnp.einsum("chp,hpe->che", key_features, later_low, preferred_element_type=f32)
        * tail_mask[:, None, None]
    )
    grad_q_raw = feature_grad(q_raw, grad_q_feat).astype(bf16).reshape(row_count, head_count * F)
    grad_k_raw = feature_grad(k_raw, grad_k_feat).astype(bf16).reshape(row_count, head_count * F)
    grad_q_win = grad_query_win.astype(bf16).reshape(row_count, width)
    grad_k_win = (
        grad_key_rows[WIN:].reshape(row_count, width)
        + jnp.concatenate([filler, right_grads[0]], axis=0)
    ).astype(bf16)
    grad_values = (
        (grad_value_rows[WIN:] + grad_value_lin).reshape(row_count, width)
        + jnp.concatenate([filler, right_grads[1]], axis=0)
    ).astype(bf16)
    grad_fq_w = contract_rows(normed, grad_q_raw)
    grad_fk_w = contract_rows(normed, grad_k_raw)
    grad_wq_w = contract_rows(normed, grad_q_win)
    grad_wk_w = contract_rows(normed, grad_k_win)
    grad_value_w = contract_rows(normed, grad_values)
    grad_normed_part = times_transposed(grad_q_raw, feat_query) + times_transposed(
        grad_k_raw, feat_key
    )
    grad_normed_part = (
        grad_normed_part
        + times_transposed(grad_q_win, win_query)
        + times_transposed(grad_k_win, win_key)
    )
    grad_normed_part = grad_normed_part + times_transposed(grad_values, value_proj)
    grad_gain_mix = jnp.sum(grad_normed_part * (x_float * inv_mix), axis=0)
    grad_normed = head_sum_scatter(grad_normed_part)
    gains = jnp.stack(low_pair(grad_gain_mix) + low_pair(grad_gain_ffn), axis=1)
    mix_grads = jnp.concatenate(
        [
            grad_wq_w.astype(bf16),
            grad_wk_w.astype(bf16),
            grad_value_w.astype(bf16),
            grad_out_w.astype(bf16),
            grad_fq_w.astype(bf16),
            grad_fk_w.astype(bf16),
            jnp.pad(gains, ((0, 0), (0, 60))),
        ],
        axis=1,
    )
    mix_grads = mix_grads.reshape(16, 128, mix_grads.shape[1])
    mix_grads = lax.all_to_all(mix_grads, "seq", 0, 0)
    mix_grads = jnp.sum(mix_grads.astype(f32), axis=0)
    grad_x_own = grad_resid + norm_back(own_rows(x_float), own_rows(inv_mix), gain_mix, grad_normed)
    grad_x = head_gather(grad_x_own.astype(bf16)).astype(f32)
    gains = mix_grads[:, 1088:1092].T
    gains = small_head_sum(gains)
    hidden = gate_proj.shape[1]
    return (
        output,
        grad_x,
        gains[0] + gains[1],
        mix_grads[:, 1024:1056],
        mix_grads[:, 1056:1088],
        mix_grads[:, :256],
        mix_grads[:, 256:512],
        mix_grads[:, 512:768],
        mix_grads[:, 768:1024].T,
        gains[2] + gains[3],
        ffn_grads[:, :hidden],
        ffn_grads[:, hidden : 2 * hidden],
        ffn_grads[:, 2 * hidden :].T,
    )


def solution(mesh):
    placed = (
        P("seq", None),
        P(),
        P(None, "head"),
        P(None, "head"),
        P(None, "head"),
        P(None, "head"),
        P(None, "head"),
        P("head", None),
        P(),
        P(None, "head"),
        P(None, "head"),
        P("head", None),
        P(),
        P("seq", None),
    )
    return jax.shard_map(
        shards,
        mesh=mesh,
        in_specs=placed,
        out_specs=(
            P("seq", None),
            P("seq", None),
            P("seq"),
            P("seq", "head"),
            P("seq", "head"),
            P("seq", "head"),
            P("seq", "head"),
            P("seq", "head"),
            P("head", "seq"),
            P("seq"),
            P("seq", "head"),
            P("seq", "head"),
            P("head", "seq"),
        ),
        check_vma=False,
    )
```

```python
import functools
import math

import jax
import jax.numpy as jnp
import numpy as np
from jax import lax
from jax.experimental import pallas as pl
from jax.experimental.pallas import tpu as pltpu
from jax.sharding import PartitionSpec as P

F = 16
VALUE_WIDTH = 128
WIN = 64
EPS = 1e-05

HEADS = 2
ROWS = 512
LANES = 256
KEPT = 160
PACKED = 176
TILE = 128
f32 = jnp.float32
bf16 = jnp.bfloat16

BASE, STARTS, CORE, PIECES = 0, 1, 5, 6


def feature_tables():
    pairs = [(a, b) for a in range(F) for b in range(a, F)]
    count = len(pairs)
    choose = np.zeros((2, 2, 128, HEADS * LANES), np.float32)
    lanes = np.zeros((8, HEADS * LANES), np.float32)
    factor = F ** (-0.25)
    for head in range(HEADS):
        at = head * LANES
        for side in range(2):
            row = side * HEADS * F + head * F
            for lane, (a, b) in enumerate(pairs):
                choose[side, 0, row + a, at + lane] = 1.0
                choose[side, 1, row + b, at + lane] = 1.0
            for a in range(F):
                choose[side, 0, row + a, at + count + a] = 1.0
        for lane, (a, b) in enumerate(pairs):
            lanes[2, at + lane] = factor * factor / math.sqrt(2.0)
            lanes[3, at + lane] = 1.0 if a == b else 2.0
        lanes[1, at + count : at + count + F + 1] = 1.0
        lanes[0, at + count + F] = 1.0
        lanes[2, at + count : at + count + F] = factor
        lanes[2, at + count + F] = 1.0
        lanes[3, at + count : at + count + F + 1] = 1.0
    lanes[4] = lanes[2] * lanes[3]
    return choose, lanes


def gain_places():
    places = np.zeros((16, 128), np.float32)
    for i in range(4):
        places[i, 64 + i] = 1.0
    return places


def mm(a, b):
    return lax.dot_general(a, b, (((1,), (0,)), ((), ())), preferred_element_type=f32)


def mm_nt(a, b):
    return lax.dot_general(a, b, (((1,), (1,)), ((), ())), preferred_element_type=f32)


def mm_tn(a, b):
    return lax.dot_general(a, b, (((0,), (0,)), ((), ())), preferred_element_type=f32)


def low_pair(part):
    high = part.astype(bf16)
    return high, (part - high.astype(f32)).astype(bf16)


def doc_of(info, position):
    count = (position >= info[STARTS]).astype(jnp.int32)
    for i in range(1, 4):
        count = count + (position >= info[STARTS + i]).astype(jnp.int32)
    return count


def column_positions(info, first, count):
    return info[BASE] + first + lax.broadcasted_iota(jnp.int32, (count, 1), 0)


def row_positions(info, first, count):
    return info[BASE] + first + lax.broadcasted_iota(jnp.int32, (1, count), 1)


def prefix_mask(info):
    before = doc_of(info, info[BASE] - 1)
    same = doc_of(info, column_positions(info, 0, ROWS)) == before
    return (same & (info[BASE] > 0)).astype(f32)


def tail_mask(info):
    last = doc_of(info, info[BASE] + ROWS - 1)
    return (doc_of(info, column_positions(info, 0, ROWS)) == last).astype(f32)


def chosen(raw, table):
    high, rest = low_pair(raw)
    left = raw - high.astype(f32) - rest.astype(f32)
    return mm(high, table) + mm(rest, table) + mm(left.astype(bf16), table)


def factors(raw, choose_ref, lanes_ref):
    return (
        chosen(raw, choose_ref[0]) + lanes_ref[0:1, :],
        chosen(raw, choose_ref[1]) + lanes_ref[1:2, :],
    )


def feature_back(gradient, left, right, choose_ref):
    total = None
    for term, table in ((gradient * right, choose_ref[0]), (gradient * left, choose_ref[1])):
        high, rest = low_pair(term)
        part = mm_nt(high, table) + mm_nt(rest, table)
        total = part if total is None else total + part
    return total


def write_packed(packed_ref, head, state, norm):
    packed_ref[head, 0:KEPT, :] = state[:KEPT].astype(bf16)
    row = lax.broadcasted_iota(jnp.int32, (16, 128), 0)
    high = norm.astype(bf16).astype(f32)
    rest = norm - high
    tile = jnp.where(row == 0, high[:, :128], 0.0)
    tile = jnp.where(row == 1, high[:, 128:], tile)
    tile = jnp.where(row == 2, rest[:, :128], tile)
    tile = jnp.where(row == 3, rest[:, 128:], tile)
    packed_ref[head, KEPT:PACKED, :] = tile.astype(bf16)


def read_total(before_ref, got_refs, head):
    total = before_ref[head]
    for ref in got_refs:
        total = total + ref[head].astype(f32)
    state = jnp.concatenate(
        [total[:KEPT], jnp.zeros((LANES - KEPT, VALUE_WIDTH), f32)], axis=0
    ).astype(bf16)
    norm = jnp.concatenate(
        [
            total[KEPT : KEPT + 1] + total[KEPT + 2 : KEPT + 3],
            total[KEPT + 1 : KEPT + 2] + total[KEPT + 3 : KEPT + 4],
        ],
        axis=1,
    )
    return state, norm


def head_lanes(head):
    return slice(head * VALUE_WIDTH, (head + 1) * VALUE_WIDTH)


def window_rows(own_ref, halo_ref, which, tile, lanes):
    first = tile * TILE
    if tile == 0:
        return jnp.concatenate([halo_ref[which, :, lanes], own_ref[0:TILE, lanes]], axis=0)
    return own_ref[first - WIN : first + TILE, lanes]


def call(body, out_shape, operands, smem=(), megabytes=40, flops=0, moved=0, scratch=()):
    specs = [
        pl.BlockSpec(memory_space=pltpu.SMEM if i in smem else pltpu.VMEM)
        for i in range(len(operands))
    ]
    return pl.pallas_call(
        body,
        out_shape=out_shape,
        in_specs=specs,
        out_specs=jax.tree.map(lambda s: pl.BlockSpec(memory_space=pltpu.VMEM), out_shape),
        scratch_shapes=scratch,
        compiler_params=pltpu.CompilerParams(vmem_limit_bytes=megabytes * 2**20),
        cost_estimate=pl.CostEstimate(
            flops=flops, bytes_accessed=moved or 8 * 2**20, transcendentals=0
        ),
    )(*operands)


def shape(*dims, dtype=bf16):
    return jax.ShapeDtypeStruct(dims, dtype)


def keys_kernel(
    info, x_ref, gain_ref, feat_ref, key_ref, value_ref, choose_ref, lanes_ref,
    normed_ref, inv_ref, raw_ref, keys_ref, values_ref, km_ref, packed_ref, edge_ref,
):
    def norm_rows(i, _):
        rows = pl.ds(pl.multiple_of(i * 64, 64), 64)
        x = x_ref[rows, :].astype(f32)
        inv = lax.rsqrt(jnp.mean(x * x, axis=-1, keepdims=True) + EPS)
        inv_ref[rows, :] = inv
        normed_ref[rows, :] = (x * inv * gain_ref[...]).astype(bf16)
        return 0

    lax.fori_loop(0, ROWS // 64, norm_rows, 0)
    normed = normed_ref[...]
    raw = mm(normed, feat_ref[...])
    raw_ref[...] = raw
    keys = mm(normed, key_ref[...]).astype(bf16)
    keys_ref[...] = keys
    values = mm(normed, value_ref[...]).astype(bf16)
    values_ref[...] = values
    edge_ref[0] = keys[ROWS - WIN :]
    edge_ref[1] = values[ROWS - WIN :]
    left, right = factors(raw, choose_ref, lanes_ref)
    features = (left * right * lanes_ref[2:3, :]).astype(bf16)
    features = (features.astype(f32) * lanes_ref[3:4, :]).astype(bf16)
    tail = tail_mask(info)
    for head in range(HEADS):
        own = features[:, head * LANES : (head + 1) * LANES]
        km_ref[head] = own
        kept = (values[:, head_lanes(head)].astype(f32) * tail).astype(bf16)
        state = mm_tn(own, kept)
        norm = jnp.sum(own.astype(f32) * tail, axis=0, keepdims=True)
        write_packed(packed_ref, head, state, norm)


def local_kernel(
    info, normed_ref, query_ref, raw_ref, choose_ref, lanes_ref, keys_ref, values_ref, km_ref,
    halo_ref, queries_ref, qf_ref, low_ref, num_ref, den_ref, probs_ref, window_ref,
):
    queries = mm(normed_ref[...], query_ref[...]).astype(bf16)
    queries_ref[...] = queries
    left, right = factors(raw_ref[...], choose_ref, lanes_ref)
    features = (left * right * lanes_ref[2:3, :]).astype(bf16)
    half = ROWS // 2
    for block in range(2):
        first, reach = block * half, (block + 1) * half
        query_at = column_positions(info, first, half)
        key_at = row_positions(info, 0, reach)
        causal = (query_at >= key_at) & (doc_of(info, query_at) == doc_of(info, key_at))
        for head in range(HEADS):
            own = features[first:reach, head * LANES : (head + 1) * LANES]
            qf_ref[head, first:reach, :] = own
            weights = jnp.where(causal, mm_nt(own, km_ref[head, :reach, :]), 0.0)
            den_ref[head, first:reach, :] = jnp.sum(weights, axis=-1, keepdims=True)
            low = weights.astype(bf16)
            low_ref[head, first:reach, 0:reach] = low
            num_ref[first:reach, head_lanes(head)] = mm(low, values_ref[:reach, head_lanes(head)])
    scale = VALUE_WIDTH ** (-0.5)
    for tile in range(ROWS // TILE):
        first = tile * TILE
        query_at = column_positions(info, first, TILE)
        key_at = row_positions(info, first - WIN, TILE + WIN)
        near = (
            (key_at <= query_at)
            & (query_at - key_at < WIN)
            & (doc_of(info, query_at) == doc_of(info, key_at))
            & (key_at >= 0)
        )
        for head in range(HEADS):
            lanes = head_lanes(head)
            key_rows = window_rows(keys_ref, halo_ref, 0, tile, lanes)
            value_rows = window_rows(values_ref, halo_ref, 1, tile, lanes)
            logits = mm_nt(queries[first : first + TILE, lanes], key_rows) * scale
            logits = jnp.where(near, logits, -1e30)
            exps = jnp.exp(logits - jnp.max(logits, axis=-1, keepdims=True))
            probs = exps / jnp.sum(exps, axis=-1, keepdims=True)
            probs_ref[head, tile] = probs
            window_ref[first : first + TILE, lanes] = mm(probs.astype(bf16), value_rows)


def mixed_kernel(
    info, before_ref, got1_ref, got2_ref, got3_ref, qf_ref, num_ref, den_ref, window_ref, out_ref,
    linear_ref, total_den_ref, mixed_ref, state_ref, norm_ref, own_ref, other_ref,
):
    use = prefix_mask(info)
    for head in range(HEADS):
        lanes = head_lanes(head)
        state, norm = read_total(before_ref, (got1_ref, got2_ref, got3_ref), head)
        state_ref[head] = state
        norm_ref[head] = jnp.broadcast_to(norm, (8, LANES))
        features = qf_ref[head]
        inter = mm(features, state) * use
        den = jnp.sum(features.astype(f32) * norm, axis=-1, keepdims=True) * use + den_ref[head]
        total_den_ref[head] = den
        linear = (inter + num_ref[:, lanes]) / den
        linear_ref[:, lanes] = linear
        mixed_ref[:, lanes] = (linear + window_ref[:, lanes]).astype(bf16)
    half = ROWS // 2
    core = info[CORE]
    weights = out_ref[...]
    other = mixed_ref[pl.ds(pl.multiple_of((1 - core) * half, half), half), :]
    other_ref[...] = mm(other, weights).astype(bf16)
    own = mixed_ref[pl.ds(pl.multiple_of(core * half, half), half), :]
    own_ref[...] = mm(own, weights)


def ffn_grads_kernel(normed_ref, top_ref, gate_ref, up_ref, act_ref, out_ref):
    hidden = gate_ref.shape[1]
    normed = normed_ref[...]
    out_ref[:, 0:hidden] = mm_tn(normed, gate_ref[...]).astype(bf16)
    out_ref[:, hidden : 2 * hidden] = mm_tn(normed, up_ref[...]).astype(bf16)
    out_ref[:, 2 * hidden : 3 * hidden] = mm_tn(top_ref[...], act_ref[...]).astype(bf16)


def mixed_back_kernel(
    info, p0, p1, p2, p3, s0, s1, s2, s3, out_ref, linear_ref, den_ref, qf_ref,
    top_ref, gm_ref, gnum_ref, gden_ref, packed_ref,
):
    for i, piece in enumerate((p0, p1, p2, p3, s0, s1, s2, s3)):
        top_ref[pl.ds(pl.multiple_of(info[PIECES + i], 64), 64), :] = piece[...]
    grad_mixed = mm_nt(top_ref[...], out_ref[...]).astype(bf16)
    gm_ref[...] = grad_mixed
    use = prefix_mask(info)
    for head in range(HEADS):
        lanes = head_lanes(head)
        wide = grad_mixed[:, lanes].astype(f32)
        den = den_ref[head]
        grad_num = (wide / den).astype(bf16)
        gnum_ref[:, lanes] = grad_num
        grad_den = -jnp.sum(wide * linear_ref[:, lanes], axis=-1, keepdims=True) / den
        gden_ref[head] = grad_den
        features = qf_ref[head]
        used = (grad_num.astype(f32) * use).astype(bf16)
        state = mm_tn(features, used)
        norm = jnp.sum(features.astype(f32) * (grad_den * use), axis=0, keepdims=True)
        write_packed(packed_ref, head, state, norm)


def local_back_kernel(
    info, gm_ref, gnum_ref, gden_ref, probs_ref, keys_ref, values_ref, halo_ref, queries_ref,
    low_ref, km_ref, qf_ref, state_ref, norm_ref, raw_ref, choose_ref, lanes_ref,
    gq_ref, gfeat_ref, gk_ref, gv_ref, gkf_ref, edge_ref, key_acc, value_acc,
):
    scale = VALUE_WIDTH ** (-0.5)
    key_acc[...] = jnp.zeros_like(key_acc)
    value_acc[...] = jnp.zeros_like(value_acc)
    for tile in range(ROWS // TILE):
        first = tile * TILE
        reach = slice(first, first + TILE + WIN)
        for head in range(HEADS):
            lanes = head_lanes(head)
            key_rows = window_rows(keys_ref, halo_ref, 0, tile, lanes)
            value_rows = window_rows(values_ref, halo_ref, 1, tile, lanes)
            top = gm_ref[first : first + TILE, lanes]
            probs = probs_ref[head, tile]
            grad_probs = mm_nt(top, value_rows)
            shared = jnp.sum(grad_probs * probs, axis=-1, keepdims=True)
            grad_logits = (probs * (grad_probs - shared)).astype(bf16)
            gq_ref[first : first + TILE, lanes] = (mm(grad_logits, key_rows) * scale).astype(bf16)
            queries = queries_ref[first : first + TILE, lanes]
            key_acc[reach, lanes] += mm_tn(grad_logits, queries) * scale
            value_acc[reach, lanes] += mm_tn(probs.astype(bf16), top)
    edge_ref[0] = key_acc[0:WIN, :].astype(bf16)
    edge_ref[1] = value_acc[0:WIN, :].astype(bf16)
    gk_ref[...] = key_acc[WIN:, :]
    use = prefix_mask(info)
    left, right = factors(raw_ref[...], choose_ref, lanes_ref)
    half = ROWS // 2
    grads = [[None, None], [None, None]]
    for head in range(HEADS):
        lanes = head_lanes(head)
        inter = mm_nt((gnum_ref[:, lanes].astype(f32) * use).astype(bf16), state_ref[head])
        inter = inter + (gden_ref[head] * use) * norm_ref[head, 0:1, :]
        gkf = None
        gvl = None
        for block in range(2):
            first, reach = block * half, (block + 1) * half
            query_at = column_positions(info, first, half)
            key_at = row_positions(info, 0, reach)
            causal = (query_at >= key_at) & (doc_of(info, query_at) == doc_of(info, key_at))
            grad_num = gnum_ref[first:reach, lanes]
            grad = mm_nt(grad_num, values_ref[:reach, lanes]) + gden_ref[head, first:reach, :]
            grad = jnp.where(causal, grad, 0.0).astype(bf16)
            grads[head][block] = mm(grad, km_ref[head, :reach, :]) + inter[first:reach]
            key_part = mm_tn(grad, qf_ref[head, first:reach, :])
            value_part = mm_tn(low_ref[head, first:reach, 0:reach], grad_num)
            if block == 0:
                gkf_ref[head] = jnp.concatenate([key_part, jnp.zeros_like(key_part)], axis=0)
                gv_ref[0:half, lanes] = value_acc[WIN : WIN + half, lanes] + value_part
                gv_ref[half:, lanes] = value_acc[WIN + half :, lanes]
            else:
                gkf_ref[head] += key_part
                gv_ref[:, lanes] += value_part
    gradient = jnp.concatenate([jnp.concatenate(g, axis=0) for g in grads], axis=1)
    gradient = gradient * lanes_ref[2:3, :]
    gfeat_ref[...] = feature_back(gradient, left, right, choose_ref)


def keys_back_kernel(
    info, before_ref, got1_ref, got2_ref, got3_ref, values_ref, km_ref, gkf_ref, gk_ref, gv_ref,
    right_ref, raw_ref, choose_ref, lanes_ref, gq_ref, gfeat_ref, wq_ref, wk_ref, wv_ref, wf_ref,
    x_ref, inv_ref,
    gkw_ref, gvw_ref, gf_ref, own_ref, other_ref, gain_ref, acc_ref,
):
    tail = tail_mask(info)
    inner = ROWS - WIN
    gkw_ref[0:inner, :] = gk_ref[0:inner, :].astype(bf16)
    gkw_ref[inner:, :] = (gk_ref[inner:, :] + right_ref[0].astype(f32)).astype(bf16)
    gradients = []
    for head in range(HEADS):
        lanes = head_lanes(head)
        later, norm = read_total(before_ref, (got1_ref, got2_ref, got3_ref), head)
        kept = (values_ref[:, lanes].astype(f32) * tail).astype(bf16)
        gradients.append(gkf_ref[head] + mm_nt(kept, later) + tail * norm)
        grad_values = gv_ref[:, lanes] + mm(km_ref[head], later) * tail
        gvw_ref[0:inner, lanes] = grad_values[0:inner].astype(bf16)
        gvw_ref[inner:, lanes] = (grad_values[inner:] + right_ref[1, :, lanes].astype(f32)).astype(
            bf16
        )
    left, right = factors(raw_ref[...], choose_ref, lanes_ref)
    gradient = jnp.concatenate(gradients, axis=1) * lanes_ref[4:5, :]
    gf_ref[...] = (feature_back(gradient, left, right, choose_ref) + gfeat_ref[...]).astype(bf16)
    half = ROWS // 2
    core = info[CORE]
    gain = None
    for mine in (False, True):
        rows = pl.ds(pl.multiple_of((core if mine else 1 - core) * half, half), half)
        for piece in range(4):
            span = slice(piece * 512, (piece + 1) * 512)
            part = mm_nt(gq_ref[rows, :], wq_ref[span, :])
            part = part + mm_nt(gkw_ref[rows, :], wk_ref[span, :])
            part = part + mm_nt(gvw_ref[rows, :], wv_ref[span, :])
            part = part + mm_nt(gf_ref[rows, :], wf_ref[span, :])
            if mine:
                own_ref[:, span] = part
            else:
                other_ref[:, span] = part.astype(bf16)
            scaled = part * (x_ref[rows, span].astype(f32) * inv_ref[rows, :])
            total = jnp.sum(scaled, axis=0, keepdims=True)
            acc_ref[0:1, span] = total + acc_ref[0:1, span] if mine else total
    gain_ref[...] = jnp.broadcast_to(acc_ref[0:1, :], gain_ref.shape)


def mix_grads_kernel(
    normed_ref, top_ref, gq_ref, gk_ref, gv_ref, gf_ref, mixed_ref, gains_ref, places_ref, out_ref
):
    normed = normed_ref[...]
    shape3 = (2, 128, 256)
    out_ref[:, :, 0:256] = mm_tn(normed, gq_ref[...]).astype(bf16).reshape(shape3)
    out_ref[:, :, 256:512] = mm_tn(normed, gk_ref[...]).astype(bf16).reshape(shape3)
    out_ref[:, :, 512:768] = mm_tn(normed, gv_ref[...]).astype(bf16).reshape(shape3)
    out_ref[:, :, 768:1024] = mm_tn(top_ref[...], mixed_ref[...]).astype(bf16).reshape(shape3)
    last = mm_tn(normed, gf_ref[...]) + mm_tn(gains_ref[...], places_ref[...])
    out_ref[:, :, 1024:1152] = last.astype(bf16).reshape(2, 128, 128)


def along_y(distance):
    return [(i, (i + 2 * distance) % 8) for i in range(8)]


def sibling():
    return [(i, i ^ 1) for i in range(8)]


def along_x(distance):
    return [(i, (i + 4 * distance) % 16) for i in range(16)]


def along_z(distance):
    return [(4 * a + z, 4 * a + (z + distance) % 4) for a in range(4) for z in range(4)]


def pick(stack, index):
    return lax.dynamic_index_in_dim(stack, index, 0, keepdims=False)


def head_sum_scatter(own, other):
    y = lax.axis_index("head") // 2
    got = lax.ppermute(other, "head", sibling())
    rows, width = own.shape
    own = own.reshape(4, rows // 4, width)
    got = got.reshape(4, rows // 4, width)

    def quarter(index):
        return pick(own, index) + pick(got, index).astype(f32)

    parts = [
        lax.ppermute(quarter((y + d) % 4).astype(bf16), "head", along_y(d)).astype(f32)
        for d in (1, 2, 3)
    ]
    return quarter(y) + parts[0] + parts[1] + parts[2]


def head_pieces(own):
    pieces = [own] + [lax.ppermute(own, "head", along_y(d)) for d in (1, 2, 3)]
    return pieces + [lax.ppermute(piece, "head", sibling()) for piece in pieces]


def piece_rows(count):
    me = lax.axis_index("head")
    y, core = me // 2, me % 2
    first = [core * 4 * count + (y + 4 - d) % 4 * count for d in range(4)]
    return first + [(1 - core) * 4 * count + (y + 4 - d) % 4 * count for d in range(4)]


def assemble(pieces):
    count, width = pieces[0].shape
    whole = jnp.zeros((8 * count, width), pieces[0].dtype)
    for piece, first in zip(pieces, piece_rows(count)):
        whole = lax.dynamic_update_slice_in_dim(whole, piece, first, 0)
    return whole


def assemble_kernel(info, p0, p1, p2, p3, s0, s1, s2, s3, out_ref):
    for i, piece in enumerate((p0, p1, p2, p3, s0, s1, s2, s3)):
        rows = pl.ds(pl.multiple_of(info[PIECES + i], 64), 64)
        out_ref[rows, :] = piece[...].astype(out_ref.dtype)


def own_rows(block):
    me = lax.axis_index("head")
    y, core = me // 2, me % 2
    count = block.shape[0] // 8
    return lax.dynamic_slice_in_dim(block, core * 4 * count + y * count, count, 0)


def small_head_sum(part):
    total = part + lax.ppermute(part, "head", sibling())
    got = [lax.ppermute(total, "head", along_y(d)) for d in (1, 2, 3)]
    return total + got[0] + got[1] + got[2]


def repack(total):
    norm = total[:, KEPT : KEPT + 2] + total[:, KEPT + 2 : KEPT + 4]
    high = norm.astype(bf16)
    rest = (norm - high.astype(f32)).astype(bf16)
    return jnp.concatenate(
        [total[:, :KEPT].astype(bf16), high, rest, total[:, KEPT + 4 :].astype(bf16)], axis=1
    )


def exclusive_parts(own, reverse):
    me = lax.axis_index("seq")
    xx, zz = me // 4, me % 4
    sign = -1 if reverse else 1
    place_x, place_z = (3 - xx, 3 - zz) if reverse else (xx, zz)
    before = jnp.zeros(own.shape, f32)
    for d in (1, 2, 3):
        got = lax.ppermute(own, "seq", along_x(sign * d)).astype(f32)
        before = before + jnp.where(place_x >= d, got, 0.0)
    low_before = repack(before)
    low_with = repack(before + own.astype(f32))
    got = [
        lax.ppermute(jnp.where(place_z + d < 4, low_with, low_before), "seq", along_z(sign * d))
        for d in (1, 2, 3)
    ]
    return [before] + got


def shifted(block, distance):
    route = [(i - distance, i) for i in range(16) if 0 <= i - distance < 16]
    return lax.ppermute(block, "seq", route)


def norm_back(in_rows, inv_rms, gain, grad_normed):
    weighted = grad_normed * gain
    return inv_rms * weighted - in_rows * inv_rms**3 * jnp.mean(
        weighted * in_rows, axis=-1, keepdims=True
    )


def shards(
    inputs,
    gain_mix,
    feat_query,
    feat_key,
    win_query,
    win_key,
    value_proj,
    out_proj,
    gain_ffn,
    gate_proj,
    up_proj,
    down_proj,
    document_starts,
    cotangent,
):
    me = lax.axis_index("head")
    base = lax.axis_index("seq") * ROWS
    info = jnp.stack([base, *document_starts[0], me % 2, *piece_rows(64)]).astype(jnp.int32)
    choose, lanes = feature_tables()
    choose = jnp.asarray(choose, bf16)
    lanes = jnp.asarray(lanes, f32)
    choose_q, choose_k = choose[0], choose[1]
    feat = jnp.concatenate([feat_query, feat_key, jnp.zeros((2048, 64), bf16)], axis=1)
    gain_row = gain_mix.reshape(1, -1)
    model = inputs.shape[1]
    width = HEADS * VALUE_WIDTH
    hidden = gate_proj.shape[1]
    head_rows = HEADS * ROWS

    with jax.named_scope("keys"):
        normed, inv_mix, raw, keys, values, km, packed, edge = call(
            keys_kernel,
            (
                shape(ROWS, model), shape(ROWS, 1, dtype=f32), shape(ROWS, 128, dtype=f32),
                shape(ROWS, width), shape(ROWS, width), shape(HEADS, ROWS, LANES),
                shape(HEADS, PACKED, 128), shape(2, WIN, width),
            ),
            (info, inputs, gain_row, feat, win_key, value_proj, choose_k, lanes),
            smem=(0,), flops=2 * ROWS * model * 640, moved=7 * 2**20,
        )
    halo = shifted(edge, 1)
    sums = exclusive_parts(packed, False)
    with jax.named_scope("local"):
        queries, qf, low, num, den, probs, window = call(
            local_kernel,
            (
                shape(ROWS, width), shape(HEADS, ROWS, LANES), shape(HEADS, ROWS, ROWS),
                shape(ROWS, width, dtype=f32), shape(HEADS, ROWS, 1, dtype=f32),
                shape(HEADS, 4, TILE, TILE + WIN, dtype=f32), shape(ROWS, width, dtype=f32),
            ),
            (info, normed, win_query, raw, choose_q, lanes, keys, values, km, halo),
            smem=(0,), flops=2 * ROWS * model * 512, moved=9 * 2**20,
        )
    with jax.named_scope("mixed"):
        linear, total_den, mixed, state, norm, own, other = call(
            mixed_kernel,
            (
                shape(ROWS, width, dtype=f32), shape(HEADS, ROWS, 1, dtype=f32),
                shape(ROWS, width), shape(HEADS, LANES, VALUE_WIDTH),
                shape(HEADS, 8, LANES, dtype=f32), shape(ROWS // 2, model, dtype=f32),
                shape(ROWS // 2, model),
            ),
            (info, *sums, qf, num, den, window, out_proj),
            smem=(0,), flops=2 * ROWS * model * 300, moved=8 * 2**20,
        )
    x_own = own_rows(inputs).astype(f32)
    resid = x_own + head_sum_scatter(own, other)
    inv_ffn = lax.rsqrt(jnp.mean(resid * resid, axis=-1, keepdims=True) + EPS)
    pieces = head_pieces((resid * inv_ffn * gain_ffn).astype(bf16))
    with jax.named_scope("assemble"):
        normed_ffn = call(
            assemble_kernel, shape(ROWS, model), (info, *pieces), smem=(0,), moved=4 * 2**20
        )
    gate = mm(normed_ffn, gate_proj)
    up_value = mm(normed_ffn, up_proj)
    sigmoid_gate = jax.nn.sigmoid(gate)
    silu_gate = gate * sigmoid_gate
    activation = (silu_gate * up_value).astype(bf16)
    grad_act = mm_nt(cotangent, down_proj)
    grad_gate = (grad_act * up_value * sigmoid_gate * (1.0 + gate * (1.0 - sigmoid_gate))).astype(
        bf16
    )
    grad_up = (grad_act * silu_gate).astype(bf16)
    core = me % 2
    half = ROWS // 2

    def half_rows(block, which):
        return lax.dynamic_slice_in_dim(block, which * half, half, 0)

    def ffn_back(which):
        return mm_nt(half_rows(grad_gate, which), gate_proj) + mm_nt(
            half_rows(grad_up, which), up_proj
        )

    grad_normed_ffn = head_sum_scatter(ffn_back(core), ffn_back(1 - core).astype(bf16))
    with jax.named_scope("ffn_grads"):
        ffn_grads = pl.pallas_call(
            ffn_grads_kernel,
            grid=(8,),
            in_specs=[
                pl.BlockSpec((ROWS, model // 8), lambda i: (0, i)),
                pl.BlockSpec((ROWS, model // 8), lambda i: (0, i)),
                pl.BlockSpec((ROWS, hidden), lambda i: (0, 0)),
                pl.BlockSpec((ROWS, hidden), lambda i: (0, 0)),
                pl.BlockSpec((ROWS, hidden), lambda i: (0, 0)),
            ],
            out_specs=pl.BlockSpec((model // 8, 3 * hidden), lambda i: (i, 0)),
            out_shape=shape(model, 3 * hidden),
            compiler_params=pltpu.CompilerParams(vmem_limit_bytes=32 * 2**20),
            cost_estimate=pl.CostEstimate(
                flops=6 * ROWS * model * hidden, bytes_accessed=15 * 2**20, transcendentals=0
            ),
        )(normed_ffn, cotangent, grad_gate, grad_up, activation)
    ffn_grads = lax.psum_scatter(ffn_grads, "seq", scatter_dimension=0, tiled=True).astype(f32)
    grad_gain_ffn = jnp.sum(grad_normed_ffn * resid * inv_ffn, axis=0)
    grad_resid = own_rows(cotangent).astype(f32) + norm_back(
        resid, inv_ffn, gain_ffn, grad_normed_ffn
    )
    pieces = head_pieces(grad_resid.astype(bf16))
    with jax.named_scope("mixed_back"):
        top, grad_mixed, grad_num, grad_den, packed = call(
            mixed_back_kernel,
            (
                shape(ROWS, model), shape(ROWS, width), shape(ROWS, width),
                shape(HEADS, ROWS, 1, dtype=f32), shape(HEADS, PACKED, 128),
            ),
            (info, *pieces, out_proj, linear, total_den, qf),
            smem=(0,), flops=2 * ROWS * model * 300, moved=7 * 2**20,
        )
    sums = exclusive_parts(packed, True)
    with jax.named_scope("local_back"):
        gq, gfeat, gk, gv, gkf, edge = call(
            local_back_kernel,
            (
                shape(ROWS, width), shape(ROWS, 128, dtype=f32), shape(ROWS, width, dtype=f32),
                shape(ROWS, width, dtype=f32), shape(HEADS, ROWS, LANES, dtype=f32),
                shape(2, WIN, width),
            ),
            (
                info, grad_mixed, grad_num, grad_den, probs, keys, values, halo, queries, low, km,
                qf, state, norm, raw, choose_q, lanes,
            ),
            smem=(0,), flops=2 * ROWS * model * 600, moved=9 * 2**20,
            scratch=[pltpu.VMEM((ROWS + WIN, width), f32)] * 2,
        )
    right = shifted(edge, -1)
    ffn_own = mm(half_rows(activation, core), down_proj)
    ffn_other = mm(half_rows(activation, 1 - core), down_proj).astype(bf16)
    output_pieces = head_pieces((resid + head_sum_scatter(ffn_own, ffn_other)).astype(bf16))
    with jax.named_scope("assemble"):
        output = call(
            assemble_kernel, shape(ROWS, model), (info, *output_pieces), smem=(0,), moved=4 * 2**20
        )
    with jax.named_scope("keys_back"):
        gkw, gvw, gf, own, other, gain_part = call(
            keys_back_kernel,
            (
                shape(ROWS, width), shape(ROWS, width), shape(ROWS, 128),
                shape(half, model, dtype=f32), shape(half, model), shape(8, model, dtype=f32),
            ),
            (
                info, *sums, values, km, gkf, gk, gv, right, raw, choose_k, lanes, gq, gfeat,
                win_query, win_key, value_proj, feat, inputs, inv_mix,
            ),
            smem=(0,), flops=2 * ROWS * model * 900, moved=14 * 2**20,
            scratch=[pltpu.VMEM((8, model), f32)],
        )
    grad_normed = head_sum_scatter(own, other)
    gains = jnp.stack(low_pair(gain_part[0]) + low_pair(grad_gain_ffn), axis=0)
    gains = jnp.pad(gains, ((0, 12), (0, 0)))
    with jax.named_scope("mix_grads"):
        whole = pl.BlockSpec((ROWS, width), lambda i: (0, 0))
        mix_grads = pl.pallas_call(
            mix_grads_kernel,
            grid=(8,),
            in_specs=[
                pl.BlockSpec((ROWS, model // 8), lambda i: (0, i)),
                pl.BlockSpec((ROWS, model // 8), lambda i: (0, i)),
                whole, whole, whole,
                pl.BlockSpec((ROWS, 128), lambda i: (0, 0)),
                whole,
                pl.BlockSpec((16, model // 8), lambda i: (0, i)),
                pl.BlockSpec((16, 128), lambda i: (0, 0)),
            ],
            out_specs=pl.BlockSpec((2, 128, 1152), lambda i: (i, 0, 0)),
            out_shape=shape(16, 128, 1152),
            compiler_params=pltpu.CompilerParams(vmem_limit_bytes=32 * 2**20),
            cost_estimate=pl.CostEstimate(
                flops=2 * ROWS * model * 1152, bytes_accessed=11 * 2**20, transcendentals=0
            ),
        )(normed, top, gq, gkw, gvw, gf, mixed, gains, jnp.asarray(gain_places(), bf16))
    mix_grads = lax.all_to_all(mix_grads, "seq", 0, 0)
    mix_grads = jnp.sum(mix_grads.astype(f32), axis=0)
    x_pieces = head_pieces(
        (grad_resid + norm_back(x_own, own_rows(inv_mix), gain_mix, grad_normed)).astype(bf16)
    )
    with jax.named_scope("assemble"):
        grad_x = call(
            assemble_kernel, shape(ROWS, model, dtype=f32), (info, *x_pieces), smem=(0,),
            moved=6 * 2**20,
        )
    gains = small_head_sum(mix_grads[:, 1088:1092].T)
    return (
        output,
        grad_x,
        gains[0] + gains[1],
        mix_grads[:, 1024:1056],
        mix_grads[:, 1056:1088],
        mix_grads[:, :256],
        mix_grads[:, 256:512],
        mix_grads[:, 512:768],
        mix_grads[:, 768:1024].T,
        gains[2] + gains[3],
        ffn_grads[:, :hidden],
        ffn_grads[:, hidden : 2 * hidden],
        ffn_grads[:, 2 * hidden :].T,
    )


def solution(mesh):
    placed = (
        P("seq", None),
        P(),
        P(None, "head"),
        P(None, "head"),
        P(None, "head"),
        P(None, "head"),
        P(None, "head"),
        P("head", None),
        P(),
        P(None, "head"),
        P(None, "head"),
        P("head", None),
        P(),
        P("seq", None),
    )
    return jax.shard_map(
        shards,
        mesh=mesh,
        in_specs=placed,
        out_specs=(
            P("seq", None),
            P("seq", None),
            P("seq"),
            P("seq", "head"),
            P("seq", "head"),
            P("seq", "head"),
            P("seq", "head"),
            P("seq", "head"),
            P("head", "seq"),
            P("seq"),
            P("seq", "head"),
            P("seq", "head"),
            P("head", "seq"),
        ),
        check_vma=False,
    )
```

```python
import functools
import math

import jax
import jax.numpy as jnp
import numpy as np
from jax import lax
from jax.experimental import pallas as pl
from jax.experimental.pallas import tpu as pltpu
from jax.sharding import PartitionSpec as P

F = 16
VALUE_WIDTH = 128
WIN = 64
EPS = 1e-05

HEADS = 2
ROWS = 512
LANES = 256
KEPT = 160
PACKED = 176
TILE = 128
OWN = 64
f32 = jnp.float32
bf16 = jnp.bfloat16


def feature_tables():
    pairs = [(a, b) for a in range(F) for b in range(a, F)]
    count = len(pairs)
    choose = np.zeros((2, 2, 128, HEADS * LANES), np.float32)
    lanes = np.zeros((8, HEADS * LANES), np.float32)
    factor = F ** (-0.25)
    for head in range(HEADS):
        at = head * LANES
        for side in range(2):
            row = side * HEADS * F + head * F
            for lane, (a, b) in enumerate(pairs):
                choose[side, 0, row + a, at + lane] = 1.0
                choose[side, 1, row + b, at + lane] = 1.0
            for a in range(F):
                choose[side, 0, row + a, at + count + a] = 1.0
        for lane, (a, b) in enumerate(pairs):
            lanes[2, at + lane] = factor * factor / math.sqrt(2.0)
            lanes[3, at + lane] = 1.0 if a == b else 2.0
        lanes[1, at + count : at + count + F + 1] = 1.0
        lanes[0, at + count + F] = 1.0
        lanes[2, at + count : at + count + F] = factor
        lanes[2, at + count + F] = 1.0
        lanes[3, at + count : at + count + F + 1] = 1.0
    lanes[4] = lanes[2] * lanes[3]
    return choose, lanes


def mm(a, b):
    return lax.dot_general(a, b, (((1,), (0,)), ((), ())), preferred_element_type=f32)


def mm_nt(a, b):
    return lax.dot_general(a, b, (((1,), (1,)), ((), ())), preferred_element_type=f32)


def mm_tn(a, b):
    return lax.dot_general(a, b, (((0,), (0,)), ((), ())), preferred_element_type=f32)


def low_pair(part):
    high = part.astype(bf16)
    return high, (part - high.astype(f32)).astype(bf16)


class Place:

    def __init__(self, starts_ref):
        me = lax.axis_index("head")
        self.base = lax.axis_index("seq") * ROWS
        self.y = lax.shift_right_logical(me, 1)
        self.core = lax.bitwise_and(me, 1)
        self.starts = None if starts_ref is None else [starts_ref[0, i] for i in range(4)]

    def rows(self, distance, other=False):
        quarter = lax.bitwise_and(self.y + distance, 3)
        core = 1 - self.core if other else self.core
        return pl.ds(pl.multiple_of(core * (ROWS // 2) + quarter * OWN, OWN), OWN)


class Loaded:

    def __init__(self, ref, copies):
        self.ref, self.copies = ref, copies
        self.shape = ref.shape

    def ready(self):
        for copy in self.copies:
            copy.wait()
        self.copies = []

    def __getitem__(self, index):
        self.ready()
        return self.ref[index]


class Stored:

    def __init__(self, ref, copy):
        self.ref, self.copy, self.sent = ref, copy, False
        self.shape, self.dtype = ref.shape, ref.dtype

    def __getitem__(self, index):
        return self.ref[index]

    def __setitem__(self, index, value):
        self.ref[index] = value

    def send(self):
        if not self.sent:
            self.copy.start()
        self.sent = True


def doc_of(info, position):
    count = (position >= info.starts[0]).astype(jnp.int32)
    for start in info.starts[1:]:
        count = count + (position >= start).astype(jnp.int32)
    return count


def column_positions(info, first, count):
    return info.base + first + lax.broadcasted_iota(jnp.int32, (count, 1), 0)


def row_positions(info, first, count):
    return info.base + first + lax.broadcasted_iota(jnp.int32, (1, count), 1)


def prefix_mask(info):
    before = doc_of(info, info.base - 1)
    same = doc_of(info, column_positions(info, 0, ROWS)) == before
    return (same & (info.base > 0)).astype(f32)


def tail_mask(info):
    last = doc_of(info, info.base + ROWS - 1)
    return (doc_of(info, column_positions(info, 0, ROWS)) == last).astype(f32)


def chosen(raw, table):
    high, rest = low_pair(raw)
    left = raw - high.astype(f32) - rest.astype(f32)
    return mm(high, table) + mm(rest, table) + mm(left.astype(bf16), table)


def factors(raw, choose_ref, lanes_ref):
    return (
        chosen(raw, choose_ref[0]) + lanes_ref[0:1, :],
        chosen(raw, choose_ref[1]) + lanes_ref[1:2, :],
    )


def feature_back(gradient, left, right, choose_ref):
    total = None
    for term, table in ((gradient * right, choose_ref[0]), (gradient * left, choose_ref[1])):
        high, rest = low_pair(term)
        part = mm_nt(high, table) + mm_nt(rest, table)
        total = part if total is None else total + part
    return total


def write_packed(packed_ref, head, state, norm):
    packed_ref[head, 0:KEPT, :] = state[:KEPT].astype(bf16)
    row = lax.broadcasted_iota(jnp.int32, (16, 128), 0)
    high = norm.astype(bf16).astype(f32)
    rest = norm - high
    tile = jnp.where(row == 0, high[:, :128], 0.0)
    tile = jnp.where(row == 1, high[:, 128:], tile)
    tile = jnp.where(row == 2, rest[:, :128], tile)
    tile = jnp.where(row == 3, rest[:, 128:], tile)
    packed_ref[head, KEPT:PACKED, :] = tile.astype(bf16)


def read_total(before_ref, got_refs, head):
    total = before_ref[head]
    for ref in got_refs:
        total = total + ref[head].astype(f32)
    state = jnp.concatenate(
        [total[:KEPT], jnp.zeros((LANES - KEPT, VALUE_WIDTH), f32)], axis=0
    ).astype(bf16)
    norm = jnp.concatenate(
        [
            total[KEPT : KEPT + 1] + total[KEPT + 2 : KEPT + 3],
            total[KEPT + 1 : KEPT + 2] + total[KEPT + 3 : KEPT + 4],
        ],
        axis=1,
    )
    return state, norm


def head_lanes(head):
    return slice(head * VALUE_WIDTH, (head + 1) * VALUE_WIDTH)


def window_rows(own_ref, halo_ref, which, tile, lanes):
    first = tile * TILE
    if tile == 0:
        return jnp.concatenate([halo_ref[which, :, lanes], own_ref[0:TILE, lanes]], axis=0)
    return own_ref[first - WIN : first + TILE, lanes]


def call(body, out_shape, operands, starts=None, megabytes=48, flops=0, scratch=()):
    operands = [o if isinstance(o, tuple) else ([o], o.shape, None) for o in operands]
    arrays = [a for group, _, _ in operands for a in group]
    out_shape = tuple(out_shape)
    count_in, count_out = len(arrays), len(out_shape)
    moves = sum(
        len(group) if places is None else places(None) for group, _, places in operands
    )
    named = starts is not None

    def kernel(*refs):
        info = Place(refs[0] if named else None)
        refs = refs[1:] if named else refs
        sources, targets = refs[:count_in], refs[count_in : count_in + count_out]
        rest = refs[count_in + count_out :]
        buffers, rest = rest[: len(operands)], rest[len(operands) :]
        results, rest = rest[:count_out], rest[count_out:]
        sems, extra = rest[0], rest[1:]
        loaded, at, sem = [], 0, 0
        for (group, _, places), buffer in zip(operands, buffers):
            own = sources[at : at + len(group)]
            at += len(group)
            pairs = [(own[0], buffer)] if places is None else places(info, own, buffer)
            copies = []
            for source, target in pairs:
                copies.append(pltpu.make_async_copy(source, target, sems.at[sem]))
                copies[-1].start()
                sem += 1
            loaded.append(Loaded(buffer, copies))
        stored = [
            Stored(buffer, pltpu.make_async_copy(buffer, target, sems.at[moves + i]))
            for i, (buffer, target) in enumerate(zip(results, targets))
        ]
        body(info, *loaded, *stored, *extra)
        for item in loaded:
            item.ready()
        for item in stored:
            item.send()
        for item in stored:
            item.copy.wait()

    specs = [pl.BlockSpec(memory_space=pl.ANY)] * count_in
    if named:
        specs = [pl.BlockSpec(memory_space=pltpu.SMEM)] + specs
    moved = sum(a.size * a.dtype.itemsize for a in arrays)
    moved += sum(math.prod(s.shape) * s.dtype.itemsize for s in out_shape)
    return pl.pallas_call(
        kernel,
        out_shape=out_shape,
        in_specs=specs,
        out_specs=tuple(pl.BlockSpec(memory_space=pl.ANY) for _ in out_shape),
        scratch_shapes=[pltpu.VMEM(tuple(dims), group[0].dtype) for group, dims, _ in operands]
        + [pltpu.VMEM(s.shape, s.dtype) for s in out_shape]
        + [pltpu.SemaphoreType.DMA((moves + count_out,))]
        + list(scratch),
        compiler_params=pltpu.CompilerParams(vmem_limit_bytes=megabytes * 2**20),
        cost_estimate=pl.CostEstimate(flops=flops, bytes_accessed=moved, transcendentals=0),
    )(*([starts] if named else []), *arrays)


def feature_weights(feat_query_t, feat_key_t):
    def places(info, sources=None, buffer=None):
        if info is None:
            return 2
        return [(sources[0], buffer.at[0:32]), (sources[1], buffer.at[32:64])]

    return [feat_query_t, feat_key_t], (128, feat_query_t.shape[1]), places


def gathered(pieces):
    def places(info, sources=None, buffer=None):
        if info is None:
            return 8
        pairs = []
        for i, source in enumerate(sources):
            rows = info.rows(4 - i % 4, other=i >= 4)
            pairs.append((source.at[0:OWN], buffer.at[rows]))
        return pairs

    return list(pieces), (ROWS, pieces[0].shape[1]), places


def gathered_extra(pieces):
    def places(info, sources=None, buffer=None):
        if info is None:
            return 8
        return [
            (source.at[OWN : OWN + 16], buffer.at[16 * i : 16 * i + 16])
            for i, source in enumerate(sources)
        ]

    return list(pieces), (128, pieces[0].shape[1]), places


def own_part(block):
    def places(info, sources=None, buffer=None):
        if info is None:
            return 1
        return [(sources[0].at[info.rows(0)], buffer)]

    return [block], (OWN, block.shape[1]), places


def shape(*dims, dtype=bf16):
    return jax.ShapeDtypeStruct(dims, dtype)


def keys_kernel(
    info, x_ref, gain_ref, key_ref, value_ref, feat_ref, choose_ref, lanes_ref,
    normed_ref, inv_ref, raw_ref, keys_ref, values_ref, km_ref, packed_ref, edge_ref,
):
    def norm_rows(i, _):
        rows = pl.ds(pl.multiple_of(i * 64, 64), 64)
        x = x_ref[rows, :].astype(f32)
        inv = lax.rsqrt(jnp.mean(x * x, axis=-1, keepdims=True) + EPS)
        inv_ref[rows, :] = inv
        normed_ref[rows, :] = (x * inv * gain_ref[...]).astype(bf16)
        return 0

    x_ref.ready()
    gain_ref.ready()
    lax.fori_loop(0, ROWS // 64, norm_rows, 0)
    normed_ref.send()
    inv_ref.send()
    normed = normed_ref[...]
    keys = mm(normed, key_ref[...]).astype(bf16)
    keys_ref[...] = keys
    keys_ref.send()
    values = mm(normed, value_ref[...]).astype(bf16)
    values_ref[...] = values
    values_ref.send()
    edge_ref[0] = keys[ROWS - WIN :]
    edge_ref[1] = values[ROWS - WIN :]
    edge_ref.send()
    feat_ref.ready()
    feat_ref.ref[64:128, :] = jnp.zeros((64, feat_ref.shape[1]), bf16)
    raw = mm_nt(normed, feat_ref[...])
    raw_ref[...] = raw
    raw_ref.send()
    left, right = factors(raw, choose_ref, lanes_ref)
    features = (left * right * lanes_ref[2:3, :]).astype(bf16)
    features = (features.astype(f32) * lanes_ref[3:4, :]).astype(bf16)
    tail = tail_mask(info)
    for head in range(HEADS):
        own = features[:, head * LANES : (head + 1) * LANES]
        km_ref[head] = own
        if head == HEADS - 1:
            km_ref.send()
        kept = (values[:, head_lanes(head)].astype(f32) * tail).astype(bf16)
        state = mm_tn(own, kept)
        norm = jnp.sum(own.astype(f32) * tail, axis=0, keepdims=True)
        write_packed(packed_ref, head, state, norm)


def local_kernel(
    info, raw_ref, choose_ref, lanes_ref, values_ref, km_ref, qf_ref, low_ref, num_ref, den_ref,
):
    left, right = factors(raw_ref[...], choose_ref, lanes_ref)
    features = (left * right * lanes_ref[2:3, :]).astype(bf16)
    half = ROWS // 2
    for block in range(2):
        first, reach = block * half, (block + 1) * half
        query_at = column_positions(info, first, half)
        key_at = row_positions(info, 0, reach)
        causal = (query_at >= key_at) & (doc_of(info, query_at) == doc_of(info, key_at))
        for head in range(HEADS):
            own = features[first:reach, head * LANES : (head + 1) * LANES]
            qf_ref[head, first:reach, :] = own
            weights = jnp.where(causal, mm_nt(own, km_ref[head, :reach, :]), 0.0)
            den_ref[head, first:reach, :] = jnp.sum(weights, axis=-1, keepdims=True)
            low = weights.astype(bf16)
            low_ref[head, first:reach, 0:reach] = low
            num_ref[first:reach, head_lanes(head)] = mm(low, values_ref[:reach, head_lanes(head)])


def window_kernel(
    info, normed_ref, query_ref, keys_ref, values_ref, halo_ref, queries_ref, probs_ref, window_ref,
):
    queries = mm(normed_ref[...], query_ref[...]).astype(bf16)
    queries_ref[...] = queries
    queries_ref.send()
    scale = VALUE_WIDTH ** (-0.5)
    for tile in range(ROWS // TILE):
        first = tile * TILE
        query_at = column_positions(info, first, TILE)
        key_at = row_positions(info, first - WIN, TILE + WIN)
        near = (
            (key_at <= query_at)
            & (query_at - key_at < WIN)
            & (doc_of(info, query_at) == doc_of(info, key_at))
            & (key_at >= 0)
        )
        for head in range(HEADS):
            lanes = head_lanes(head)
            key_rows = window_rows(keys_ref, halo_ref, 0, tile, lanes)
            value_rows = window_rows(values_ref, halo_ref, 1, tile, lanes)
            logits = mm_nt(queries[first : first + TILE, lanes], key_rows) * scale
            logits = jnp.where(near, logits, -1e30)
            exps = jnp.exp(logits - jnp.max(logits, axis=-1, keepdims=True))
            probs = exps / jnp.sum(exps, axis=-1, keepdims=True)
            probs_ref[head, tile] = probs
            window_ref[first : first + TILE, lanes] = mm(probs.astype(bf16), value_rows)


def by_distance(ref, info, other):
    return jnp.concatenate([ref[info.rows(d, other), :] for d in range(4)], axis=0)


def mixed_kernel(
    info, before_ref, got1_ref, got2_ref, got3_ref, qf_ref, num_ref, den_ref, window_ref, out_ref,
    mixed_ref, linear_ref, total_den_ref, state_ref, norm_ref, own_ref, other_ref,
):
    use = prefix_mask(info)
    for head in range(HEADS):
        lanes = head_lanes(head)
        state, norm = read_total(before_ref, (got1_ref, got2_ref, got3_ref), head)
        state_ref[head] = state
        norm_ref[head] = jnp.broadcast_to(norm, (8, LANES))
        features = qf_ref[head]
        inter = mm(features, state) * use
        den = jnp.sum(features.astype(f32) * norm, axis=-1, keepdims=True) * use + den_ref[head]
        total_den_ref[head] = den
        linear = (inter + num_ref[:, lanes]) / den
        linear_ref[:, lanes] = linear
        mixed_ref[:, lanes] = (linear + window_ref[:, lanes]).astype(bf16)
    weights = out_ref[...]
    other_ref[...] = mm(by_distance(mixed_ref, info, True), weights).astype(bf16)
    other_ref.send()
    own_ref[...] = mm(by_distance(mixed_ref, info, False), weights).astype(bf16)


def quarters_kernel(info, own_ref, got_ref, *out_refs):
    for d in (1, 2, 3, 0):
        rows = slice(d * OWN, (d + 1) * OWN)
        total = own_ref[rows, :].astype(f32) + got_ref[rows, :].astype(f32)
        ref = out_refs[d]
        ref[0:OWN, :] = total.astype(ref.dtype)
        if own_ref.shape[0] > 4 * OWN:
            extra = own_ref[4 * OWN :, :].astype(f32) + got_ref[4 * OWN :, :].astype(f32)
            pair = extra[0:1] + extra[1:2]
            ref[OWN:, :] = extra_rows(pair).astype(ref.dtype)
        ref.send()


def extra_rows(row):
    at = lax.broadcasted_iota(jnp.int32, (16, row.shape[1]), 0)
    high = row.astype(bf16).astype(f32)
    return jnp.where(at == 0, high, jnp.where(at == 1, row - high, 0.0))


def resid_kernel(
    info, mine_ref, x_ref, gain_ref, got1_ref, got2_ref, got3_ref, normed_ref, resid_ref, inv_ref
):
    resid = x_ref[...].astype(f32) + mine_ref[...]
    for ref in (got1_ref, got2_ref, got3_ref):
        resid = resid + ref[...].astype(f32)
    inv = lax.rsqrt(jnp.mean(resid * resid, axis=-1, keepdims=True) + EPS)
    normed_ref[...] = (resid * inv * gain_ref[...]).astype(bf16)
    normed_ref.send()
    resid_ref[...] = resid
    inv_ref[...] = inv


def grad_resid_kernel(
    info, mine_ref, resid_ref, inv_ref, top_ref, gain_ref, got1_ref, got2_ref, got3_ref,
    sent_ref, grad_ref,
):
    grad = mine_ref[...]
    for ref in (got1_ref, got2_ref, got3_ref):
        grad = grad + ref[...].astype(f32)
    resid = resid_ref[...]
    inv = inv_ref[...]
    grad_resid = top_ref[...].astype(f32) + norm_back(resid, inv, gain_ref[...], grad)
    sent_ref[0:OWN, :] = grad_resid.astype(bf16)
    sent_ref[OWN:, :] = extra_rows(jnp.sum(grad * resid * inv, axis=0, keepdims=True)).astype(bf16)
    sent_ref.send()
    grad_ref[...] = grad_resid


def grad_x_kernel(
    info, mine_ref, x_ref, grad_resid_ref, gain_ref, gain_ffn_ref, got1_ref, got2_ref, got3_ref,
    sent_ref, gains_ref,
):
    grad = mine_ref[...]
    for ref in (got1_ref, got2_ref, got3_ref):
        grad = grad + ref[...].astype(f32)
    x = x_ref[...].astype(f32)
    inv = lax.rsqrt(jnp.mean(x * x, axis=-1, keepdims=True) + EPS)
    back = norm_back(x, inv, gain_ref[...], grad[0:OWN])
    sent_ref[...] = (grad_resid_ref[...] + back).astype(bf16)
    sent_ref.send()
    gain_mix = jnp.sum(grad[OWN:], axis=0, keepdims=True)
    at = lax.broadcasted_iota(jnp.int32, gains_ref.shape, 0)
    gains_ref[...] = jnp.where(at == 0, gain_mix, gain_ffn_ref[0:1, :])


def norm_back(in_rows, inv_rms, gain, grad_normed):
    weighted = grad_normed * gain
    return inv_rms * weighted - in_rows * inv_rms**3 * jnp.mean(
        weighted * in_rows, axis=-1, keepdims=True
    )


def grad_x_out_kernel(info, sent_ref, out_ref):
    out_ref[...] = sent_ref[...].astype(f32)


def copy_kernel(info, in_ref, out_ref):
    out_ref[...] = in_ref[...]


def ffn_grads_kernel(normed_ref, top_ref, gate_ref, up_ref, act_ref, out_ref):
    hidden = gate_ref.shape[1]
    normed = normed_ref[...]
    out_ref[:, 0:hidden] = mm_tn(normed, gate_ref[...]).astype(bf16)
    out_ref[:, hidden : 2 * hidden] = mm_tn(normed, up_ref[...]).astype(bf16)
    out_ref[:, 2 * hidden : 3 * hidden] = mm_tn(top_ref[...], act_ref[...]).astype(bf16)


def mixed_back_kernel(
    info, in_ref, out_ref, linear_ref, den_ref, qf_ref, extra_ref,
    packed_ref, top_ref, gm_ref, gnum_ref, gden_ref, gain_ref,
):
    top = in_ref[...]
    grad_mixed = mm_nt(top, out_ref[...]).astype(bf16)
    gm_ref[...] = grad_mixed
    gm_ref.send()
    top_ref[...] = top
    top_ref.send()
    use = prefix_mask(info)
    for head in range(HEADS):
        lanes = head_lanes(head)
        wide = grad_mixed[:, lanes].astype(f32)
        den = den_ref[head]
        grad_num = (wide / den).astype(bf16)
        gnum_ref[:, lanes] = grad_num
        grad_den = -jnp.sum(wide * linear_ref[:, lanes], axis=-1, keepdims=True) / den
        gden_ref[head] = grad_den
        features = qf_ref[head]
        used = (grad_num.astype(f32) * use).astype(bf16)
        state = mm_tn(features, used)
        norm = jnp.sum(features.astype(f32) * (grad_den * use), axis=0, keepdims=True)
        write_packed(packed_ref, head, state, norm)
    packed_ref.send()
    total = jnp.sum(extra_ref[...].astype(f32), axis=0, keepdims=True)
    gain_ref[...] = jnp.broadcast_to(total, gain_ref.shape)


def local_back_kernel(
    info, gm_ref, gnum_ref, gden_ref, probs_ref, keys_ref, values_ref, halo_ref, queries_ref,
    low_ref, km_ref, qf_ref, state_ref, norm_ref, raw_ref, choose_ref, lanes_ref,
    gq_ref, gfeat_ref, gk_ref, gv_ref, gkf_ref, edge_ref, key_acc, value_acc,
):
    scale = VALUE_WIDTH ** (-0.5)
    key_acc[...] = jnp.zeros_like(key_acc)
    value_acc[...] = jnp.zeros_like(value_acc)
    for tile in range(ROWS // TILE):
        first = tile * TILE
        reach = slice(first, first + TILE + WIN)
        for head in range(HEADS):
            lanes = head_lanes(head)
            key_rows = window_rows(keys_ref, halo_ref, 0, tile, lanes)
            value_rows = window_rows(values_ref, halo_ref, 1, tile, lanes)
            top = gm_ref[first : first + TILE, lanes]
            probs = probs_ref[head, tile]
            grad_probs = mm_nt(top, value_rows)
            shared = jnp.sum(grad_probs * probs, axis=-1, keepdims=True)
            grad_logits = (probs * (grad_probs - shared)).astype(bf16)
            gq_ref[first : first + TILE, lanes] = (mm(grad_logits, key_rows) * scale).astype(bf16)
            queries = queries_ref[first : first + TILE, lanes]
            key_acc[reach, lanes] += mm_tn(grad_logits, queries) * scale
            value_acc[reach, lanes] += mm_tn(probs.astype(bf16), top)
    edge_ref[0] = key_acc[0:WIN, :].astype(bf16)
    edge_ref[1] = value_acc[0:WIN, :].astype(bf16)
    edge_ref.send()
    gq_ref.send()
    gk_ref[...] = key_acc[WIN:, :]
    gk_ref.send()
    use = prefix_mask(info)
    left, right = factors(raw_ref[...], choose_ref, lanes_ref)
    half = ROWS // 2
    grads = [[None, None], [None, None]]
    for head in range(HEADS):
        lanes = head_lanes(head)
        inter = mm_nt((gnum_ref[:, lanes].astype(f32) * use).astype(bf16), state_ref[head])
        inter = inter + (gden_ref[head] * use) * norm_ref[head, 0:1, :]
        gkf = None
        gvl = None
        for block in range(2):
            first, reach = block * half, (block + 1) * half
            query_at = column_positions(info, first, half)
            key_at = row_positions(info, 0, reach)
            causal = (query_at >= key_at) & (doc_of(info, query_at) == doc_of(info, key_at))
            grad_num = gnum_ref[first:reach, lanes]
            grad = mm_nt(grad_num, values_ref[:reach, lanes]) + gden_ref[head, first:reach, :]
            grad = jnp.where(causal, grad, 0.0).astype(bf16)
            grads[head][block] = mm(grad, km_ref[head, :reach, :]) + inter[first:reach]
            key_part = mm_tn(grad, qf_ref[head, first:reach, :])
            value_part = mm_tn(low_ref[head, first:reach, 0:reach], grad_num)
            if block == 0:
                gkf_ref[head] = jnp.concatenate([key_part, jnp.zeros_like(key_part)], axis=0)
                gv_ref[0:half, lanes] = value_acc[WIN : WIN + half, lanes] + value_part
                gv_ref[half:, lanes] = value_acc[WIN + half :, lanes]
            else:
                gkf_ref[head] += key_part
                gv_ref[:, lanes] += value_part
    gradient = jnp.concatenate([jnp.concatenate(g, axis=0) for g in grads], axis=1)
    gradient = gradient * lanes_ref[2:3, :]
    gfeat_ref[...] = feature_back(gradient, left, right, choose_ref)


def keys_back_kernel(
    info, before_ref, got1_ref, got2_ref, got3_ref, values_ref, km_ref, gkf_ref, gk_ref, gv_ref,
    right_ref, raw_ref, choose_ref, lanes_ref, gq_ref, gfeat_ref, wq_ref, wk_ref, wv_ref, wf_ref,
    x_ref, inv_ref,
    other_ref, gkw_ref, gvw_ref, gf_ref, own_ref,
    acc_ref,
):
    tail = tail_mask(info)
    inner = ROWS - WIN
    gkw_ref[0:inner, :] = gk_ref[0:inner, :].astype(bf16)
    gkw_ref[inner:, :] = (gk_ref[inner:, :] + right_ref[0].astype(f32)).astype(bf16)
    gradients = []
    for head in range(HEADS):
        lanes = head_lanes(head)
        later, norm = read_total(before_ref, (got1_ref, got2_ref, got3_ref), head)
        kept = (values_ref[:, lanes].astype(f32) * tail).astype(bf16)
        gradients.append(gkf_ref[head] + mm_nt(kept, later) + tail * norm)
        grad_values = gv_ref[:, lanes] + mm(km_ref[head], later) * tail
        gvw_ref[0:inner, lanes] = grad_values[0:inner].astype(bf16)
        gvw_ref[inner:, lanes] = (grad_values[inner:] + right_ref[1, :, lanes].astype(f32)).astype(
            bf16
        )
    left, right = factors(raw_ref[...], choose_ref, lanes_ref)
    gradient = jnp.concatenate(gradients, axis=1) * lanes_ref[4:5, :]
    gf_ref[...] = (feature_back(gradient, left, right, choose_ref) + gfeat_ref[...]).astype(bf16)
    for ref in (gkw_ref, gvw_ref, gf_ref):
        ref.send()
    wf_ref.ready()
    wf_ref.ref[64:128, :] = jnp.zeros((64, wf_ref.shape[1]), bf16)
    half = ROWS // 2
    for mine in (True, False):
        grads = [by_distance(ref, info, not mine) for ref in (gq_ref, gkw_ref, gvw_ref, gf_ref)]
        scaled_by = by_distance(inv_ref, info, not mine)
        target = own_ref if mine else other_ref
        for piece in range(4):
            span = slice(piece * 512, (piece + 1) * 512)
            part = mm_nt(grads[0], wq_ref[span, :])
            part = part + mm_nt(grads[1], wk_ref[span, :])
            part = part + mm_nt(grads[2], wv_ref[span, :])
            part = part + mm(grads[3], wf_ref[:, span])
            target[0:half, span] = part.astype(bf16)
            x_rows = jnp.concatenate([x_ref[info.rows(d, not mine), span] for d in range(4)], axis=0)
            scaled = part * (x_rows.astype(f32) * scaled_by)
            total = jnp.sum(scaled, axis=0, keepdims=True)
            acc_ref[0:1, span] = total if mine else total + acc_ref[0:1, span]
    gain = extra_rows(acc_ref[0:1, :]).astype(bf16)
    other_ref[half:, :] = gain
    other_ref.send()
    own_ref[half:, :] = gain


def early_grads_kernel(info, normed_ref, gq_ref, top_ref, mixed_ref, out_ref):
    for block in range(4):
        span = slice(block * 512, (block + 1) * 512)
        rows = slice(block * 4, (block + 1) * 4)
        query = mm_tn(normed_ref[:, span], gq_ref[...])
        out_ref[rows, :, 0:256] = query.astype(bf16).reshape(4, 128, 256)
        out = mm_tn(top_ref[:, span], mixed_ref[...])
        out_ref[rows, :, 256:512] = out.astype(bf16).reshape(4, 128, 256)


def late_grads_kernel(info, normed_ref, gk_ref, gv_ref, gf_ref, out_ref):
    for block in range(4):
        span = slice(block * 512, (block + 1) * 512)
        rows = slice(block * 4, (block + 1) * 4)
        normed = normed_ref[:, span]
        out_ref[rows, :, 0:256] = mm_tn(normed, gk_ref[...]).astype(bf16).reshape(4, 128, 256)
        out_ref[rows, :, 256:512] = mm_tn(normed, gv_ref[...]).astype(bf16).reshape(4, 128, 256)
        out_ref[rows, :, 512:640] = mm_tn(normed, gf_ref[...]).astype(bf16).reshape(4, 128, 128)


def sum_of(ref, lanes):
    total = ref[0, :, lanes].astype(f32)
    for i in range(1, ref.shape[0]):
        total = total + ref[i, :, lanes].astype(f32)
    return total


def early_sum_kernel(info, in_ref, query_ref, out_ref):
    query_ref[...] = sum_of(in_ref, slice(0, 256))
    query_ref.send()
    out_ref[...] = sum_of(in_ref, slice(256, 512)).T


def late_sum_kernel(info, in_ref, key_ref, value_ref, feat_query_ref, feat_key_ref):
    key_ref[...] = sum_of(in_ref, slice(0, 256))
    key_ref.send()
    value_ref[...] = sum_of(in_ref, slice(256, 512))
    value_ref.send()
    feat = sum_of(in_ref, slice(512, 640)).T
    feat_query_ref[...] = feat[0:32]
    feat_key_ref[...] = feat[32:64]


def ffn_sum_kernel(info, in_ref, gate_ref, up_ref, down_ref):
    hidden = gate_ref.shape[0]
    whole = in_ref[...].astype(f32).T
    for i, ref in enumerate((gate_ref, up_ref, down_ref)):
        ref[...] = whole[i * hidden : (i + 1) * hidden]
        ref.send()


def along_y(distance):
    return [(i, (i + 2 * distance) % 8) for i in range(8)]


def sibling():
    return [(i, i ^ 1) for i in range(8)]


def along_x(distance):
    return [(i, (i + 4 * distance) % 16) for i in range(16)]


def along_z(distance):
    return [(4 * a + z, 4 * a + (z + distance) % 4) for a in range(4) for z in range(4)]


def pick(stack, index):
    return lax.dynamic_index_in_dim(stack, index, 0, keepdims=False)


def head_quarters(own, other):
    got = lax.ppermute(other, "head", sibling())
    extra = own.shape[0] - 4 * OWN
    rows, width = OWN + extra, own.shape[1]
    with jax.named_scope("quarters"):
        mine, *sent = call(
            quarters_kernel, [shape(rows, width, dtype=f32)] + [shape(rows, width)] * 3, (own, got)
        )
    parts = [lax.ppermute(sent[d - 1], "head", along_y(d)) for d in (1, 2, 3)]
    return mine, parts, got


def head_pieces(own):
    pieces = [own] + [lax.ppermute(own, "head", along_y(d)) for d in (1, 2, 3)]
    return pieces + [lax.ppermute(piece, "head", sibling()) for piece in pieces]


def seq_sum_scatter(part):
    me = lax.axis_index("seq")
    for place, route in ((me // 4, along_x), (me % 4, along_z)):
        stack = jnp.moveaxis(part.reshape(2, 4, -1), 1, 0)
        part = pick(stack, place)
        for d in (1, 2, 3):
            part = part + lax.ppermute(pick(stack, (place + d) % 4), "seq", route(d))
    return part


def repack(total):
    norm = total[:, KEPT : KEPT + 2] + total[:, KEPT + 2 : KEPT + 4]
    high = norm.astype(bf16)
    rest = (norm - high.astype(f32)).astype(bf16)
    return jnp.concatenate(
        [total[:, :KEPT].astype(bf16), high, rest, total[:, KEPT + 4 :].astype(bf16)], axis=1
    )


def exclusive_parts(own, reverse):
    me = lax.axis_index("seq")
    xx, zz = me // 4, me % 4
    sign = -1 if reverse else 1
    place_x, place_z = (3 - xx, 3 - zz) if reverse else (xx, zz)
    before = jnp.zeros(own.shape, f32)
    for d in (1, 2, 3):
        got = lax.ppermute(own, "seq", along_x(sign * d)).astype(f32)
        before = before + jnp.where(place_x >= d, got, 0.0)
    low_before = repack(before)
    low_with = repack(before + own.astype(f32))
    got = [
        lax.ppermute(jnp.where(place_z + d < 4, low_with, low_before), "seq", along_z(sign * d))
        for d in (1, 2, 3)
    ]
    return [before] + got


def shifted(block, distance):
    route = [(i - distance, i) for i in range(16) if 0 <= i - distance < 16]
    return lax.ppermute(block, "seq", route)


def shards(
    inputs,
    gain_mix,
    feat_query,
    feat_key,
    win_query,
    win_key,
    value_proj,
    out_proj,
    gain_ffn,
    gate_proj,
    up_proj,
    down_proj,
    document_starts,
    cotangent,
):
    choose, lanes = feature_tables()
    choose = jnp.asarray(choose, bf16)
    lanes = jnp.asarray(lanes, f32)
    choose_q, choose_k = choose[0], choose[1]
    feat = feature_weights(feat_query.T, feat_key.T)
    gain_mix = gain_mix.reshape(1, -1)
    gain_ffn = gain_ffn.reshape(1, -1)
    model = inputs.shape[1]
    width = HEADS * VALUE_WIDTH
    hidden = gate_proj.shape[1]
    half = ROWS // 2
    unit = 2 * ROWS * model
    starts = document_starts

    with jax.named_scope("keys"):
        normed, inv_mix, raw, keys, values, km, packed, edge = call(
            keys_kernel,
            (
                shape(ROWS, model), shape(ROWS, 1, dtype=f32), shape(ROWS, 128, dtype=f32),
                shape(ROWS, width), shape(ROWS, width), shape(HEADS, ROWS, LANES),
                shape(HEADS, PACKED, 128), shape(2, WIN, width),
            ),
            (inputs, gain_mix, win_key, value_proj, feat, choose_k, lanes),
            starts=starts, flops=unit * 640,
        )
    sums = exclusive_parts(packed, False)
    halo = shifted(edge, 1)
    with jax.named_scope("local"):
        qf, low, num, den = call(
            local_kernel,
            (
                shape(HEADS, ROWS, LANES), shape(HEADS, ROWS, ROWS),
                shape(ROWS, width, dtype=f32), shape(HEADS, ROWS, 1, dtype=f32),
            ),
            (raw, choose_q, lanes, values, km),
            starts=starts, flops=unit * 300,
        )
    with jax.named_scope("window"):
        queries, probs, window = call(
            window_kernel,
            (
                shape(ROWS, width), shape(HEADS, 4, TILE, TILE + WIN, dtype=f32),
                shape(ROWS, width, dtype=f32),
            ),
            (normed, win_query, keys, values, halo),
            starts=starts, flops=unit * 400,
        )
    with jax.named_scope("mixed"):
        mixed, linear, total_den, state, norm, own, other = call(
            mixed_kernel,
            (
                shape(ROWS, width), shape(ROWS, width, dtype=f32),
                shape(HEADS, ROWS, 1, dtype=f32), shape(HEADS, LANES, VALUE_WIDTH),
                shape(HEADS, 8, LANES, dtype=f32), shape(half, model), shape(half, model),
            ),
            (*sums, qf, num, den, window, out_proj),
            starts=starts, flops=unit * 300,
        )
    mine, parts, _ = head_quarters(own, other)
    grad_act = mm_nt(cotangent, down_proj)
    mine, grad_act = lax.optimization_barrier((mine, grad_act))
    with jax.named_scope("resid"):
        own_normed, resid, inv_ffn = call(
            resid_kernel,
            (shape(OWN, model), shape(OWN, model, dtype=f32), shape(OWN, 1, dtype=f32)),
            (mine, own_part(inputs), gain_ffn, *parts),
        )
    pieces = head_pieces(own_normed)
    with jax.named_scope("assemble"):
        (normed_ffn,) = call(copy_kernel, (shape(ROWS, model),), (gathered(pieces),))
    gate = mm(normed_ffn, gate_proj)
    up_value = mm(normed_ffn, up_proj)
    sigmoid_gate = jax.nn.sigmoid(gate)
    silu_gate = gate * sigmoid_gate
    activation = (silu_gate * up_value).astype(bf16)
    grad_gate = (grad_act * up_value * sigmoid_gate * (1.0 + gate * (1.0 - sigmoid_gate))).astype(
        bf16
    )
    grad_up = (grad_act * silu_gate).astype(bf16)

    y, core = lax.axis_index("head") // 2, lax.axis_index("head") % 2

    def rows_for(block, which):
        quarters = block.reshape(8, OWN, block.shape[1])
        return jnp.concatenate(
            [pick(quarters, which * 4 + (y + d) % 4) for d in range(4)], axis=0
        )

    def ffn_back(which):
        return (
            mm_nt(rows_for(grad_gate, which), gate_proj) + mm_nt(rows_for(grad_up, which), up_proj)
        ).astype(bf16)

    mine, parts, got = head_quarters(ffn_back(core), ffn_back(1 - core))
    normed_late, gate_late, up_late, act_late, _ = lax.optimization_barrier(
        (normed_ffn, grad_gate, grad_up, activation, got)
    )
    with jax.named_scope("ffn_grads"):
        ffn_grads = pl.pallas_call(
            ffn_grads_kernel,
            grid=(8,),
            in_specs=[
                pl.BlockSpec((ROWS, model // 8), lambda i: (0, i)),
                pl.BlockSpec((ROWS, model // 8), lambda i: (0, i)),
                pl.BlockSpec((ROWS, hidden), lambda i: (0, 0)),
                pl.BlockSpec((ROWS, hidden), lambda i: (0, 0)),
                pl.BlockSpec((ROWS, hidden), lambda i: (0, 0)),
            ],
            out_specs=pl.BlockSpec((model // 8, 3 * hidden), lambda i: (i, 0)),
            out_shape=shape(model, 3 * hidden),
            compiler_params=pltpu.CompilerParams(vmem_limit_bytes=48 * 2**20),
            cost_estimate=pl.CostEstimate(
                flops=unit * 3 * hidden, bytes_accessed=15 * 2**20, transcendentals=0
            ),
        )(normed_late, cotangent, gate_late, up_late, act_late)
    ffn_grads = lax.psum_scatter(ffn_grads, "seq", scatter_dimension=0, tiled=True)
    with jax.named_scope("grad_resid"):
        sent, grad_resid = call(
            grad_resid_kernel,
            (shape(OWN + 16, model), shape(OWN, model, dtype=f32)),
            (mine, resid, inv_ffn, own_part(cotangent), gain_ffn, *parts),
        )
    pieces = head_pieces(sent)
    with jax.named_scope("mixed_back"):
        packed, top, grad_mixed, grad_num, grad_den, gain_ffn_part = call(
            mixed_back_kernel,
            (
                shape(HEADS, PACKED, 128), shape(ROWS, model), shape(ROWS, width),
                shape(ROWS, width), shape(HEADS, ROWS, 1, dtype=f32), shape(8, model, dtype=f32),
            ),
            (gathered(pieces), out_proj, linear, total_den, qf, gathered_extra(pieces)),
            starts=starts, flops=unit * 300,
        )
    sums = exclusive_parts(packed, True)
    with jax.named_scope("local_back"):
        gq, gfeat, gk, gv, gkf, edge = call(
            local_back_kernel,
            (
                shape(ROWS, width), shape(ROWS, 128, dtype=f32), shape(ROWS, width, dtype=f32),
                shape(ROWS, width, dtype=f32), shape(HEADS, ROWS, LANES, dtype=f32),
                shape(2, WIN, width),
            ),
            (
                grad_mixed, grad_num, grad_den, probs, keys, values, halo, queries, low, km,
                qf, state, norm, raw, choose_q, lanes,
            ),
            starts=starts, flops=unit * 600,
            scratch=[pltpu.VMEM((ROWS + WIN, width), f32)] * 2,
        )
    right = shifted(edge, -1)
    with jax.named_scope("early_grads"):
        (early,) = call(
            early_grads_kernel, (shape(16, 128, 512),), (normed, gq, top, mixed), flops=unit * 512
        )
    early = lax.all_to_all(early, "seq", 0, 0)
    act_last, _ = lax.optimization_barrier((activation, packed))

    def ffn_out(which):
        return mm(rows_for(act_last, which), down_proj).astype(bf16)

    out_mine, out_parts, _ = head_quarters(ffn_out(core), ffn_out(1 - core))
    out_sum = resid + out_mine + sum(part.astype(f32) for part in out_parts)
    out_pieces = head_pieces(out_sum.astype(bf16))
    with jax.named_scope("keys_back"):
        other, gkw, gvw, gf, own = call(
            keys_back_kernel,
            (
                shape(half + 16, model), shape(ROWS, width), shape(ROWS, width),
                shape(ROWS, 128), shape(half + 16, model),
            ),
            (
                *sums, values, km, gkf, gk, gv, right, raw, choose_k, lanes, gq, gfeat,
                win_query, win_key, value_proj, feat, inputs, inv_mix,
            ),
            starts=starts, flops=unit * 900,
            scratch=[pltpu.VMEM((8, model), f32)],
        )
    mine, parts, got = head_quarters(own, other)
    normed_late, gkw_late, _ = lax.optimization_barrier((normed, gkw, got))
    with jax.named_scope("late_grads"):
        (late,) = call(
            late_grads_kernel, (shape(16, 128, 640),), (normed_late, gkw_late, gvw, gf),
            flops=unit * 640,
        )
    late = lax.all_to_all(late, "seq", 0, 0)
    with jax.named_scope("grad_x"):
        sent, gains = call(
            grad_x_kernel,
            (shape(OWN, model), shape(2, model, dtype=f32)),
            (mine, own_part(inputs), grad_resid, gain_mix, gain_ffn_part, *parts),
        )
    pieces = head_pieces(sent)
    gains = seq_sum_scatter(gains)
    with jax.named_scope("ffn_sum"):
        grad_gate_t, grad_up_t, grad_down = call(
            ffn_sum_kernel, (shape(hidden, 128, dtype=f32),) * 3, (ffn_grads,)
        )
    with jax.named_scope("early_sum"):
        grad_wq, grad_out = call(
            early_sum_kernel, (shape(128, 256, dtype=f32), shape(256, 128, dtype=f32)), (early,)
        )
    with jax.named_scope("assemble"):
        (output,) = call(copy_kernel, (shape(ROWS, model),), (gathered(out_pieces),))
    with jax.named_scope("grad_x_out"):
        (grad_x,) = call(grad_x_out_kernel, (shape(ROWS, model, dtype=f32),), (gathered(pieces),))
    with jax.named_scope("late_sum"):
        grad_wk, grad_wv, grad_fq_t, grad_fk_t = call(
            late_sum_kernel,
            (shape(128, 256, dtype=f32),) * 2 + (shape(32, 128, dtype=f32),) * 2,
            (late,),
        )
    return (
        output,
        grad_x,
        gains[0],
        grad_fq_t.T,
        grad_fk_t.T,
        grad_wq,
        grad_wk,
        grad_wv,
        grad_out,
        gains[1],
        grad_gate_t.T,
        grad_up_t.T,
        grad_down,
    )


def solution(mesh):
    placed = (
        P("seq", None),
        P(),
        P(None, "head"),
        P(None, "head"),
        P(None, "head"),
        P(None, "head"),
        P(None, "head"),
        P("head", None),
        P(),
        P(None, "head"),
        P(None, "head"),
        P("head", None),
        P(),
        P("seq", None),
    )
    return jax.shard_map(
        shards,
        mesh=mesh,
        in_specs=placed,
        out_specs=(
            P("seq", None),
            P("seq", None),
            P("seq"),
            P("seq", "head"),
            P("seq", "head"),
            P("seq", "head"),
            P("seq", "head"),
            P("seq", "head"),
            P("head", "seq"),
            P("seq"),
            P("seq", "head"),
            P("seq", "head"),
            P("head", "seq"),
        ),
        check_vma=False,
    )
```

```python
import functools
import math

import jax
import jax.numpy as jnp
import numpy as np
from jax import lax
from jax.experimental import pallas as pl
from jax.experimental.pallas import tpu as pltpu
from jax.sharding import PartitionSpec as P

F = 16
VALUE_WIDTH = 128
WIN = 64
EPS = 1e-05

HEADS = 2
ROWS = 512
LANES = 256
KEPT = 160
PACKED = 176
TILE = 128
OWN = 64
f32 = jnp.float32
bf16 = jnp.bfloat16


def feature_tables():
    pairs = [(a, b) for a in range(F) for b in range(a, F)]
    count = len(pairs)
    choose = np.zeros((2, 2, 128, HEADS * LANES), np.float32)
    lanes = np.zeros((8, HEADS * LANES), np.float32)
    factor = F ** (-0.25)
    for head in range(HEADS):
        at = head * LANES
        for side in range(2):
            row = side * HEADS * F + head * F
            for lane, (a, b) in enumerate(pairs):
                choose[side, 0, row + a, at + lane] = 1.0
                choose[side, 1, row + b, at + lane] = 1.0
            for a in range(F):
                choose[side, 0, row + a, at + count + a] = 1.0
        for lane, (a, b) in enumerate(pairs):
            lanes[2, at + lane] = factor * factor / math.sqrt(2.0)
            lanes[3, at + lane] = 1.0 if a == b else 2.0
        lanes[1, at + count : at + count + F + 1] = 1.0
        lanes[0, at + count + F] = 1.0
        lanes[2, at + count : at + count + F] = factor
        lanes[2, at + count + F] = 1.0
        lanes[3, at + count : at + count + F + 1] = 1.0
    lanes[4] = lanes[2] * lanes[3]
    return choose, lanes


def mm(a, b):
    return lax.dot_general(a, b, (((1,), (0,)), ((), ())), preferred_element_type=f32)


def mm_nt(a, b):
    return lax.dot_general(a, b, (((1,), (1,)), ((), ())), preferred_element_type=f32)


def mm_tn(a, b):
    return lax.dot_general(a, b, (((0,), (0,)), ((), ())), preferred_element_type=f32)


def low_pair(part):
    high = part.astype(bf16)
    return high, (part - high.astype(f32)).astype(bf16)


class Place:

    def __init__(self, starts):
        me, seq = lax.axis_index("head"), lax.axis_index("seq")
        self.base = seq * ROWS
        self.x, self.z = lax.shift_right_logical(seq, 2), lax.bitwise_and(seq, 3)
        self.y, self.core = lax.shift_right_logical(me, 1), lax.bitwise_and(me, 1)
        self.loaded = starts

    def starts(self):
        return [self.loaded[0, i] for i in range(4)]

    def rows(self, distance, other=False):
        quarter = lax.bitwise_and(self.y + distance, 3)
        core = 1 - self.core if other else self.core
        return pl.ds(pl.multiple_of(quarter * (2 * OWN) + core * OWN, OWN), OWN)


class Loaded:

    def __init__(self, ref, copies):
        self.ref, self.copies = ref, list(copies)
        self.shape = ref.shape

    def part(self, index):
        if self.copies and self.copies[index] is not None:
            self.copies[index].wait()
            self.copies[index] = None

    def ready(self):
        for index in range(len(self.copies)):
            self.part(index)

    def __getitem__(self, index):
        self.ready()
        return self.ref[index]


class Stored:

    def __init__(self, ref, copies):
        self.ref, self.copies, self.sent = ref, copies, set()
        self.shape, self.dtype = ref.shape, ref.dtype

    def __getitem__(self, index):
        return self.ref[index]

    def __setitem__(self, index, value):
        self.ref[index] = value

    def send(self, part=None):
        for index in range(len(self.copies)) if part is None else (part,):
            if index not in self.sent:
                self.copies[index].start()
                self.sent.add(index)


def doc_of(info, position):
    starts = info.starts()
    count = (position >= starts[0]).astype(jnp.int32)
    for start in starts[1:]:
        count = count + (position >= start).astype(jnp.int32)
    return count


def column_positions(info, first, count):
    return info.base + first + lax.broadcasted_iota(jnp.int32, (count, 1), 0)


def row_positions(info, first, count):
    return info.base + first + lax.broadcasted_iota(jnp.int32, (1, count), 1)


def prefix_mask(info):
    before = doc_of(info, info.base - 1)
    same = doc_of(info, column_positions(info, 0, ROWS)) == before
    return (same & (info.base > 0)).astype(f32)


def tail_mask(info):
    last = doc_of(info, info.base + ROWS - 1)
    return (doc_of(info, column_positions(info, 0, ROWS)) == last).astype(f32)


def chosen(raw, table):
    high, rest = low_pair(raw)
    left = raw - high.astype(f32) - rest.astype(f32)
    return mm(high, table) + mm(rest, table) + mm(left.astype(bf16), table)


def factors(raw, choose_ref, lanes_ref):
    return (
        chosen(raw, choose_ref[0]) + lanes_ref[0:1, :],
        chosen(raw, choose_ref[1]) + lanes_ref[1:2, :],
    )


def feature_back(gradient, left, right, choose_ref):
    total = None
    for term, table in ((gradient * right, choose_ref[0]), (gradient * left, choose_ref[1])):
        high, rest = low_pair(term)
        part = mm_nt(high, table) + mm_nt(rest, table)
        total = part if total is None else total + part
    return total


def write_packed(packed_ref, head, state, norm):
    packed_ref[head, 0:KEPT, :] = state[:KEPT].astype(bf16)
    row = lax.broadcasted_iota(jnp.int32, (16, 128), 0)
    high = norm.astype(bf16).astype(f32)
    rest = norm - high
    tile = jnp.where(row == 0, high[:, :128], 0.0)
    tile = jnp.where(row == 1, high[:, 128:], tile)
    tile = jnp.where(row == 2, rest[:, :128], tile)
    tile = jnp.where(row == 3, rest[:, 128:], tile)
    packed_ref[head, KEPT:PACKED, :] = tile.astype(bf16)


def read_total(before_ref, got_refs, head):
    total = before_ref[head]
    for ref in got_refs:
        total = total + ref[head].astype(f32)
    state = jnp.concatenate(
        [total[:KEPT], jnp.zeros((LANES - KEPT, VALUE_WIDTH), f32)], axis=0
    ).astype(bf16)
    norm = jnp.concatenate(
        [
            total[KEPT : KEPT + 1] + total[KEPT + 2 : KEPT + 3],
            total[KEPT + 1 : KEPT + 2] + total[KEPT + 3 : KEPT + 4],
        ],
        axis=1,
    )
    return state, norm


def head_lanes(head):
    return slice(head * VALUE_WIDTH, (head + 1) * VALUE_WIDTH)


def window_rows(own_ref, halo_ref, which, tile, lanes):
    first = tile * TILE
    if tile == 0:
        return jnp.concatenate([halo_ref[which, :, lanes], own_ref[0:TILE, lanes]], axis=0)
    return own_ref[first - WIN : first + TILE, lanes]


class Near:
    near = True

    def __init__(self, arrays, dims=None, places=None, parts=1):
        self.arrays = [
            a.arrays[0] if isinstance(a, Near) else a
            for a in (arrays if isinstance(arrays, (list, tuple)) else [arrays])
        ]
        self.dims = tuple(dims or self.arrays[0].shape)
        self.dtype = self.arrays[0].dtype
        self.places, self.parts = places, parts

    def copies(self, info, refs, buffer):
        if self.places is None:
            return pieces_of(refs[0], buffer, self.parts)
        return self.places(info, refs, buffer)

    def count(self):
        return self.parts if self.places is None else self.places(None)

    def copied(self):
        return self.places is not None


class Far(Near):
    near = False

    def copied(self):
        return True


class Into(Far):

    def __init__(self, array, result, first, parts):
        super().__init__(array, parts=parts)
        self.result, self.first = result, first

    def copied(self):
        return False


class Out:

    def __init__(self, *dims, dtype=bf16, near=False, far=False, parts=1):
        self.dims, self.dtype, self.parts = dims, dtype, parts
        self.near, self.far = near, far

    def shapes(self):
        kinds = [jax.ShapeDtypeStruct] * self.near + [pltpu.HBM] * self.far
        return [kind(self.dims, self.dtype) for kind in kinds]

    def spaces(self):
        return [pltpu.VMEM] * self.near + [pltpu.HBM] * self.far


def near(*dims, dtype=bf16):
    return Out(*dims, dtype=dtype, near=True)


def far(*dims, dtype=bf16, parts=1):
    return Out(*dims, dtype=dtype, far=True, parts=parts)


def both(*dims, dtype=bf16):
    return Out(*dims, dtype=dtype, near=True, far=True)


def pieces_of(source, target, parts):
    if parts == 1:
        return [(source, target)]
    count = source.shape[0] // parts
    return [
        (source.at[i * count : (i + 1) * count], target.at[i * count : (i + 1) * count])
        for i in range(parts)
    ]


def in_hbm(array):
    return pltpu.with_memory_space_constraint(array, pltpu.HBM)


def call(body, results, operands, starts=None, after=(), flops=0, scratch=(), megabytes=28):
    operands = [o if isinstance(o, Near) else Far(o) for o in operands]
    waits = [pl.ANY if isinstance(o, Near) else pltpu.HBM for o in after]
    after = [o.arrays[0] if isinstance(o, Near) else in_hbm(o) for o in after]
    arrays = [a for o in operands for a in o.arrays]
    copied = [o for o in operands if o.copied()]
    held = [o for o in results if not o.near]
    count_out = sum(o.near + o.far for o in results)
    moves = sum(o.count() for o in operands if not o.near or o.copied()) + sum(o.parts for o in results if o.far)
    named = starts is not None

    def kernel(*refs):
        sources, refs = refs[: len(arrays)], refs[len(arrays) + len(after) :]
        named_ref, refs = (refs[0], refs[1:]) if named else (None, refs)
        targets, rest = list(refs[:count_out]), refs[count_out:]
        buffers, rest = list(rest[: len(copied)]), rest[len(copied) :]
        leaving, rest = list(rest[: len(held)]), rest[len(held) :]
        sems, rest = rest[0], rest[1:]
        marks = None
        if named:
            copy = pltpu.make_async_copy(named_ref, rest[0], sems.at[moves])
            copy.start()
            marks, rest = Loaded(rest[0], [copy]), rest[1:]
        info = Place(marks)
        loaded, at, sem = [], 0, 0

        def copies_of(pairs):
            nonlocal sem
            sem += len(pairs)
            return [
                pltpu.make_async_copy(source, target, sems.at[sem - len(pairs) + i])
                for i, (source, target) in enumerate(pairs)
            ]

        for operand in operands:
            own = sources[at : at + len(operand.arrays)]
            at += len(own)
            if isinstance(operand, Into):
                loaded.append((operand, own[0]))
                continue
            if not operand.copied():
                loaded.append(Loaded(own[0], []))
                continue
            buffer = buffers.pop(0)
            loaded.append(Loaded(buffer, copies_of(operand.copies(info, own, buffer))))
            for copy in loaded[-1].copies:
                copy.start()
        stored = []
        for result in results:
            buffer = targets.pop(0) if result.near else leaving.pop(0)
            target = targets.pop(0) if result.far else None
            pairs = pieces_of(buffer, target, result.parts) if result.far else []
            stored.append(Stored(buffer, copies_of(pairs)))
        for i, item in enumerate(loaded):
            if isinstance(item, tuple):
                operand, source = item
                buffer = stored[operand.result].ref
                columns = buffer.at[:, operand.first : operand.first + source.shape[1]]
                loaded[i] = Loaded(buffer, copies_of(pieces_of(source, columns, operand.parts)))
                for copy in loaded[i].copies:
                    copy.start()
        body(info, *loaded, *stored, *rest)
        for item in loaded + ([marks] if named else []):
            item.ready()
        for item in stored:
            item.send()
        for item in stored:
            for copy in item.copies:
                copy.wait()

    spaces = [pltpu.VMEM if o.near else pltpu.HBM for o in operands for _ in o.arrays]
    placed = [a if space is pltpu.VMEM else in_hbm(a) for a, space in zip(arrays, spaces)]
    spaces += waits + [pltpu.HBM] * named
    moved = sum(a.size * a.dtype.itemsize for a in arrays)
    moved += sum(math.prod(o.dims) * jnp.dtype(o.dtype).itemsize for o in results)
    given = pl.pallas_call(
        kernel,
        name=getattr(body, "func", body).__name__,
        out_shape=tuple(s for o in results for s in o.shapes()),
        in_specs=[pl.BlockSpec(memory_space=space) for space in spaces],
        out_specs=tuple(pl.BlockSpec(memory_space=s) for o in results for s in o.spaces()),
        scratch_shapes=[pltpu.VMEM(o.dims, o.dtype) for o in copied]
        + [pltpu.VMEM(o.dims, o.dtype) for o in held]
        + [pltpu.SemaphoreType.DMA((max(1, moves + named),))]
        + [pltpu.SMEM((1, 4), jnp.int32)] * named
        + list(scratch),
        compiler_params=pltpu.CompilerParams(vmem_limit_bytes=megabytes * 2**20),
        cost_estimate=pl.CostEstimate(flops=0, bytes_accessed=1024, transcendentals=0),
    )(*placed, *after, *([in_hbm(starts)] if named else []))
    given, answer = list(given), []
    for result in results:
        item = (Near(given.pop(0)),) if result.near else ()
        item += (given.pop(0),) if result.far else ()
        answer.append(item if len(item) == 2 else item[0])
    return answer


def moved_by(array, axis, route):
    array = array.arrays[0] if isinstance(array, Near) else array
    return Near(lax.ppermute(array, axis, route))


def feature_weights(feat_query_t, feat_key_t):
    def places(info, sources=None, buffer=None):
        if info is None:
            return 2
        return [(sources[0], buffer.at[0:32]), (sources[1], buffer.at[32:64])]

    return Far([feat_query_t, feat_key_t], (128, feat_query_t.shape[1]), places)


def gathered(pieces):
    def places(info, sources=None, buffer=None):
        if info is None:
            return 8
        pairs = []
        for i, source in enumerate(sources):
            rows = info.rows(4 - i % 4, other=i >= 4)
            pairs.append((source.at[0:OWN], buffer.at[rows]))
        return pairs

    return Near(list(pieces), (ROWS, pieces[0].dims[1]), places)


def own_part(block):
    def places(info, sources=None, buffer=None):
        if info is None:
            return 1
        return [(sources[0].at[info.rows(0)], buffer)]

    return Far(block, (OWN, block.shape[1]), places)


def keys_kernel(
    info, x_ref, gain_ref, key_ref, value_ref, feat_ref, choose_ref, lanes_ref,
    normed_ref, inv_ref, raw_ref, keys_ref, values_ref, km_ref, packed_ref, edge_ref,
):
    gain = gain_ref[...]
    for part in range(4):
        x_ref.part(part)
        for i in range(2):
            rows = slice(part * 128 + i * 64, part * 128 + i * 64 + 64)
            x = x_ref.ref[rows, :].astype(f32)
            inv = lax.rsqrt(jnp.mean(x * x, axis=-1, keepdims=True) + EPS)
            inv_ref[rows, :] = inv
            normed_ref[rows, :] = (x * inv * gain).astype(bf16)
    normed_ref.send()
    inv_ref.send()
    normed = normed_ref[...]
    keys = mm(normed, key_ref[...]).astype(bf16)
    keys_ref[...] = keys
    keys_ref.send()
    values = mm(normed, value_ref[...]).astype(bf16)
    values_ref[...] = values
    values_ref.send()
    edge_ref[0] = keys[ROWS - WIN :]
    edge_ref[1] = values[ROWS - WIN :]
    edge_ref.send()
    feat_ref.ready()
    feat_ref.ref[64:128, :] = jnp.zeros((64, feat_ref.shape[1]), bf16)
    raw = mm_nt(normed, feat_ref[...])
    raw_ref[...] = raw
    raw_ref.send()
    left, right = factors(raw, choose_ref, lanes_ref)
    features = (left * right * lanes_ref[2:3, :]).astype(bf16)
    features = (features.astype(f32) * lanes_ref[3:4, :]).astype(bf16)
    tail = tail_mask(info)
    for head in range(HEADS):
        own = features[:, head * LANES : (head + 1) * LANES]
        km_ref[head] = own
        if head == HEADS - 1:
            km_ref.send()
        kept = (values[:, head_lanes(head)].astype(f32) * tail).astype(bf16)
        state = mm_tn(own, kept)
        norm = jnp.sum(own.astype(f32) * tail, axis=0, keepdims=True)
        write_packed(packed_ref, head, state, norm)


def local_kernel(
    info, raw_ref, choose_ref, lanes_ref, values_ref, km_ref, qf_ref, low_ref, num_ref, den_ref,
):
    left, right = factors(raw_ref[...], choose_ref, lanes_ref)
    features = (left * right * lanes_ref[2:3, :]).astype(bf16)
    half = ROWS // 2
    for block in range(2):
        first, reach = block * half, (block + 1) * half
        query_at = column_positions(info, first, half)
        key_at = row_positions(info, 0, reach)
        causal = (query_at >= key_at) & (doc_of(info, query_at) == doc_of(info, key_at))
        for head in range(HEADS):
            own = features[first:reach, head * LANES : (head + 1) * LANES]
            qf_ref[head, first:reach, :] = own
            weights = jnp.where(causal, mm_nt(own, km_ref[head, :reach, :]), 0.0)
            den_ref[head, first:reach, :] = jnp.sum(weights, axis=-1, keepdims=True)
            low = weights.astype(bf16)
            low_ref[head, first:reach, 0:reach] = low
            num_ref[first:reach, head_lanes(head)] = mm(low, values_ref[:reach, head_lanes(head)])


def window_kernel(
    info, normed_ref, query_ref, keys_ref, values_ref, halo_ref,
    queries_ref, probs_ref, window_ref, kept_ref,
):
    kept_ref[...] = halo_ref[...]
    queries = mm(normed_ref[...], query_ref[...]).astype(bf16)
    queries_ref[...] = queries
    queries_ref.send()
    scale = VALUE_WIDTH ** (-0.5)
    for tile in range(ROWS // TILE):
        first = tile * TILE
        query_at = column_positions(info, first, TILE)
        key_at = row_positions(info, first - WIN, TILE + WIN)
        near = (
            (key_at <= query_at)
            & (query_at - key_at < WIN)
            & (doc_of(info, query_at) == doc_of(info, key_at))
            & (key_at >= 0)
        )
        for head in range(HEADS):
            lanes = head_lanes(head)
            key_rows = window_rows(keys_ref, halo_ref, 0, tile, lanes)
            value_rows = window_rows(values_ref, halo_ref, 1, tile, lanes)
            logits = mm_nt(queries[first : first + TILE, lanes], key_rows) * scale
            logits = jnp.where(near, logits, -1e30)
            exps = jnp.exp(logits - jnp.max(logits, axis=-1, keepdims=True))
            probs = exps / jnp.sum(exps, axis=-1, keepdims=True)
            probs_ref[head, tile] = probs
            window_ref[first : first + TILE, lanes] = mm(probs.astype(bf16), value_rows)


def by_distance(ref, info, other):
    return jnp.concatenate([ref[info.rows(d, other), :] for d in range(4)], axis=0)


def mixed_kernel(
    info, before_ref, got1_ref, got2_ref, got3_ref, qf_ref, num_ref, den_ref, window_ref, out_ref,
    mixed_ref, linear_ref, total_den_ref, state_ref, norm_ref, own_ref, other_ref,
):
    use = prefix_mask(info)
    for head in range(HEADS):
        lanes = head_lanes(head)
        state, norm = read_total(before_ref, (got1_ref, got2_ref, got3_ref), head)
        state_ref[head] = state
        norm_ref[head] = jnp.broadcast_to(norm, (8, LANES))
        features = qf_ref[head]
        inter = mm(features, state) * use
        den = jnp.sum(features.astype(f32) * norm, axis=-1, keepdims=True) * use + den_ref[head]
        total_den_ref[head] = den
        linear = (inter + num_ref[:, lanes]) / den
        linear_ref[:, lanes] = linear
        mixed_ref[:, lanes] = (linear + window_ref[:, lanes]).astype(bf16)
    weights = out_ref[...]
    other_ref[...] = mm(by_distance(mixed_ref, info, True), weights).astype(bf16)
    other_ref.send()
    own_ref[...] = mm(by_distance(mixed_ref, info, False), weights).astype(bf16)


def quarters_kernel(info, own_ref, got_ref, *out_refs):
    out_refs[4][...] = got_ref[0:16, 0:128]
    for d in (1, 2, 3, 0):
        rows = slice(d * OWN, (d + 1) * OWN)
        total = own_ref[rows, :].astype(f32) + got_ref[rows, :].astype(f32)
        out_refs[d][...] = total.astype(out_refs[d].dtype)
        out_refs[d].send()


def resid_kernel(
    info, mine_ref, x_ref, gain_ref, got1_ref, got2_ref, got3_ref, normed_ref, resid_ref, inv_ref
):
    resid = x_ref[...].astype(f32) + mine_ref[...]
    for ref in (got1_ref, got2_ref, got3_ref):
        resid = resid + ref[...].astype(f32)
    inv = lax.rsqrt(jnp.mean(resid * resid, axis=-1, keepdims=True) + EPS)
    normed_ref[...] = (resid * inv * gain_ref[...]).astype(bf16)
    normed_ref.send()
    resid_ref[...] = resid
    inv_ref[...] = inv


def grad_resid_kernel(
    info, mine_ref, resid_ref, inv_ref, top_ref, gain_ref, got1_ref, got2_ref, got3_ref,
    sent_ref, grad_ref, gains_ref,
):
    grad = mine_ref[...]
    for ref in (got1_ref, got2_ref, got3_ref):
        grad = grad + ref[...].astype(f32)
    resid = resid_ref[...]
    inv = inv_ref[...]
    grad_resid = top_ref[...].astype(f32) + norm_back(resid, inv, gain_ref[...], grad)
    sent_ref[...] = grad_resid.astype(bf16)
    sent_ref.send()
    grad_ref[...] = grad_resid
    gains_ref[0:1, :] = jnp.sum(grad * resid * inv, axis=0, keepdims=True)


def grad_x_kernel(
    info, mine_ref, x_ref, grad_resid_ref, gain_ref, resid_ref, out_ref, got1_ref, got2_ref, got3_ref,
    out1_ref, out2_ref, out3_ref, sent_ref,
):
    total = resid_ref[...] + out_ref[...]
    for ref in (out1_ref, out2_ref, out3_ref):
        total = total + ref[...].astype(f32)
    sent_ref[0:OWN, :] = total.astype(bf16)
    grad = mine_ref[...]
    for ref in (got1_ref, got2_ref, got3_ref):
        grad = grad + ref[...].astype(f32)
    x = x_ref[...].astype(f32)
    inv = lax.rsqrt(jnp.mean(x * x, axis=-1, keepdims=True) + EPS)
    sent_ref[OWN:, :] = (grad_resid_ref[...] + norm_back(x, inv, gain_ref[...], grad)).astype(bf16)


def norm_back(in_rows, inv_rms, gain, grad_normed):
    weighted = grad_normed * gain
    return inv_rms * weighted - in_rows * inv_rms**3 * jnp.mean(
        weighted * in_rows, axis=-1, keepdims=True
    )


def grad_act_kernel(info, top_ref, down_ref, out_ref):
    top = top_ref[...]
    for first in range(0, down_ref.shape[0], 256):
        span = slice(first, min(first + 256, down_ref.shape[0]))
        out_ref[:, span] = mm_nt(top, down_ref[span, :])


def ffn_kernel(
    info, in_ref, gate_ref, up_ref, grad_act_ref,
    other_ref, own_ref, normed_ref, act_ref, grad_gate_ref, grad_up_ref,
):
    normed = in_ref[...]
    normed_ref[...] = normed
    normed_ref.send()
    hidden = gate_ref.shape[0]
    for first in range(0, hidden, 256):
        span = slice(first, min(first + 256, hidden))
        gate = mm_nt(normed, gate_ref[span, :])
        up_value = mm_nt(normed, up_ref[span, :])
        sigmoid_gate = jax.nn.sigmoid(gate)
        silu_gate = gate * sigmoid_gate
        act_ref[:, span] = (silu_gate * up_value).astype(bf16)
        grad_act = grad_act_ref[:, span]
        grad_gate_ref[:, span] = (
            grad_act * up_value * sigmoid_gate * (1.0 + gate * (1.0 - sigmoid_gate))
        ).astype(bf16)
        grad_up_ref[:, span] = (grad_act * silu_gate).astype(bf16)
    for ref in (act_ref, grad_gate_ref, grad_up_ref):
        ref.send()
    for target, other in ((other_ref, True), (own_ref, False)):
        grad_gate = by_distance(grad_gate_ref, info, other)
        grad_up = by_distance(grad_up_ref, info, other)
        for first in range(0, target.shape[1], 512):
            span = slice(first, first + 512)
            part = mm(grad_gate, gate_ref[:, span]) + mm(grad_up, up_ref[:, span])
            target[:, span] = part.astype(bf16)
        target.send()


def ffn_out_kernel(info, act_ref, down_ref, other_ref, own_ref):
    for target, other in ((other_ref, True), (own_ref, False)):
        act = by_distance(act_ref, info, other)
        for first in range(0, target.shape[1], 512):
            span = slice(first, first + 512)
            target[:, span] = mm(act, down_ref[:, span]).astype(bf16)
        target.send()


def ffn_grads_kernel(info, normed_ref, gate_ref, up_ref, out_ref):
    hidden = gate_ref.shape[1]
    gate, up = gate_ref[...], up_ref[...]
    for part in range(4):
        span = slice(part * 512, (part + 1) * 512)
        normed = normed_ref[:, span]
        out_ref[span, 0:hidden] = mm_tn(normed, gate).astype(bf16)
        out_ref[span, hidden : 2 * hidden] = mm_tn(normed, up).astype(bf16)
        out_ref.send(part)


def down_grads_kernel(info, top_ref, act_ref, out_ref):
    act = act_ref[...]
    for part in range(4):
        span = slice(part * 512, (part + 1) * 512)
        out_ref[span, :] = mm_tn(top_ref[:, span], act).astype(bf16)
        out_ref.send(part)


def grad_x_out_kernel(info, p0, p1, p2, p3, s0, s1, s2, s3, output_ref, grad_ref):
    for i, piece in enumerate((p0, p1, p2, p3, s0, s1, s2, s3)):
        rows = info.rows(4 - i % 4, other=i >= 4)
        output_ref[rows, :] = piece[0:OWN, :]
        grad_ref[rows, :] = piece[OWN : 2 * OWN, :].astype(f32)


def mixed_back_kernel(
    info, in_ref, out_ref, linear_ref, den_ref, qf_ref,
    packed_ref, top_ref, gm_ref, gnum_ref, gden_ref,
):
    top = in_ref[...]
    grad_mixed = mm_nt(top, out_ref[...]).astype(bf16)
    gm_ref[...] = grad_mixed
    gm_ref.send()
    top_ref[...] = top
    top_ref.send()
    use = prefix_mask(info)
    for head in range(HEADS):
        lanes = head_lanes(head)
        wide = grad_mixed[:, lanes].astype(f32)
        den = den_ref[head]
        grad_num = (wide / den).astype(bf16)
        gnum_ref[:, lanes] = grad_num
        grad_den = -jnp.sum(wide * linear_ref[:, lanes], axis=-1, keepdims=True) / den
        gden_ref[head] = grad_den
        features = qf_ref[head]
        used = (grad_num.astype(f32) * use).astype(bf16)
        state = mm_tn(features, used)
        norm = jnp.sum(features.astype(f32) * (grad_den * use), axis=0, keepdims=True)
        write_packed(packed_ref, head, state, norm)
    packed_ref.send()


def window_back_kernel(
    info, gm_ref, probs_ref, keys_ref, values_ref, halo_ref, queries_ref,
    edge_ref, gq_ref, gk_ref, gv_ref, key_acc, value_acc,
):
    scale = VALUE_WIDTH ** (-0.5)
    key_acc[...] = jnp.zeros_like(key_acc)
    value_acc[...] = jnp.zeros_like(value_acc)
    for tile in range(ROWS // TILE):
        first = tile * TILE
        reach = slice(first, first + TILE + WIN)
        for head in range(HEADS):
            lanes = head_lanes(head)
            key_rows = window_rows(keys_ref, halo_ref, 0, tile, lanes)
            value_rows = window_rows(values_ref, halo_ref, 1, tile, lanes)
            top = gm_ref[first : first + TILE, lanes]
            probs = probs_ref[head, tile]
            grad_probs = mm_nt(top, value_rows)
            shared = jnp.sum(grad_probs * probs, axis=-1, keepdims=True)
            grad_logits = (probs * (grad_probs - shared)).astype(bf16)
            gq_ref[first : first + TILE, lanes] = (mm(grad_logits, key_rows) * scale).astype(bf16)
            queries = queries_ref[first : first + TILE, lanes]
            key_acc[reach, lanes] += mm_tn(grad_logits, queries) * scale
            value_acc[reach, lanes] += mm_tn(probs.astype(bf16), top)
    edge_ref[0] = key_acc[0:WIN, :].astype(bf16)
    edge_ref[1] = value_acc[0:WIN, :].astype(bf16)
    gk_ref[...] = key_acc[WIN:, :]
    gv_ref[...] = value_acc[WIN:, :]


def linear_back_kernel(
    info, gnum_ref, gden_ref, values_ref, low_ref, km_ref, qf_ref, state_ref, norm_ref, raw_ref,
    choose_ref, lanes_ref, window_gv_ref, gfeat_ref, gv_ref, gkf_ref,
):
    use = prefix_mask(info)
    half = ROWS // 2
    grads = [[None, None], [None, None]]
    for head in range(HEADS):
        lanes = head_lanes(head)
        inter = mm_nt((gnum_ref[:, lanes].astype(f32) * use).astype(bf16), state_ref[head])
        inter = inter + (gden_ref[head] * use) * norm_ref[head, 0:1, :]
        for block in range(2):
            first, reach = block * half, (block + 1) * half
            query_at = column_positions(info, first, half)
            key_at = row_positions(info, 0, reach)
            causal = (query_at >= key_at) & (doc_of(info, query_at) == doc_of(info, key_at))
            grad_num = gnum_ref[first:reach, lanes]
            grad = mm_nt(grad_num, values_ref[:reach, lanes]) + gden_ref[head, first:reach, :]
            grad = jnp.where(causal, grad, 0.0).astype(bf16)
            grads[head][block] = mm(grad, km_ref[head, :reach, :]) + inter[first:reach]
            key_part = mm_tn(grad, qf_ref[head, first:reach, :])
            value_part = mm_tn(low_ref[head, first:reach, 0:reach], grad_num)
            if block == 0:
                gkf_ref[head, 0:half] = key_part
                gv_ref[0:half, lanes] = window_gv_ref[0:half, lanes] + value_part
            else:
                gkf_ref[head, 0:half] += key_part[0:half]
                gkf_ref[head, half:] = key_part[half:]
                gv_ref[0:half, lanes] += value_part[0:half]
                gv_ref[half:, lanes] = window_gv_ref[half:, lanes] + value_part[half:]
    left, right = factors(raw_ref[...], choose_ref, lanes_ref)
    gradient = jnp.concatenate([jnp.concatenate(g, axis=0) for g in grads], axis=1)
    gradient = gradient * lanes_ref[2:3, :]
    gfeat_ref[...] = feature_back(gradient, left, right, choose_ref)


def keys_back_kernel(
    info, before_ref, got1_ref, got2_ref, got3_ref, values_ref, km_ref, gkf_ref, gk_ref, gv_ref,
    right_ref, raw_ref, choose_ref, lanes_ref, gfeat_ref,
    gkw_ref, gvw_ref, gf_ref,
):
    tail = tail_mask(info)
    inner = ROWS - WIN
    gkw_ref[0:inner, :] = gk_ref[0:inner, :].astype(bf16)
    gkw_ref[inner:, :] = (gk_ref[inner:, :] + right_ref[0].astype(f32)).astype(bf16)
    gradients = []
    for head in range(HEADS):
        lanes = head_lanes(head)
        later, norm = read_total(before_ref, (got1_ref, got2_ref, got3_ref), head)
        kept = (values_ref[:, lanes].astype(f32) * tail).astype(bf16)
        gradients.append(gkf_ref[head] + mm_nt(kept, later) + tail * norm)
        grad_values = gv_ref[:, lanes] + mm(km_ref[head], later) * tail
        gvw_ref[0:inner, lanes] = grad_values[0:inner].astype(bf16)
        gvw_ref[inner:, lanes] = (grad_values[inner:] + right_ref[1, :, lanes].astype(f32)).astype(
            bf16
        )
    left, right = factors(raw_ref[...], choose_ref, lanes_ref)
    gradient = jnp.concatenate(gradients, axis=1) * lanes_ref[4:5, :]
    gf_ref[...] = (feature_back(gradient, left, right, choose_ref) + gfeat_ref[...]).astype(bf16)


def normed_back_kernel(
    info, gq_ref, gkw_ref, gvw_ref, gf_ref, wq_ref, wk_ref, wv_ref, wf_ref, x_ref, inv_ref, gain_ffn_ref,
    other_ref, own_ref, gains_ref,
):
    wf_ref.ready()
    wf_ref.ref[64:128, :] = jnp.zeros((64, wf_ref.shape[1]), bf16)
    for target, other in ((other_ref, True), (own_ref, False)):
        grads = [by_distance(ref, info, other) for ref in (gq_ref, gkw_ref, gvw_ref, gf_ref)]
        scaled_by = by_distance(inv_ref, info, other)
        for piece in range(4):
            span = slice(piece * 512, (piece + 1) * 512)
            part = mm_nt(grads[0], wq_ref[span, :])
            part = part + mm_nt(grads[1], wk_ref[span, :])
            part = part + mm_nt(grads[2], wv_ref[span, :])
            part = part + mm(grads[3], wf_ref[:, span])
            target[:, span] = part.astype(bf16)
            x_rows = jnp.concatenate([x_ref[info.rows(d, other), span] for d in range(4)], axis=0)
            total = jnp.sum(part * (x_rows.astype(f32) * scaled_by), axis=0, keepdims=True)
            gains_ref[0:1, span] = total if other else total + gains_ref[0:1, span]
    gains_ref[1:2, :] = gain_ffn_ref[0:1, :]


def mix_grads_kernel(
    info, normed_ref, gq_ref, gk_ref, gv_ref, gf_ref, top_ref, mixed_ref, down_ref, out_ref
):
    gq, gk, gv, gf, mixed = gq_ref[...], gk_ref[...], gv_ref[...], gf_ref[...], mixed_ref[...]
    for part in range(4):
        span = slice(part * 512, (part + 1) * 512)
        normed = normed_ref[:, span]
        out_ref[span, 0:256] = mm_tn(normed, gq).astype(bf16)
        out_ref[span, 256:512] = mm_tn(normed, gk).astype(bf16)
        out_ref[span, 512:768] = mm_tn(normed, gv).astype(bf16)
        out_ref[span, 768:1024] = mm_tn(top_ref[:, span], mixed).astype(bf16)
        out_ref[span, 1024:1152] = mm_tn(normed, gf).astype(bf16)
        down_ref.part(part)
        out_ref.send(part)


def mix_sum_kernel(
    info, in_ref, grad_q_ref, grad_k_ref, grad_v_ref, grad_out_ref, feat_query_ref, feat_key_ref,
    down_ref,
):
    for i, target in enumerate((grad_q_ref, grad_k_ref, grad_v_ref)):
        target[...] = in_ref[:, i * 256 : (i + 1) * 256].astype(f32)
        target.send()
    grad_out_ref[...] = in_ref[:, 768:1024].astype(f32).T
    feat = in_ref[:, 1024:1152].astype(f32).T
    feat_query_ref[...] = feat[0:32]
    feat_key_ref[...] = feat[32:64]
    down_ref[...] = in_ref[:, 1152:].astype(f32).T


def total_of(refs):
    total = refs[0][...]
    for ref in refs[1:]:
        total = total + ref[...]
    return total


def gains_kernel(info, *refs):
    refs[-1][...] = total_of(refs[:-1])


def spread_kernel(along, info, *refs):
    total, (*to_refs, acc_ref) = total_of(refs[:-5]), refs[-5:]
    acc_ref[...] = total
    for d, ref in enumerate(to_refs):
        count = ref.shape[1]
        at = lax.bitwise_and((info.x if along == "x" else info.z) + d, 3) * count
        ref[...] = acc_ref[:, pl.ds(pl.multiple_of(at, count), count)]


def ffn_sum_kernel(info, in_ref, gate_ref, up_ref):
    hidden = gate_ref.shape[0]
    whole = in_ref[...].astype(f32).T
    for i, ref in enumerate((gate_ref, up_ref)):
        ref[...] = whole[i * hidden : (i + 1) * hidden]
        ref.send()


def along_y(distance):
    return [(i, (i + 2 * distance) % 8) for i in range(8)]


def sibling():
    return [(i, i ^ 1) for i in range(8)]


def along_x(distance):
    return [(i, (i + 4 * distance) % 16) for i in range(16)]


def along_z(distance):
    return [(4 * a + z, 4 * a + (z + distance) % 4) for a in range(4) for z in range(4)]


def head_quarters(own, other, after=()):
    got = moved_by(other, "head", sibling())
    width = own.dims[1]
    with jax.named_scope("quarters"):
        mine, *sent, token = call(
            quarters_kernel,
            [near(OWN, width, dtype=f32)] + [near(OWN, width)] * 3 + [near(16, 128)],
            (own, got), after=after,
        )
    parts = [moved_by(sent[d - 1], "head", along_y(d)) for d in (1, 2, 3)]
    return mine, parts, moved_by(token, "head", sibling())


def head_pieces(own):
    pieces = [own] + [moved_by(own, "head", along_y(d)) for d in (1, 2, 3)]
    return pieces + [moved_by(piece, "head", sibling()) for piece in pieces]


def spread(parts, along):
    rows, width = parts[0].dims
    with jax.named_scope("gains"):
        return call(
            functools.partial(spread_kernel, along), [near(rows, width // 4, dtype=f32)] * 4, parts,
            scratch=[pltpu.VMEM((rows, width), f32)],
        )


def gains_over_head(gains):
    with jax.named_scope("gains"):
        (pair,) = call(
            gains_kernel, [near(*gains.dims, dtype=f32)], (gains, moved_by(gains, "head", sibling()))
        )
    return spread([pair] + [moved_by(pair, "head", along_y(d)) for d in (1, 2, 3)], "x")


def gains_over_seq(gains):
    own, *sent = gains
    own, *sent = spread([own] + [moved_by(s, "seq", along_x(d)) for d, s in enumerate(sent, 1)], "z")
    parts = [own] + [moved_by(s, "seq", along_z(d)) for d, s in enumerate(sent, 1)]
    with jax.named_scope("gains"):
        (total,) = call(gains_kernel, [far(*own.dims, dtype=f32)], parts)
    return total


def scan_kernel(reverse, info, own_ref, got1_ref, got2_ref, got3_ref, before_ref, *sent_refs):
    place_x, place_z = (3 - info.x, 3 - info.z) if reverse else (info.x, info.z)
    before = jnp.zeros(own_ref.shape, f32)
    for d, ref in enumerate((got1_ref, got2_ref, got3_ref), 1):
        before = before + ref[...].astype(f32) * (place_x >= d).astype(f32)
    before_ref[...] = before
    row = lax.broadcasted_iota(jnp.int32, (HEADS, 16, 128), 1)
    sent = []
    for total in (before, before + own_ref[...].astype(f32)):
        norm = total[:, KEPT:]
        norm = norm + jnp.roll(norm, -2, axis=1)
        high = norm.astype(bf16).astype(f32)
        rest = jnp.roll(norm - high, 2, axis=1)
        norm = jnp.where(row < 2, high, jnp.where(row < 4, rest, 0.0))
        sent.append((total[:, :KEPT], norm))
    for d, ref in enumerate(sent_refs, 1):
        with_own = (place_z + d < 4).astype(f32)
        for part, rows in ((0, slice(0, KEPT)), (1, slice(KEPT, PACKED))):
            less, more = sent[0][part], sent[1][part]
            ref[:, rows, :] = (more * with_own + less * (1.0 - with_own)).astype(bf16)


def exclusive_parts(own, reverse, after=()):
    sign = -1 if reverse else 1
    got = [moved_by(own, "seq", along_x(sign * d)) for d in (1, 2, 3)]
    with jax.named_scope("scan"):
        before, *sent = call(
            functools.partial(scan_kernel, reverse),
            [near(*own.dims, dtype=f32)] + [near(*own.dims)] * 3, (own, *got), after=after,
        )
    return [before] + [
        moved_by(sent[d - 1], "seq", along_z(sign * d)) for d in (1, 2, 3)
    ]


def shifted(block, distance):
    route = [(i - distance, i) for i in range(16) if 0 <= i - distance < 16]
    return moved_by(block, "seq", route)


def shards(
    inputs,
    gain_mix,
    feat_query,
    feat_key,
    win_query,
    win_key,
    value_proj,
    out_proj,
    gain_ffn,
    gate_proj,
    up_proj,
    down_proj,
    document_starts,
    cotangent,
):
    choose, lanes = feature_tables()
    choose = jnp.asarray(choose, bf16)
    lanes = jnp.asarray(lanes, f32)
    choose_q, choose_k = choose[0], choose[1]
    feat = feature_weights(feat_query.T, feat_key.T)
    gain_mix = gain_mix.reshape(1, -1)
    gain_ffn = gain_ffn.reshape(1, -1)
    model = inputs.shape[1]
    width = HEADS * VALUE_WIDTH
    hidden = gate_proj.shape[1]
    half = ROWS // 2
    unit = 2 * ROWS * model
    starts = document_starts

    (normed, normed_far), inv_mix, (raw, raw_far), (keys, keys_far), (values, values_far), *rest = call(
        keys_kernel,
        (
            both(ROWS, model), far(ROWS, 1, dtype=f32), both(ROWS, 128, dtype=f32),
            both(ROWS, width), both(ROWS, width), both(HEADS, ROWS, LANES),
            near(HEADS, PACKED, 128), near(2, WIN, width),
        ),
        (Far(inputs, parts=4), gain_mix, win_key, value_proj, feat, choose_k, lanes),
        starts=starts, flops=unit * 640,
    )
    (km, km_far), packed, edge = rest
    halo = shifted(edge, 1)
    (qf, qf_far), low, num, den = call(
        local_kernel,
        (
            both(HEADS, ROWS, LANES), far(HEADS, ROWS, ROWS), near(ROWS, width, dtype=f32),
            near(HEADS, ROWS, 1, dtype=f32),
        ),
        (raw, choose_q, lanes, values, km),
        starts=starts, flops=unit * 300,
    )
    sums = exclusive_parts(packed, False, after=(qf, halo))
    queries, probs, window, halo_far = call(
        window_kernel,
        (
            far(ROWS, width), far(HEADS, 4, TILE, TILE + WIN, dtype=f32),
            near(ROWS, width, dtype=f32), far(2, WIN, width),
        ),
        (normed, win_query, keys, values, halo),
        starts=starts, flops=unit * 400,
    )
    mixed, linear, total_den, state, norm, own, other = call(
        mixed_kernel,
        (
            far(ROWS, width), far(ROWS, width, dtype=f32), far(HEADS, ROWS, 1, dtype=f32),
            far(HEADS, LANES, VALUE_WIDTH), far(HEADS, 8, LANES, dtype=f32),
            near(half, model), near(half, model),
        ),
        (*sums, qf, num, den, window, out_proj),
        starts=starts, flops=unit * 300,
    )
    mine, parts, signal = head_quarters(own, other)
    (grad_act,) = call(
        grad_act_kernel, (far(ROWS, hidden, dtype=f32),), (cotangent, down_proj),
        after=(signal,), flops=unit * hidden,
    )
    own_normed, resid, inv_ffn = call(
        resid_kernel,
        (near(OWN, model), far(OWN, model, dtype=f32), far(OWN, 1, dtype=f32)),
        (mine, own_part(inputs), gain_ffn, *parts), after=(grad_act,),
    )
    pieces = head_pieces(own_normed)
    other, own, normed_ffn, activation, grad_gate, grad_up = call(
        ffn_kernel,
        (
            near(half, model), near(half, model), near(ROWS, model), far(ROWS, hidden),
            near(ROWS, hidden), near(ROWS, hidden),
        ),
        (gathered(pieces), gate_proj.T, up_proj.T, grad_act),
        flops=unit * 4 * hidden,
    )
    (ffn_grads_part,) = call(
        ffn_grads_kernel, (far(model, 2 * hidden, parts=4),), (normed_ffn, grad_gate, grad_up),
        flops=unit * 2 * hidden,
    )
    ffn_grads = lax.psum_scatter(ffn_grads_part, "seq", scatter_dimension=0, tiled=True)
    mine, parts, signal = head_quarters(own, other, after=(ffn_grads_part,))
    (down_grads,) = call(
        down_grads_kernel, (far(model, hidden, parts=4),), (cotangent, activation),
        after=(signal,), flops=unit * hidden,
    )
    sent, grad_resid, gain_ffn_part = call(
        grad_resid_kernel,
        (near(OWN, model), far(OWN, model, dtype=f32), far(8, model, dtype=f32)),
        (mine, resid, inv_ffn, own_part(cotangent), gain_ffn, *parts), after=(down_grads,),
    )
    pieces = head_pieces(sent)
    packed, top, grad_mixed, grad_num, grad_den = call(
        mixed_back_kernel,
        (
            near(HEADS, PACKED, 128), far(ROWS, model), near(ROWS, width), near(ROWS, width),
            near(HEADS, ROWS, 1, dtype=f32),
        ),
        (gathered(pieces), out_proj, linear, total_den, qf_far),
        starts=starts, flops=unit * 300,
    )
    edge, gq, gk, gv = call(
        window_back_kernel,
        (
            near(2, WIN, width), near(ROWS, width), near(ROWS, width, dtype=f32),
            near(ROWS, width, dtype=f32),
        ),
        (grad_mixed, probs, keys_far, values_far, halo_far, queries),
        flops=unit * 300, scratch=[pltpu.VMEM((ROWS + WIN, width), f32)] * 2,
    )
    right = shifted(edge, -1)
    sums = exclusive_parts(packed, True, after=(edge,))
    gfeat, gv, gkf = call(
        linear_back_kernel,
        (
            near(ROWS, 128, dtype=f32), near(ROWS, width, dtype=f32),
            near(HEADS, ROWS, LANES, dtype=f32),
        ),
        (
            grad_num, grad_den, values_far, low, km_far, qf_far, state, norm, raw_far, choose_q,
            lanes, gv,
        ),
        starts=starts, after=(sums[0],), flops=unit * 300,
    )
    gkw, gvw, gf = call(
        keys_back_kernel,
        (near(ROWS, width), near(ROWS, width), near(ROWS, 128)),
        (
            *sums, values_far, km_far, gkf, gk, gv, right, raw_far, choose_k, lanes, gfeat,
        ),
        starts=starts, flops=unit * 300,
    )
    (mix_grads_part,) = call(
        mix_grads_kernel, (far(model, 1152 + hidden, parts=4),),
        (normed_far, gq, gkw, gvw, gf, top, mixed, Into(down_grads, 0, 1152, 4)), flops=unit * 1152,
    )
    mix_grads = lax.psum_scatter(mix_grads_part, "seq", scatter_dimension=0, tiled=True)
    other, own, gains = call(
        normed_back_kernel, (near(half, model), near(half, model), near(2, model, dtype=f32)),
        (
            gq, gkw, gvw, gf, win_query, win_key, value_proj, feat, inputs, inv_mix, gain_ffn_part,
        ),
        after=(mix_grads_part,),
        flops=unit * 900,
    )
    mine, parts, signal = head_quarters(own, other)
    other, own = call(
        ffn_out_kernel, (near(half, model), near(half, model)), (activation, down_proj),
        after=(signal,), flops=unit * hidden,
    )
    out_mine, out_parts, signal = head_quarters(own, other)
    gains = gains_over_seq(gains_over_head(gains))
    grad_gate_t, grad_up_t = call(
        ffn_sum_kernel, (far(hidden, 128, dtype=f32),) * 2, (ffn_grads,), after=(signal,)
    )
    (sent,) = call(
        grad_x_kernel, (near(2 * OWN, model),),
        (mine, own_part(inputs), grad_resid, gain_mix, resid, out_mine, *parts, *out_parts),
        after=(gains, grad_up_t),
    )
    pieces = head_pieces(sent)
    output, grad_x = call(
        grad_x_out_kernel, (far(ROWS, model), far(ROWS, model, dtype=f32)), pieces,
    )
    grad_wq, grad_wk, grad_wv, grad_out, grad_fq_t, grad_fk_t, grad_down = call(
        mix_sum_kernel,
        (far(128, 256, dtype=f32),) * 3
        + (far(256, 128, dtype=f32), far(32, 128, dtype=f32), far(32, 128, dtype=f32))
        + (far(hidden, 128, dtype=f32),),
        (mix_grads,), after=(grad_x,),
    )
    return (
        output,
        grad_x,
        gains[0],
        grad_fq_t.T,
        grad_fk_t.T,
        grad_wq,
        grad_wk,
        grad_wv,
        grad_out,
        gains[1],
        grad_gate_t.T,
        grad_up_t.T,
        grad_down,
    )


def solution(mesh):
    placed = (
        P("seq", None),
        P(),
        P(None, "head"),
        P(None, "head"),
        P(None, "head"),
        P(None, "head"),
        P(None, "head"),
        P("head", None),
        P(),
        P(None, "head"),
        P(None, "head"),
        P("head", None),
        P(),
        P("seq", None),
    )
    return jax.shard_map(
        shards,
        mesh=mesh,
        in_specs=placed,
        out_specs=(
            P("seq", None),
            P("seq", None),
            P("seq"),
            P("seq", "head"),
            P("seq", "head"),
            P("seq", "head"),
            P("seq", "head"),
            P("seq", "head"),
            P("head", "seq"),
            P("seq"),
            P("seq", "head"),
            P("seq", "head"),
            P("head", "seq"),
        ),
        check_vma=False,
    )
```

```python
import functools
import math

import jax
import jax.numpy as jnp
import numpy as np
from jax import lax
from jax.experimental import pallas as pl
from jax.experimental.pallas import tpu as pltpu
from jax.sharding import PartitionSpec as P

F = 16
VALUE_WIDTH = 128
WIN = 64
EPS = 1e-05

HEADS = 2
ROWS = 512
LANES = 256
KEPT = 160
PACKED = 176
TILE = 128
OWN = 64
f32 = jnp.float32
bf16 = jnp.bfloat16


def feature_tables():
    pairs = [(a, b) for a in range(F) for b in range(a, F)]
    count = len(pairs)
    choose = np.zeros((2, 2, 128, HEADS * LANES), np.float32)
    lanes = np.zeros((8, HEADS * LANES), np.float32)
    factor = F ** (-0.25)
    for head in range(HEADS):
        at = head * LANES
        for side in range(2):
            row = side * HEADS * F + head * F
            for lane, (a, b) in enumerate(pairs):
                choose[side, 0, row + a, at + lane] = 1.0
                choose[side, 1, row + b, at + lane] = 1.0
            for a in range(F):
                choose[side, 0, row + a, at + count + a] = 1.0
        for lane, (a, b) in enumerate(pairs):
            lanes[2, at + lane] = factor * factor / math.sqrt(2.0)
            lanes[3, at + lane] = 1.0 if a == b else 2.0
        lanes[1, at + count : at + count + F + 1] = 1.0
        lanes[0, at + count + F] = 1.0
        lanes[2, at + count : at + count + F] = factor
        lanes[2, at + count + F] = 1.0
        lanes[3, at + count : at + count + F + 1] = 1.0
    lanes[4] = lanes[2] * lanes[3]
    return choose, lanes


def mm(a, b):
    return lax.dot_general(a, b, (((1,), (0,)), ((), ())), preferred_element_type=f32)


def mm_nt(a, b):
    return lax.dot_general(a, b, (((1,), (1,)), ((), ())), preferred_element_type=f32)


def mm_tn(a, b):
    return lax.dot_general(a, b, (((0,), (0,)), ((), ())), preferred_element_type=f32)


def low_pair(part):
    high = part.astype(bf16)
    return high, (part - high.astype(f32)).astype(bf16)


class Place:

    def __init__(self, starts):
        me, seq = lax.axis_index("head"), lax.axis_index("seq")
        self.base = seq * ROWS
        self.x, self.z = lax.shift_right_logical(seq, 2), lax.bitwise_and(seq, 3)
        self.y, self.core = lax.shift_right_logical(me, 1), lax.bitwise_and(me, 1)
        self.loaded = starts

    def starts(self):
        return [self.loaded[0, i] for i in range(4)]

    def rows(self, distance, other=False):
        quarter = lax.bitwise_and(self.y + distance, 3)
        core = 1 - self.core if other else self.core
        return pl.ds(pl.multiple_of(quarter * (2 * OWN) + core * OWN, OWN), OWN)


class Loaded:

    def __init__(self, ref, copies):
        self.ref, self.copies = ref, list(copies)
        self.shape = ref.shape

    def part(self, index):
        if self.copies and self.copies[index] is not None:
            self.copies[index].wait()
            self.copies[index] = None

    def ready(self):
        for index in range(len(self.copies)):
            self.part(index)

    def __getitem__(self, index):
        self.ready()
        return self.ref[index]


class Stored:

    def __init__(self, ref, copies):
        self.ref, self.copies, self.sent = ref, copies, set()
        self.shape, self.dtype = ref.shape, ref.dtype

    def __getitem__(self, index):
        return self.ref[index]

    def __setitem__(self, index, value):
        self.ref[index] = value

    def send(self, part=None):
        for index in range(len(self.copies)) if part is None else (part,):
            if index not in self.sent:
                self.copies[index].start()
                self.sent.add(index)


def doc_of(info, position):
    starts = info.starts()
    count = (position >= starts[0]).astype(jnp.int32)
    for start in starts[1:]:
        count = count + (position >= start).astype(jnp.int32)
    return count


def column_positions(info, first, count):
    return info.base + first + lax.broadcasted_iota(jnp.int32, (count, 1), 0)


def row_positions(info, first, count):
    return info.base + first + lax.broadcasted_iota(jnp.int32, (1, count), 1)


def prefix_mask(info):
    before = doc_of(info, info.base - 1)
    same = doc_of(info, column_positions(info, 0, ROWS)) == before
    return (same & (info.base > 0)).astype(f32)


def tail_mask(info):
    last = doc_of(info, info.base + ROWS - 1)
    return (doc_of(info, column_positions(info, 0, ROWS)) == last).astype(f32)


def factors(raw, choose_ref, lanes_ref):
    high, rest = low_pair(raw)
    left = (raw - high.astype(f32) - rest.astype(f32)).astype(bf16)
    return [
        mm(high, choose_ref[i]) + mm(rest, choose_ref[i]) + mm(left, choose_ref[i]) + lanes_ref[i : i + 1, :]
        for i in range(2)
    ]


def factors_back(raw, choose_ref, lanes_ref):
    high, rest = low_pair(raw)
    return [
        mm(high, choose_ref[i]) + mm(rest, choose_ref[i]) + lanes_ref[i : i + 1, :]
        for i in range(2)
    ]


def feature_back(gradient, left, right, choose_ref):
    total = None
    for term, table in ((gradient * right, choose_ref[0]), (gradient * left, choose_ref[1])):
        high, rest = low_pair(term)
        part = mm_nt(high, table) + mm_nt(rest, table)
        total = part if total is None else total + part
    return total


def write_packed(packed_ref, head, state, norm):
    packed_ref[head, 0:KEPT, :] = state[:KEPT].astype(bf16)
    row = lax.broadcasted_iota(jnp.int32, (16, 128), 0)
    high = norm.astype(bf16).astype(f32)
    rest = norm - high
    tile = jnp.where(row == 0, high[:, :128], 0.0)
    tile = jnp.where(row == 1, high[:, 128:], tile)
    tile = jnp.where(row == 2, rest[:, :128], tile)
    tile = jnp.where(row == 3, rest[:, 128:], tile)
    packed_ref[head, KEPT:PACKED, :] = tile.astype(bf16)


def read_total(before_ref, got_refs, head):
    total = before_ref[head]
    for ref in got_refs:
        total = total + ref[head].astype(f32)
    state = jnp.concatenate(
        [total[:KEPT], jnp.zeros((LANES - KEPT, VALUE_WIDTH), f32)], axis=0
    ).astype(bf16)
    norm = jnp.concatenate(
        [
            total[KEPT : KEPT + 1] + total[KEPT + 2 : KEPT + 3],
            total[KEPT + 1 : KEPT + 2] + total[KEPT + 3 : KEPT + 4],
        ],
        axis=1,
    )
    return state, norm


def head_lanes(head):
    return slice(head * VALUE_WIDTH, (head + 1) * VALUE_WIDTH)


def window_rows(own_ref, halo_ref, which, tile, lanes):
    first = tile * TILE
    if tile == 0:
        return jnp.concatenate([halo_ref[which, :, lanes], own_ref[0:TILE, lanes]], axis=0)
    return own_ref[first - WIN : first + TILE, lanes]


class Near:
    near = True

    def __init__(self, arrays, dims=None, places=None, parts=1):
        self.arrays = [
            a.arrays[0] if isinstance(a, Near) else a
            for a in (arrays if isinstance(arrays, (list, tuple)) else [arrays])
        ]
        self.dims = tuple(dims or self.arrays[0].shape)
        self.dtype = self.arrays[0].dtype
        self.places, self.parts = places, parts

    def copies(self, info, refs, buffer):
        if self.places is None:
            return pieces_of(refs[0], buffer, self.parts)
        return self.places(info, refs, buffer)

    def count(self):
        return self.parts if self.places is None else self.places(None)

    def copied(self):
        return self.places is not None


class Far(Near):
    near = False

    def copied(self):
        return True


class Out:

    def __init__(self, *dims, dtype=bf16, near=False, far=False, parts=1, width=None, first=0, onto=None):
        self.dims, self.dtype, self.parts = dims, dtype, parts
        self.near, self.far = near, far
        self.whole = dims if width is None else (dims[0], width)
        self.first, self.onto = first, onto

    def shapes(self):
        near = [jax.ShapeDtypeStruct(self.dims, self.dtype)] * self.near
        return near + [pltpu.HBM(self.whole, self.dtype)] * self.far

    def spaces(self):
        return [pltpu.VMEM] * self.near + [pltpu.HBM] * self.far

    def copies(self, buffer, target):
        if self.whole != self.dims:
            target = target.at[:, self.first : self.first + self.dims[1]]
        return pieces_of(buffer, target, self.parts)


class Stage:
    near, far, parts, onto = True, False, 1, None

    def __init__(self, source):
        self.source = source if isinstance(source, Far) else Far(source)
        self.dims, self.dtype = self.source.dims, self.source.dtype

    def shapes(self):
        return [jax.ShapeDtypeStruct(self.dims, self.dtype)]

    def spaces(self):
        return [pltpu.VMEM]


def near(*dims, dtype=bf16):
    return Out(*dims, dtype=dtype, near=True)


def far(*dims, dtype=bf16, parts=1, **columns):
    return Out(*dims, dtype=dtype, far=True, parts=parts, **columns)


def both(*dims, dtype=bf16):
    return Out(*dims, dtype=dtype, near=True, far=True)


def pieces_of(source, target, parts):
    if parts == 1:
        return [(source, target)]
    count = source.shape[0] // parts
    return [
        (source.at[i * count : (i + 1) * count], target.at[i * count : (i + 1) * count])
        for i in range(parts)
    ]


def in_hbm(array):
    return pltpu.with_memory_space_constraint(array, pltpu.HBM)


def call(body, results, operands, starts=None, after=(), flops=0, scratch=(), megabytes=28):
    operands = [o if isinstance(o, Near) else Far(o) for o in operands]
    waits = [pl.ANY if isinstance(o, Near) else pltpu.HBM for o in after]
    after = [o.arrays[0] if isinstance(o, Near) else in_hbm(o) for o in after]
    staged = [o for o in results if isinstance(o, Stage)]
    inputs = operands + [o.source for o in staged]
    arrays = [a for o in inputs for a in o.arrays]
    copied = [o for o in operands if o.copied()]
    held = [o for o in results if not o.near]
    count_out = sum(o.near + o.far for o in results)
    onto = {o: i for i, o in enumerate(results) if o.onto is not None}
    aliases = {len(arrays) + len(after) + i: onto[o] for i, o in enumerate(onto)}
    waits += [pltpu.HBM] * len(onto)
    after += [in_hbm(o.onto) for o in onto]
    moves = sum(o.count() for o in copied) + sum(o.source.count() for o in staged) + sum(o.parts for o in results if o.far)
    named = starts is not None

    def kernel(*refs):
        sources, refs = refs[: len(arrays)], refs[len(arrays) + len(after) :]
        named_ref, refs = (refs[0], refs[1:]) if named else (None, refs)
        targets, rest = list(refs[:count_out]), refs[count_out:]
        buffers, rest = list(rest[: len(copied)]), rest[len(copied) :]
        leaving, rest = list(rest[: len(held)]), rest[len(held) :]
        sems, rest = rest[0], rest[1:]
        marks = None
        if named:
            copy = pltpu.make_async_copy(named_ref, rest[0], sems.at[moves])
            copy.start()
            marks, rest = Loaded(rest[0], [copy]), rest[1:]
        info = Place(marks)
        loaded, at, sem = [], 0, 0

        def copies_of(pairs):
            nonlocal sem
            sem += len(pairs)
            return [
                pltpu.make_async_copy(source, target, sems.at[sem - len(pairs) + i])
                for i, (source, target) in enumerate(pairs)
            ]

        for operand in operands:
            own = sources[at : at + len(operand.arrays)]
            at += len(own)
            if not operand.copied():
                loaded.append(Loaded(own[0], []))
                continue
            buffer = buffers.pop(0)
            loaded.append(Loaded(buffer, copies_of(operand.copies(info, own, buffer))))
            for copy in loaded[-1].copies:
                copy.start()
        stored, staging = [], []
        for result in results:
            buffer = targets.pop(0) if result.near else leaving.pop(0)
            if isinstance(result, Stage):
                own = sources[at : at + len(result.source.arrays)]
                at += len(own)
                staging += copies_of(result.source.copies(info, own, buffer))
                continue
            target = targets.pop(0) if result.far else None
            pairs = result.copies(buffer, target) if result.far else []
            stored.append(Stored(buffer, copies_of(pairs)))
        for copy in staging:
            copy.start()
        body(info, *loaded, *stored, *rest)
        for copy in staging:
            copy.wait()
        for item in loaded + ([marks] if named else []):
            item.ready()
        for item in stored:
            item.send()
        for item in stored:
            for copy in item.copies:
                copy.wait()

    spaces = [pltpu.VMEM if o.near else pltpu.HBM for o in inputs for _ in o.arrays]
    placed = [a if space is pltpu.VMEM else in_hbm(a) for a, space in zip(arrays, spaces)]
    spaces += waits + [pltpu.HBM] * named
    moved = sum(a.size * a.dtype.itemsize for a in arrays)
    moved += sum(math.prod(o.dims) * jnp.dtype(o.dtype).itemsize for o in results)
    given = pl.pallas_call(
        kernel,
        name=getattr(body, "func", body).__name__,
        out_shape=tuple(s for o in results for s in o.shapes()),
        in_specs=[pl.BlockSpec(memory_space=space) for space in spaces],
        out_specs=tuple(pl.BlockSpec(memory_space=s) for o in results for s in o.spaces()),
        input_output_aliases=aliases,
        scratch_shapes=[pltpu.VMEM(o.dims, o.dtype) for o in copied]
        + [pltpu.VMEM(o.dims, o.dtype) for o in held]
        + [pltpu.SemaphoreType.DMA((max(1, moves + named),))]
        + [pltpu.SMEM((1, 4), jnp.int32)] * named
        + list(scratch),
        compiler_params=pltpu.CompilerParams(vmem_limit_bytes=megabytes * 2**20),
        cost_estimate=pl.CostEstimate(flops=0, bytes_accessed=1024, transcendentals=0),
    )(*placed, *after, *([in_hbm(starts)] if named else []))
    given, answer = list(given), []
    for result in results:
        item = (Near(given.pop(0)),) if result.near else ()
        item += (given.pop(0),) if result.far else ()
        answer.append(item if len(item) == 2 else item[0])
    return answer


def moved_by(array, axis, route):
    array = array.arrays[0] if isinstance(array, Near) else array
    return Near(lax.ppermute(array, axis, route))


def feature_weights(feat_query_t, feat_key_t):
    def places(info, sources=None, buffer=None):
        if info is None:
            return 2
        return [(sources[0], buffer.at[0:32]), (sources[1], buffer.at[32:64])]

    return Far([feat_query_t, feat_key_t], (128, feat_query_t.shape[1]), places)


def gathered(pieces):
    def places(info, sources=None, buffer=None):
        if info is None:
            return 8
        pairs = []
        for i, source in enumerate(sources):
            rows = info.rows(4 - i % 4, other=i >= 4)
            pairs.append((source.at[0:OWN], buffer.at[rows]))
        return pairs

    return Near(list(pieces), (ROWS, pieces[0].dims[1]), places)


def own_part(block):
    def places(info, sources=None, buffer=None):
        if info is None:
            return 1
        return [(sources[0].at[info.rows(0)], buffer)]

    return Far(block, (OWN, block.shape[1]), places)


def keys_kernel(
    info, x_ref, gain_ref, key_ref, value_ref, feat_ref, choose_ref, lanes_ref,
    normed_ref, inv_ref, raw_ref, keys_ref, values_ref, km_ref, packed_ref, edge_ref,
):
    gain = gain_ref[...]
    for part in range(4):
        x_ref.part(part)
        for i in range(2):
            rows = slice(part * 128 + i * 64, part * 128 + i * 64 + 64)
            x = x_ref.ref[rows, :].astype(f32)
            inv = lax.rsqrt(jnp.mean(x * x, axis=-1, keepdims=True) + EPS)
            inv_ref[rows, :] = inv
            normed_ref[rows, :] = (x * inv * gain).astype(bf16)
    normed_ref.send()
    inv_ref.send()
    normed = normed_ref[...]
    keys = mm(normed, key_ref[...]).astype(bf16)
    keys_ref[...] = keys
    keys_ref.send()
    values = mm(normed, value_ref[...]).astype(bf16)
    values_ref[...] = values
    values_ref.send()
    edge_ref[0] = keys[ROWS - WIN :]
    edge_ref[1] = values[ROWS - WIN :]
    edge_ref.send()
    feat_ref.ready()
    feat_ref.ref[64:128, :] = jnp.zeros((64, feat_ref.shape[1]), bf16)
    raw = mm_nt(normed, feat_ref[...])
    raw_ref[...] = raw
    raw_ref.send()
    left, right = factors(raw, choose_ref, lanes_ref)
    features = (left * right * lanes_ref[2:3, :]).astype(bf16)
    features = (features.astype(f32) * lanes_ref[3:4, :]).astype(bf16)
    tail = tail_mask(info)
    for head in range(HEADS):
        own = features[:, head * LANES : (head + 1) * LANES]
        km_ref[head] = own
        if head == HEADS - 1:
            km_ref.send()
        kept = (values[:, head_lanes(head)].astype(f32) * tail).astype(bf16)
        state = mm_tn(own, kept)
        norm = jnp.sum(own.astype(f32) * tail, axis=0, keepdims=True)
        write_packed(packed_ref, head, state, norm)


def local_kernel(
    info, raw_ref, choose_ref, lanes_ref, values_ref, km_ref, qf_ref, low_ref, num_ref, den_ref,
):
    left, right = factors(raw_ref[...], choose_ref, lanes_ref)
    features = (left * right * lanes_ref[2:3, :]).astype(bf16)
    half = ROWS // 2
    for block in range(2):
        first, reach = block * half, (block + 1) * half
        query_at = column_positions(info, first, half)
        key_at = row_positions(info, 0, reach)
        causal = (query_at >= key_at) & (doc_of(info, query_at) == doc_of(info, key_at))
        for head in range(HEADS):
            own = features[first:reach, head * LANES : (head + 1) * LANES]
            qf_ref[head, first:reach, :] = own
            weights = jnp.where(causal, mm_nt(own, km_ref[head, :reach, :]), 0.0)
            den_ref[head, first:reach, :] = jnp.sum(weights, axis=-1, keepdims=True)
            low = weights.astype(bf16)
            low_ref[head, first:reach, 0:reach] = low
            num_ref[first:reach, head_lanes(head)] = mm(low, values_ref[:reach, head_lanes(head)])


def window_kernel(
    info, normed_ref, query_ref, keys_ref, values_ref, halo_ref,
    queries_ref, probs_ref, window_ref, kept_ref,
):
    kept_ref[...] = halo_ref[...]
    queries = mm(normed_ref[...], query_ref[...]).astype(bf16)
    queries_ref[...] = queries
    queries_ref.send()
    scale = VALUE_WIDTH ** (-0.5)
    for tile in range(ROWS // TILE):
        first = tile * TILE
        query_at = column_positions(info, first, TILE)
        key_at = row_positions(info, first - WIN, TILE + WIN)
        near = (
            (key_at <= query_at)
            & (query_at - key_at < WIN)
            & (doc_of(info, query_at) == doc_of(info, key_at))
            & (key_at >= 0)
        )
        for head in range(HEADS):
            lanes = head_lanes(head)
            key_rows = window_rows(keys_ref, halo_ref, 0, tile, lanes)
            value_rows = window_rows(values_ref, halo_ref, 1, tile, lanes)
            logits = mm_nt(queries[first : first + TILE, lanes], key_rows) * scale
            logits = jnp.where(near, logits, -1e30)
            exps = jnp.exp(logits - jnp.max(logits, axis=-1, keepdims=True))
            probs = exps / jnp.sum(exps, axis=-1, keepdims=True)
            probs_ref[head, tile] = probs
            window_ref[first : first + TILE, lanes] = mm(probs.astype(bf16), value_rows)


def by_distance(ref, info, other):
    return jnp.concatenate([ref[info.rows(d, other), :] for d in range(4)], axis=0)


def mixed_kernel(
    info, before_ref, got1_ref, got2_ref, got3_ref, qf_ref, num_ref, den_ref, window_ref, out_ref,
    mixed_ref, linear_ref, total_den_ref, state_ref, norm_ref, own_ref, other_ref,
):
    use = prefix_mask(info)
    for head in range(HEADS):
        lanes = head_lanes(head)
        state, norm = read_total(before_ref, (got1_ref, got2_ref, got3_ref), head)
        state_ref[head] = state
        norm_ref[head] = jnp.broadcast_to(norm, (8, LANES))
        features = qf_ref[head]
        inter = mm(features, state) * use
        den = jnp.sum(features.astype(f32) * norm, axis=-1, keepdims=True) * use + den_ref[head]
        total_den_ref[head] = den
        linear = (inter + num_ref[:, lanes]) / den
        linear_ref[:, lanes] = linear
        mixed_ref[:, lanes] = (linear + window_ref[:, lanes]).astype(bf16)
    weights = out_ref[...]
    other_ref[...] = mm(by_distance(mixed_ref, info, True), weights).astype(bf16)
    other_ref.send()
    own_ref[...] = mm(by_distance(mixed_ref, info, False), weights).astype(bf16)


def quarters_kernel(info, own_ref, got_ref, *out_refs):
    out_refs[4][...] = got_ref[0:16, 0:128]
    for d in (1, 2, 3, 0):
        rows = slice(d * OWN, (d + 1) * OWN)
        total = own_ref[rows, :].astype(f32) + got_ref[rows, :].astype(f32)
        out_refs[d][...] = total.astype(out_refs[d].dtype)
        out_refs[d].send()


def resid_kernel(
    info, mine_ref, x_ref, gain_ref, got1_ref, got2_ref, got3_ref, normed_ref, resid_ref, inv_ref
):
    resid = x_ref[...].astype(f32) + mine_ref[...]
    for ref in (got1_ref, got2_ref, got3_ref):
        resid = resid + ref[...].astype(f32)
    resid_ref[...] = resid
    resid_ref.send()
    inv = lax.rsqrt(jnp.mean(resid * resid, axis=-1, keepdims=True) + EPS)
    inv_ref[...] = inv
    inv_ref.send()
    normed_ref[...] = (resid * inv * gain_ref[...]).astype(bf16)


def grad_resid_kernel(
    info, mine_ref, resid_ref, inv_ref, top_ref, gain_ref, got1_ref, got2_ref, got3_ref,
    sent_ref, grad_ref, gains_ref,
):
    grad = mine_ref[...]
    for ref in (got1_ref, got2_ref, got3_ref):
        grad = grad + ref[...].astype(f32)
    resid = resid_ref[...]
    inv = inv_ref[...]
    grad_resid = top_ref[...].astype(f32) + norm_back(resid, inv, gain_ref[...], grad)
    sent_ref[...] = grad_resid.astype(bf16)
    sent_ref.send()
    grad_ref[...] = grad_resid
    gains_ref[0:1, :] = jnp.sum(grad * resid * inv, axis=0, keepdims=True)


def grad_x_kernel(
    info, mine_ref, x_ref, grad_resid_ref, gain_ref, resid_ref, out_ref, got1_ref, got2_ref, got3_ref,
    out1_ref, out2_ref, out3_ref, sent_ref,
):
    total = resid_ref[...] + out_ref[...]
    for ref in (out1_ref, out2_ref, out3_ref):
        total = total + ref[...].astype(f32)
    sent_ref[0:OWN, :] = total.astype(bf16)
    grad = mine_ref[...]
    for ref in (got1_ref, got2_ref, got3_ref):
        grad = grad + ref[...].astype(f32)
    x = x_ref[...].astype(f32)
    inv = lax.rsqrt(jnp.mean(x * x, axis=-1, keepdims=True) + EPS)
    sent_ref[OWN:, :] = (grad_resid_ref[...] + norm_back(x, inv, gain_ref[...], grad)).astype(bf16)


def norm_back(in_rows, inv_rms, gain, grad_normed):
    weighted = grad_normed * gain
    return inv_rms * weighted - in_rows * inv_rms**3 * jnp.mean(
        weighted * in_rows, axis=-1, keepdims=True
    )


def grad_act_kernel(info, top_ref, down_ref, out_ref):
    top = top_ref[...]
    for first in range(0, down_ref.shape[0], 256):
        span = slice(first, min(first + 256, down_ref.shape[0]))
        out_ref[:, span] = mm_nt(top, down_ref[span, :])


def ffn_kernel(
    info, in_ref, gate_ref, up_ref, grad_act_ref,
    other_ref, own_ref, normed_ref, act_ref, grad_gate_ref, grad_up_ref,
):
    normed = in_ref[...]
    normed_ref[...] = normed
    normed_ref.send()
    hidden = gate_ref.shape[0]
    for first in range(0, hidden, 256):
        span = slice(first, min(first + 256, hidden))
        gate = mm_nt(normed, gate_ref[span, :])
        up_value = mm_nt(normed, up_ref[span, :])
        sigmoid_gate = jax.nn.sigmoid(gate)
        silu_gate = gate * sigmoid_gate
        act_ref[:, span] = (silu_gate * up_value).astype(bf16)
        grad_act = grad_act_ref[:, span]
        grad_gate_ref[:, span] = (
            grad_act * up_value * sigmoid_gate * (1.0 + gate * (1.0 - sigmoid_gate))
        ).astype(bf16)
        grad_up_ref[:, span] = (grad_act * silu_gate).astype(bf16)
    for ref in (act_ref, grad_gate_ref, grad_up_ref):
        ref.send()
    for target, other in ((other_ref, True), (own_ref, False)):
        grad_gate = by_distance(grad_gate_ref, info, other)
        grad_up = by_distance(grad_up_ref, info, other)
        for first in range(0, target.shape[1], 512):
            span = slice(first, first + 512)
            part = mm(grad_gate, gate_ref[:, span]) + mm(grad_up, up_ref[:, span])
            target[:, span] = part.astype(bf16)
        target.send()


def ffn_out_kernel(info, act_ref, down_ref, other_ref, own_ref):
    for target, other in ((other_ref, True), (own_ref, False)):
        act = by_distance(act_ref, info, other)
        for first in range(0, target.shape[1], 512):
            span = slice(first, first + 512)
            target[:, span] = mm(act, down_ref[:, span]).astype(bf16)
        target.send()


def ffn_grads_kernel(info, normed_ref, gate_ref, up_ref, out_ref):
    hidden = gate_ref.shape[1]
    gate, up = gate_ref[...], up_ref[...]
    for part in range(4):
        span = slice(part * 512, (part + 1) * 512)
        normed = normed_ref[:, span]
        out_ref[span, 0:hidden] = mm_tn(normed, gate).astype(bf16)
        out_ref[span, hidden : 2 * hidden] = mm_tn(normed, up).astype(bf16)
        out_ref.send(part)


def column_grads(pairs, out_ref):
    for part in range(4):
        first = 0
        for rows_ref, grad in pairs:
            count = rows_ref.shape[1] // 4
            span = slice(part * count, (part + 1) * count)
            last = first + grad.shape[1]
            out_ref[span, first:last] = mm_tn(rows_ref[:, span], grad).astype(bf16)
            first = last
        if first < out_ref.shape[1]:
            out_ref[span, first:] = jnp.zeros((count, out_ref.shape[1] - first), bf16)
        out_ref.send(part)


def gate_grads_kernel(info, normed_ref, gate_ref, up_ref, out_ref):
    column_grads(((normed_ref, gate_ref[...]), (normed_ref, up_ref[...])), out_ref)


def down_grads_kernel(info, top_ref, act_ref, out_ref):
    column_grads(((top_ref, act_ref[...]),), out_ref)


def grad_x_out_kernel(info, p0, p1, p2, p3, s0, s1, s2, s3, output_ref, grad_ref):
    for i, piece in enumerate((p0, p1, p2, p3, s0, s1, s2, s3)):
        rows = info.rows(4 - i % 4, other=i >= 4)
        output_ref[rows, :] = piece[0:OWN, :]
        grad_ref[rows, :] = piece[OWN : 2 * OWN, :].astype(f32)


def mixed_back_kernel(
    info, in_ref, out_ref, linear_ref, den_ref, qf_ref,
    packed_ref, top_ref, gm_ref, gnum_ref, gden_ref,
):
    top = in_ref[...]
    grad_mixed = mm_nt(top, out_ref[...]).astype(bf16)
    gm_ref[...] = grad_mixed
    gm_ref.send()
    top_ref[...] = top
    use = prefix_mask(info)
    for head in range(HEADS):
        lanes = head_lanes(head)
        wide = grad_mixed[:, lanes].astype(f32)
        den = den_ref[head]
        grad_num = (wide / den).astype(bf16)
        gnum_ref[:, lanes] = grad_num
        grad_den = -jnp.sum(wide * linear_ref[:, lanes], axis=-1, keepdims=True) / den
        gden_ref[head] = grad_den
        features = qf_ref[head]
        used = (grad_num.astype(f32) * use).astype(bf16)
        state = mm_tn(features, used)
        norm = jnp.sum(features.astype(f32) * (grad_den * use), axis=0, keepdims=True)
        write_packed(packed_ref, head, state, norm)
    packed_ref.send()


def window_back_kernel(
    info, gm_ref, probs_ref, keys_ref, values_ref, halo_ref, queries_ref,
    edge_ref, gq_ref, gk_ref, gv_ref, key_acc, value_acc,
):
    scale = VALUE_WIDTH ** (-0.5)
    key_acc[...] = jnp.zeros_like(key_acc)
    value_acc[...] = jnp.zeros_like(value_acc)
    for tile in range(ROWS // TILE):
        first = tile * TILE
        reach = slice(first, first + TILE + WIN)
        for head in range(HEADS):
            lanes = head_lanes(head)
            key_rows = window_rows(keys_ref, halo_ref, 0, tile, lanes)
            value_rows = window_rows(values_ref, halo_ref, 1, tile, lanes)
            top = gm_ref[first : first + TILE, lanes]
            probs = probs_ref[head, tile]
            grad_probs = mm_nt(top, value_rows)
            shared = jnp.sum(grad_probs * probs, axis=-1, keepdims=True)
            grad_logits = (probs * (grad_probs - shared)).astype(bf16)
            gq_ref[first : first + TILE, lanes] = (mm(grad_logits, key_rows) * scale).astype(bf16)
            queries = queries_ref[first : first + TILE, lanes]
            key_acc[reach, lanes] += mm_tn(grad_logits, queries) * scale
            value_acc[reach, lanes] += mm_tn(probs.astype(bf16), top)
    edge_ref[0] = key_acc[0:WIN, :].astype(bf16)
    edge_ref[1] = value_acc[0:WIN, :].astype(bf16)
    gk_ref[...] = key_acc[WIN:, :]
    gv_ref[...] = value_acc[WIN:, :]


def linear_back_kernel(
    info, gnum_ref, gden_ref, values_ref, low_ref, km_ref, qf_ref, state_ref, norm_ref, raw_ref,
    choose_ref, lanes_ref, window_gv_ref, gfeat_ref, gv_ref, gkf_ref,
):
    use = prefix_mask(info)
    half = ROWS // 2
    grads = [[None, None], [None, None]]
    for head in range(HEADS):
        lanes = head_lanes(head)
        inter = mm_nt((gnum_ref[:, lanes].astype(f32) * use).astype(bf16), state_ref[head])
        inter = inter + (gden_ref[head] * use) * norm_ref[head, 0:1, :]
        for block in range(2):
            first, reach = block * half, (block + 1) * half
            query_at = column_positions(info, first, half)
            key_at = row_positions(info, 0, reach)
            causal = (query_at >= key_at) & (doc_of(info, query_at) == doc_of(info, key_at))
            grad_num = gnum_ref[first:reach, lanes]
            grad = mm_nt(grad_num, values_ref[:reach, lanes]) + gden_ref[head, first:reach, :]
            grad = jnp.where(causal, grad, 0.0).astype(bf16)
            grads[head][block] = mm(grad, km_ref[head, :reach, :]) + inter[first:reach]
            key_part = mm_tn(grad, qf_ref[head, first:reach, :])
            value_part = mm_tn(low_ref[head, first:reach, 0:reach], grad_num)
            if block == 0:
                gkf_ref[head, 0:half] = key_part
                gv_ref[0:half, lanes] = window_gv_ref[0:half, lanes] + value_part
            else:
                gkf_ref[head, 0:half] += key_part[0:half]
                gkf_ref[head, half:] = key_part[half:]
                gv_ref[0:half, lanes] += value_part[0:half]
                gv_ref[half:, lanes] = window_gv_ref[half:, lanes] + value_part[half:]
    left, right = factors_back(raw_ref[...], choose_ref, lanes_ref)
    gradient = jnp.concatenate([jnp.concatenate(g, axis=0) for g in grads], axis=1)
    gradient = gradient * lanes_ref[2:3, :]
    gfeat_ref[...] = feature_back(gradient, left, right, choose_ref)


def keys_back_kernel(
    info, before_ref, got1_ref, got2_ref, got3_ref, values_ref, km_ref, gkf_ref, gk_ref, gv_ref,
    right_ref, raw_ref, choose_ref, lanes_ref, gfeat_ref, normed_ref, top_ref, mixed_ref, gq_ref,
    gkw_ref, gvw_ref, gf_ref, out_ref,
):
    tail = tail_mask(info)
    inner = ROWS - WIN
    gkw_ref[0:inner, :] = gk_ref[0:inner, :].astype(bf16)
    gkw_ref[inner:, :] = (gk_ref[inner:, :] + right_ref[0].astype(f32)).astype(bf16)
    gradients = []
    for head in range(HEADS):
        lanes = head_lanes(head)
        later, norm = read_total(before_ref, (got1_ref, got2_ref, got3_ref), head)
        kept = (values_ref[:, lanes].astype(f32) * tail).astype(bf16)
        gradients.append(gkf_ref[head] + mm_nt(kept, later) + tail * norm)
        grad_values = gv_ref[:, lanes] + mm(km_ref[head], later) * tail
        gvw_ref[0:inner, lanes] = grad_values[0:inner].astype(bf16)
        gvw_ref[inner:, lanes] = (grad_values[inner:] + right_ref[1, :, lanes].astype(f32)).astype(
            bf16
        )
    left, right = factors_back(raw_ref[...], choose_ref, lanes_ref)
    gradient = jnp.concatenate(gradients, axis=1) * lanes_ref[4:5, :]
    gf_ref[...] = (feature_back(gradient, left, right, choose_ref) + gfeat_ref[...]).astype(bf16)
    column_grads(
        (
            (top_ref, mixed_ref[...]), (normed_ref, gq_ref[...]), (normed_ref, gkw_ref[...]),
            (normed_ref, gvw_ref[...]), (normed_ref, gf_ref[...]),
        ),
        out_ref,
    )


def normed_back_kernel(
    info, gq_ref, gkw_ref, gvw_ref, gf_ref, wq_ref, wk_ref, wv_ref, wf_ref, x_ref, inv_ref, gain_ffn_ref,
    other_ref, own_ref, gains_ref,
):
    wf_ref.ready()
    wf_ref.ref[64:128, :] = jnp.zeros((64, wf_ref.shape[1]), bf16)
    for target, other in ((other_ref, True), (own_ref, False)):
        grads = [by_distance(ref, info, other) for ref in (gq_ref, gkw_ref, gvw_ref, gf_ref)]
        scaled_by = by_distance(inv_ref, info, other)
        for piece in range(4):
            span = slice(piece * 512, (piece + 1) * 512)
            part = mm_nt(grads[0], wq_ref[span, :])
            part = part + mm_nt(grads[1], wk_ref[span, :])
            part = part + mm_nt(grads[2], wv_ref[span, :])
            part = part + mm(grads[3], wf_ref[:, span])
            target[:, span] = part.astype(bf16)
            x_rows = jnp.concatenate([x_ref[info.rows(d, other), span] for d in range(4)], axis=0)
            total = jnp.sum(part * (x_rows.astype(f32) * scaled_by), axis=0, keepdims=True)
            gains_ref[0:1, span] = total if other else total + gains_ref[0:1, span]
    gains_ref[1:2, :] = gain_ffn_ref[0:1, :]


def grads_out_kernel(
    info, in_ref, gate_ref, up_ref, down_ref, out_ref, grad_q_ref, grad_k_ref, grad_v_ref,
    feat_query_ref, feat_key_ref,
):
    hidden, width = gate_ref.shape[0], out_ref.shape[0]
    padded = -(-hidden // 128) * 128
    both = in_ref[:, 0 : 2 * hidden].astype(f32).T
    gate_ref[...] = both[0:hidden]
    gate_ref.send()
    up_ref[...] = both[hidden:]
    up_ref.send()
    at = 2 * hidden
    down_ref[...] = in_ref[:, at : at + padded].astype(f32).T[0:hidden]
    down_ref.send()
    at += padded
    out_ref[...] = in_ref[:, at : at + width].astype(f32).T
    out_ref.send()
    for ref in (grad_q_ref, grad_k_ref, grad_v_ref):
        at += width
        ref[...] = in_ref[:, at : at + width].astype(f32)
        ref.send()
    feat = in_ref[:, at + width :].astype(f32).T
    feat_query_ref[...] = feat[0:32]
    feat_key_ref[...] = feat[32:64]


def total_of(refs):
    total = refs[0][...]
    for ref in refs[1:]:
        total = total + ref[...]
    return total


def gains_kernel(info, *refs):
    refs[-1][...] = total_of(refs[:-1])


def spread_kernel(along, info, *refs):
    total, (*to_refs, acc_ref) = total_of(refs[:-5]), refs[-5:]
    acc_ref[...] = total
    for d, ref in enumerate(to_refs):
        count = ref.shape[1]
        at = lax.bitwise_and((info.x if along == "x" else info.z) + d, 3) * count
        ref[...] = acc_ref[:, pl.ds(pl.multiple_of(at, count), count)]


def along_y(distance):
    return [(i, (i + 2 * distance) % 8) for i in range(8)]


def sibling():
    return [(i, i ^ 1) for i in range(8)]


def along_x(distance):
    return [(i, (i + 4 * distance) % 16) for i in range(16)]


def along_z(distance):
    return [(4 * a + z, 4 * a + (z + distance) % 4) for a in range(4) for z in range(4)]


def head_quarters(own, other, after=()):
    got = moved_by(other, "head", sibling())
    width = own.dims[1]
    with jax.named_scope("quarters"):
        mine, *sent, token = call(
            quarters_kernel,
            [near(OWN, width, dtype=f32)] + [near(OWN, width)] * 3 + [near(16, 128)],
            (own, got), after=after,
        )
    parts = [moved_by(sent[d - 1], "head", along_y(d)) for d in (2, 1, 3)]
    return mine, parts, moved_by(token, "head", sibling())


def head_pieces(own):
    pieces = [own] + [moved_by(own, "head", along_y(d)) for d in (1, 2, 3)]
    return pieces + [moved_by(piece, "head", sibling()) for piece in pieces]


def spread(parts, along):
    rows, width = parts[0].dims
    with jax.named_scope("gains"):
        return call(
            functools.partial(spread_kernel, along), [near(rows, width // 4, dtype=f32)] * 4, parts,
            scratch=[pltpu.VMEM((rows, width), f32)],
        )


def gains_over_head(gains):
    with jax.named_scope("gains"):
        (pair,) = call(
            gains_kernel, [near(*gains.dims, dtype=f32)], (gains, moved_by(gains, "head", sibling()))
        )
    return spread([pair] + [moved_by(pair, "head", along_y(d)) for d in (1, 2, 3)], "x")


def gains_over_seq(gains):
    own, *sent = gains
    own, *sent = spread([own] + [moved_by(s, "seq", along_x(d)) for d, s in enumerate(sent, 1)], "z")
    parts = [own] + [moved_by(s, "seq", along_z(d)) for d, s in enumerate(sent, 1)]
    with jax.named_scope("gains"):
        (total,) = call(gains_kernel, [far(*own.dims, dtype=f32)], parts)
    return total


def scan_kernel(reverse, info, own_ref, got1_ref, got2_ref, got3_ref, before_ref, *sent_refs):
    place_x, place_z = (3 - info.x, 3 - info.z) if reverse else (info.x, info.z)
    before = jnp.zeros(own_ref.shape, f32)
    for d, ref in enumerate((got1_ref, got2_ref, got3_ref), 1):
        before = before + ref[...].astype(f32) * (place_x >= d).astype(f32)
    before_ref[...] = before
    row = lax.broadcasted_iota(jnp.int32, (HEADS, 16, 128), 1)
    sent = []
    for total in (before, before + own_ref[...].astype(f32)):
        norm = total[:, KEPT:]
        norm = norm + jnp.roll(norm, -2, axis=1)
        high = norm.astype(bf16).astype(f32)
        rest = jnp.roll(norm - high, 2, axis=1)
        norm = jnp.where(row < 2, high, jnp.where(row < 4, rest, 0.0))
        sent.append((total[:, :KEPT], norm))
    for d, ref in enumerate(sent_refs, 1):
        with_own = (place_z + d < 4).astype(f32)
        for part, rows in ((0, slice(0, KEPT)), (1, slice(KEPT, PACKED))):
            less, more = sent[0][part], sent[1][part]
            ref[:, rows, :] = (more * with_own + less * (1.0 - with_own)).astype(bf16)


def exclusive_parts(own, reverse, after=()):
    sign = -1 if reverse else 1
    got = [moved_by(own, "seq", along_x(sign * d)) for d in (1, 2, 3)]
    with jax.named_scope("scan"):
        before, *sent = call(
            functools.partial(scan_kernel, reverse),
            [near(*own.dims, dtype=f32)] + [near(*own.dims)] * 3, (own, *got), after=after,
        )
    return [before] + [
        moved_by(sent[d - 1], "seq", along_z(sign * d)) for d in (1, 2, 3)
    ]


def shifted(block, distance):
    route = [(i - distance, i) for i in range(16) if 0 <= i - distance < 16]
    return moved_by(block, "seq", route)


def shards(
    inputs,
    gain_mix,
    feat_query,
    feat_key,
    win_query,
    win_key,
    value_proj,
    out_proj,
    gain_ffn,
    gate_proj,
    up_proj,
    down_proj,
    document_starts,
    cotangent,
):
    choose, lanes = feature_tables()
    choose = jnp.asarray(choose, bf16)
    lanes = jnp.asarray(lanes, f32)
    choose_q, choose_k = choose[0], choose[1]
    feat = feature_weights(feat_query.T, feat_key.T)
    gain_mix = gain_mix.reshape(1, -1)
    gain_ffn = gain_ffn.reshape(1, -1)
    model = inputs.shape[1]
    width = HEADS * VALUE_WIDTH
    hidden = gate_proj.shape[1]
    half = ROWS // 2
    unit = 2 * ROWS * model
    starts = document_starts

    (normed, normed_far), inv_mix, (raw, raw_far), (keys, keys_far), (values, values_far), *rest = call(
        keys_kernel,
        (
            both(ROWS, model), far(ROWS, 1, dtype=f32), both(ROWS, 128, dtype=f32),
            both(ROWS, width), both(ROWS, width), both(HEADS, ROWS, LANES),
            near(HEADS, PACKED, 128), near(2, WIN, width),
        ),
        (Far(inputs, parts=4), gain_mix, win_key, value_proj, feat, choose_k, lanes),
        starts=starts, flops=unit * 640,
    )
    (km, km_far), packed, edge = rest
    halo = shifted(edge, 1)
    (qf, qf_far), low, num, den, near_query, near_out = call(
        local_kernel,
        (
            both(HEADS, ROWS, LANES), far(HEADS, ROWS, ROWS), near(ROWS, width, dtype=f32),
            near(HEADS, ROWS, 1, dtype=f32), Stage(win_query), Stage(out_proj),
        ),
        (raw, choose_q, lanes, values, km),
        starts=starts, flops=unit * 300,
    )
    sums = exclusive_parts(packed, False, after=(qf, halo))
    queries, probs, window, halo_far = call(
        window_kernel,
        (
            far(ROWS, width), far(HEADS, 4, TILE, TILE + WIN, dtype=f32),
            near(ROWS, width, dtype=f32), far(2, WIN, width),
        ),
        (normed, near_query, keys, values, halo),
        starts=starts, flops=unit * 400,
    )
    mixed, linear, total_den, state, norm, own, other = call(
        mixed_kernel,
        (
            far(ROWS, width), far(ROWS, width, dtype=f32), far(HEADS, ROWS, 1, dtype=f32),
            far(HEADS, LANES, VALUE_WIDTH), far(HEADS, 8, LANES, dtype=f32),
            near(half, model), near(half, model),
        ),
        (*sums, qf, num, den, window, near_out),
        starts=starts, flops=unit * 300,
    )
    mine, parts, signal = head_quarters(own, other)
    grad_act, x_own, near_gain, near_gate, near_up = call(
        grad_act_kernel,
        (
            near(ROWS, hidden, dtype=f32), Stage(own_part(inputs)), Stage(gain_ffn),
            Stage(gate_proj.T), Stage(up_proj.T),
        ),
        (cotangent, down_proj),
        after=(signal,), flops=unit * hidden,
    )
    own_normed, resid, inv_ffn = call(
        resid_kernel,
        (near(OWN, model), far(OWN, model, dtype=f32), far(OWN, 1, dtype=f32)),
        (mine, x_own, near_gain, *parts), after=(grad_act,),
    )
    pieces = head_pieces(own_normed)
    other, own, normed_ffn, activation, grad_gate, grad_up = call(
        ffn_kernel,
        (
            near(half, model), near(half, model), near(ROWS, model), far(ROWS, hidden),
            near(ROWS, hidden), near(ROWS, hidden),
        ),
        (gathered(pieces), near_gate, near_up, grad_act),
        flops=unit * 4 * hidden,
    )
    mine, parts, signal = head_quarters(own, other)
    padded = -(-hidden // 128) * 128
    place = dict(parts=4, width=2 * hidden + padded + 4 * width + 128)
    grads, *near_resid = call(
        gate_grads_kernel,
        (
            far(model, 2 * hidden, **place), Stage(resid), Stage(inv_ffn),
            Stage(own_part(cotangent)), Stage(gain_ffn), Stage(out_proj), Stage(linear),
            Stage(total_den), Stage(qf_far),
        ),
        (normed_ffn, grad_gate, grad_up), after=(signal,), flops=unit * 2 * hidden,
    )
    near_resid, near_mixed = near_resid[:4], near_resid[4:]
    at = 2 * hidden
    grads, *near_back = call(
        down_grads_kernel,
        (
            far(model, padded, first=at, onto=grads, **place), Stage(probs), Stage(keys_far),
            Stage(values_far), Stage(halo_far), Stage(queries), Stage(low), Stage(km_far),
            Stage(state), Stage(norm), Stage(raw_far), Stage(choose_q), Stage(choose_k),
            Stage(lanes), Stage(normed_far), Stage(mixed),
        ),
        (cotangent, activation), after=(signal,), flops=unit * hidden,
    )
    probs, keys, values, halo, queries, low, km, state, norm, raw, choose_q, choose_k, *rest = near_back
    lanes, normed, mixed = rest
    at += padded
    sent, grad_resid, gain_ffn_part = call(
        grad_resid_kernel,
        (near(OWN, model), far(OWN, model, dtype=f32), far(8, model, dtype=f32)),
        (mine, *near_resid, *parts), after=(grads,),
    )
    pieces = head_pieces(sent)
    packed, top, grad_mixed, grad_num, grad_den = call(
        mixed_back_kernel,
        (
            near(HEADS, PACKED, 128), near(ROWS, model), near(ROWS, width), near(ROWS, width),
            near(HEADS, ROWS, 1, dtype=f32),
        ),
        (gathered(pieces), *near_mixed),
        starts=starts, flops=unit * 300,
    )
    edge, gq, gk, gv = call(
        window_back_kernel,
        (
            near(2, WIN, width), near(ROWS, width), near(ROWS, width, dtype=f32),
            near(ROWS, width, dtype=f32),
        ),
        (grad_mixed, probs, keys, values, halo, queries),
        flops=unit * 300, scratch=[pltpu.VMEM((ROWS + WIN, width), f32)] * 2,
    )
    right = shifted(edge, -1)
    sums = exclusive_parts(packed, True, after=(edge,))
    gfeat, gv, gkf = call(
        linear_back_kernel,
        (
            near(ROWS, 128, dtype=f32), near(ROWS, width, dtype=f32),
            near(HEADS, ROWS, LANES, dtype=f32),
        ),
        (
            grad_num, grad_den, values, low, km, near_mixed[3], state, norm, raw, choose_q, lanes, gv,
        ),
        starts=starts, after=(sums[0],), flops=unit * 300,
    )
    gkw, gvw, gf, grads = call(
        keys_back_kernel,
        (
            near(ROWS, width), near(ROWS, width), near(ROWS, 128),
            far(model, 4 * width + 128, first=at, onto=grads, **place),
        ),
        (
            *sums, values, km, gkf, gk, gv, right, raw, choose_k, lanes, gfeat, normed, top, mixed,
            gq,
        ),
        starts=starts, flops=unit * 1400,
    )
    grads_sum = lax.psum_scatter(grads, "seq", scatter_dimension=0, tiled=True)
    other, own, gains = call(
        normed_back_kernel, (near(half, model), near(half, model), near(2, model, dtype=f32)),
        (
            gq, gkw, gvw, gf, win_query, win_key, value_proj, feat, inputs, inv_mix, gain_ffn_part,
        ),
        after=(grads,),
        flops=unit * 900,
    )
    mine, parts, signal = head_quarters(own, other)
    other, own = call(
        ffn_out_kernel, (near(half, model), near(half, model)), (activation, down_proj),
        after=(signal,), flops=unit * hidden,
    )
    out_mine, out_parts, signal = head_quarters(own, other)
    gains = gains_over_seq(gains_over_head(gains))
    (sent,) = call(
        grad_x_kernel, (near(2 * OWN, model),),
        (mine, own_part(inputs), grad_resid, gain_mix, resid, out_mine, *parts, *out_parts),
        after=(gains,),
    )
    pieces = head_pieces(sent)
    output, grad_x = call(
        grad_x_out_kernel, (far(ROWS, model), far(ROWS, model, dtype=f32)), pieces,
    )
    grad_gate_t, grad_up_t, grad_down, grad_out, *rest = call(
        grads_out_kernel,
        (far(hidden, 128, dtype=f32),) * 3 + (far(width, 128, dtype=f32),)
        + (far(128, width, dtype=f32),) * 3 + (far(32, 128, dtype=f32),) * 2,
        (grads_sum,), after=(grad_x,),
    )
    grad_wq, grad_wk, grad_wv, grad_fq_t, grad_fk_t = rest
    return (
        output,
        grad_x,
        gains[0],
        grad_fq_t.T,
        grad_fk_t.T,
        grad_wq,
        grad_wk,
        grad_wv,
        grad_out,
        gains[1],
        grad_gate_t.T,
        grad_up_t.T,
        grad_down,
    )


def solution(mesh):
    placed = (
        P("seq", None),
        P(),
        P(None, "head"),
        P(None, "head"),
        P(None, "head"),
        P(None, "head"),
        P(None, "head"),
        P("head", None),
        P(),
        P(None, "head"),
        P(None, "head"),
        P("head", None),
        P(),
        P("seq", None),
    )
    return jax.shard_map(
        shards,
        mesh=mesh,
        in_specs=placed,
        out_specs=(
            P("seq", None),
            P("seq", None),
            P("seq"),
            P("seq", "head"),
            P("seq", "head"),
            P("seq", "head"),
            P("seq", "head"),
            P("seq", "head"),
            P("head", "seq"),
            P("seq"),
            P("seq", "head"),
            P("seq", "head"),
            P("head", "seq"),
        ),
        check_vma=False,
    )
```

```python
import functools
import math

import jax
import jax.numpy as jnp
import numpy as np
from jax import lax
from jax.experimental import pallas as pl
from jax.experimental.pallas import tpu as pltpu
from jax.sharding import PartitionSpec as P

F = 16
VALUE_WIDTH = 128
WIN = 64
EPS = 1e-05

HEADS = 2
ROWS = 512
LANES = 256
KEPT = 160
PACKED = 176
TILE = 128
EDGE = 2 * WIN
OWN = 64
f32 = jnp.float32
bf16 = jnp.bfloat16


def feature_tables():
    pairs = [(a, b) for a in range(F) for b in range(a, F)]
    count = len(pairs)
    choose = np.zeros((2, 2, 128, HEADS * LANES), np.float32)
    lanes = np.zeros((8, HEADS * LANES), np.float32)
    factor = F ** (-0.25)
    for head in range(HEADS):
        at = head * LANES
        for side in range(2):
            for first in (side * HEADS * F, 64, 96):
                row = first + head * F
                for lane, (a, b) in enumerate(pairs):
                    choose[side, 0, row + a, at + lane] = 1.0
                    choose[side, 1, row + b, at + lane] = 1.0
                for a in range(F):
                    choose[side, 0, row + a, at + count + a] = 1.0
        for lane, (a, b) in enumerate(pairs):
            lanes[2, at + lane] = factor * factor / math.sqrt(2.0)
            lanes[3, at + lane] = 1.0 if a == b else 2.0
        lanes[1, at + count : at + count + F + 1] = 1.0
        lanes[0, at + count + F] = 1.0
        lanes[2, at + count : at + count + F] = factor
        lanes[2, at + count + F] = 1.0
        lanes[3, at + count : at + count + F + 1] = 1.0
    lanes[4] = lanes[2] * lanes[3]
    return choose, lanes


def mm(a, b):
    return lax.dot_general(a, b, (((1,), (0,)), ((), ())), preferred_element_type=f32)


def mm_nt(a, b):
    return lax.dot_general(a, b, (((1,), (1,)), ((), ())), preferred_element_type=f32)


def mm_tn(a, b):
    return lax.dot_general(a, b, (((0,), (0,)), ((), ())), preferred_element_type=f32)


def low_pair(part):
    high = part.astype(bf16)
    return high, (part - high.astype(f32)).astype(bf16)


class Place:

    def __init__(self, starts):
        me, seq = lax.axis_index("head"), lax.axis_index("seq")
        self.base = seq * ROWS
        self.x, self.z = lax.shift_right_logical(seq, 2), lax.bitwise_and(seq, 3)
        self.y, self.core = lax.shift_right_logical(me, 1), lax.bitwise_and(me, 1)
        self.loaded = starts

    def starts(self):
        return [self.loaded[0, i] for i in range(4)]

    def rows(self, distance, other=False):
        quarter = lax.bitwise_and(self.y + distance, 3)
        core = 1 - self.core if other else self.core
        return pl.ds(pl.multiple_of(quarter * (2 * OWN) + core * OWN, OWN), OWN)


class Loaded:

    def __init__(self, ref, copies):
        self.ref, self.copies = ref, list(copies)
        self.shape = ref.shape

    def part(self, index):
        if self.copies and self.copies[index] is not None:
            self.copies[index].wait()
            self.copies[index] = None

    def ready(self):
        for index in range(len(self.copies)):
            self.part(index)

    def __getitem__(self, index):
        self.ready()
        return self.ref[index]


class Stored:

    def __init__(self, ref, copies):
        self.ref, self.copies, self.sent = ref, copies, set()
        self.shape, self.dtype = ref.shape, ref.dtype

    def __getitem__(self, index):
        return self.ref[index]

    def __setitem__(self, index, value):
        self.ref[index] = value

    def send(self, part=None):
        for index in range(len(self.copies)) if part is None else (part,):
            if index not in self.sent:
                self.copies[index].start()
                self.sent.add(index)


def doc_of(info, position):
    starts = info.starts()
    count = (position >= starts[0]).astype(jnp.int32)
    for start in starts[1:]:
        count = count + (position >= start).astype(jnp.int32)
    return count


def column_positions(info, first, count):
    return info.base + first + lax.broadcasted_iota(jnp.int32, (count, 1), 0)


def row_positions(info, first, count):
    return info.base + first + lax.broadcasted_iota(jnp.int32, (1, count), 1)


def prefix_mask(info):
    before = doc_of(info, info.base - 1)
    same = doc_of(info, column_positions(info, 0, ROWS)) == before
    return (same & (info.base > 0)).astype(f32)


def tail_mask(info):
    last = doc_of(info, info.base + ROWS - 1)
    return (doc_of(info, column_positions(info, 0, ROWS)) == last).astype(f32)


def factors(raw, side, choose_ref, lanes_ref):
    high, rest = low_pair(raw)
    high, rest = high.astype(f32), rest.astype(f32)
    left = raw - high - rest
    at = side * HEADS * F
    lane = lax.broadcasted_iota(jnp.int32, (1, 128), 1)
    parts = jnp.where(lane < 96, pltpu.roll(rest, 64 - at, 1), pltpu.roll(left, 96 - at, 1))
    parts = jnp.where(lane < 64, high, parts).astype(bf16)
    return [mm(parts, choose_ref[i]) + lanes_ref[i : i + 1, :] for i in range(2)]


def feature_back(gradient, left, right, choose_ref):
    first = mm_nt((gradient * right).astype(bf16), choose_ref[0])
    return first + mm_nt((gradient * left).astype(bf16), choose_ref[1])


def write_packed(packed_ref, head, state, norm):
    packed_ref[head, 0:KEPT, :] = state[:KEPT].astype(bf16)
    row = lax.broadcasted_iota(jnp.int32, (16, 128), 0)
    high = norm.astype(bf16).astype(f32)
    rest = norm - high
    tile = jnp.where(row == 0, high[:, :128], 0.0)
    tile = jnp.where(row == 1, high[:, 128:], tile)
    tile = jnp.where(row == 2, rest[:, :128], tile)
    tile = jnp.where(row == 3, rest[:, 128:], tile)
    packed_ref[head, KEPT:PACKED, :] = tile.astype(bf16)


def read_total(before_ref, got_refs, head):
    total = before_ref[head]
    for ref in got_refs:
        total = total + ref[head, 0:PACKED, :].astype(f32)
    state = jnp.concatenate(
        [total[:KEPT], jnp.zeros((LANES - KEPT, VALUE_WIDTH), f32)], axis=0
    ).astype(bf16)
    norm = jnp.concatenate(
        [
            total[KEPT : KEPT + 1] + total[KEPT + 2 : KEPT + 3],
            total[KEPT + 1 : KEPT + 2] + total[KEPT + 3 : KEPT + 4],
        ],
        axis=1,
    )
    return state, norm


def head_lanes(head):
    return slice(head * VALUE_WIDTH, (head + 1) * VALUE_WIDTH)


def window_rows(own_ref, halo_ref, which, head, tile):
    first, lanes = tile * TILE, head_lanes(head)
    if tile == 0:
        halo = halo_ref[head, which * WIN : (which + 1) * WIN, :]
        return jnp.concatenate([halo, own_ref[0:TILE, lanes]], axis=0)
    return own_ref[first - WIN : first + TILE, lanes]


def window_tile(info, head, tile, queries, key_rows, value_rows):
    first = tile * TILE
    query_at = column_positions(info, first, TILE)
    key_at = row_positions(info, first - WIN, TILE + WIN)
    near_by = (
        (key_at <= query_at)
        & (query_at - key_at < WIN)
        & (doc_of(info, query_at) == doc_of(info, key_at))
        & (key_at >= 0)
    )
    logits = mm_nt(queries, key_rows) * VALUE_WIDTH ** (-0.5)
    logits = jnp.where(near_by, logits, -1e30)
    exps = jnp.exp(logits - jnp.max(logits, axis=-1, keepdims=True))
    probs = exps / jnp.sum(exps, axis=-1, keepdims=True)
    return probs, mm(probs.astype(bf16), value_rows)


class Near:
    near = True

    def __init__(self, arrays, dims=None, places=None, parts=1):
        self.arrays = [
            a.arrays[0] if isinstance(a, Near) else a
            for a in (arrays if isinstance(arrays, (list, tuple)) else [arrays])
        ]
        self.dims = tuple(dims or self.arrays[0].shape)
        self.dtype = self.arrays[0].dtype
        self.places, self.parts = places, parts

    def copies(self, info, refs, buffer):
        if self.places is None:
            return pieces_of(refs[0], buffer, self.parts)
        return self.places(info, refs, buffer)

    def count(self):
        return self.parts if self.places is None else self.places(None)

    def copied(self):
        return self.places is not None


class Far(Near):
    near = False

    def copied(self):
        return True


class Out:

    def __init__(self, *dims, dtype=bf16, near=False, far=False, parts=1, width=None, first=0, onto=None):
        self.dims, self.dtype, self.parts = dims, dtype, parts
        self.near, self.far = near, far
        self.whole = dims if width is None else (dims[0], width)
        self.first, self.onto = first, onto

    def shapes(self):
        near = [jax.ShapeDtypeStruct(self.dims, self.dtype)] * self.near
        return near + [pltpu.HBM(self.whole, self.dtype)] * self.far

    def spaces(self):
        return [pltpu.VMEM] * self.near + [pltpu.HBM] * self.far

    def copies(self, buffer, target):
        if self.whole != self.dims:
            target = target.at[:, self.first : self.first + self.dims[1]]
        return pieces_of(buffer, target, self.parts)


class Stage:
    near, far, parts, onto = True, False, 1, None

    def __init__(self, source):
        self.source = source if isinstance(source, Far) else Far(source)
        self.dims, self.dtype = self.source.dims, self.source.dtype

    def shapes(self):
        return [jax.ShapeDtypeStruct(self.dims, self.dtype)]

    def spaces(self):
        return [pltpu.VMEM]


def near(*dims, dtype=bf16):
    return Out(*dims, dtype=dtype, near=True)


def far(*dims, dtype=bf16, parts=1, **columns):
    return Out(*dims, dtype=dtype, far=True, parts=parts, **columns)


def both(*dims, dtype=bf16):
    return Out(*dims, dtype=dtype, near=True, far=True)


def pieces_of(source, target, parts):
    if parts == 1:
        return [(source, target)]
    count = source.shape[0] // parts
    return [
        (source.at[i * count : (i + 1) * count], target.at[i * count : (i + 1) * count])
        for i in range(parts)
    ]


def in_hbm(array):
    return pltpu.with_memory_space_constraint(array, pltpu.HBM)


def call(body, results, operands, starts=None, after=(), flops=0, scratch=(), megabytes=28):
    operands = [o if isinstance(o, Near) else Far(o) for o in operands]
    waits = [pl.ANY if isinstance(o, Near) else pltpu.HBM for o in after]
    after = [o.arrays[0] if isinstance(o, Near) else in_hbm(o) for o in after]
    staged = [o for o in results if isinstance(o, Stage)]
    inputs = operands + [o.source for o in staged]
    arrays = [a for o in inputs for a in o.arrays]
    copied = [o for o in operands if o.copied()]
    held = [o for o in results if not o.near]
    count_out = sum(o.near + o.far for o in results)
    onto = {o: i for i, o in enumerate(results) if o.onto is not None}
    aliases = {len(arrays) + len(after) + i: onto[o] for i, o in enumerate(onto)}
    waits += [pltpu.HBM] * len(onto)
    after += [in_hbm(o.onto) for o in onto]
    moves = sum(o.count() for o in copied) + sum(o.source.count() for o in staged) + sum(o.parts for o in results if o.far)
    named = starts is not None

    def kernel(*refs):
        sources, refs = refs[: len(arrays)], refs[len(arrays) + len(after) :]
        named_ref, refs = (refs[0], refs[1:]) if named else (None, refs)
        targets, rest = list(refs[:count_out]), refs[count_out:]
        buffers, rest = list(rest[: len(copied)]), rest[len(copied) :]
        leaving, rest = list(rest[: len(held)]), rest[len(held) :]
        sems, rest = rest[0], rest[1:]
        marks = None
        if named:
            copy = pltpu.make_async_copy(named_ref, rest[0], sems.at[moves])
            copy.start()
            marks, rest = Loaded(rest[0], [copy]), rest[1:]
        info = Place(marks)
        loaded, at, sem = [], 0, 0

        def copies_of(pairs):
            nonlocal sem
            sem += len(pairs)
            return [
                pltpu.make_async_copy(source, target, sems.at[sem - len(pairs) + i])
                for i, (source, target) in enumerate(pairs)
            ]

        for operand in operands:
            own = sources[at : at + len(operand.arrays)]
            at += len(own)
            if not operand.copied():
                loaded.append(Loaded(own[0], []))
                continue
            buffer = buffers.pop(0)
            loaded.append(Loaded(buffer, copies_of(operand.copies(info, own, buffer))))
            for copy in loaded[-1].copies:
                copy.start()
        stored, staging = [], []
        for result in results:
            buffer = targets.pop(0) if result.near else leaving.pop(0)
            if isinstance(result, Stage):
                own = sources[at : at + len(result.source.arrays)]
                at += len(own)
                staging += copies_of(result.source.copies(info, own, buffer))
                continue
            target = targets.pop(0) if result.far else None
            pairs = result.copies(buffer, target) if result.far else []
            stored.append(Stored(buffer, copies_of(pairs)))
        for copy in staging:
            copy.start()
        body(info, *loaded, *stored, *rest)
        for copy in staging:
            copy.wait()
        for item in loaded + ([marks] if named else []):
            item.ready()
        for item in stored:
            item.send()
        for item in stored:
            for copy in item.copies:
                copy.wait()

    spaces = [pltpu.VMEM if o.near else pltpu.HBM for o in inputs for _ in o.arrays]
    placed = [a if space is pltpu.VMEM else in_hbm(a) for a, space in zip(arrays, spaces)]
    spaces += waits + [pltpu.HBM] * named
    moved = sum(a.size * a.dtype.itemsize for a in arrays)
    moved += sum(math.prod(o.dims) * jnp.dtype(o.dtype).itemsize for o in results)
    given = pl.pallas_call(
        kernel,
        name=getattr(body, "func", body).__name__,
        out_shape=tuple(s for o in results for s in o.shapes()),
        in_specs=[pl.BlockSpec(memory_space=space) for space in spaces],
        out_specs=tuple(pl.BlockSpec(memory_space=s) for o in results for s in o.spaces()),
        input_output_aliases=aliases,
        scratch_shapes=[pltpu.VMEM(o.dims, o.dtype) for o in copied]
        + [pltpu.VMEM(o.dims, o.dtype) for o in held]
        + [pltpu.SemaphoreType.DMA((max(1, moves + named),))]
        + [pltpu.SMEM((1, 4), jnp.int32)] * named
        + list(scratch),
        compiler_params=pltpu.CompilerParams(vmem_limit_bytes=megabytes * 2**20),
        cost_estimate=pl.CostEstimate(flops=0, bytes_accessed=1024, transcendentals=0),
    )(*placed, *after, *([in_hbm(starts)] if named else []))
    given, answer = list(given), []
    for result in results:
        item = (Near(given.pop(0)),) if result.near else ()
        item += (given.pop(0),) if result.far else ()
        answer.append(item if len(item) == 2 else item[0])
    return answer


def moved_by(array, axis, route):
    array = array.arrays[0] if isinstance(array, Near) else array
    return Near(lax.ppermute(array, axis, route))


def feature_weights(feat_query_t, feat_key_t):
    def places(info, sources=None, buffer=None):
        if info is None:
            return 2
        return [(sources[0], buffer.at[0:32]), (sources[1], buffer.at[32:64])]

    return Far([feat_query_t, feat_key_t], (128, feat_query_t.shape[1]), places)


def gathered(pieces):
    def places(info, sources=None, buffer=None):
        if info is None:
            return 8
        pairs = []
        for i, source in enumerate(sources):
            rows = info.rows(4 - i % 4, other=i >= 4)
            pairs.append((source.at[0:OWN], buffer.at[rows]))
        return pairs

    return Near(list(pieces), (ROWS, pieces[0].dims[1]), places)


def own_part(block):
    def places(info, sources=None, buffer=None):
        if info is None:
            return 1
        return [(sources[0].at[info.rows(0)], buffer)]

    return Far(block, (OWN, block.shape[1]), places)


def keys_kernel(
    info, x_ref, gain_ref, key_ref, value_ref, feat_ref, choose_ref, lanes_ref,
    normed_ref, inv_ref, raw_ref, keys_ref, values_ref, km_ref, packed_ref, wide_ref,
):
    gain = gain_ref[...]

    def norm_rows(part):
        for i in range(2):
            rows = slice(part * 128 + i * 64, part * 128 + i * 64 + 64)
            x = x_ref.ref[rows, :].astype(f32)
            inv = lax.rsqrt(jnp.mean(x * x, axis=-1, keepdims=True) + EPS)
            inv_ref[rows, :] = inv
            normed_ref[rows, :] = (x * inv * gain).astype(bf16)

    x_ref.part(0)
    norm_rows(0)
    x_ref.part(1)
    norm_rows(1)
    for ref in (x_ref, feat_ref, key_ref, value_ref, choose_ref, lanes_ref):
        ref.ready()
    feat_ref.ref[64:128, :] = jnp.zeros((64, feat_ref.shape[1]), bf16)
    half = ROWS // 2
    features = []
    for first in (0, half):
        rows = slice(first, first + half)
        normed = normed_ref[rows, :]
        raw = mm_nt(normed, feat_ref[...])
        raw_ref[rows, :] = raw
        if first == 0:
            norm_rows(2)
            norm_rows(3)
        keys_ref[rows, :] = mm(normed, key_ref[...]).astype(bf16)
        values_ref[rows, :] = mm(normed, value_ref[...]).astype(bf16)
        left, right = factors(raw, 1, choose_ref, lanes_ref)
        part = (left * right * lanes_ref[2:3, :]).astype(bf16)
        features.append((part.astype(f32) * lanes_ref[3:4, :]).astype(bf16))
    for ref in (normed_ref, inv_ref, raw_ref, keys_ref, values_ref):
        ref.send()
    features = jnp.concatenate(features, axis=0)
    values = values_ref[...]
    for head in range(HEADS):
        km_ref[head] = features[:, head * LANES : (head + 1) * LANES]
    km_ref.send()
    tail = tail_mask(info)
    for head in range(HEADS):
        own = features[:, head * LANES : (head + 1) * LANES]
        lanes = head_lanes(head)
        kept = (values[:, lanes].astype(f32) * tail).astype(bf16)
        state = mm_tn(own, kept)
        norm = jnp.sum(own.astype(f32) * tail, axis=0, keepdims=True)
        write_packed(packed_ref, head, state, norm)
        wide_ref[head, 0:PACKED, :] = packed_ref[head]
        wide_ref[head, PACKED : PACKED + WIN, :] = keys_ref[ROWS - WIN :, lanes]
        wide_ref[head, PACKED + WIN :, :] = values[ROWS - WIN :, lanes]


def local_kernel(
    info, raw_ref, choose_ref, lanes_ref, values_ref, km_ref, qf_ref, low_ref, num_ref, den_ref,
):
    left, right = factors(raw_ref[...], 0, choose_ref, lanes_ref)
    features = (left * right * lanes_ref[2:3, :]).astype(bf16)
    for head in range(HEADS):
        qf_ref[head] = features[:, head * LANES : (head + 1) * LANES]
    qf_ref.send()
    half = ROWS // 2
    causal = []
    for block in range(2):
        query_at = column_positions(info, block * half, half)
        key_at = row_positions(info, 0, (block + 1) * half)
        causal.append((query_at >= key_at) & (doc_of(info, query_at) == doc_of(info, key_at)))
    for head in range(HEADS):
        for block in range(2):
            first, reach = block * half, (block + 1) * half
            own = qf_ref[head, first:reach, :]
            weights = jnp.where(causal[block], mm_nt(own, km_ref[head, :reach, :]), 0.0)
            den_ref[head, first:reach, :] = jnp.sum(weights, axis=-1, keepdims=True)
            weights = weights.astype(bf16)
            low_ref[head, first:reach, 0:reach] = weights
            num_ref[first:reach, head_lanes(head)] = mm(
                weights, values_ref[:reach, head_lanes(head)]
            )
        low_ref.send(head)


def window_kernel(
    info, normed_ref, query_ref, keys_ref, values_ref, queries_ref, probs_ref, window_ref,
):
    queries = mm(normed_ref[...], query_ref[...]).astype(bf16)
    queries_ref[...] = queries
    queries_ref.send()
    for head in range(HEADS):
        lanes = head_lanes(head)
        for tile in range(1, ROWS // TILE):
            rows = slice(tile * TILE, (tile + 1) * TILE)
            probs, result = window_tile(
                info, head, tile, queries[rows, lanes],
                window_rows(keys_ref, None, 0, head, tile), window_rows(values_ref, None, 1, head, tile),
            )
            probs_ref[head, tile - 1] = probs
            window_ref[rows, lanes] = result
        probs_ref.send(head)


def by_distance(ref, info, other):
    return jnp.concatenate([ref[info.rows(d, other), :] for d in range(4)], axis=0)


def mixed_kernel(
    info, before_ref, got1_ref, got2_ref, got3_ref, qf_ref, num_ref, den_ref, window_ref, out_ref,
    queries_ref, keys_ref, values_ref,
    mixed_ref, linear_ref, total_den_ref, state_ref, norm_ref, probs_ref, halo_ref, own_ref, other_ref,
):
    use = prefix_mask(info)
    for head in range(HEADS):
        halo_ref[head] = got1_ref[head, PACKED:, :]
    halo_ref.send()
    for head in range(HEADS):
        lanes = head_lanes(head)
        state, norm = read_total(before_ref, (got1_ref, got2_ref, got3_ref), head)
        state_ref[head] = state
        norm_ref[head] = jnp.broadcast_to(norm, (8, LANES))
        features = qf_ref[head]
        inter = mm(features, state) * use
        den = jnp.sum(features.astype(f32) * norm, axis=-1, keepdims=True) * use + den_ref[head]
        total_den_ref[head] = den
        linear = (inter + num_ref[:, lanes]) / den
        linear_ref[:, lanes] = linear
        probs, window = window_tile(
            info, head, 0, queries_ref[0:TILE, lanes],
            window_rows(keys_ref, halo_ref, 0, head, 0), window_rows(values_ref, halo_ref, 1, head, 0),
        )
        probs_ref[head] = probs
        mixed_ref[0:TILE, lanes] = (linear[0:TILE] + window).astype(bf16)
        mixed_ref[TILE:, lanes] = (linear[TILE:] + window_ref[TILE:, lanes]).astype(bf16)
    for ref in (mixed_ref, linear_ref, total_den_ref, state_ref, norm_ref, probs_ref):
        ref.send()
    weights = out_ref[...]
    other_ref[...] = mm(by_distance(mixed_ref, info, True), weights).astype(bf16)
    own_ref[...] = mm(by_distance(mixed_ref, info, False), weights).astype(bf16)


def quarters_kernel(info, own_ref, got_ref, *out_refs):
    out_refs[4][...] = got_ref[0:16, 0:128]
    for d in (1, 2, 3, 0):
        rows = slice(d * OWN, (d + 1) * OWN)
        total = own_ref[rows, :].astype(f32) + got_ref[rows, :].astype(f32)
        out_refs[d][...] = total.astype(out_refs[d].dtype)
        out_refs[d].send()


def resid_kernel(
    info, mine_ref, x_ref, gain_ref, got1_ref, got2_ref, got3_ref, normed_ref, resid_ref, inv_ref
):
    resid = x_ref[...].astype(f32) + mine_ref[...]
    for ref in (got1_ref, got2_ref, got3_ref):
        resid = resid + ref[...].astype(f32)
    resid_ref[...] = resid
    resid_ref.send()
    inv = lax.rsqrt(jnp.mean(resid * resid, axis=-1, keepdims=True) + EPS)
    inv_ref[...] = inv
    inv_ref.send()
    normed_ref[...] = (resid * inv * gain_ref[...]).astype(bf16)


def grad_resid_kernel(
    info, mine_ref, resid_ref, inv_ref, top_ref, gain_ref, got1_ref, got2_ref, got3_ref,
    sent_ref, grad_ref, gains_ref,
):
    grad = mine_ref[...]
    for ref in (got1_ref, got2_ref, got3_ref):
        grad = grad + ref[...].astype(f32)
    resid = resid_ref[...]
    inv = inv_ref[...]
    grad_resid = top_ref[...].astype(f32) + norm_back(resid, inv, gain_ref[...], grad)
    sent_ref[...] = grad_resid.astype(bf16)
    sent_ref.send()
    grad_ref[...] = grad_resid
    gains_ref[0:1, :] = jnp.sum(grad * resid * inv, axis=0, keepdims=True)


def grad_x_kernel(
    info, mine_ref, x_ref, grad_resid_ref, gain_ref, resid_ref, out_ref, got1_ref, got2_ref, got3_ref,
    out1_ref, out2_ref, out3_ref, sent_ref,
):
    total = resid_ref[...] + out_ref[...]
    for ref in (out1_ref, out2_ref, out3_ref):
        total = total + ref[...].astype(f32)
    sent_ref[0:OWN, :] = total.astype(bf16)
    grad = mine_ref[...]
    for ref in (got1_ref, got2_ref, got3_ref):
        grad = grad + ref[...].astype(f32)
    x = x_ref[...].astype(f32)
    inv = lax.rsqrt(jnp.mean(x * x, axis=-1, keepdims=True) + EPS)
    sent_ref[OWN:, :] = (grad_resid_ref[...] + norm_back(x, inv, gain_ref[...], grad)).astype(bf16)


def norm_back(in_rows, inv_rms, gain, grad_normed):
    weighted = grad_normed * gain
    return inv_rms * weighted - in_rows * inv_rms**3 * jnp.mean(
        weighted * in_rows, axis=-1, keepdims=True
    )


def by_halves(block):
    def places(info, sources=None, buffer=None):
        if info is None:
            return 8
        return [
            (sources[0].at[info.rows(i % 4, other=i >= 4)], buffer.at[i * OWN : (i + 1) * OWN])
            for i in range(8)
        ]

    return Far(block, block.shape, places)


def halves(own, other):
    def places(info, sources=None, buffer=None):
        if info is None:
            return 2
        count = ROWS // 2
        return [(sources[0], buffer.at[0:count]), (sources[1], buffer.at[count : 2 * count])]

    return Far([own, other], (ROWS, own.shape[1]), places)


def grad_act_kernel(info, top_ref, down_ref, own_ref, other_ref):
    top = top_ref[...]
    half = ROWS // 2
    for first in range(0, down_ref.shape[0], 256):
        span = slice(first, min(first + 256, down_ref.shape[0]))
        grad = mm_nt(top, down_ref[span, :])
        own_ref[:, span] = grad[:half]
        other_ref[:, span] = grad[half:]


def ffn_rows(pieces, gate_ref, up_ref, grad_act_ref, normed_ref, act_ref, grad_gate_ref, grad_up_ref):
    normed = jnp.concatenate([piece[...] for piece in pieces], axis=0)
    normed_ref[...] = normed
    hidden = gate_ref.shape[0]
    for first in range(0, hidden, 256):
        span = slice(first, min(first + 256, hidden))
        gate = mm_nt(normed, gate_ref[span, :])
        up_value = mm_nt(normed, up_ref[span, :])
        sigmoid_gate = jax.nn.sigmoid(gate)
        silu_gate = gate * sigmoid_gate
        act_ref[:, span] = (silu_gate * up_value).astype(bf16)
        grad_act = grad_act_ref[:, span]
        grad_gate_ref[:, span] = (
            grad_act * up_value * sigmoid_gate * (1.0 + gate * (1.0 - sigmoid_gate))
        ).astype(bf16)
        grad_up_ref[:, span] = (grad_act * silu_gate).astype(bf16)
    act_ref.send()


def ffn_own_kernel(info, p0, p3, p2, p1, gate_ref, up_ref, grad_act_ref, *out_refs):
    ffn_rows((p0, p3, p2, p1), gate_ref, up_ref, grad_act_ref, *out_refs)


def ffn_other_kernel(info, s0, s3, s2, s1, gate_ref, up_ref, grad_act_ref, back_ref, *out_refs):
    ffn_rows((s0, s3, s2, s1), gate_ref, up_ref, grad_act_ref, *out_refs)
    ffn_back_kernel(info, out_refs[2], out_refs[3], gate_ref, up_ref, back_ref)


def ffn_back_kernel(info, grad_gate_ref, grad_up_ref, gate_ref, up_ref, back_ref):
    grad_gate, grad_up = grad_gate_ref[...], grad_up_ref[...]
    for first in range(0, back_ref.shape[1], 512):
        span = slice(first, first + 512)
        part = mm(grad_gate, gate_ref[:, span]) + mm(grad_up, up_ref[:, span])
        back_ref[:, span] = part.astype(bf16)


def ffn_out_kernel(info, act_own_ref, act_other_ref, down_ref, other_ref, own_ref):
    for target, act_ref in ((other_ref, act_other_ref), (own_ref, act_own_ref)):
        act = act_ref[...]
        for first in range(0, target.shape[1], 512):
            span = slice(first, first + 512)
            target[:, span] = mm(act, down_ref[:, span]).astype(bf16)


def column_grads(pairs, out_ref):
    count = out_ref.shape[0] // 4
    for part in range(4):
        span = slice(part * count, (part + 1) * count)
        first = 0
        for rows_refs, grads in pairs:
            rows_refs = rows_refs if isinstance(rows_refs, tuple) else (rows_refs,)
            grads = grads if isinstance(grads, tuple) else (grads,)
            total = sum(mm_tn(rows[:, span], grad) for rows, grad in zip(rows_refs, grads))
            last = first + total.shape[1]
            out_ref[span, first:last] = total.astype(bf16)
            first = last
        if first < out_ref.shape[1]:
            out_ref[span, first:] = jnp.zeros((count, out_ref.shape[1] - first), bf16)
        out_ref.send(part)


def gate_grads_kernel(
    info, own_ref, other_ref, gate_own_ref, gate_other_ref, up_own_ref, up_other_ref, out_ref
):
    rows = (own_ref, other_ref)
    gate = (gate_own_ref[...], gate_other_ref[...])
    up = (up_own_ref[...], up_other_ref[...])
    column_grads(((rows, gate), (rows, up)), out_ref)


def down_grads_kernel(info, top_ref, act_ref, out_ref):
    column_grads(((top_ref, act_ref[...]),), out_ref)


def grad_x_out_kernel(info, p0, p1, p2, p3, s0, s1, s2, s3, output_ref, grad_ref):
    for i, piece in enumerate((p0, p1, p2, p3, s0, s1, s2, s3)):
        rows = info.rows(4 - i % 4, other=i >= 4)
        output_ref[rows, :] = piece[0:OWN, :]
        grad_ref[rows, :] = piece[OWN : 2 * OWN, :].astype(f32)


def mixed_back_kernel(
    info, in_ref, out_ref, linear_ref, den_ref, qf_ref,
    packed_ref, top_ref, gm_ref, gnum_ref, gden_ref,
):
    top = in_ref[...]
    grad_mixed = mm_nt(top, out_ref[...]).astype(bf16)
    gm_ref[...] = grad_mixed
    gm_ref.send()
    top_ref[...] = top
    use = prefix_mask(info)
    for head in range(HEADS):
        lanes = head_lanes(head)
        wide = grad_mixed[:, lanes].astype(f32)
        den = den_ref[head]
        grad_num = (wide / den).astype(bf16)
        gnum_ref[:, lanes] = grad_num
        grad_den = -jnp.sum(wide * linear_ref[:, lanes], axis=-1, keepdims=True) / den
        gden_ref[head] = grad_den
        features = qf_ref[head]
        used = (grad_num.astype(f32) * use).astype(bf16)
        state = mm_tn(features, used)
        norm = jnp.sum(features.astype(f32) * (grad_den * use), axis=0, keepdims=True)
        write_packed(packed_ref, head, state, norm)
    packed_ref.send()


def window_back_kernel(
    info, gm_ref, probs0_ref, probs_ref, keys_ref, values_ref, halo_ref, queries_ref,
    edge_ref, gq_ref, gk_ref, gv_ref, key_acc, value_acc,
):
    scale = VALUE_WIDTH ** (-0.5)
    key_acc[...] = jnp.zeros_like(key_acc)
    value_acc[...] = jnp.zeros_like(value_acc)
    for tile in range(ROWS // TILE):
        first = tile * TILE
        reach = slice(first, first + TILE + WIN)
        for head in range(HEADS):
            lanes = head_lanes(head)
            key_rows = window_rows(keys_ref, halo_ref, 0, head, tile)
            value_rows = window_rows(values_ref, halo_ref, 1, head, tile)
            top = gm_ref[first : first + TILE, lanes]
            probs = probs0_ref[head] if tile == 0 else probs_ref[head, tile - 1]
            grad_probs = mm_nt(top, value_rows)
            shared = jnp.sum(grad_probs * probs, axis=-1, keepdims=True)
            grad_logits = (probs * (grad_probs - shared)).astype(bf16)
            gq_ref[first : first + TILE, lanes] = (mm(grad_logits, key_rows) * scale).astype(bf16)
            queries = queries_ref[first : first + TILE, lanes]
            key_acc[reach, lanes] += mm_tn(grad_logits, queries) * scale
            value_acc[reach, lanes] += mm_tn(probs.astype(bf16), top)
    edge_ref[0] = key_acc[0:WIN, :].astype(bf16)
    edge_ref[1] = value_acc[0:WIN, :].astype(bf16)
    gk_ref[...] = key_acc[WIN:, :]
    gv_ref[...] = value_acc[WIN:, :]


def linear_back_kernel(
    info, gnum_ref, gden_ref, values_ref, low_ref, km_ref, qf_ref, state_ref, norm_ref, raw_ref,
    choose_ref, lanes_ref, window_gv_ref, gfeat_ref, gv_ref, gkf_ref,
):
    use = prefix_mask(info)
    half = ROWS // 2
    grads = [[None, None], [None, None]]
    for head in range(HEADS):
        lanes = head_lanes(head)
        inter = mm_nt((gnum_ref[:, lanes].astype(f32) * use).astype(bf16), state_ref[head])
        inter = inter + (gden_ref[head] * use) * norm_ref[head, 0:1, :]
        for block in range(2):
            first, reach = block * half, (block + 1) * half
            query_at = column_positions(info, first, half)
            key_at = row_positions(info, 0, reach)
            causal = (query_at >= key_at) & (doc_of(info, query_at) == doc_of(info, key_at))
            grad_num = gnum_ref[first:reach, lanes]
            grad = mm_nt(grad_num, values_ref[:reach, lanes]) + gden_ref[head, first:reach, :]
            grad = jnp.where(causal, grad, 0.0).astype(bf16)
            grads[head][block] = mm(grad, km_ref[head, :reach, :]) + inter[first:reach]
            key_part = mm_tn(grad, qf_ref[head, first:reach, :])
            value_part = mm_tn(low_ref[head, first:reach, 0:reach], grad_num)
            if block == 0:
                gkf_ref[head, 0:half] = key_part
                gv_ref[0:half, lanes] = window_gv_ref[0:half, lanes] + value_part
            else:
                gkf_ref[head, 0:half] += key_part[0:half]
                gkf_ref[head, half:] = key_part[half:]
                gv_ref[0:half, lanes] += value_part[0:half]
                gv_ref[half:, lanes] = window_gv_ref[half:, lanes] + value_part[half:]
    left, right = factors(raw_ref[...], 0, choose_ref, lanes_ref)
    gradient = jnp.concatenate([jnp.concatenate(g, axis=0) for g in grads], axis=1)
    gradient = gradient * lanes_ref[2:3, :]
    gfeat_ref[...] = feature_back(gradient, left, right, choose_ref)


def keys_back_kernel(
    info, before_ref, got1_ref, got2_ref, got3_ref, values_ref, km_ref, gkf_ref, gk_ref, gv_ref,
    right_ref, raw_ref, choose_ref, lanes_ref, gfeat_ref, normed_ref, top_ref, mixed_ref, gq_ref,
    gkw_ref, gvw_ref, gf_ref, out_ref,
):
    tail = tail_mask(info)
    inner = ROWS - WIN
    gkw_ref[0:inner, :] = gk_ref[0:inner, :].astype(bf16)
    gkw_ref[inner:, :] = (gk_ref[inner:, :] + right_ref[0].astype(f32)).astype(bf16)
    gradients = []
    for head in range(HEADS):
        lanes = head_lanes(head)
        later, norm = read_total(before_ref, (got1_ref, got2_ref, got3_ref), head)
        kept = (values_ref[:, lanes].astype(f32) * tail).astype(bf16)
        gradients.append(gkf_ref[head] + mm_nt(kept, later) + tail * norm)
        grad_values = gv_ref[:, lanes] + mm(km_ref[head], later) * tail
        gvw_ref[0:inner, lanes] = grad_values[0:inner].astype(bf16)
        gvw_ref[inner:, lanes] = (grad_values[inner:] + right_ref[1, :, lanes].astype(f32)).astype(
            bf16
        )
    left, right = factors(raw_ref[...], 1, choose_ref, lanes_ref)
    gradient = jnp.concatenate(gradients, axis=1) * lanes_ref[4:5, :]
    gf_ref[...] = (feature_back(gradient, left, right, choose_ref) + gfeat_ref[...]).astype(bf16)
    column_grads(
        (
            (top_ref, mixed_ref[...]), (normed_ref, gq_ref[...]), (normed_ref, gkw_ref[...]),
            (normed_ref, gvw_ref[...]), (normed_ref, gf_ref[...]),
        ),
        out_ref,
    )


def normed_back_kernel(
    info, gq_ref, gkw_ref, gvw_ref, gf_ref, wq_ref, wk_ref, wv_ref, wf_ref, x_ref, inv_ref, gain_ffn_ref,
    other_ref, own_ref, gains_ref,
):
    wf_ref.ready()
    wf_ref.ref[64:128, :] = jnp.zeros((64, wf_ref.shape[1]), bf16)
    for target, other in ((other_ref, True), (own_ref, False)):
        grads = [by_distance(ref, info, other) for ref in (gq_ref, gkw_ref, gvw_ref, gf_ref)]
        scaled_by = by_distance(inv_ref, info, other)
        for piece in range(4):
            span = slice(piece * 512, (piece + 1) * 512)
            part = mm_nt(grads[0], wq_ref[span, :])
            part = part + mm_nt(grads[1], wk_ref[span, :])
            part = part + mm_nt(grads[2], wv_ref[span, :])
            part = part + mm(grads[3], wf_ref[:, span])
            target[:, span] = part.astype(bf16)
            x_rows = jnp.concatenate([x_ref[info.rows(d, other), span] for d in range(4)], axis=0)
            total = jnp.sum(part * (x_rows.astype(f32) * scaled_by), axis=0, keepdims=True)
            gains_ref[0:1, span] = total if other else total + gains_ref[0:1, span]
    gains_ref[1:2, :] = gain_ffn_ref[0:1, :]


def grads_out_kernel(
    info, in_ref, gate_ref, up_ref, down_ref, out_ref, grad_q_ref, grad_k_ref, grad_v_ref,
    feat_query_ref, feat_key_ref,
):
    hidden, width = gate_ref.shape[0], out_ref.shape[0]
    padded = -(-hidden // 128) * 128
    both = in_ref[:, 0 : 2 * hidden].astype(f32).T
    gate_ref[...] = both[0:hidden]
    gate_ref.send()
    up_ref[...] = both[hidden:]
    up_ref.send()
    at = 2 * hidden
    down_ref[...] = in_ref[:, at : at + padded].astype(f32).T[0:hidden]
    down_ref.send()
    at += padded
    out_ref[...] = in_ref[:, at : at + width].astype(f32).T
    out_ref.send()
    for ref in (grad_q_ref, grad_k_ref, grad_v_ref):
        at += width
        ref[...] = in_ref[:, at : at + width].astype(f32)
        ref.send()
    feat = in_ref[:, at + width :].astype(f32).T
    feat_query_ref[...] = feat[0:32]
    feat_key_ref[...] = feat[32:64]


def total_of(refs):
    total = refs[0][...]
    for ref in refs[1:]:
        total = total + ref[...]
    return total


def gains_kernel(info, *refs):
    refs[-1][...] = total_of(refs[:-1])


def spread_kernel(info, *refs):
    total, out_ref = total_of(refs[:-1]), refs[-1]
    for i in range(out_ref.shape[0]):
        out_ref[i, 0:2, :] = total[:, i * 128 : (i + 1) * 128]
        out_ref[i, 2:, :] = jnp.zeros((6, 128), f32)


def gathered_sum_kernel(info, in_ref, out_ref):
    total = in_ref[0]
    for i in range(1, in_ref.shape[0]):
        total = total + in_ref[i]
    out_ref[...] = total


def along_y(distance):
    return [(i, (i + 2 * distance) % 8) for i in range(8)]


def sibling():
    return [(i, i ^ 1) for i in range(8)]


def along_x(distance):
    return [(i, (i + 4 * distance) % 16) for i in range(16)]


def along_z(distance):
    return [(4 * a + z, 4 * a + (z + distance) % 4) for a in range(4) for z in range(4)]


def head_quarters(own, other, after=()):
    got = moved_by(other, "head", sibling())
    width = own.dims[1]
    with jax.named_scope("quarters"):
        mine, *sent, token = call(
            quarters_kernel,
            [near(OWN, width, dtype=f32)] + [near(OWN, width)] * 3 + [near(16, 128)],
            (own, got), after=after,
        )
    parts = [moved_by(sent[d - 1], "head", along_y(d)) for d in (2, 1, 3)]
    return mine, parts, moved_by(token, "head", sibling())


def head_pieces(own):
    far_piece = moved_by(own, "head", along_y(2))
    pieces = [own, moved_by(own, "head", along_y(1)), far_piece, moved_by(own, "head", along_y(3))]
    return pieces + [moved_by(piece, "head", sibling()) for piece in pieces]


def gains_sum(gains):
    with jax.named_scope("gains"):
        (pair,) = call(
            gains_kernel, [near(*gains.dims, dtype=f32)], (gains, moved_by(gains, "head", sibling()))
        )
        parts = [pair] + [moved_by(pair, "head", along_y(d)) for d in (2, 1, 3)]
        (blocks,) = call(spread_kernel, [far(16, 8, 128, dtype=f32)], parts)
        blocks = lax.all_to_all(blocks, "seq", 0, 0)
        (total,) = call(gathered_sum_kernel, [far(8, 128, dtype=f32)], (blocks,))
    return total


def scan_kernel(reverse, info, own_ref, got1_ref, got2_ref, got3_ref, before_ref, *sent_refs):
    place_x, place_z = (3 - info.x, 3 - info.z) if reverse else (info.x, info.z)
    before = jnp.zeros(before_ref.shape, f32)
    for d, ref in enumerate((got1_ref, got2_ref, got3_ref), 1):
        before = before + ref[:, 0:PACKED, :].astype(f32) * (place_x >= d).astype(f32)
    before_ref[...] = before
    row = lax.broadcasted_iota(jnp.int32, (HEADS, 16, 128), 1)
    sent = []
    for total in (before, before + own_ref[:, 0:PACKED, :].astype(f32)):
        norm = total[:, KEPT:]
        norm = norm + jnp.roll(norm, -2, axis=1)
        high = norm.astype(bf16).astype(f32)
        rest = jnp.roll(norm - high, 2, axis=1)
        norm = jnp.where(row < 2, high, jnp.where(row < 4, rest, 0.0))
        sent.append((total[:, :KEPT], norm))
    for d, ref in enumerate(sent_refs, 1):
        with_own = (place_z + d < 4).astype(f32)
        for part, rows in ((0, slice(0, KEPT)), (1, slice(KEPT, PACKED))):
            less, more = sent[0][part], sent[1][part]
            ref[:, rows, :] = (more * with_own + less * (1.0 - with_own)).astype(bf16)
        if ref.shape[1] > PACKED:
            own, earlier = own_ref[:, PACKED:, :].astype(f32), got1_ref[:, PACKED:, :].astype(f32)
            ref[:, PACKED:, :] = (own * with_own + earlier * (1.0 - with_own)).astype(bf16)


def exclusive_parts(own, reverse, after=(), wide=None):
    sign = -1 if reverse else 1
    first = own if wide is None else wide
    got = [moved_by(first if d == 1 else own, "seq", along_x(sign * d)) for d in (1, 2, 3)]
    with jax.named_scope("scan"):
        before, *sent = call(
            functools.partial(scan_kernel, reverse),
            [near(*own.dims, dtype=f32), near(*first.dims), near(*own.dims), near(*own.dims)],
            (first, *got), after=after,
        )
    return [before] + [
        moved_by(sent[d - 1], "seq", along_z(sign * d)) for d in (1, 2, 3)
    ]


def shifted(block, distance):
    route = [(i - distance, i) for i in range(16) if 0 <= i - distance < 16]
    return moved_by(block, "seq", route)


def shards(
    inputs,
    gain_mix,
    feat_query,
    feat_key,
    win_query,
    win_key,
    value_proj,
    out_proj,
    gain_ffn,
    gate_proj,
    up_proj,
    down_proj,
    document_starts,
    cotangent,
):
    choose, lanes = feature_tables()
    choose = jnp.asarray(choose, bf16)
    lanes = jnp.asarray(lanes, f32)
    choose_q, choose_k = choose[0], choose[1]
    feat = feature_weights(feat_query.T, feat_key.T)
    gain_mix = gain_mix.reshape(1, -1)
    gain_ffn = gain_ffn.reshape(1, -1)
    model = inputs.shape[1]
    width = HEADS * VALUE_WIDTH
    hidden = gate_proj.shape[1]
    half = ROWS // 2
    unit = 2 * ROWS * model
    starts = document_starts

    (normed, normed_far), inv_mix, (raw, raw_far), (keys, keys_far), (values, values_far), *rest = call(
        keys_kernel,
        (
            both(ROWS, model), far(ROWS, 1, dtype=f32), both(ROWS, 128, dtype=f32),
            both(ROWS, width), both(ROWS, width), both(HEADS, ROWS, LANES),
            near(HEADS, PACKED, 128), near(HEADS, PACKED + EDGE, 128),
        ),
        (Far(inputs, parts=4), gain_mix, win_key, value_proj, feat, choose_k, lanes),
        starts=starts, flops=unit * 640,
    )
    (km, km_far), packed, wide = rest
    (qf, qf_far), low, num, den, near_query, near_out = call(
        local_kernel,
        (
            both(HEADS, ROWS, LANES), far(HEADS, ROWS, ROWS, parts=HEADS), near(ROWS, width, dtype=f32),
            near(HEADS, ROWS, 1, dtype=f32), Stage(win_query), Stage(out_proj),
        ),
        (raw, choose_q, lanes, values, km),
        starts=starts, flops=unit * 300,
    )
    sums = exclusive_parts(packed, False, after=(qf,), wide=wide)
    (queries, queries_far), probs, window = call(
        window_kernel,
        (
            both(ROWS, width), far(HEADS, 3, TILE, TILE + WIN, dtype=f32, parts=HEADS),
            near(ROWS, width, dtype=f32),
        ),
        (normed, near_query, keys, values),
        starts=starts, flops=unit * 400,
    )
    mixed, linear, total_den, state, norm, probs_first, halo, own, other = call(
        mixed_kernel,
        (
            far(ROWS, width), far(ROWS, width, dtype=f32), far(HEADS, ROWS, 1, dtype=f32),
            far(HEADS, LANES, VALUE_WIDTH), far(HEADS, 8, LANES, dtype=f32),
            far(HEADS, TILE, TILE + WIN, dtype=f32), far(HEADS, EDGE, 128),
            near(half, model), near(half, model),
        ),
        (*sums, qf, num, den, window, near_out, queries, keys, values),
        starts=starts, flops=unit * 300,
    )
    mine, parts, signal = head_quarters(own, other)
    grad_act_own, grad_act_other, x_own, near_gain, near_gate, near_up = call(
        grad_act_kernel,
        (
            near(half, hidden, dtype=f32), near(half, hidden, dtype=f32), Stage(own_part(inputs)), Stage(gain_ffn),
            Stage(gate_proj.T), Stage(up_proj.T),
        ),
        (by_halves(cotangent), down_proj),
        after=(signal,), flops=unit * hidden,
    )
    own_normed, resid, inv_ffn = call(
        resid_kernel,
        (near(OWN, model), far(OWN, model, dtype=f32), far(OWN, 1, dtype=f32)),
        (mine, x_own, near_gain, *parts), after=(grad_act_own,),
    )
    pieces = head_pieces(own_normed)
    def ffn_half(body, pieces, grad_act, *more):
        order = [pieces[i] for i in (0, 3, 2, 1)]
        return call(
            body,
            (
                *more, near(half, model), far(half, hidden), near(half, hidden), near(half, hidden),
            ),
            (*order, near_gate, near_up, grad_act), flops=unit * 2 * hidden,
        )

    normed_own, act_own, gate_own, up_own = ffn_half(ffn_own_kernel, pieces[:4], grad_act_own)
    other, normed_other, act_other, gate_other, up_other = ffn_half(
        ffn_other_kernel, pieces[4:], grad_act_other, near(half, model)
    )
    (own,) = call(
        ffn_back_kernel, (near(half, model),), (gate_own, up_own, near_gate, near_up),
        after=(other,), flops=unit * hidden,
    )
    mine, parts, signal = head_quarters(own, other)
    padded = -(-hidden // 128) * 128
    place = dict(parts=4, width=2 * hidden + padded + 4 * width + 128)
    grads, *near_resid = call(
        gate_grads_kernel,
        (
            far(model, 2 * hidden, **place), Stage(resid), Stage(inv_ffn),
            Stage(own_part(cotangent)), Stage(gain_ffn), Stage(out_proj), Stage(linear),
            Stage(total_den), Stage(qf_far),
        ),
        (normed_own, normed_other, gate_own, gate_other, up_own, up_other),
        after=(signal,), flops=unit * 2 * hidden,
    )
    near_resid, near_mixed = near_resid[:4], near_resid[4:]
    at = 2 * hidden
    grads, *near_back = call(
        down_grads_kernel,
        (
            far(model, padded, first=at, onto=grads, **place), Stage(probs_first), Stage(probs),
            Stage(keys_far), Stage(values_far), Stage(halo), Stage(queries_far), Stage(low),
            Stage(km_far),
            Stage(state), Stage(norm), Stage(raw_far), Stage(choose_q), Stage(choose_k),
            Stage(lanes),
        ),
        (by_halves(cotangent), halves(act_own, act_other)), after=(signal,), flops=unit * hidden,
    )
    probs_first, probs, keys, values, halo, queries, low, km, state, norm, raw, *rest = near_back
    choose_q, choose_k, lanes = rest
    at += padded
    sent, grad_resid, gain_ffn_part = call(
        grad_resid_kernel,
        (near(OWN, model), far(OWN, model, dtype=f32), far(8, model, dtype=f32)),
        (mine, *near_resid, *parts), after=(grads,),
    )
    pieces = head_pieces(sent)
    packed, top, grad_mixed, grad_num, grad_den = call(
        mixed_back_kernel,
        (
            near(HEADS, PACKED, 128), near(ROWS, model), near(ROWS, width), near(ROWS, width),
            near(HEADS, ROWS, 1, dtype=f32),
        ),
        (gathered(pieces), *near_mixed),
        starts=starts, flops=unit * 300,
    )
    edge, gq, gk, gv = call(
        window_back_kernel,
        (
            near(2, WIN, width), near(ROWS, width), near(ROWS, width, dtype=f32),
            near(ROWS, width, dtype=f32),
        ),
        (grad_mixed, probs_first, probs, keys, values, halo, queries),
        flops=unit * 300, scratch=[pltpu.VMEM((ROWS + WIN, width), f32)] * 2,
    )
    right = shifted(edge, -1)
    sums = exclusive_parts(packed, True, after=(edge,))
    gfeat, gv, gkf, normed, mixed = call(
        linear_back_kernel,
        (
            near(ROWS, 128, dtype=f32), near(ROWS, width, dtype=f32),
            near(HEADS, ROWS, LANES, dtype=f32), Stage(normed_far), Stage(mixed),
        ),
        (
            grad_num, grad_den, values, low, km, near_mixed[3], state, norm, raw, choose_q, lanes, gv,
        ),
        starts=starts, after=(sums[0],), flops=unit * 300,
    )
    gkw, gvw, gf, grads = call(
        keys_back_kernel,
        (
            near(ROWS, width), near(ROWS, width), near(ROWS, 128),
            far(model, 4 * width + 128, first=at, onto=grads, **place),
        ),
        (
            *sums, values, km, gkf, gk, gv, right, raw, choose_k, lanes, gfeat, normed, top, mixed,
            gq,
        ),
        starts=starts, flops=unit * 1400,
    )
    grads_sum = lax.psum_scatter(grads, "seq", scatter_dimension=0, tiled=True)
    other, own, gains = call(
        normed_back_kernel, (near(half, model), near(half, model), near(2, model, dtype=f32)),
        (
            gq, gkw, gvw, gf, win_query, win_key, value_proj, feat, inputs, inv_mix, gain_ffn_part,
        ),
        after=(grads,),
        flops=unit * 900,
    )
    mine, parts, signal = head_quarters(own, other)
    other, own = call(
        ffn_out_kernel, (near(half, model), near(half, model)), (act_own, act_other, down_proj),
        after=(signal,), flops=unit * hidden,
    )
    out_mine, out_parts, signal = head_quarters(own, other)
    gains = gains_sum(gains)
    (sent,) = call(
        grad_x_kernel, (near(2 * OWN, model),),
        (mine, own_part(inputs), grad_resid, gain_mix, resid, out_mine, *parts, *out_parts),
        after=(gains,),
    )
    pieces = head_pieces(sent)
    output, grad_x = call(
        grad_x_out_kernel, (far(ROWS, model), far(ROWS, model, dtype=f32)), pieces,
    )
    grad_gate_t, grad_up_t, grad_down, grad_out, *rest = call(
        grads_out_kernel,
        (far(hidden, 128, dtype=f32),) * 3 + (far(width, 128, dtype=f32),)
        + (far(128, width, dtype=f32),) * 3 + (far(32, 128, dtype=f32),) * 2,
        (grads_sum,), after=(grad_x,),
    )
    grad_wq, grad_wk, grad_wv, grad_fq_t, grad_fk_t = rest
    return (
        output,
        grad_x,
        gains[0],
        grad_fq_t.T,
        grad_fk_t.T,
        grad_wq,
        grad_wk,
        grad_wv,
        grad_out,
        gains[1],
        grad_gate_t.T,
        grad_up_t.T,
        grad_down,
    )


def solution(mesh):
    placed = (
        P("seq", None),
        P(),
        P(None, "head"),
        P(None, "head"),
        P(None, "head"),
        P(None, "head"),
        P(None, "head"),
        P("head", None),
        P(),
        P(None, "head"),
        P(None, "head"),
        P("head", None),
        P(),
        P("seq", None),
    )
    return jax.shard_map(
        shards,
        mesh=mesh,
        in_specs=placed,
        out_specs=(
            P("seq", None),
            P("seq", None),
            P("seq"),
            P("seq", "head"),
            P("seq", "head"),
            P("seq", "head"),
            P("seq", "head"),
            P("seq", "head"),
            P("head", "seq"),
            P("seq"),
            P("seq", "head"),
            P("seq", "head"),
            P("head", "seq"),
        ),
        check_vma=False,
    )
```

```python
import functools
import math

import jax
import jax.numpy as jnp
import numpy as np
from jax import lax
from jax.experimental import pallas as pl
from jax.experimental.pallas import tpu as pltpu
from jax.sharding import PartitionSpec as P

F = 16
VALUE_WIDTH = 128
WIN = 64
EPS = 1e-05

HEADS = 2
ROWS = 512
LANES = 256
KEPT = 160
PACKED = 176
TILE = 128
EDGE = 2 * WIN
OWN = 64
f32 = jnp.float32
bf16 = jnp.bfloat16


def feature_tables():
    pairs = [(a, b) for a in range(F) for b in range(a, F)]
    count = len(pairs)
    choose = np.zeros((2, 2, 128, HEADS * LANES), np.float32)
    lanes = np.zeros((8, HEADS * LANES), np.float32)
    factor = F ** (-0.25)
    for head in range(HEADS):
        at = head * LANES
        for side in range(2):
            for first in (side * HEADS * F, 64, 96):
                row = first + head * F
                for lane, (a, b) in enumerate(pairs):
                    choose[side, 0, row + a, at + lane] = 1.0
                    choose[side, 1, row + b, at + lane] = 1.0
                for a in range(F):
                    choose[side, 0, row + a, at + count + a] = 1.0
        for lane, (a, b) in enumerate(pairs):
            lanes[2, at + lane] = factor * factor / math.sqrt(2.0)
            lanes[3, at + lane] = 1.0 if a == b else 2.0
        lanes[1, at + count : at + count + F + 1] = 1.0
        lanes[0, at + count + F] = 1.0
        lanes[2, at + count : at + count + F] = factor
        lanes[2, at + count + F] = 1.0
        lanes[3, at + count : at + count + F + 1] = 1.0
    lanes[4] = lanes[2] * lanes[3]
    return choose, lanes


def mm(a, b):
    return lax.dot_general(a, b, (((1,), (0,)), ((), ())), preferred_element_type=f32)


def mm_nt(a, b):
    return lax.dot_general(a, b, (((1,), (1,)), ((), ())), preferred_element_type=f32)


def mm_tn(a, b):
    return lax.dot_general(a, b, (((0,), (0,)), ((), ())), preferred_element_type=f32)


def low_pair(part):
    high = part.astype(bf16)
    return high, (part - high.astype(f32)).astype(bf16)


class Place:

    def __init__(self, starts):
        me, seq = lax.axis_index("head"), lax.axis_index("seq")
        self.base = seq * ROWS
        self.x, self.z = lax.shift_right_logical(seq, 2), lax.bitwise_and(seq, 3)
        self.y, self.core = lax.shift_right_logical(me, 1), lax.bitwise_and(me, 1)
        self.loaded = starts

    def starts(self):
        return [self.loaded[0, i] for i in range(4)]

    def rows(self, distance, other=False):
        quarter = lax.bitwise_and(self.y + distance, 3)
        core = 1 - self.core if other else self.core
        return pl.ds(pl.multiple_of(quarter * (2 * OWN) + core * OWN, OWN), OWN)


class Loaded:

    def __init__(self, ref, copies):
        self.ref, self.copies = ref, list(copies)
        self.shape = ref.shape

    def part(self, index):
        if self.copies and self.copies[index] is not None:
            self.copies[index].wait()
            self.copies[index] = None

    def ready(self):
        for index in range(len(self.copies)):
            self.part(index)

    def __getitem__(self, index):
        self.ready()
        return self.ref[index]


class Stored:

    def __init__(self, ref, copies):
        self.ref, self.copies, self.sent = ref, copies, set()
        self.shape, self.dtype = ref.shape, ref.dtype

    def __getitem__(self, index):
        return self.ref[index]

    def __setitem__(self, index, value):
        self.ref[index] = value

    def send(self, part=None):
        for index in range(len(self.copies)) if part is None else (part,):
            if index not in self.sent:
                self.copies[index].start()
                self.sent.add(index)


def doc_of(info, position):
    starts = info.starts()
    count = (position >= starts[0]).astype(jnp.int32)
    for start in starts[1:]:
        count = count + (position >= start).astype(jnp.int32)
    return count


def column_positions(info, first, count):
    return info.base + first + lax.broadcasted_iota(jnp.int32, (count, 1), 0)


def row_positions(info, first, count):
    return info.base + first + lax.broadcasted_iota(jnp.int32, (1, count), 1)


def prefix_mask(info):
    before = doc_of(info, info.base - 1)
    same = doc_of(info, column_positions(info, 0, ROWS)) == before
    return (same & (info.base > 0)).astype(f32)


def tail_mask(info):
    last = doc_of(info, info.base + ROWS - 1)
    return (doc_of(info, column_positions(info, 0, ROWS)) == last).astype(f32)


def factors(raw, side, choose_ref, lanes_ref):
    high, rest = low_pair(raw)
    high, rest = high.astype(f32), rest.astype(f32)
    left = raw - high - rest
    at = side * HEADS * F
    lane = lax.broadcasted_iota(jnp.int32, (1, 128), 1)
    parts = jnp.where(lane < 96, pltpu.roll(rest, 64 - at, 1), pltpu.roll(left, 96 - at, 1))
    parts = jnp.where(lane < 64, high, parts).astype(bf16)
    return [mm(parts, choose_ref[i]) + lanes_ref[i : i + 1, :] for i in range(2)]


def feature_back(gradient, left, right, choose_ref):
    first = mm_nt((gradient * right).astype(bf16), choose_ref[0])
    return first + mm_nt((gradient * left).astype(bf16), choose_ref[1])


def write_packed(packed_ref, head, state, norm):
    packed_ref[head, 0:KEPT, :] = state[:KEPT].astype(bf16)
    row = lax.broadcasted_iota(jnp.int32, (16, 128), 0)
    high = norm.astype(bf16).astype(f32)
    rest = norm - high
    tile = jnp.where(row == 0, high[:, :128], 0.0)
    tile = jnp.where(row == 1, high[:, 128:], tile)
    tile = jnp.where(row == 2, rest[:, :128], tile)
    tile = jnp.where(row == 3, rest[:, 128:], tile)
    packed_ref[head, KEPT:PACKED, :] = tile.astype(bf16)


def read_total(before_ref, got_refs, head):
    total = before_ref[head]
    for ref in got_refs:
        total = total + ref[head, 0:PACKED, :].astype(f32)
    state = jnp.concatenate(
        [total[:KEPT], jnp.zeros((LANES - KEPT, VALUE_WIDTH), f32)], axis=0
    ).astype(bf16)
    norm = jnp.concatenate(
        [
            total[KEPT : KEPT + 1] + total[KEPT + 2 : KEPT + 3],
            total[KEPT + 1 : KEPT + 2] + total[KEPT + 3 : KEPT + 4],
        ],
        axis=1,
    )
    return state, norm


def head_lanes(head):
    return slice(head * VALUE_WIDTH, (head + 1) * VALUE_WIDTH)


def window_rows(own_ref, halo_ref, which, head, tile):
    first, lanes = tile * TILE, head_lanes(head)
    if tile == 0:
        after = halo_ref.shape[1] - EDGE + which * WIN
        halo = halo_ref[head, after : after + WIN, :]
        return jnp.concatenate([halo, own_ref[0:TILE, lanes]], axis=0)
    return own_ref[first - WIN : first + TILE, lanes]


def window_tile(info, head, tile, queries, key_rows, value_rows):
    first = tile * TILE
    query_at = column_positions(info, first, TILE)
    key_at = row_positions(info, first - WIN, TILE + WIN)
    near_by = (
        (key_at <= query_at)
        & (query_at - key_at < WIN)
        & (doc_of(info, query_at) == doc_of(info, key_at))
        & (key_at >= 0)
    )
    logits = mm_nt(queries, key_rows) * VALUE_WIDTH ** (-0.5)
    logits = jnp.where(near_by, logits, -1e30)
    exps = jnp.exp(logits - jnp.max(logits, axis=-1, keepdims=True))
    probs = exps / jnp.sum(exps, axis=-1, keepdims=True)
    return probs, mm(probs.astype(bf16), value_rows)


class Near:
    near = True

    def __init__(self, arrays, dims=None, places=None, parts=1):
        self.arrays = [
            a.arrays[0] if isinstance(a, Near) else a
            for a in (arrays if isinstance(arrays, (list, tuple)) else [arrays])
        ]
        self.dims = tuple(dims or self.arrays[0].shape)
        self.dtype = self.arrays[0].dtype
        self.places, self.parts = places, parts

    def copies(self, info, refs, buffer):
        if self.places is None:
            return pieces_of(refs[0], buffer, self.parts)
        return self.places(info, refs, buffer)

    def count(self):
        return self.parts if self.places is None else self.places(None)

    def copied(self):
        return self.places is not None


class Far(Near):
    near = False

    def copied(self):
        return True


class Out:

    def __init__(self, *dims, dtype=bf16, near=False, far=False, parts=1, width=None, first=0, onto=None):
        self.dims, self.dtype, self.parts = dims, dtype, parts
        self.near, self.far = near, far
        self.whole = dims if width is None else (dims[0], width)
        self.first, self.onto = first, onto

    def shapes(self):
        near = [jax.ShapeDtypeStruct(self.dims, self.dtype)] * self.near
        return near + [pltpu.HBM(self.whole, self.dtype)] * self.far

    def spaces(self):
        return [pltpu.VMEM] * self.near + [pltpu.HBM] * self.far

    def copies(self, buffer, target):
        if self.whole != self.dims:
            target = target.at[:, self.first : self.first + self.dims[1]]
        return pieces_of(buffer, target, self.parts)


class Stage:
    near, far, parts, onto = True, False, 1, None

    def __init__(self, source):
        self.source = source if isinstance(source, Far) else Far(source)
        self.dims, self.dtype = self.source.dims, self.source.dtype

    def shapes(self):
        return [jax.ShapeDtypeStruct(self.dims, self.dtype)]

    def spaces(self):
        return [pltpu.VMEM]


class Export:
    near, far, parts, onto = False, True, 1, None

    def __init__(self, source, dims=None, view=None):
        self.source, self.view = source, view
        self.dims, self.dtype = tuple(dims or source.dims), source.dtype

    def shapes(self):
        return [pltpu.HBM(self.dims, self.dtype)]

    def spaces(self):
        return [pltpu.HBM]

    def copies(self, ref, target):
        return [(ref if self.view is None else self.view(ref), target)]


def near(*dims, dtype=bf16):
    return Out(*dims, dtype=dtype, near=True)


def far(*dims, dtype=bf16, parts=1, **columns):
    return Out(*dims, dtype=dtype, far=True, parts=parts, **columns)


def both(*dims, dtype=bf16):
    return Out(*dims, dtype=dtype, near=True, far=True)


def pieces_of(source, target, parts):
    if parts == 1:
        return [(source, target)]
    count = source.shape[0] // parts
    return [
        (source.at[i * count : (i + 1) * count], target.at[i * count : (i + 1) * count])
        for i in range(parts)
    ]


def in_hbm(array):
    return pltpu.with_memory_space_constraint(array, pltpu.HBM)


def call(body, results, operands, starts=None, after=(), flops=0, scratch=(), megabytes=28):
    operands = [o if isinstance(o, Near) else Far(o) for o in operands]
    waits = [pl.ANY if isinstance(o, Near) else pltpu.HBM for o in after]
    after = [o.arrays[0] if isinstance(o, Near) else in_hbm(o) for o in after]
    staged = [o for o in results if isinstance(o, Stage)]
    inputs = operands + [o.source for o in results if isinstance(o, (Stage, Export))]
    arrays = [a for o in inputs for a in o.arrays]
    copied = [o for o in operands if o.copied()]
    held = [o for o in results if not o.near and not isinstance(o, Export)]
    count_out = sum(o.near + o.far for o in results)
    onto = {o: i for i, o in enumerate(results) if o.onto is not None}
    aliases = {len(arrays) + len(after) + i: onto[o] for i, o in enumerate(onto)}
    waits += [pltpu.HBM] * len(onto)
    after += [in_hbm(o.onto) for o in onto]
    moves = sum(o.count() for o in copied) + sum(o.source.count() for o in staged) + sum(o.parts for o in results if o.far)
    named = starts is not None

    def kernel(*refs):
        sources, refs = refs[: len(arrays)], refs[len(arrays) + len(after) :]
        named_ref, refs = (refs[0], refs[1:]) if named else (None, refs)
        targets, rest = list(refs[:count_out]), refs[count_out:]
        buffers, rest = list(rest[: len(copied)]), rest[len(copied) :]
        leaving, rest = list(rest[: len(held)]), rest[len(held) :]
        sems, rest = rest[0], rest[1:]
        marks = None
        if named:
            copy = pltpu.make_async_copy(named_ref, rest[0], sems.at[moves])
            copy.start()
            marks, rest = Loaded(rest[0], [copy]), rest[1:]
        info = Place(marks)
        loaded, at, sem = [], 0, 0

        def copies_of(pairs):
            nonlocal sem
            sem += len(pairs)
            return [
                pltpu.make_async_copy(source, target, sems.at[sem - len(pairs) + i])
                for i, (source, target) in enumerate(pairs)
            ]

        for operand in operands:
            own = sources[at : at + len(operand.arrays)]
            at += len(own)
            if not operand.copied():
                loaded.append(Loaded(own[0], []))
                continue
            buffer = buffers.pop(0)
            loaded.append(Loaded(buffer, copies_of(operand.copies(info, own, buffer))))
            for copy in loaded[-1].copies:
                copy.start()
        stored, staging = [], []
        for result in results:
            if isinstance(result, Export):
                staging += copies_of(result.copies(sources[at], targets.pop(0)))
                at += 1
                continue
            buffer = targets.pop(0) if result.near else leaving.pop(0)
            if isinstance(result, Stage):
                own = sources[at : at + len(result.source.arrays)]
                at += len(own)
                staging += copies_of(result.source.copies(info, own, buffer))
                continue
            target = targets.pop(0) if result.far else None
            pairs = result.copies(buffer, target) if result.far else []
            stored.append(Stored(buffer, copies_of(pairs)))
        for copy in staging:
            copy.start()
        body(info, *loaded, *stored, *rest)
        for copy in staging:
            copy.wait()
        for item in loaded + ([marks] if named else []):
            item.ready()
        for item in stored:
            item.send()
        for item in stored:
            for copy in item.copies:
                copy.wait()

    spaces = [pltpu.VMEM if o.near else pltpu.HBM for o in inputs for _ in o.arrays]
    placed = [a if space is pltpu.VMEM else in_hbm(a) for a, space in zip(arrays, spaces)]
    spaces += waits + [pltpu.HBM] * named
    moved = sum(a.size * a.dtype.itemsize for a in arrays)
    moved += sum(math.prod(o.dims) * jnp.dtype(o.dtype).itemsize for o in results)
    given = pl.pallas_call(
        kernel,
        name=getattr(body, "func", body).__name__,
        out_shape=tuple(s for o in results for s in o.shapes()),
        in_specs=[pl.BlockSpec(memory_space=space) for space in spaces],
        out_specs=tuple(pl.BlockSpec(memory_space=s) for o in results for s in o.spaces()),
        input_output_aliases=aliases,
        scratch_shapes=[pltpu.VMEM(o.dims, o.dtype) for o in copied]
        + [pltpu.VMEM(o.dims, o.dtype) for o in held]
        + [pltpu.SemaphoreType.DMA((max(1, moves + named),))]
        + [pltpu.SMEM((1, 4), jnp.int32)] * named
        + list(scratch),
        compiler_params=pltpu.CompilerParams(vmem_limit_bytes=megabytes * 2**20),
        cost_estimate=pl.CostEstimate(flops=0, bytes_accessed=1024, transcendentals=0),
    )(*placed, *after, *([in_hbm(starts)] if named else []))
    given, answer = list(given), []
    for result in results:
        item = (Near(given.pop(0)),) if result.near else ()
        item += (given.pop(0),) if result.far else ()
        answer.append(item if len(item) == 2 else item[0])
    return answer


def moved_by(array, axis, route):
    array = array.arrays[0] if isinstance(array, Near) else array
    return Near(lax.ppermute(array, axis, route))


def feature_weights(feat_query_t, feat_key_t):
    def places(info, sources=None, buffer=None):
        if info is None:
            return 2
        return [(sources[0], buffer.at[0:32]), (sources[1], buffer.at[32:64])]

    return Far([feat_query_t, feat_key_t], (128, feat_query_t.shape[1]), places)


def own_part(block):
    def places(info, sources=None, buffer=None):
        if info is None:
            return 1
        return [(sources[0].at[info.rows(0)], buffer)]

    return Far(block, (OWN, block.shape[1]), places)


def keys_kernel(
    info, x_ref, gain_ref, key_ref, value_ref, feat_ref, choose_ref, lanes_ref,
    normed_ref, inv_ref, raw_ref, keys_ref, values_ref, km_ref, packed_ref, wide_ref,
):
    gain = gain_ref[...]

    def norm_rows(part):
        for i in range(2):
            rows = slice(part * 128 + i * 64, part * 128 + i * 64 + 64)
            x = x_ref.ref[rows, :].astype(f32)
            inv = lax.rsqrt(jnp.mean(x * x, axis=-1, keepdims=True) + EPS)
            inv_ref[rows, :] = inv
            normed_ref[rows, :] = (x * inv * gain).astype(bf16)

    x_ref.part(0)
    norm_rows(0)
    x_ref.part(1)
    norm_rows(1)
    for ref in (x_ref, feat_ref, key_ref, value_ref, choose_ref, lanes_ref):
        ref.ready()
    feat_ref.ref[64:128, :] = jnp.zeros((64, feat_ref.shape[1]), bf16)
    half = ROWS // 2
    features = []
    for first in (0, half):
        rows = slice(first, first + half)
        normed = normed_ref[rows, :]
        raw = mm_nt(normed, feat_ref[...])
        raw_ref[rows, :] = raw
        if first == 0:
            norm_rows(2)
            norm_rows(3)
        keys_ref[rows, :] = mm(normed, key_ref[...]).astype(bf16)
        values_ref[rows, :] = mm(normed, value_ref[...]).astype(bf16)
        left, right = factors(raw, 1, choose_ref, lanes_ref)
        part = (left * right * lanes_ref[2:3, :]).astype(bf16)
        features.append((part.astype(f32) * lanes_ref[3:4, :]).astype(bf16))
    features = jnp.concatenate(features, axis=0)
    values = values_ref[...]
    for head in range(HEADS):
        km_ref[head] = features[:, head * LANES : (head + 1) * LANES]
    tail = tail_mask(info)
    for head in range(HEADS):
        own = features[:, head * LANES : (head + 1) * LANES]
        lanes = head_lanes(head)
        kept = (values[:, lanes].astype(f32) * tail).astype(bf16)
        state = mm_tn(own, kept)
        norm = jnp.sum(own.astype(f32) * tail, axis=0, keepdims=True)
        write_packed(packed_ref, head, state, norm)
        wide_ref[head, 0:PACKED, :] = packed_ref[head]
        wide_ref[head, PACKED : PACKED + WIN, :] = keys_ref[ROWS - WIN :, lanes]
        wide_ref[head, PACKED + WIN :, :] = values[ROWS - WIN :, lanes]


def local_kernel(
    info, raw_ref, choose_ref, lanes_ref, values_ref, km_ref, qf_ref, low_ref, num_ref, den_ref,
):
    left, right = factors(raw_ref[...], 0, choose_ref, lanes_ref)
    features = (left * right * lanes_ref[2:3, :]).astype(bf16)
    for head in range(HEADS):
        qf_ref[head] = features[:, head * LANES : (head + 1) * LANES]
    half = ROWS // 2
    causal = []
    for block in range(2):
        query_at = column_positions(info, block * half, half)
        key_at = row_positions(info, 0, (block + 1) * half)
        causal.append((query_at >= key_at) & (doc_of(info, query_at) == doc_of(info, key_at)))
    for head in range(HEADS):
        for block in range(2):
            first, reach = block * half, (block + 1) * half
            own = qf_ref[head, first:reach, :]
            weights = jnp.where(causal[block], mm_nt(own, km_ref[head, :reach, :]), 0.0)
            den_ref[head, first:reach, :] = jnp.sum(weights, axis=-1, keepdims=True)
            weights = weights.astype(bf16)
            low_ref[head, first:reach, 0:reach] = weights
            num_ref[first:reach, head_lanes(head)] = mm(
                weights, values_ref[:reach, head_lanes(head)]
            )


def window_kernel(
    info, normed_ref, query_ref, keys_ref, values_ref, queries_ref, probs_ref, window_ref,
):
    queries = mm(normed_ref[...], query_ref[...]).astype(bf16)
    queries_ref[...] = queries
    for head in range(HEADS):
        lanes = head_lanes(head)
        for tile in range(1, ROWS // TILE):
            rows = slice(tile * TILE, (tile + 1) * TILE)
            probs, result = window_tile(
                info, head, tile, queries[rows, lanes],
                window_rows(keys_ref, None, 0, head, tile), window_rows(values_ref, None, 1, head, tile),
            )
            probs_ref[head, tile - 1] = probs
            window_ref[rows, lanes] = result


def by_distance(ref, info, other):
    return jnp.concatenate([ref[info.rows(d, other), :] for d in range(4)], axis=0)


def mixed_kernel(
    info, before_ref, got1_ref, got2_ref, got3_ref, qf_ref, num_ref, den_ref, window_ref, out_ref,
    queries_ref, keys_ref, values_ref,
    mixed_ref, linear_ref, total_den_ref, state_ref, norm_ref, probs_ref, other_ref,
):
    use = prefix_mask(info)
    for head in range(HEADS):
        lanes = head_lanes(head)
        state, norm = read_total(before_ref, (got1_ref, got2_ref, got3_ref), head)
        state_ref[head] = state
        norm_ref[head] = jnp.broadcast_to(norm, (8, LANES))
        features = qf_ref[head]
        inter = mm(features, state) * use
        den = jnp.sum(features.astype(f32) * norm, axis=-1, keepdims=True) * use + den_ref[head]
        total_den_ref[head] = den
        linear = (inter + num_ref[:, lanes]) / den
        linear_ref[:, lanes] = linear
        probs, window = window_tile(
            info, head, 0, queries_ref[0:TILE, lanes],
            window_rows(keys_ref, got1_ref, 0, head, 0), window_rows(values_ref, got1_ref, 1, head, 0),
        )
        probs_ref[head] = probs
        mixed_ref[0:TILE, lanes] = (linear[0:TILE] + window).astype(bf16)
        mixed_ref[TILE:, lanes] = (linear[TILE:] + window_ref[TILE:, lanes]).astype(bf16)
    other_ref[...] = mm(by_distance(mixed_ref, info, True), out_ref[...]).astype(bf16)


def mixed_own_kernel(info, mixed_ref, out_ref, own_ref):
    own_ref[...] = mm(by_distance(mixed_ref, info, False), out_ref[...]).astype(bf16)


def quarters_kernel(info, own_ref, got_ref, *out_refs):
    out_refs[4][...] = got_ref[0:16, 0:128]
    for d in (1, 2, 3, 0):
        rows = slice(d * OWN, (d + 1) * OWN)
        total = own_ref[rows, :].astype(f32) + got_ref[rows, :].astype(f32)
        out_refs[d][...] = total.astype(out_refs[d].dtype)
        out_refs[d].send()


def resid_kernel(
    info, mine_ref, x_ref, gain_ref, got1_ref, got2_ref, got3_ref, normed_ref, resid_ref, inv_ref
):
    resid = x_ref[...].astype(f32) + mine_ref[...]
    for ref in (got1_ref, got2_ref, got3_ref):
        resid = resid + ref[...].astype(f32)
    resid_ref[...] = resid
    inv = lax.rsqrt(jnp.mean(resid * resid, axis=-1, keepdims=True) + EPS)
    inv_ref[...] = inv
    normed_ref[...] = (resid * inv * gain_ref[...]).astype(bf16)


def grad_resid_kernel(
    info, mine_ref, resid_ref, inv_ref, top_ref, gain_ref, got1_ref, got2_ref, got3_ref,
    sent_ref, grad_ref, gains_ref,
):
    grad = mine_ref[...]
    for ref in (got1_ref, got2_ref, got3_ref):
        grad = grad + ref[...].astype(f32)
    resid = resid_ref[...]
    inv = inv_ref[...]
    grad_resid = top_ref[...].astype(f32) + norm_back(resid, inv, gain_ref[...], grad)
    sent_ref[...] = grad_resid.astype(bf16)
    sent_ref.send()
    grad_ref[...] = grad_resid
    gains_ref[0:1, :] = jnp.sum(grad * resid * inv, axis=0, keepdims=True)


def grad_x_kernel(
    info, mine_ref, x_ref, grad_resid_ref, gain_ref, resid_ref, out_ref, got1_ref, got2_ref, got3_ref,
    out1_ref, out2_ref, out3_ref, sent_ref,
):
    total = resid_ref[...] + out_ref[...]
    for ref in (out1_ref, out2_ref, out3_ref):
        total = total + ref[...].astype(f32)
    sent_ref[0:OWN, :] = total.astype(bf16)
    grad = mine_ref[...]
    for ref in (got1_ref, got2_ref, got3_ref):
        grad = grad + ref[...].astype(f32)
    x = x_ref[...].astype(f32)
    inv = lax.rsqrt(jnp.mean(x * x, axis=-1, keepdims=True) + EPS)
    sent_ref[OWN:, :] = (grad_resid_ref[...] + norm_back(x, inv, gain_ref[...], grad)).astype(bf16)


def norm_back(in_rows, inv_rms, gain, grad_normed):
    weighted = grad_normed * gain
    return inv_rms * weighted - in_rows * inv_rms**3 * jnp.mean(
        weighted * in_rows, axis=-1, keepdims=True
    )


def by_halves(block):
    def places(info, sources=None, buffer=None):
        if info is None:
            return 8
        return [
            (sources[0].at[info.rows(i % 4, other=i >= 4)], buffer.at[i * OWN : (i + 1) * OWN])
            for i in range(8)
        ]

    return Far(block, block.shape, places)


def grad_act_kernel(info, top_ref, down_ref, own_ref, other_ref):
    top = top_ref[...]
    half = ROWS // 2
    for first in range(0, down_ref.shape[0], 256):
        span = slice(first, min(first + 256, down_ref.shape[0]))
        grad = mm_nt(top, down_ref[span, :])
        own_ref[:, span] = grad[:half]
        other_ref[:, span] = grad[half:]


def ffn_rows(pieces, gate_ref, up_ref, grad_act_ref, normed_ref, act_ref, grad_gate_ref, grad_up_ref):
    normed = jnp.concatenate([piece[...] for piece in pieces], axis=0)
    normed_ref[...] = normed
    hidden = gate_ref.shape[0]
    for first in range(0, hidden, 256):
        span = slice(first, min(first + 256, hidden))
        gate = mm_nt(normed, gate_ref[span, :])
        up_value = mm_nt(normed, up_ref[span, :])
        sigmoid_gate = jax.nn.sigmoid(gate)
        silu_gate = gate * sigmoid_gate
        act_ref[:, span] = (silu_gate * up_value).astype(bf16)
        grad_act = grad_act_ref[:, span]
        grad_gate_ref[:, span] = (
            grad_act * up_value * sigmoid_gate * (1.0 + gate * (1.0 - sigmoid_gate))
        ).astype(bf16)
        grad_up_ref[:, span] = (grad_act * silu_gate).astype(bf16)


def ffn_own_kernel(info, p0, p3, p2, p1, gate_ref, up_ref, grad_act_ref, *out_refs):
    ffn_rows((p0, p3, p2, p1), gate_ref, up_ref, grad_act_ref, *out_refs)


def ffn_other_kernel(info, s0, s3, s2, s1, gate_ref, up_ref, grad_act_ref, back_ref, *out_refs):
    ffn_rows((s0, s3, s2, s1), gate_ref, up_ref, grad_act_ref, *out_refs)
    ffn_back_kernel(info, out_refs[2], out_refs[3], gate_ref, up_ref, back_ref)


def ffn_back_kernel(info, grad_gate_ref, grad_up_ref, gate_ref, up_ref, back_ref):
    grad_gate, grad_up = grad_gate_ref[...], grad_up_ref[...]
    for first in range(0, back_ref.shape[1], 512):
        span = slice(first, first + 512)
        part = mm(grad_gate, gate_ref[:, span]) + mm(grad_up, up_ref[:, span])
        back_ref[:, span] = part.astype(bf16)


def ffn_out_kernel(info, act_own_ref, act_other_ref, down_ref, other_ref, own_ref):
    for target, act_ref in ((other_ref, act_other_ref), (own_ref, act_own_ref)):
        act = act_ref[...]
        for first in range(0, target.shape[1], 512):
            span = slice(first, first + 512)
            target[:, span] = mm(act, down_ref[:, span]).astype(bf16)


def column_grads(pairs, out_ref):
    count = out_ref.shape[0] // 4
    for part in range(4):
        span = slice(part * count, (part + 1) * count)
        first = 0
        for rows_refs, grads in pairs:
            rows_refs = rows_refs if isinstance(rows_refs, tuple) else (rows_refs,)
            grads = grads if isinstance(grads, tuple) else (grads,)
            total = sum(mm_tn(rows[:, span], grad) for rows, grad in zip(rows_refs, grads))
            last = first + total.shape[1]
            out_ref[span, first:last] = total.astype(bf16)
            first = last
        if first < out_ref.shape[1]:
            out_ref[span, first:] = jnp.zeros((count, out_ref.shape[1] - first), bf16)
        out_ref.send(part)


def gate_grads_kernel(
    info, own_ref, other_ref, gate_own_ref, gate_other_ref, up_own_ref, up_other_ref, out_ref
):
    rows = (own_ref, other_ref)
    gate = (gate_own_ref[...], gate_other_ref[...])
    up = (up_own_ref[...], up_other_ref[...])
    column_grads(((rows, gate), (rows, up)), out_ref)


class Rows:

    def __init__(self, ref, first, count):
        self.ref, self.rows = ref, slice(first, first + count)

    def __getitem__(self, index):
        return self.ref[self.rows, index[1]]


def down_grads_kernel(info, top_ref, act_own_ref, act_other_ref, out_ref):
    half = ROWS // 2
    rows = (Rows(top_ref, 0, half), Rows(top_ref, half, half))
    column_grads(((rows, (act_own_ref[...], act_other_ref[...])),), out_ref)


def grad_x_out_kernel(info, p0, p1, p2, p3, s0, s1, s2, s3, output_ref, grad_ref):
    for i, piece in enumerate((p0, p1, p2, p3, s0, s1, s2, s3)):
        rows = info.rows(4 - i % 4, other=i >= 4)
        output_ref[rows, :] = piece[0:OWN, :]
        grad_ref[rows, :] = piece[OWN : 2 * OWN, :].astype(f32)


def window_tile_back(top, probs, key_rows, value_rows):
    grad_probs = mm_nt(top, value_rows)
    shared = jnp.sum(grad_probs * probs, axis=-1, keepdims=True)
    return (probs * (grad_probs - shared)).astype(bf16)


def mixed_back_kernel(
    info, p0, p1, p2, p3, s0, s1, s2, s3, out_ref, linear_ref, den_ref, qf_ref, probs0_ref, keys_ref,
    values_ref, halo_ref, queries_ref, packed_ref, wide_ref, top_ref, gm_ref, gnum_ref, gden_ref,
):
    for i, piece in enumerate((p0, p1, p2, p3, s0, s1, s2, s3)):
        top_ref[info.rows(4 - i % 4, other=i >= 4), :] = piece[...]
    grad_mixed = mm_nt(top_ref[...], out_ref[...]).astype(bf16)
    gm_ref[...] = grad_mixed
    use = prefix_mask(info)
    for head in range(HEADS):
        lanes = head_lanes(head)
        wide = grad_mixed[:, lanes].astype(f32)
        den = den_ref[head]
        grad_num = (wide / den).astype(bf16)
        gnum_ref[:, lanes] = grad_num
        grad_den = -jnp.sum(wide * linear_ref[:, lanes], axis=-1, keepdims=True) / den
        gden_ref[head] = grad_den
        features = qf_ref[head]
        used = (grad_num.astype(f32) * use).astype(bf16)
        state = mm_tn(features, used)
        norm = jnp.sum(features.astype(f32) * (grad_den * use), axis=0, keepdims=True)
        write_packed(packed_ref, head, state, norm)
        wide_ref[head, 0:PACKED, :] = packed_ref[head]
        top, probs = grad_mixed[0:TILE, lanes], probs0_ref[head]
        grad_logits = window_tile_back(
            top, probs, window_rows(keys_ref, halo_ref, 0, head, 0),
            window_rows(values_ref, halo_ref, 1, head, 0),
        )
        grad_keys = mm_tn(grad_logits, queries_ref[0:TILE, lanes]) * VALUE_WIDTH ** (-0.5)
        wide_ref[head, PACKED : PACKED + WIN, :] = grad_keys[0:WIN].astype(bf16)
        grad_values = mm_tn(probs.astype(bf16), top)
        wide_ref[head, PACKED + WIN :, :] = grad_values[0:WIN].astype(bf16)


def window_back_kernel(
    info, gm_ref, probs0_ref, probs_ref, keys_ref, values_ref, halo_ref, queries_ref,
    top_ref, mixed_ref, gq_ref, gk_ref, gv_ref, out_ref, key_acc, value_acc,
):
    column_grads(((top_ref, mixed_ref[...]),), out_ref)
    scale = VALUE_WIDTH ** (-0.5)
    key_acc[...] = jnp.zeros_like(key_acc)
    value_acc[...] = jnp.zeros_like(value_acc)
    for tile in range(ROWS // TILE):
        first = tile * TILE
        reach = slice(first, first + TILE + WIN)
        for head in range(HEADS):
            lanes = head_lanes(head)
            key_rows = window_rows(keys_ref, halo_ref, 0, head, tile)
            value_rows = window_rows(values_ref, halo_ref, 1, head, tile)
            top = gm_ref[first : first + TILE, lanes]
            probs = probs0_ref[head] if tile == 0 else probs_ref[head, tile - 1]
            grad_logits = window_tile_back(top, probs, key_rows, value_rows)
            gq_ref[first : first + TILE, lanes] = (mm(grad_logits, key_rows) * scale).astype(bf16)
            queries = queries_ref[first : first + TILE, lanes]
            key_acc[reach, lanes] += mm_tn(grad_logits, queries) * scale
            value_acc[reach, lanes] += mm_tn(probs.astype(bf16), top)
    gk_ref[...] = key_acc[WIN:, :]
    gv_ref[...] = value_acc[WIN:, :]


def linear_back_kernel(
    info, gnum_ref, gden_ref, values_ref, low_ref, km_ref, qf_ref, state_ref, norm_ref, raw_ref,
    choose_ref, lanes_ref, window_gv_ref, normed_ref, gq_ref, gfeat_ref, gv_ref, gkf_ref, out_ref,
):
    column_grads(((normed_ref, gq_ref[...]),), out_ref)
    use = prefix_mask(info)
    half = ROWS // 2
    grads = [[None, None], [None, None]]
    for head in range(HEADS):
        lanes = head_lanes(head)
        inter = mm_nt((gnum_ref[:, lanes].astype(f32) * use).astype(bf16), state_ref[head])
        inter = inter + (gden_ref[head] * use) * norm_ref[head, 0:1, :]
        for block in range(2):
            first, reach = block * half, (block + 1) * half
            query_at = column_positions(info, first, half)
            key_at = row_positions(info, 0, reach)
            causal = (query_at >= key_at) & (doc_of(info, query_at) == doc_of(info, key_at))
            grad_num = gnum_ref[first:reach, lanes]
            grad = mm_nt(grad_num, values_ref[:reach, lanes]) + gden_ref[head, first:reach, :]
            grad = jnp.where(causal, grad, 0.0).astype(bf16)
            grads[head][block] = mm(grad, km_ref[head, :reach, :]) + inter[first:reach]
            key_part = mm_tn(grad, qf_ref[head, first:reach, :])
            value_part = mm_tn(low_ref[head, first:reach, 0:reach], grad_num)
            if block == 0:
                gkf_ref[head, 0:half] = key_part
                gv_ref[0:half, lanes] = window_gv_ref[0:half, lanes] + value_part
            else:
                gkf_ref[head, 0:half] += key_part[0:half]
                gkf_ref[head, half:] = key_part[half:]
                gv_ref[0:half, lanes] += value_part[0:half]
                gv_ref[half:, lanes] = window_gv_ref[half:, lanes] + value_part[half:]
    left, right = factors(raw_ref[...], 0, choose_ref, lanes_ref)
    gradient = jnp.concatenate([jnp.concatenate(g, axis=0) for g in grads], axis=1)
    gradient = gradient * lanes_ref[2:3, :]
    gfeat_ref[...] = feature_back(gradient, left, right, choose_ref)


def keys_back_kernel(
    info, before_ref, got1_ref, got2_ref, got3_ref, values_ref, km_ref, gkf_ref, gk_ref, gv_ref,
    raw_ref, choose_ref, lanes_ref, gfeat_ref, normed_ref,
    gkw_ref, gvw_ref, gf_ref, out_ref,
):
    tail = tail_mask(info)
    inner = ROWS - WIN
    gkw_ref[0:inner, :] = gk_ref[0:inner, :].astype(bf16)
    gradients = []
    for head in range(HEADS):
        lanes = head_lanes(head)
        later, norm = read_total(before_ref, (got1_ref, got2_ref, got3_ref), head)
        kept = (values_ref[:, lanes].astype(f32) * tail).astype(bf16)
        gradients.append(gkf_ref[head] + mm_nt(kept, later) + tail * norm)
        grad_values = gv_ref[:, lanes] + mm(km_ref[head], later) * tail
        gvw_ref[0:inner, lanes] = grad_values[0:inner].astype(bf16)
        right = got1_ref[head, PACKED:, :].astype(f32)
        gkw_ref[inner:, lanes] = (gk_ref[inner:, lanes] + right[0:WIN]).astype(bf16)
        gvw_ref[inner:, lanes] = (grad_values[inner:] + right[WIN:]).astype(bf16)
    left, right = factors(raw_ref[...], 1, choose_ref, lanes_ref)
    gradient = jnp.concatenate(gradients, axis=1) * lanes_ref[4:5, :]
    gf_ref[...] = (feature_back(gradient, left, right, choose_ref) + gfeat_ref[...]).astype(bf16)
    column_grads(
        (
            (normed_ref, gkw_ref[...]), (normed_ref, gvw_ref[...]), (normed_ref, gf_ref[...]),
        ),
        out_ref,
    )


def normed_back_kernel(
    info, gq_ref, gkw_ref, gvw_ref, gf_ref, wq_ref, wk_ref, wv_ref, wf_ref, x_ref, inv_ref, gain_ffn_ref,
    other_ref, own_ref, gains_ref,
):
    wf_ref.ready()
    wf_ref.ref[64:128, :] = jnp.zeros((64, wf_ref.shape[1]), bf16)
    for target, other in ((other_ref, True), (own_ref, False)):
        grads = [by_distance(ref, info, other) for ref in (gq_ref, gkw_ref, gvw_ref, gf_ref)]
        scaled_by = by_distance(inv_ref, info, other)
        for piece in range(4):
            span = slice(piece * 512, (piece + 1) * 512)
            part = mm_nt(grads[0], wq_ref[span, :])
            part = part + mm_nt(grads[1], wk_ref[span, :])
            part = part + mm_nt(grads[2], wv_ref[span, :])
            part = part + mm(grads[3], wf_ref[:, span])
            target[:, span] = part.astype(bf16)
            x_rows = jnp.concatenate([x_ref[info.rows(d, other), span] for d in range(4)], axis=0)
            total = jnp.sum(part * (x_rows.astype(f32) * scaled_by), axis=0, keepdims=True)
            gains_ref[0:1, span] = total if other else total + gains_ref[0:1, span]
    gains_ref[1:2, :] = gain_ffn_ref[0:1, :]


def grads_out_kernel(
    info, in_ref, gate_ref, up_ref, down_ref, out_ref, grad_q_ref, grad_k_ref, grad_v_ref,
    feat_query_ref, feat_key_ref,
):
    hidden, width = gate_ref.shape[0], out_ref.shape[0]
    padded = -(-hidden // 128) * 128
    both = in_ref[:, 0 : 2 * hidden].astype(f32).T
    gate_ref[...] = both[0:hidden]
    gate_ref.send()
    up_ref[...] = both[hidden:]
    up_ref.send()
    at = 2 * hidden
    down_ref[...] = in_ref[:, at : at + padded].astype(f32).T[0:hidden]
    down_ref.send()
    at += padded
    out_ref[...] = in_ref[:, at : at + width].astype(f32).T
    out_ref.send()
    for ref in (grad_q_ref, grad_k_ref, grad_v_ref):
        at += width
        ref[...] = in_ref[:, at : at + width].astype(f32)
        ref.send()
    feat = in_ref[:, at + width :].astype(f32).T
    feat_query_ref[...] = feat[0:32]
    feat_key_ref[...] = feat[32:64]


def total_of(refs):
    total = refs[0][...]
    for ref in refs[1:]:
        total = total + ref[...]
    return total


def gains_kernel(info, *refs):
    refs[-1][...] = total_of(refs[:-1])


def spread_kernel(info, *refs):
    total, out_ref = total_of(refs[:-1]), refs[-1]
    for i in range(out_ref.shape[0]):
        out_ref[i, 0:2, :] = total[:, i * 128 : (i + 1) * 128]
        out_ref[i, 2:, :] = jnp.zeros((6, 128), f32)


def gathered_sum_kernel(info, in_ref, out_ref):
    total = in_ref[0]
    for i in range(1, in_ref.shape[0]):
        total = total + in_ref[i]
    out_ref[...] = total


def along_y(distance):
    return [(i, (i + 2 * distance) % 8) for i in range(8)]


def sibling():
    return [(i, i ^ 1) for i in range(8)]


def along_x(distance):
    return [(i, (i + 4 * distance) % 16) for i in range(16)]


def along_z(distance):
    return [(4 * a + z, 4 * a + (z + distance) % 4) for a in range(4) for z in range(4)]


def head_quarters(own, other, after=()):
    got = moved_by(other, "head", sibling())
    width = own.dims[1]
    with jax.named_scope("quarters"):
        mine, *sent, token = call(
            quarters_kernel,
            [near(OWN, width, dtype=f32)] + [near(OWN, width)] * 3 + [near(16, 128)],
            (own, got), after=after,
        )
    parts = [moved_by(sent[d - 1], "head", along_y(d)) for d in (2, 1, 3)]
    return mine, parts, moved_by(token, "head", sibling())


def head_pieces(own):
    far_piece = moved_by(own, "head", along_y(2))
    pieces = [own, moved_by(own, "head", along_y(1)), far_piece, moved_by(own, "head", along_y(3))]
    return pieces + [moved_by(piece, "head", sibling()) for piece in pieces]


def gains_sum(gains):
    with jax.named_scope("gains"):
        (pair,) = call(
            gains_kernel, [near(*gains.dims, dtype=f32)], (gains, moved_by(gains, "head", sibling()))
        )
        parts = [pair] + [moved_by(pair, "head", along_y(d)) for d in (2, 1, 3)]
        (blocks,) = call(spread_kernel, [far(16, 8, 128, dtype=f32)], parts)
        blocks = lax.all_to_all(blocks, "seq", 0, 0)
        (total,) = call(gathered_sum_kernel, [far(8, 128, dtype=f32)], (blocks,))
    return total


def scan_kernel(reverse, info, own_ref, got1_ref, got2_ref, got3_ref, before_ref, *sent_refs):
    place_x, place_z = (3 - info.x, 3 - info.z) if reverse else (info.x, info.z)
    before = jnp.zeros(before_ref.shape, f32)
    for d, ref in enumerate((got1_ref, got2_ref, got3_ref), 1):
        before = before + ref[:, 0:PACKED, :].astype(f32) * (place_x >= d).astype(f32)
    before_ref[...] = before
    row = lax.broadcasted_iota(jnp.int32, (HEADS, 16, 128), 1)
    sent = []
    for total in (before, before + own_ref[:, 0:PACKED, :].astype(f32)):
        norm = total[:, KEPT:]
        norm = norm + jnp.roll(norm, -2, axis=1)
        high = norm.astype(bf16).astype(f32)
        rest = jnp.roll(norm - high, 2, axis=1)
        norm = jnp.where(row < 2, high, jnp.where(row < 4, rest, 0.0))
        sent.append((total[:, :KEPT], norm))
    for d, ref in enumerate(sent_refs, 1):
        with_own = (place_z + d < 4).astype(f32)
        for part, rows in ((0, slice(0, KEPT)), (1, slice(KEPT, PACKED))):
            less, more = sent[0][part], sent[1][part]
            ref[:, rows, :] = (more * with_own + less * (1.0 - with_own)).astype(bf16)
        if ref.shape[1] > PACKED:
            own, earlier = own_ref[:, PACKED:, :].astype(f32), got1_ref[:, PACKED:, :].astype(f32)
            ref[:, PACKED:, :] = (own * with_own + earlier * (1.0 - with_own)).astype(bf16)


def exclusive_parts(own, reverse, after=(), wide=None):
    sign = -1 if reverse else 1
    first = own if wide is None else wide
    got = [moved_by(first if d == 1 else own, "seq", along_x(sign * d)) for d in (1, 2, 3)]
    with jax.named_scope("scan"):
        before, *sent = call(
            functools.partial(scan_kernel, reverse),
            [near(*own.dims, dtype=f32), near(*first.dims), near(*own.dims), near(*own.dims)],
            (first, *got), after=after,
        )
    return [before] + [
        moved_by(sent[d - 1], "seq", along_z(sign * d)) for d in (1, 2, 3)
    ]


def shards(
    inputs,
    gain_mix,
    feat_query,
    feat_key,
    win_query,
    win_key,
    value_proj,
    out_proj,
    gain_ffn,
    gate_proj,
    up_proj,
    down_proj,
    document_starts,
    cotangent,
):
    choose, lanes = feature_tables()
    choose = jnp.asarray(choose, bf16)
    lanes = jnp.asarray(lanes, f32)
    choose_q, choose_k = choose[0], choose[1]
    feat = feature_weights(feat_query.T, feat_key.T)
    gain_mix = gain_mix.reshape(1, -1)
    gain_ffn = gain_ffn.reshape(1, -1)
    model = inputs.shape[1]
    width = HEADS * VALUE_WIDTH
    hidden = gate_proj.shape[1]
    half = ROWS // 2
    unit = 2 * ROWS * model
    starts = document_starts

    normed, inv_mix, raw, keys, values, km, packed, wide = call(
        keys_kernel,
        (
            near(ROWS, model), near(ROWS, 1, dtype=f32), near(ROWS, 128, dtype=f32),
            near(ROWS, width), near(ROWS, width), near(HEADS, ROWS, LANES),
            near(HEADS, PACKED, 128), near(HEADS, PACKED + EDGE, 128),
        ),
        (Far(inputs, parts=4), gain_mix, win_key, value_proj, feat, choose_k, lanes),
        starts=starts, flops=unit * 640,
    )
    qf, low, num, den, near_query, near_out, normed_far, inv_mix, raw_far, keys_far, values_far, km_far = call(
        local_kernel,
        (
            near(HEADS, ROWS, LANES), near(HEADS, ROWS, ROWS), near(ROWS, width, dtype=f32),
            near(HEADS, ROWS, 1, dtype=f32), Stage(win_query), Stage(out_proj), Export(normed),
            Export(inv_mix), Export(raw), Export(keys), Export(values), Export(km),
        ),
        (raw, choose_q, lanes, values, km),
        starts=starts, flops=unit * 300,
    )
    sums = exclusive_parts(packed, False, after=(qf,), wide=wide)
    queries, probs, window, qf_far, low = call(
        window_kernel,
        (
            near(ROWS, width), near(HEADS, 3, TILE, TILE + WIN, dtype=f32),
            near(ROWS, width, dtype=f32), Export(qf), Export(low),
        ),
        (normed, near_query, keys, values),
        starts=starts, flops=unit * 400,
    )
    mixed, linear, total_den, state, norm, probs_first, other = call(
        mixed_kernel,
        (
            near(ROWS, width), near(ROWS, width, dtype=f32), near(HEADS, ROWS, 1, dtype=f32),
            near(HEADS, LANES, VALUE_WIDTH), near(HEADS, 8, LANES, dtype=f32),
            near(HEADS, TILE, TILE + WIN, dtype=f32), near(half, model),
        ),
        (*sums, qf, num, den, window, near_out, queries, keys, values),
        starts=starts, flops=unit * 300,
    )
    own, halo, *rest = call(
        mixed_own_kernel,
        (
            near(half, model),
            Export(sums[1], (HEADS, EDGE, 128), lambda ref: ref.at[:, PACKED:, :]),
            *map(Export, (mixed, linear, total_den, state, norm, probs_first, probs, queries)),
        ),
        (mixed, near_out), after=(other,), flops=unit * 100,
    )
    mixed, linear, total_den, state, norm, probs_first, probs, queries_far = rest
    mine, parts, signal = head_quarters(own, other)
    grad_act_own, grad_act_other, x_own, near_gain, near_gate, near_up = call(
        grad_act_kernel,
        (
            near(half, hidden, dtype=f32), near(half, hidden, dtype=f32), Stage(own_part(inputs)), Stage(gain_ffn),
            Stage(gate_proj.T), Stage(up_proj.T),
        ),
        (by_halves(cotangent), down_proj),
        after=(signal,), flops=unit * hidden,
    )
    own_normed, resid, inv_ffn = call(
        resid_kernel,
        (near(OWN, model), near(OWN, model, dtype=f32), near(OWN, 1, dtype=f32)),
        (mine, x_own, near_gain, *parts), after=(grad_act_own,),
    )
    pieces = head_pieces(own_normed)
    def ffn_half(body, pieces, grad_act, *more, after=()):
        order = [pieces[i] for i in (0, 3, 2, 1)]
        return call(
            body,
            (
                *more, near(half, model), near(half, hidden), near(half, hidden), near(half, hidden),
            ),
            (*order, near_gate, near_up, grad_act), after=after, flops=unit * 2 * hidden,
        )

    normed_own, act_own, gate_own, up_own = ffn_half(ffn_own_kernel, pieces[:4], grad_act_own)
    other, normed_other, act_other, gate_other, up_other = ffn_half(
        ffn_other_kernel, pieces[4:], grad_act_other, near(half, model), after=(gate_own,)
    )
    (own,) = call(
        ffn_back_kernel, (near(half, model),), (gate_own, up_own, near_gate, near_up),
        after=(other,), flops=unit * hidden,
    )
    mine, parts, signal = head_quarters(own, other)
    padded = -(-hidden // 128) * 128
    place = dict(parts=4, width=2 * hidden + padded + 4 * width + 128)
    grads, resid_far, near_top, near_gain, *near_mixed = call(
        gate_grads_kernel,
        (
            far(model, 2 * hidden, **place), Export(resid), Stage(own_part(cotangent)),
            Stage(gain_ffn), Stage(out_proj), Stage(linear), Stage(total_den), Stage(qf_far),
        ),
        (normed_own, normed_other, gate_own, gate_other, up_own, up_other),
        after=(signal,), flops=unit * 2 * hidden,
    )
    at = 2 * hidden
    grads, *near_back = call(
        down_grads_kernel,
        (
            far(model, padded, first=at, onto=grads, **place), Stage(probs_first), Stage(probs),
            Stage(keys_far), Stage(values_far), Stage(halo), Stage(queries_far), Stage(low),
            Stage(km_far),
            Stage(state), Stage(norm), Stage(raw_far), Stage(choose_q), Stage(choose_k),
            Stage(lanes), Stage(mixed), Export(act_own), Export(act_other),
        ),
        (by_halves(cotangent), act_own, act_other), after=(signal,), flops=unit * hidden,
    )
    probs_first, probs, keys, values, halo, queries, low, km, state, norm, raw, *rest = near_back
    choose_q, choose_k, lanes, mixed, act_own, act_other = rest
    at += padded
    sent, grad_resid, gain_ffn_part = call(
        grad_resid_kernel,
        (near(OWN, model), near(OWN, model, dtype=f32), near(8, model, dtype=f32)),
        (mine, resid, inv_ffn, near_top, near_gain, *parts), after=(grads,),
    )
    pieces = head_pieces(sent)
    packed, wide, top, grad_mixed, grad_num, grad_den = call(
        mixed_back_kernel,
        (
            near(HEADS, PACKED, 128), near(HEADS, PACKED + EDGE, 128), near(ROWS, model), near(ROWS, width), near(ROWS, width),
            near(HEADS, ROWS, 1, dtype=f32),
        ),
        (*pieces, *near_mixed, probs_first, keys, values, halo, queries),
        starts=starts, flops=unit * 300,
    )
    gq, gk, gv, grads, normed = call(
        window_back_kernel,
        (
            near(ROWS, width), near(ROWS, width, dtype=f32),
            near(ROWS, width, dtype=f32), far(model, width, first=at, onto=grads, **place),
            Stage(normed_far),
        ),
        (grad_mixed, probs_first, probs, keys, values, halo, queries, top, mixed),
        flops=unit * 300, scratch=[pltpu.VMEM((ROWS + WIN, width), f32)] * 2,
    )
    sums = exclusive_parts(packed, True, after=(gq,), wide=wide)
    gfeat, gv, gkf, grads = call(
        linear_back_kernel,
        (
            near(ROWS, 128, dtype=f32), near(ROWS, width, dtype=f32),
            near(HEADS, ROWS, LANES, dtype=f32),
            far(model, width, first=at + width, onto=grads, **place),
        ),
        (
            grad_num, grad_den, values, low, km, near_mixed[3], state, norm, raw, choose_q, lanes, gv,
            normed, gq,
        ),
        starts=starts, after=(sums[0],), flops=unit * 300,
    )
    gkw, gvw, gf, grads = call(
        keys_back_kernel,
        (
            near(ROWS, width), near(ROWS, width), near(ROWS, 128),
            far(model, 2 * width + 128, first=at + 2 * width, onto=grads, **place),
        ),
        (
            *sums, values, km, gkf, gk, gv, raw, choose_k, lanes, gfeat, normed,
        ),
        starts=starts, flops=unit * 1400,
    )
    grads_sum = lax.psum_scatter(grads, "seq", scatter_dimension=0, tiled=True)
    other, own, gains = call(
        normed_back_kernel, (near(half, model), near(half, model), near(2, model, dtype=f32)),
        (
            gq, gkw, gvw, gf, win_query, win_key, value_proj, feat, inputs, inv_mix, gain_ffn_part,
        ),
        after=(grads,),
        flops=unit * 900,
    )
    mine, parts, signal = head_quarters(own, other)
    other, own = call(
        ffn_out_kernel, (near(half, model), near(half, model)), (act_own, act_other, down_proj),
        after=(signal,), flops=unit * hidden,
    )
    out_mine, out_parts, signal = head_quarters(own, other)
    gains = gains_sum(gains)
    (sent,) = call(
        grad_x_kernel, (near(2 * OWN, model),),
        (mine, own_part(inputs), grad_resid, gain_mix, resid_far, out_mine, *parts, *out_parts),
        after=(gains,),
    )
    pieces = head_pieces(sent)
    output, grad_x = call(
        grad_x_out_kernel, (far(ROWS, model), far(ROWS, model, dtype=f32)), pieces,
    )
    grad_gate_t, grad_up_t, grad_down, grad_out, *rest = call(
        grads_out_kernel,
        (far(hidden, 128, dtype=f32),) * 3 + (far(width, 128, dtype=f32),)
        + (far(128, width, dtype=f32),) * 3 + (far(32, 128, dtype=f32),) * 2,
        (grads_sum,), after=(grad_x,),
    )
    grad_wq, grad_wk, grad_wv, grad_fq_t, grad_fk_t = rest
    return (
        output,
        grad_x,
        gains[0],
        grad_fq_t.T,
        grad_fk_t.T,
        grad_wq,
        grad_wk,
        grad_wv,
        grad_out,
        gains[1],
        grad_gate_t.T,
        grad_up_t.T,
        grad_down,
    )


def solution(mesh):
    placed = (
        P("seq", None),
        P(),
        P(None, "head"),
        P(None, "head"),
        P(None, "head"),
        P(None, "head"),
        P(None, "head"),
        P("head", None),
        P(),
        P(None, "head"),
        P(None, "head"),
        P("head", None),
        P(),
        P("seq", None),
    )
    return jax.shard_map(
        shards,
        mesh=mesh,
        in_specs=placed,
        out_specs=(
            P("seq", None),
            P("seq", None),
            P("seq"),
            P("seq", "head"),
            P("seq", "head"),
            P("seq", "head"),
            P("seq", "head"),
            P("seq", "head"),
            P("head", "seq"),
            P("seq"),
            P("seq", "head"),
            P("seq", "head"),
            P("head", "seq"),
        ),
        check_vma=False,
    )
```

```python
import functools
import math

import jax
import jax.numpy as jnp
import numpy as np
from jax import lax
from jax.experimental import pallas as pl
from jax.experimental.pallas import tpu as pltpu
from jax.sharding import PartitionSpec as P

F = 16
VALUE_WIDTH = 128
WIN = 64
EPS = 1e-05

HEADS = 2
ROWS = 512
LANES = 256
KEPT = 160
PACKED = 176
TILE = 128
EDGE = 2 * WIN
OWN = 64
f32 = jnp.float32
bf16 = jnp.bfloat16


def feature_tables():
    pairs = [(a, b) for a in range(F) for b in range(a, F)]
    count = len(pairs)
    choose = np.zeros((2, 2, 128, HEADS * LANES), np.float32)
    lanes = np.zeros((8, HEADS * LANES), np.float32)
    factor = F ** (-0.25)
    for head in range(HEADS):
        at = head * LANES
        for side in range(2):
            for first in (side * HEADS * F, 64, 96):
                row = first + head * F
                for lane, (a, b) in enumerate(pairs):
                    choose[side, 0, row + a, at + lane] = 1.0
                    choose[side, 1, row + b, at + lane] = 1.0
                for a in range(F):
                    choose[side, 0, row + a, at + count + a] = 1.0
        for lane, (a, b) in enumerate(pairs):
            lanes[2, at + lane] = factor * factor / math.sqrt(2.0)
            lanes[3, at + lane] = 1.0 if a == b else 2.0
        lanes[1, at + count : at + count + F + 1] = 1.0
        lanes[0, at + count + F] = 1.0
        lanes[2, at + count : at + count + F] = factor
        lanes[2, at + count + F] = 1.0
        lanes[3, at + count : at + count + F + 1] = 1.0
    lanes[4] = lanes[2] * lanes[3]
    return choose, lanes


def mm(a, b):
    return lax.dot_general(a, b, (((1,), (0,)), ((), ())), preferred_element_type=f32)


def mm_nt(a, b):
    return lax.dot_general(a, b, (((1,), (1,)), ((), ())), preferred_element_type=f32)


def mm_tn(a, b):
    return lax.dot_general(a, b, (((0,), (0,)), ((), ())), preferred_element_type=f32)


def low_pair(part):
    high = part.astype(bf16)
    return high, (part - high.astype(f32)).astype(bf16)


class Place:

    def __init__(self, starts):
        me, seq = lax.axis_index("head"), lax.axis_index("seq")
        self.base = seq * ROWS
        self.x, self.z = lax.shift_right_logical(seq, 2), lax.bitwise_and(seq, 3)
        self.y, self.core = lax.shift_right_logical(me, 1), lax.bitwise_and(me, 1)
        self.loaded = starts

    def starts(self):
        return [self.loaded[0, i] for i in range(4)]

    def rows(self, distance, other=False):
        quarter = lax.bitwise_and(self.y + distance, 3)
        core = 1 - self.core if other else self.core
        return pl.ds(pl.multiple_of(quarter * (2 * OWN) + core * OWN, OWN), OWN)


class Loaded:

    def __init__(self, ref, copies):
        self.ref, self.copies = ref, list(copies)
        self.shape = ref.shape

    def part(self, index):
        if self.copies and self.copies[index] is not None:
            self.copies[index].wait()
            self.copies[index] = None

    def ready(self):
        for index in range(len(self.copies)):
            self.part(index)

    def __getitem__(self, index):
        self.ready()
        return self.ref[index]


class Stored:

    def __init__(self, ref, copies):
        self.ref, self.copies, self.sent = ref, copies, set()
        self.shape, self.dtype = ref.shape, ref.dtype

    def __getitem__(self, index):
        return self.ref[index]

    def __setitem__(self, index, value):
        self.ref[index] = value

    def send(self, part=None):
        for index in range(len(self.copies)) if part is None else (part,):
            if index not in self.sent:
                self.copies[index].start()
                self.sent.add(index)


def doc_of(info, position):
    starts = info.starts()
    count = (position >= starts[0]).astype(jnp.int32)
    for start in starts[1:]:
        count = count + (position >= start).astype(jnp.int32)
    return count


def column_positions(info, first, count):
    return info.base + first + lax.broadcasted_iota(jnp.int32, (count, 1), 0)


def row_positions(info, first, count):
    return info.base + first + lax.broadcasted_iota(jnp.int32, (1, count), 1)


def prefix_mask(info):
    before = doc_of(info, info.base - 1)
    same = doc_of(info, column_positions(info, 0, ROWS)) == before
    return (same & (info.base > 0)).astype(f32)


def tail_mask(info):
    last = doc_of(info, info.base + ROWS - 1)
    return (doc_of(info, column_positions(info, 0, ROWS)) == last).astype(f32)


def factors(raw, side, choose_ref, lanes_ref):
    high, rest = low_pair(raw)
    high, rest = high.astype(f32), rest.astype(f32)
    left = raw - high - rest
    at = side * HEADS * F
    lane = lax.broadcasted_iota(jnp.int32, (1, 128), 1)
    parts = jnp.where(lane < 96, pltpu.roll(rest, 64 - at, 1), pltpu.roll(left, 96 - at, 1))
    parts = jnp.where(lane < 64, high, parts).astype(bf16)
    return [mm(parts, choose_ref[i]) + lanes_ref[i : i + 1, :] for i in range(2)]


def feature_back(gradient, left, right, choose_ref):
    first = mm_nt((gradient * right).astype(bf16), choose_ref[0])
    return first + mm_nt((gradient * left).astype(bf16), choose_ref[1])


def write_packed(packed_ref, head, state, norm):
    packed_ref[head, 0:KEPT, :] = state[:KEPT].astype(bf16)
    row = lax.broadcasted_iota(jnp.int32, (16, 128), 0)
    high = norm.astype(bf16).astype(f32)
    rest = norm - high
    tile = jnp.where(row == 0, high[:, :128], 0.0)
    tile = jnp.where(row == 1, high[:, 128:], tile)
    tile = jnp.where(row == 2, rest[:, :128], tile)
    tile = jnp.where(row == 3, rest[:, 128:], tile)
    packed_ref[head, KEPT:PACKED, :] = tile.astype(bf16)


def read_total(before_ref, got_refs, head):
    total = before_ref[head]
    for ref in got_refs:
        total = total + ref[head, 0:PACKED, :].astype(f32)
    state = jnp.concatenate(
        [total[:KEPT], jnp.zeros((LANES - KEPT, VALUE_WIDTH), f32)], axis=0
    ).astype(bf16)
    norm = jnp.concatenate(
        [
            total[KEPT : KEPT + 1] + total[KEPT + 2 : KEPT + 3],
            total[KEPT + 1 : KEPT + 2] + total[KEPT + 3 : KEPT + 4],
        ],
        axis=1,
    )
    return state, norm


def head_lanes(head):
    return slice(head * VALUE_WIDTH, (head + 1) * VALUE_WIDTH)


def window_rows(own_ref, halo_ref, which, head, tile):
    first, lanes = tile * TILE, head_lanes(head)
    if tile == 0:
        after = halo_ref.shape[1] - EDGE + which * WIN
        halo = halo_ref[head, after : after + WIN, :]
        return jnp.concatenate([halo, own_ref[0:TILE, lanes]], axis=0)
    return own_ref[first - WIN : first + TILE, lanes]


def window_tile(info, head, tile, queries, key_rows, value_rows):
    first = tile * TILE
    query_at = column_positions(info, first, TILE)
    key_at = row_positions(info, first - WIN, TILE + WIN)
    near_by = (
        (key_at <= query_at)
        & (query_at - key_at < WIN)
        & (doc_of(info, query_at) == doc_of(info, key_at))
        & (key_at >= 0)
    )
    logits = mm_nt(queries, key_rows) * VALUE_WIDTH ** (-0.5)
    logits = jnp.where(near_by, logits, -1e30)
    exps = jnp.exp(logits - jnp.max(logits, axis=-1, keepdims=True))
    probs = exps / jnp.sum(exps, axis=-1, keepdims=True)
    return probs, mm(probs.astype(bf16), value_rows)


class Near:
    near = True

    def __init__(self, arrays, dims=None, places=None, parts=1):
        self.arrays = [
            a.arrays[0] if isinstance(a, Near) else a
            for a in (arrays if isinstance(arrays, (list, tuple)) else [arrays])
        ]
        self.dims = tuple(dims or self.arrays[0].shape)
        self.dtype = self.arrays[0].dtype
        self.places, self.parts = places, parts

    def copies(self, info, refs, buffer):
        if self.places is None:
            return pieces_of(refs[0], buffer, self.parts)
        return self.places(info, refs, buffer)

    def count(self):
        return self.parts if self.places is None else self.places(None)

    def copied(self):
        return self.places is not None


class Far(Near):
    near = False

    def copied(self):
        return True


class Out:

    def __init__(self, *dims, dtype=bf16, near=False, far=False, parts=1, width=None, first=0, onto=None):
        self.dims, self.dtype, self.parts = dims, dtype, parts
        self.near, self.far = near, far
        self.whole = dims if width is None else (dims[0], width)
        self.first, self.onto = first, onto

    def shapes(self):
        near = [jax.ShapeDtypeStruct(self.dims, self.dtype)] * self.near
        return near + [pltpu.HBM(self.whole, self.dtype)] * self.far

    def spaces(self):
        return [pltpu.VMEM] * self.near + [pltpu.HBM] * self.far

    def copies(self, buffer, target):
        if self.whole != self.dims:
            target = target.at[:, self.first : self.first + self.dims[1]]
        return pieces_of(buffer, target, self.parts)


class Stage:
    near, far, parts, onto = True, False, 1, None

    def __init__(self, source):
        self.source = source if isinstance(source, Far) else Far(source)
        self.dims, self.dtype = self.source.dims, self.source.dtype

    def shapes(self):
        return [jax.ShapeDtypeStruct(self.dims, self.dtype)]

    def spaces(self):
        return [pltpu.VMEM]


class Export:
    near, far, parts, onto = False, True, 1, None

    def __init__(self, source, dims=None, view=None):
        self.source, self.view = source, view
        self.dims, self.dtype = tuple(dims or source.dims), source.dtype

    def shapes(self):
        return [pltpu.HBM(self.dims, self.dtype)]

    def spaces(self):
        return [pltpu.HBM]

    def copies(self, ref, target):
        return [(ref if self.view is None else self.view(ref), target)]


def near(*dims, dtype=bf16):
    return Out(*dims, dtype=dtype, near=True)


def far(*dims, dtype=bf16, parts=1, **columns):
    return Out(*dims, dtype=dtype, far=True, parts=parts, **columns)


def both(*dims, dtype=bf16):
    return Out(*dims, dtype=dtype, near=True, far=True)


def pieces_of(source, target, parts):
    if parts == 1:
        return [(source, target)]
    count = source.shape[0] // parts
    return [
        (source.at[i * count : (i + 1) * count], target.at[i * count : (i + 1) * count])
        for i in range(parts)
    ]


def in_hbm(array):
    return pltpu.with_memory_space_constraint(array, pltpu.HBM)


def call(body, results, operands, starts=None, after=(), flops=0, scratch=(), megabytes=28):
    operands = [o if isinstance(o, Near) else Far(o) for o in operands]
    waits = [pl.ANY if isinstance(o, Near) else pltpu.HBM for o in after]
    after = [o.arrays[0] if isinstance(o, Near) else in_hbm(o) for o in after]
    staged = [o for o in results if isinstance(o, Stage)]
    inputs = operands + [o.source for o in results if isinstance(o, (Stage, Export))]
    arrays = [a for o in inputs for a in o.arrays]
    copied = [o for o in operands if o.copied()]
    held = [o for o in results if not o.near and not isinstance(o, Export)]
    count_out = sum(o.near + o.far for o in results)
    onto = {o: i for i, o in enumerate(results) if o.onto is not None}
    aliases = {len(arrays) + len(after) + i: onto[o] for i, o in enumerate(onto)}
    waits += [pltpu.HBM] * len(onto)
    after += [in_hbm(o.onto) for o in onto]
    moves = sum(o.count() for o in copied) + sum(o.source.count() for o in staged) + sum(o.parts for o in results if o.far)
    named = starts is not None

    def kernel(*refs):
        sources, refs = refs[: len(arrays)], refs[len(arrays) + len(after) :]
        named_ref, refs = (refs[0], refs[1:]) if named else (None, refs)
        targets, rest = list(refs[:count_out]), refs[count_out:]
        buffers, rest = list(rest[: len(copied)]), rest[len(copied) :]
        leaving, rest = list(rest[: len(held)]), rest[len(held) :]
        sems, rest = rest[0], rest[1:]
        marks = None
        if named:
            copy = pltpu.make_async_copy(named_ref, rest[0], sems.at[moves])
            copy.start()
            marks, rest = Loaded(rest[0], [copy]), rest[1:]
        info = Place(marks)
        loaded, at, sem = [], 0, 0

        def copies_of(pairs):
            nonlocal sem
            sem += len(pairs)
            return [
                pltpu.make_async_copy(source, target, sems.at[sem - len(pairs) + i])
                for i, (source, target) in enumerate(pairs)
            ]

        for operand in operands:
            own = sources[at : at + len(operand.arrays)]
            at += len(own)
            if not operand.copied():
                loaded.append(Loaded(own[0], []))
                continue
            buffer = buffers.pop(0)
            loaded.append(Loaded(buffer, copies_of(operand.copies(info, own, buffer))))
            for copy in loaded[-1].copies:
                copy.start()
        stored, staging = [], []
        for result in results:
            if isinstance(result, Export):
                staging += copies_of(result.copies(sources[at], targets.pop(0)))
                at += 1
                continue
            buffer = targets.pop(0) if result.near else leaving.pop(0)
            if isinstance(result, Stage):
                own = sources[at : at + len(result.source.arrays)]
                at += len(own)
                staging += copies_of(result.source.copies(info, own, buffer))
                continue
            target = targets.pop(0) if result.far else None
            pairs = result.copies(buffer, target) if result.far else []
            stored.append(Stored(buffer, copies_of(pairs)))
        for copy in staging:
            copy.start()
        body(info, *loaded, *stored, *rest)
        for copy in staging:
            copy.wait()
        for item in loaded + ([marks] if named else []):
            item.ready()
        for item in stored:
            item.send()
        for item in stored:
            for copy in item.copies:
                copy.wait()

    spaces = [pltpu.VMEM if o.near else pltpu.HBM for o in inputs for _ in o.arrays]
    placed = [a if space is pltpu.VMEM else in_hbm(a) for a, space in zip(arrays, spaces)]
    spaces += waits + [pltpu.HBM] * named
    moved = sum(a.size * a.dtype.itemsize for a in arrays)
    moved += sum(math.prod(o.dims) * jnp.dtype(o.dtype).itemsize for o in results)
    given = pl.pallas_call(
        kernel,
        name=getattr(body, "func", body).__name__,
        out_shape=tuple(s for o in results for s in o.shapes()),
        in_specs=[pl.BlockSpec(memory_space=space) for space in spaces],
        out_specs=tuple(pl.BlockSpec(memory_space=s) for o in results for s in o.spaces()),
        input_output_aliases=aliases,
        scratch_shapes=[pltpu.VMEM(o.dims, o.dtype) for o in copied]
        + [pltpu.VMEM(o.dims, o.dtype) for o in held]
        + [pltpu.SemaphoreType.DMA((max(1, moves + named),))]
        + [pltpu.SMEM((1, 4), jnp.int32)] * named
        + list(scratch),
        compiler_params=pltpu.CompilerParams(vmem_limit_bytes=megabytes * 2**20),
        cost_estimate=pl.CostEstimate(flops=0, bytes_accessed=1024, transcendentals=0),
    )(*placed, *after, *([in_hbm(starts)] if named else []))
    given, answer = list(given), []
    for result in results:
        item = (Near(given.pop(0)),) if result.near else ()
        item += (given.pop(0),) if result.far else ()
        answer.append(item if len(item) == 2 else item[0])
    return answer


def moved_by(array, axis, route):
    array = array.arrays[0] if isinstance(array, Near) else array
    return Near(lax.ppermute(array, axis, route))


def feature_weights(feat_query_t, feat_key_t):
    def places(info, sources=None, buffer=None):
        if info is None:
            return 2
        return [(sources[0], buffer.at[0:32]), (sources[1], buffer.at[32:64])]

    return Far([feat_query_t, feat_key_t], (128, feat_query_t.shape[1]), places)


def own_part(block):
    def places(info, sources=None, buffer=None):
        if info is None:
            return 1
        return [(sources[0].at[info.rows(0)], buffer)]

    return Far(block, (OWN, block.shape[1]), places)


def keys_kernel(
    info, x_ref, gain_ref, key_ref, value_ref, feat_ref, choose_ref, lanes_ref,
    normed_ref, inv_ref, raw_ref, keys_ref, values_ref, km_ref, packed_ref, wide_ref,
):
    gain = gain_ref[...]

    def norm_rows(part):
        for i in range(2):
            rows = slice(part * 128 + i * 64, part * 128 + i * 64 + 64)
            x = x_ref.ref[rows, :].astype(f32)
            inv = lax.rsqrt(jnp.mean(x * x, axis=-1, keepdims=True) + EPS)
            inv_ref[rows, :] = inv
            normed_ref[rows, :] = (x * inv * gain).astype(bf16)

    x_ref.part(0)
    norm_rows(0)
    x_ref.part(1)
    norm_rows(1)
    for ref in (x_ref, feat_ref, key_ref, value_ref, choose_ref, lanes_ref):
        ref.ready()
    feat_ref.ref[64:128, :] = jnp.zeros((64, feat_ref.shape[1]), bf16)
    half = ROWS // 2
    features = []
    for first in (0, half):
        rows = slice(first, first + half)
        normed = normed_ref[rows, :]
        raw = mm_nt(normed, feat_ref[...])
        raw_ref[rows, :] = raw
        if first == 0:
            norm_rows(2)
            norm_rows(3)
        keys_ref[rows, :] = mm(normed, key_ref[...]).astype(bf16)
        values_ref[rows, :] = mm(normed, value_ref[...]).astype(bf16)
        left, right = factors(raw, 1, choose_ref, lanes_ref)
        part = (left * right * lanes_ref[2:3, :]).astype(bf16)
        features.append((part.astype(f32) * lanes_ref[3:4, :]).astype(bf16))
    features = jnp.concatenate(features, axis=0)
    values = values_ref[...]
    for head in range(HEADS):
        km_ref[head] = features[:, head * LANES : (head + 1) * LANES]
    tail = tail_mask(info)
    for head in range(HEADS):
        own = features[:, head * LANES : (head + 1) * LANES]
        lanes = head_lanes(head)
        kept = (values[:, lanes].astype(f32) * tail).astype(bf16)
        state = mm_tn(own, kept)
        norm = jnp.sum(own.astype(f32) * tail, axis=0, keepdims=True)
        write_packed(packed_ref, head, state, norm)
        wide_ref[head, 0:PACKED, :] = packed_ref[head]
        wide_ref[head, PACKED : PACKED + WIN, :] = keys_ref[ROWS - WIN :, lanes]
        wide_ref[head, PACKED + WIN :, :] = values[ROWS - WIN :, lanes]


def local_kernel(
    info, raw_ref, choose_ref, lanes_ref, values_ref, km_ref, normed_ref, query_ref,
    qf_ref, low_ref, num_ref, den_ref, queries_ref,
):
    left, right = factors(raw_ref[...], 0, choose_ref, lanes_ref)
    features = (left * right * lanes_ref[2:3, :]).astype(bf16)
    for head in range(HEADS):
        qf_ref[head] = features[:, head * LANES : (head + 1) * LANES]
    half = ROWS // 2
    causal = []
    for block in range(2):
        query_at = column_positions(info, block * half, half)
        key_at = row_positions(info, 0, (block + 1) * half)
        causal.append((query_at >= key_at) & (doc_of(info, query_at) == doc_of(info, key_at)))
    for head in range(HEADS):
        for block in range(2):
            first, reach = block * half, (block + 1) * half
            own = qf_ref[head, first:reach, :]
            weights = jnp.where(causal[block], mm_nt(own, km_ref[head, :reach, :]), 0.0)
            den_ref[head, first:reach, :] = jnp.sum(weights, axis=-1, keepdims=True)
            weights = weights.astype(bf16)
            low_ref[head, first:reach, 0:reach] = weights
            num_ref[first:reach, head_lanes(head)] = mm(
                weights, values_ref[:reach, head_lanes(head)]
            )
    queries_ref[...] = mm(normed_ref[...], query_ref[...]).astype(bf16)


def window_kernel(
    info, queries_ref, keys_ref, values_ref, probs_ref, window_ref,
):
    queries = queries_ref[...]
    for head in range(HEADS):
        lanes = head_lanes(head)
        for tile in range(1, ROWS // TILE):
            rows = slice(tile * TILE, (tile + 1) * TILE)
            probs, result = window_tile(
                info, head, tile, queries[rows, lanes],
                window_rows(keys_ref, None, 0, head, tile), window_rows(values_ref, None, 1, head, tile),
            )
            probs_ref[head, tile - 1] = probs
            window_ref[rows, lanes] = result


def by_distance(ref, info, other):
    return jnp.concatenate([ref[info.rows(d, other), :] for d in range(4)], axis=0)


def mixed_kernel(
    info, before_ref, got1_ref, got2_ref, got3_ref, qf_ref, num_ref, den_ref, window_ref, out_ref,
    queries_ref, keys_ref, values_ref,
    mixed_ref, linear_ref, total_den_ref, state_ref, norm_ref, probs_ref, other_ref,
):
    use = prefix_mask(info)
    for head in range(HEADS):
        lanes = head_lanes(head)
        state, norm = read_total(before_ref, (got1_ref, got2_ref, got3_ref), head)
        state_ref[head] = state
        norm_ref[head] = jnp.broadcast_to(norm, (8, LANES))
        features = qf_ref[head]
        inter = mm(features, state) * use
        den = jnp.sum(features.astype(f32) * norm, axis=-1, keepdims=True) * use + den_ref[head]
        total_den_ref[head] = den
        linear = (inter + num_ref[:, lanes]) / den
        linear_ref[:, lanes] = linear
        probs, window = window_tile(
            info, head, 0, queries_ref[0:TILE, lanes],
            window_rows(keys_ref, got1_ref, 0, head, 0), window_rows(values_ref, got1_ref, 1, head, 0),
        )
        probs_ref[head] = probs
        mixed_ref[0:TILE, lanes] = (linear[0:TILE] + window).astype(bf16)
        mixed_ref[TILE:, lanes] = (linear[TILE:] + window_ref[TILE:, lanes]).astype(bf16)
    other_ref[...] = mm(by_distance(mixed_ref, info, True), out_ref[...]).astype(bf16)


def mixed_own_kernel(info, mixed_ref, out_ref, own_ref):
    own_ref[...] = mm(by_distance(mixed_ref, info, False), out_ref[...]).astype(bf16)


def quarters_kernel(info, own_ref, got_ref, *out_refs):
    out_refs[4][...] = got_ref[0:16, 0:128]
    for d in (1, 2, 3, 0):
        rows = slice(d * OWN, (d + 1) * OWN)
        total = own_ref[rows, :].astype(f32) + got_ref[rows, :].astype(f32)
        out_refs[d][...] = total.astype(out_refs[d].dtype)
        out_refs[d].send()


def resid_kernel(
    info, mine_ref, x_ref, gain_ref, got1_ref, got2_ref, got3_ref, normed_ref, resid_ref, inv_ref
):
    resid = x_ref[...].astype(f32) + mine_ref[...]
    for ref in (got1_ref, got2_ref, got3_ref):
        resid = resid + ref[...].astype(f32)
    resid_ref[...] = resid
    inv = lax.rsqrt(jnp.mean(resid * resid, axis=-1, keepdims=True) + EPS)
    inv_ref[...] = inv
    normed_ref[...] = (resid * inv * gain_ref[...]).astype(bf16)


def grad_resid_kernel(
    info, mine_ref, resid_ref, inv_ref, top_ref, gain_ref, got1_ref, got2_ref, got3_ref,
    sent_ref, grad_ref, gains_ref,
):
    grad = mine_ref[...]
    for ref in (got1_ref, got2_ref, got3_ref):
        grad = grad + ref[...].astype(f32)
    resid = resid_ref[...]
    inv = inv_ref[...]
    grad_resid = top_ref[...].astype(f32) + norm_back(resid, inv, gain_ref[...], grad)
    sent_ref[...] = grad_resid.astype(bf16)
    sent_ref.send()
    grad_ref[...] = grad_resid
    gains_ref[0:1, :] = jnp.sum(grad * resid * inv, axis=0, keepdims=True)


def grad_x_kernel(
    info, mine_ref, x_ref, grad_resid_ref, gain_ref, resid_ref, out_ref, got1_ref, got2_ref, got3_ref,
    out1_ref, out2_ref, out3_ref, sent_ref,
):
    total = resid_ref[...] + out_ref[...]
    for ref in (out1_ref, out2_ref, out3_ref):
        total = total + ref[...].astype(f32)
    sent_ref[0:OWN, :] = total.astype(bf16)
    grad = mine_ref[...]
    for ref in (got1_ref, got2_ref, got3_ref):
        grad = grad + ref[...].astype(f32)
    x = x_ref[...].astype(f32)
    inv = lax.rsqrt(jnp.mean(x * x, axis=-1, keepdims=True) + EPS)
    sent_ref[OWN:, :] = (grad_resid_ref[...] + norm_back(x, inv, gain_ref[...], grad)).astype(bf16)


def norm_back(in_rows, inv_rms, gain, grad_normed):
    weighted = grad_normed * gain
    return inv_rms * weighted - in_rows * inv_rms**3 * jnp.mean(
        weighted * in_rows, axis=-1, keepdims=True
    )


def by_halves(block):
    def places(info, sources=None, buffer=None):
        if info is None:
            return 8
        return [
            (sources[0].at[info.rows(i % 4, other=i >= 4)], buffer.at[i * OWN : (i + 1) * OWN])
            for i in range(8)
        ]

    return Far(block, block.shape, places)


def grad_act_kernel(info, top_ref, down_ref, own_ref, other_ref):
    top = top_ref[...]
    half = ROWS // 2
    for first in range(0, down_ref.shape[0], 256):
        span = slice(first, min(first + 256, down_ref.shape[0]))
        grad = mm_nt(top, down_ref[span, :])
        own_ref[:, span] = grad[:half]
        other_ref[:, span] = grad[half:]


def ffn_rows(pieces, gate_ref, up_ref, grad_act_ref, normed_ref, act_ref, grad_gate_ref, grad_up_ref):
    normed = jnp.concatenate([piece[...] for piece in pieces], axis=0)
    normed_ref[...] = normed
    hidden = gate_ref.shape[0]
    for first in range(0, hidden, 256):
        span = slice(first, min(first + 256, hidden))
        gate = mm_nt(normed, gate_ref[span, :])
        up_value = mm_nt(normed, up_ref[span, :])
        sigmoid_gate = jax.nn.sigmoid(gate)
        silu_gate = gate * sigmoid_gate
        act_ref[:, span] = (silu_gate * up_value).astype(bf16)
        grad_act = grad_act_ref[:, span]
        grad_gate_ref[:, span] = (
            grad_act * up_value * sigmoid_gate * (1.0 + gate * (1.0 - sigmoid_gate))
        ).astype(bf16)
        grad_up_ref[:, span] = (grad_act * silu_gate).astype(bf16)


def ffn_own_kernel(info, p0, p3, p1, p2, gate_ref, up_ref, grad_act_ref, *out_refs):
    ffn_rows((p0, p3, p2, p1), gate_ref, up_ref, grad_act_ref, *out_refs)


def ffn_other_kernel(info, s0, s3, s1, s2, gate_ref, up_ref, grad_act_ref, back_ref, *out_refs):
    ffn_rows((s0, s3, s2, s1), gate_ref, up_ref, grad_act_ref, *out_refs)
    ffn_back_kernel(info, out_refs[2], out_refs[3], gate_ref, up_ref, back_ref)


def ffn_back_kernel(info, grad_gate_ref, grad_up_ref, gate_ref, up_ref, back_ref):
    grad_gate, grad_up = grad_gate_ref[...], grad_up_ref[...]
    for first in range(0, back_ref.shape[1], 512):
        span = slice(first, first + 512)
        part = mm(grad_gate, gate_ref[:, span]) + mm(grad_up, up_ref[:, span])
        back_ref[:, span] = part.astype(bf16)


def ffn_out_kernel(info, act_own_ref, act_other_ref, down_ref, other_ref, own_ref):
    for target, act_ref in ((other_ref, act_other_ref), (own_ref, act_own_ref)):
        act = act_ref[...]
        for first in range(0, target.shape[1], 512):
            span = slice(first, first + 512)
            target[:, span] = mm(act, down_ref[:, span]).astype(bf16)


def column_grads(pairs, out_ref, last=None):
    count = out_ref.shape[0] // 4
    for part in range(4):
        span = slice(part * count, (part + 1) * count)
        first = 0
        for i, (rows_refs, grads) in enumerate(pairs):
            rows_refs = rows_refs if isinstance(rows_refs, tuple) else (rows_refs,)
            grads = grads if isinstance(grads, tuple) else (grads,)
            total = sum(mm_tn(rows[:, span], grad) for rows, grad in zip(rows_refs, grads))
            if last is not None and i == len(pairs) - 1:
                total = total + last[span, :].astype(f32)
            end = first + total.shape[1]
            out_ref[span, first:end] = total.astype(bf16)
            first = end
        out_ref.send(part)


def gate_grads_kernel(
    info, own_ref, other_ref, gate_own_ref, gate_other_ref, up_own_ref, up_other_ref, out_ref
):
    rows = (own_ref, other_ref)
    gate = (gate_own_ref[...], gate_other_ref[...])
    up = (up_own_ref[...], up_other_ref[...])
    column_grads(((rows, gate), (rows, up)), out_ref)


class Rows:

    def __init__(self, ref, first, count):
        self.ref, self.rows = ref, slice(first, first + count)

    def __getitem__(self, index):
        return self.ref[self.rows, index[1]]


def down_grads_kernel(info, top_ref, act_own_ref, act_other_ref, out_ref, tail_ref):
    half, whole = ROWS // 2, out_ref.shape[1]
    rows = (Rows(top_ref, 0, half), Rows(top_ref, half, half))
    acts = (act_own_ref[...], act_other_ref[...])
    column_grads(((rows, tuple(act[:, :whole] for act in acts)),), out_ref)
    room = jnp.zeros((half, 128 - acts[0].shape[1] % 128), bf16)
    rest = [jnp.concatenate([act[:, whole:], room], axis=1) for act in acts]
    tail_ref[...] = sum(mm_tn(row[:, :], act) for row, act in zip(rows, rest)).astype(bf16)


def grad_x_out_kernel(info, p0, p1, p2, p3, s0, s1, s2, s3, output_ref, grad_ref):
    for i, piece in enumerate((p0, p1, p2, p3, s0, s1, s2, s3)):
        rows = info.rows(4 - i % 4, other=i >= 4)
        output_ref[rows, :] = piece[0:OWN, :]
        grad_ref[rows, :] = piece[OWN : 2 * OWN, :].astype(f32)


def window_tile_back(top, probs, key_rows, value_rows):
    grad_probs = mm_nt(top, value_rows)
    shared = jnp.sum(grad_probs * probs, axis=-1, keepdims=True)
    return (probs * (grad_probs - shared)).astype(bf16)


def mixed_back_kernel(
    info, p0, p3, p1, p2, s0, s3, s1, s2, out_ref, linear_ref, den_ref, qf_ref, probs0_ref, keys_ref,
    values_ref, halo_ref, queries_ref, packed_ref, wide_ref, top_ref, gm_ref, gnum_ref, gden_ref,
):
    for i, piece in enumerate((p0, p1, p2, p3, s0, s1, s2, s3)):
        top_ref[info.rows(4 - i % 4, other=i >= 4), :] = piece[...]
    grad_mixed = mm_nt(top_ref[...], out_ref[...]).astype(bf16)
    gm_ref[...] = grad_mixed
    use = prefix_mask(info)
    for head in range(HEADS):
        lanes = head_lanes(head)
        wide = grad_mixed[:, lanes].astype(f32)
        den = den_ref[head]
        grad_num = (wide / den).astype(bf16)
        gnum_ref[:, lanes] = grad_num
        grad_den = -jnp.sum(wide * linear_ref[:, lanes], axis=-1, keepdims=True) / den
        gden_ref[head] = grad_den
        features = qf_ref[head]
        used = (grad_num.astype(f32) * use).astype(bf16)
        state = mm_tn(features, used)
        norm = jnp.sum(features.astype(f32) * (grad_den * use), axis=0, keepdims=True)
        write_packed(packed_ref, head, state, norm)
        wide_ref[head, 0:PACKED, :] = packed_ref[head]
        top, probs = grad_mixed[0:TILE, lanes], probs0_ref[head]
        grad_logits = window_tile_back(
            top, probs, window_rows(keys_ref, halo_ref, 0, head, 0),
            window_rows(values_ref, halo_ref, 1, head, 0),
        )
        grad_keys = mm_tn(grad_logits, queries_ref[0:TILE, lanes]) * VALUE_WIDTH ** (-0.5)
        wide_ref[head, PACKED : PACKED + WIN, :] = grad_keys[0:WIN].astype(bf16)
        grad_values = mm_tn(probs.astype(bf16), top)
        wide_ref[head, PACKED + WIN :, :] = grad_values[0:WIN].astype(bf16)


def window_back_kernel(
    info, gm_ref, probs0_ref, probs_ref, keys_ref, values_ref, halo_ref, queries_ref,
    top_ref, mixed_ref, gq_ref, gk_ref, gv_ref, out_ref, key_acc, value_acc,
):
    column_grads(((top_ref, mixed_ref[...]),), out_ref)
    scale = VALUE_WIDTH ** (-0.5)
    key_acc[...] = jnp.zeros_like(key_acc)
    value_acc[...] = jnp.zeros_like(value_acc)
    for tile in range(ROWS // TILE):
        first = tile * TILE
        reach = slice(first, first + TILE + WIN)
        for head in range(HEADS):
            lanes = head_lanes(head)
            key_rows = window_rows(keys_ref, halo_ref, 0, head, tile)
            value_rows = window_rows(values_ref, halo_ref, 1, head, tile)
            top = gm_ref[first : first + TILE, lanes]
            probs = probs0_ref[head] if tile == 0 else probs_ref[head, tile - 1]
            grad_logits = window_tile_back(top, probs, key_rows, value_rows)
            gq_ref[first : first + TILE, lanes] = (mm(grad_logits, key_rows) * scale).astype(bf16)
            queries = queries_ref[first : first + TILE, lanes]
            key_acc[reach, lanes] += mm_tn(grad_logits, queries) * scale
            value_acc[reach, lanes] += mm_tn(probs.astype(bf16), top)
    gk_ref[...] = key_acc[WIN:, :]
    gv_ref[...] = value_acc[WIN:, :]


def linear_back_kernel(
    info, gnum_ref, gden_ref, values_ref, low_ref, km_ref, qf_ref, state_ref, norm_ref, raw_ref,
    choose_ref, choose_k_ref, lanes_ref, window_gv_ref, normed_ref, gq_ref,
    gfeat_ref, gv_ref, gkf_ref, left_ref, right_ref, out_ref,
):
    column_grads(((normed_ref, gq_ref[...]),), out_ref)
    use = prefix_mask(info)
    half = ROWS // 2
    grads = [[None, None], [None, None]]
    for head in range(HEADS):
        lanes = head_lanes(head)
        inter = mm_nt((gnum_ref[:, lanes].astype(f32) * use).astype(bf16), state_ref[head])
        inter = inter + (gden_ref[head] * use) * norm_ref[head, 0:1, :]
        for block in range(2):
            first, reach = block * half, (block + 1) * half
            query_at = column_positions(info, first, half)
            key_at = row_positions(info, 0, reach)
            causal = (query_at >= key_at) & (doc_of(info, query_at) == doc_of(info, key_at))
            grad_num = gnum_ref[first:reach, lanes]
            grad = mm_nt(grad_num, values_ref[:reach, lanes]) + gden_ref[head, first:reach, :]
            grad = jnp.where(causal, grad, 0.0).astype(bf16)
            grads[head][block] = mm(grad, km_ref[head, :reach, :]) + inter[first:reach]
            key_part = mm_tn(grad, qf_ref[head, first:reach, :])
            value_part = mm_tn(low_ref[head, first:reach, 0:reach], grad_num)
            if block == 0:
                gkf_ref[head, 0:half] = key_part
                gv_ref[0:half, lanes] = window_gv_ref[0:half, lanes] + value_part
            else:
                gkf_ref[head, 0:half] += key_part[0:half]
                gkf_ref[head, half:] = key_part[half:]
                gv_ref[0:half, lanes] += value_part[0:half]
                gv_ref[half:, lanes] = window_gv_ref[half:, lanes] + value_part[half:]
    left, right = factors(raw_ref[...], 0, choose_ref, lanes_ref)
    gradient = jnp.concatenate([jnp.concatenate(g, axis=0) for g in grads], axis=1)
    gradient = gradient * lanes_ref[2:3, :]
    gfeat_ref[...] = feature_back(gradient, left, right, choose_ref)
    left_ref[...], right_ref[...] = factors(raw_ref[...], 1, choose_k_ref, lanes_ref)


def keys_back_kernel(
    info, before_ref, got1_ref, got2_ref, got3_ref, values_ref, km_ref, gkf_ref, gk_ref, gv_ref,
    left_ref, right_ref, choose_ref, lanes_ref, gfeat_ref, normed_ref, tail_ref,
    gkw_ref, gvw_ref, gf_ref, out_ref,
):
    tail = tail_mask(info)
    inner = ROWS - WIN
    gkw_ref[0:inner, :] = gk_ref[0:inner, :].astype(bf16)
    gradients = []
    for head in range(HEADS):
        lanes = head_lanes(head)
        later, norm = read_total(before_ref, (got1_ref, got2_ref, got3_ref), head)
        kept = (values_ref[:, lanes].astype(f32) * tail).astype(bf16)
        gradients.append(gkf_ref[head] + mm_nt(kept, later) + tail * norm)
        grad_values = gv_ref[:, lanes] + mm(km_ref[head], later) * tail
        gvw_ref[0:inner, lanes] = grad_values[0:inner].astype(bf16)
        right = got1_ref[head, PACKED:, :].astype(f32)
        gkw_ref[inner:, lanes] = (gk_ref[inner:, lanes] + right[0:WIN]).astype(bf16)
        gvw_ref[inner:, lanes] = (grad_values[inner:] + right[WIN:]).astype(bf16)
    gradient = jnp.concatenate(gradients, axis=1) * lanes_ref[4:5, :]
    gradient = feature_back(gradient, left_ref[...], right_ref[...], choose_ref) + gfeat_ref[...]
    gf_ref[...] = gradient.astype(bf16)
    lane = lax.broadcasted_iota(jnp.int32, (1, 128), 1)
    beside = jnp.where(lane < 64, 0.0, pltpu.roll(gradient, 64, 1)).astype(bf16)
    column_grads(
        (
            (normed_ref, gkw_ref[...]), (normed_ref, gvw_ref[...]), (normed_ref, beside),
        ),
        out_ref, last=tail_ref,
    )


def normed_back_kernel(
    info, gq_ref, gkw_ref, gvw_ref, gf_ref, wq_ref, wk_ref, wv_ref, wf_ref, x_ref, inv_ref, gain_ffn_ref,
    other_ref, own_ref, gains_ref,
):
    wf_ref.ready()
    wf_ref.ref[64:128, :] = jnp.zeros((64, wf_ref.shape[1]), bf16)
    for target, other in ((other_ref, True), (own_ref, False)):
        grads = [by_distance(ref, info, other) for ref in (gq_ref, gkw_ref, gvw_ref, gf_ref)]
        scaled_by = by_distance(inv_ref, info, other)
        for piece in range(4):
            span = slice(piece * 512, (piece + 1) * 512)
            part = mm_nt(grads[0], wq_ref[span, :])
            part = part + mm_nt(grads[1], wk_ref[span, :])
            part = part + mm_nt(grads[2], wv_ref[span, :])
            part = part + mm(grads[3], wf_ref[:, span])
            target[:, span] = part.astype(bf16)
            x_rows = jnp.concatenate([x_ref[info.rows(d, other), span] for d in range(4)], axis=0)
            total = jnp.sum(part * (x_rows.astype(f32) * scaled_by), axis=0, keepdims=True)
            gains_ref[0:1, span] = total if other else total + gains_ref[0:1, span]
    gains_ref[1:2, :] = gain_ffn_ref[0:1, :]


def columns(block, first, last):
    def places(info, sources=None, buffer=None):
        return 1 if info is None else [(sources[0].at[:, first:last], buffer)]

    return Far(block, (block.shape[0], last - first), places)


def grads_out_kernel(
    info, both_ref, in_ref, gate_ref, up_ref, down_ref, out_ref, grad_q_ref, grad_k_ref, grad_v_ref,
    feat_query_ref, feat_key_ref,
):
    hidden, width = gate_ref.shape[0], out_ref.shape[0]
    whole = hidden // 128 * 128
    both = both_ref[...].astype(f32).T
    gate_ref[...] = both[0:hidden]
    gate_ref.send()
    up_ref[...] = both[hidden:]
    up_ref.send()
    down_ref[0:whole, :] = in_ref[:, 0:whole].astype(f32).T
    at = whole
    out_ref[...] = in_ref[:, at : at + width].astype(f32).T
    out_ref.send()
    for ref in (grad_q_ref, grad_k_ref, grad_v_ref):
        at += width
        ref[...] = in_ref[:, at : at + width].astype(f32)
        ref.send()
    tail = in_ref[:, at + width :].astype(f32).T
    down_ref[whole:, :] = tail[0 : hidden - whole]
    down_ref.send()
    feat_query_ref[...] = tail[64:96]
    feat_key_ref[...] = tail[96:128]


def total_of(refs):
    total = refs[0][...]
    for ref in refs[1:]:
        total = total + ref[...]
    return total


def gains_kernel(info, *refs):
    refs[-1][...] = total_of(refs[:-1])


def spread_kernel(info, *refs):
    total, out_ref = total_of(refs[:-1]), refs[-1]
    for i in range(out_ref.shape[0]):
        out_ref[i, 0:2, :] = total[:, i * 128 : (i + 1) * 128]
        out_ref[i, 2:, :] = jnp.zeros((6, 128), f32)


def gathered_sum_kernel(info, in_ref, out_ref):
    total = in_ref[0]
    for i in range(1, in_ref.shape[0]):
        total = total + in_ref[i]
    out_ref[...] = total


def along_y(distance):
    return [(i, (i + 2 * distance) % 8) for i in range(8)]


def sibling():
    return [(i, i ^ 1) for i in range(8)]


def along_x(distance):
    return [(i, (i + 4 * distance) % 16) for i in range(16)]


def along_z(distance):
    return [(4 * a + z, 4 * a + (z + distance) % 4) for a in range(4) for z in range(4)]


def head_quarters(own, other, after=()):
    got = moved_by(other, "head", sibling())
    width = own.dims[1]
    with jax.named_scope("quarters"):
        mine, *sent, token = call(
            quarters_kernel,
            [near(OWN, width, dtype=f32)] + [near(OWN, width)] * 3 + [near(16, 128)],
            (own, got), after=after,
        )
    parts = [moved_by(sent[d - 1], "head", along_y(d)) for d in (2, 1, 3)]
    return mine, parts, moved_by(token, "head", sibling())


def head_pieces(own):
    far_piece = moved_by(own, "head", along_y(2))
    pieces = [own, moved_by(own, "head", along_y(1)), far_piece, moved_by(own, "head", along_y(3))]
    return pieces + [moved_by(piece, "head", sibling()) for piece in pieces]


def gains_sum(gains):
    with jax.named_scope("gains"):
        (pair,) = call(
            gains_kernel, [near(*gains.dims, dtype=f32)], (gains, moved_by(gains, "head", sibling()))
        )
        parts = [pair] + [moved_by(pair, "head", along_y(d)) for d in (2, 1, 3)]
        (blocks,) = call(spread_kernel, [far(16, 8, 128, dtype=f32)], parts)
        blocks = lax.all_to_all(blocks, "seq", 0, 0)
        (total,) = call(gathered_sum_kernel, [far(8, 128, dtype=f32)], (blocks,))
    return total


def scan_kernel(reverse, info, own_ref, got1_ref, got2_ref, got3_ref, before_ref, *sent_refs):
    place_x, place_z = (3 - info.x, 3 - info.z) if reverse else (info.x, info.z)
    before = jnp.zeros(before_ref.shape, f32)
    for d, ref in enumerate((got1_ref, got2_ref, got3_ref), 1):
        before = before + ref[:, 0:PACKED, :].astype(f32) * (place_x >= d).astype(f32)
    before_ref[...] = before
    row = lax.broadcasted_iota(jnp.int32, (HEADS, 16, 128), 1)
    sent = []
    for total in (before, before + own_ref[:, 0:PACKED, :].astype(f32)):
        norm = total[:, KEPT:]
        norm = norm + jnp.roll(norm, -2, axis=1)
        high = norm.astype(bf16).astype(f32)
        rest = jnp.roll(norm - high, 2, axis=1)
        norm = jnp.where(row < 2, high, jnp.where(row < 4, rest, 0.0))
        sent.append((total[:, :KEPT], norm))
    for d, ref in enumerate(sent_refs, 1):
        with_own = (place_z + d < 4).astype(f32)
        for part, rows in ((0, slice(0, KEPT)), (1, slice(KEPT, PACKED))):
            less, more = sent[0][part], sent[1][part]
            ref[:, rows, :] = (more * with_own + less * (1.0 - with_own)).astype(bf16)
        if ref.shape[1] > PACKED:
            own, earlier = own_ref[:, PACKED:, :].astype(f32), got1_ref[:, PACKED:, :].astype(f32)
            ref[:, PACKED:, :] = (own * with_own + earlier * (1.0 - with_own)).astype(bf16)


def exclusive_parts(own, reverse, after=(), wide=None):
    sign = -1 if reverse else 1
    first = own if wide is None else wide
    got = [moved_by(first if d == 1 else own, "seq", along_x(sign * d)) for d in (1, 2, 3)]
    with jax.named_scope("scan"):
        before, *sent = call(
            functools.partial(scan_kernel, reverse),
            [near(*own.dims, dtype=f32), near(*first.dims), near(*own.dims), near(*own.dims)],
            (first, *got), after=after,
        )
    return [before] + [
        moved_by(sent[d - 1], "seq", along_z(sign * d)) for d in (1, 2, 3)
    ]


def shards(
    inputs,
    gain_mix,
    feat_query,
    feat_key,
    win_query,
    win_key,
    value_proj,
    out_proj,
    gain_ffn,
    gate_proj,
    up_proj,
    down_proj,
    document_starts,
    cotangent,
):
    choose, lanes = feature_tables()
    choose = jnp.asarray(choose, bf16)
    lanes = jnp.asarray(lanes, f32)
    choose_q, choose_k = choose[0], choose[1]
    feat = feature_weights(feat_query.T, feat_key.T)
    gain_mix = gain_mix.reshape(1, -1)
    gain_ffn = gain_ffn.reshape(1, -1)
    model = inputs.shape[1]
    width = HEADS * VALUE_WIDTH
    hidden = gate_proj.shape[1]
    half = ROWS // 2
    unit = 2 * ROWS * model
    starts = document_starts

    normed, inv_mix, raw, keys, values, km, packed, wide = call(
        keys_kernel,
        (
            near(ROWS, model), near(ROWS, 1, dtype=f32), near(ROWS, 128, dtype=f32),
            near(ROWS, width), near(ROWS, width), near(HEADS, ROWS, LANES),
            near(HEADS, PACKED, 128), near(HEADS, PACKED + EDGE, 128),
        ),
        (Far(inputs, parts=4), gain_mix, win_key, value_proj, feat, choose_k, lanes),
        starts=starts, flops=unit * 640,
    )
    qf, low, num, den, queries, near_out, normed_far, inv_mix, raw_far, keys_far, values_far, km_far = call(
        local_kernel,
        (
            near(HEADS, ROWS, LANES), near(HEADS, ROWS, ROWS), near(ROWS, width, dtype=f32),
            near(HEADS, ROWS, 1, dtype=f32), near(ROWS, width), Stage(out_proj), Export(normed),
            Export(inv_mix), Export(raw), Export(keys), Export(values), Export(km),
        ),
        (raw, choose_q, lanes, values, km, normed, win_query),
        starts=starts, flops=unit * 300,
    )
    sums = exclusive_parts(packed, False, after=(qf,), wide=wide)
    probs, window, qf_far, low = call(
        window_kernel,
        (
            near(HEADS, 3, TILE, TILE + WIN, dtype=f32),
            near(ROWS, width, dtype=f32), Export(qf), Export(low),
        ),
        (queries, keys, values),
        starts=starts, flops=unit * 400,
    )
    mixed, linear, total_den, state, norm, probs_first, other = call(
        mixed_kernel,
        (
            near(ROWS, width), near(ROWS, width, dtype=f32), near(HEADS, ROWS, 1, dtype=f32),
            near(HEADS, LANES, VALUE_WIDTH), near(HEADS, 8, LANES, dtype=f32),
            near(HEADS, TILE, TILE + WIN, dtype=f32), near(half, model),
        ),
        (*sums, qf, num, den, window, near_out, queries, keys, values),
        starts=starts, flops=unit * 300,
    )
    own, halo, *rest = call(
        mixed_own_kernel,
        (
            near(half, model),
            Export(sums[1], (HEADS, EDGE, 128), lambda ref: ref.at[:, PACKED:, :]),
            *map(Export, (mixed, linear, total_den, state, norm, probs_first, probs, queries)),
        ),
        (mixed, near_out), after=(other,), flops=unit * 100,
    )
    mixed, linear, total_den, state, norm, probs_first, probs, queries_far = rest
    mine, parts, signal = head_quarters(own, other)
    grad_act_own, grad_act_other, x_own, near_gain, near_gate, near_up = call(
        grad_act_kernel,
        (
            near(half, hidden, dtype=f32), near(half, hidden, dtype=f32), Stage(own_part(inputs)), Stage(gain_ffn),
            Stage(gate_proj.T), Stage(up_proj.T),
        ),
        (by_halves(cotangent), down_proj),
        after=(signal,), flops=unit * hidden,
    )
    own_normed, resid, inv_ffn = call(
        resid_kernel,
        (near(OWN, model), near(OWN, model, dtype=f32), near(OWN, 1, dtype=f32)),
        (mine, x_own, near_gain, *parts), after=(grad_act_own,),
    )
    pieces = head_pieces(own_normed)
    def ffn_half(body, pieces, grad_act, *more, after=()):
        order = [pieces[i] for i in (0, 3, 1, 2)]
        return call(
            body,
            (
                *more, near(half, model), near(half, hidden), near(half, hidden), near(half, hidden),
            ),
            (*order, near_gate, near_up, grad_act), after=after, flops=unit * 2 * hidden,
        )

    normed_own, act_own, gate_own, up_own = ffn_half(ffn_own_kernel, pieces[:4], grad_act_own)
    other, normed_other, act_other, gate_other, up_other = ffn_half(
        ffn_other_kernel, pieces[4:], grad_act_other, near(half, model), after=(gate_own,)
    )
    (own,) = call(
        ffn_back_kernel, (near(half, model),), (gate_own, up_own, near_gate, near_up),
        after=(other,), flops=unit * hidden,
    )
    mine, parts, signal = head_quarters(own, other)
    whole = hidden // 128 * 128
    place = dict(parts=4, width=2 * hidden + whole + 4 * width + 128)
    grads, resid_far, near_top, near_gain, *near_mixed = call(
        gate_grads_kernel,
        (
            far(model, 2 * hidden, **place), Export(resid), Stage(own_part(cotangent)),
            Stage(gain_ffn), Stage(out_proj), Stage(linear), Stage(total_den), Stage(qf_far),
            Stage(probs_first), Stage(probs), Stage(keys_far), Stage(values_far), Stage(halo),
            Stage(queries_far),
        ),
        (normed_own, normed_other, gate_own, gate_other, up_own, up_other),
        after=(signal,), flops=unit * 2 * hidden,
    )
    at = 2 * hidden
    *near_mixed, probs_first, probs, keys, values, halo, queries = near_mixed
    grads, tail, *near_back = call(
        down_grads_kernel,
        (
            far(model, whole, first=at, onto=grads, **place), near(model, 128), Stage(low),
            Stage(km_far),
            Stage(state), Stage(norm), Stage(raw_far), Stage(choose_q), Stage(choose_k),
            Stage(lanes), Stage(mixed), Export(act_own), Export(act_other),
        ),
        (by_halves(cotangent), act_own, act_other), after=(signal,), flops=unit * hidden,
    )
    low, km, state, norm, raw, *rest = near_back
    choose_q, choose_k, lanes, mixed, act_own, act_other = rest
    at += whole
    sent, grad_resid, gain_ffn_part = call(
        grad_resid_kernel,
        (near(OWN, model), near(OWN, model, dtype=f32), near(8, model, dtype=f32)),
        (mine, resid, inv_ffn, near_top, near_gain, *parts), after=(grads,),
    )
    pieces = head_pieces(sent)
    packed, wide, top, grad_mixed, grad_num, grad_den = call(
        mixed_back_kernel,
        (
            near(HEADS, PACKED, 128), near(HEADS, PACKED + EDGE, 128), near(ROWS, model), near(ROWS, width), near(ROWS, width),
            near(HEADS, ROWS, 1, dtype=f32),
        ),
        (
            *[pieces[i] for i in (0, 3, 1, 2, 4, 7, 5, 6)], *near_mixed, probs_first, keys, values,
            halo, queries,
        ),
        starts=starts, flops=unit * 300,
    )
    gq, gk, gv, grads, normed = call(
        window_back_kernel,
        (
            near(ROWS, width), near(ROWS, width, dtype=f32),
            near(ROWS, width, dtype=f32), far(model, width, first=at, onto=grads, **place),
            Stage(normed_far),
        ),
        (grad_mixed, probs_first, probs, keys, values, halo, queries, top, mixed),
        flops=unit * 300, scratch=[pltpu.VMEM((ROWS + WIN, width), f32)] * 2,
    )
    sums = exclusive_parts(packed, True, after=(gq,), wide=wide)
    gfeat, gv, gkf, left, right, grads = call(
        linear_back_kernel,
        (
            near(ROWS, 128, dtype=f32), near(ROWS, width, dtype=f32),
            near(HEADS, ROWS, LANES, dtype=f32), near(ROWS, HEADS * LANES, dtype=f32),
            near(ROWS, HEADS * LANES, dtype=f32),
            far(model, width, first=at + width, onto=grads, **place),
        ),
        (
            grad_num, grad_den, values, low, km, near_mixed[3], state, norm, raw, choose_q, choose_k,
            lanes, gv, normed, gq,
        ),
        starts=starts, after=(sums[0],), flops=unit * 300,
    )
    gkw, gvw, gf, grads = call(
        keys_back_kernel,
        (
            near(ROWS, width), near(ROWS, width), near(ROWS, 128),
            far(model, 2 * width + 128, first=at + 2 * width, onto=grads, **place),
        ),
        (
            *sums, values, km, gkf, gk, gv, left, right, choose_k, lanes, gfeat, normed, tail,
        ),
        starts=starts, flops=unit * 1400,
    )
    grads_sum = lax.psum_scatter(grads, "seq", scatter_dimension=0, tiled=True)
    other, own, gains = call(
        normed_back_kernel, (near(half, model), near(half, model), near(2, model, dtype=f32)),
        (
            gq, gkw, gvw, gf, win_query, win_key, value_proj, feat, inputs, inv_mix, gain_ffn_part,
        ),
        after=(grads,),
        flops=unit * 900,
    )
    mine, parts, signal = head_quarters(own, other)
    other, own = call(
        ffn_out_kernel, (near(half, model), near(half, model)), (act_own, act_other, down_proj),
        after=(signal,), flops=unit * hidden,
    )
    out_mine, out_parts, signal = head_quarters(own, other)
    gains = gains_sum(gains)
    (sent,) = call(
        grad_x_kernel, (near(2 * OWN, model),),
        (mine, own_part(inputs), grad_resid, gain_mix, resid_far, out_mine, *parts, *out_parts),
        after=(gains,),
    )
    pieces = head_pieces(sent)
    output, grad_x = call(
        grad_x_out_kernel, (far(ROWS, model), far(ROWS, model, dtype=f32)), pieces,
    )
    grad_gate_t, grad_up_t, grad_down, grad_out, *rest = call(
        grads_out_kernel,
        (far(hidden, 128, dtype=f32),) * 3 + (far(width, 128, dtype=f32),)
        + (far(128, width, dtype=f32),) * 3 + (far(32, 128, dtype=f32),) * 2,
        (columns(grads_sum, 0, 2 * hidden), columns(grads_sum, 2 * hidden, grads_sum.shape[1])),
        after=(grad_x,),
    )
    grad_wq, grad_wk, grad_wv, grad_fq_t, grad_fk_t = rest
    return (
        output,
        grad_x,
        gains[0],
        grad_fq_t.T,
        grad_fk_t.T,
        grad_wq,
        grad_wk,
        grad_wv,
        grad_out,
        gains[1],
        grad_gate_t.T,
        grad_up_t.T,
        grad_down,
    )


def solution(mesh):
    placed = (
        P("seq", None),
        P(),
        P(None, "head"),
        P(None, "head"),
        P(None, "head"),
        P(None, "head"),
        P(None, "head"),
        P("head", None),
        P(),
        P(None, "head"),
        P(None, "head"),
        P("head", None),
        P(),
        P("seq", None),
    )
    return jax.shard_map(
        shards,
        mesh=mesh,
        in_specs=placed,
        out_specs=(
            P("seq", None),
            P("seq", None),
            P("seq"),
            P("seq", "head"),
            P("seq", "head"),
            P("seq", "head"),
            P("seq", "head"),
            P("seq", "head"),
            P("head", "seq"),
            P("seq"),
            P("seq", "head"),
            P("seq", "head"),
            P("head", "seq"),
        ),
        check_vma=False,
    )
```

```python
import functools
import math

import jax
import jax.numpy as jnp
import numpy as np
from jax import lax
from jax.experimental import pallas as pl
from jax.experimental.pallas import tpu as pltpu
from jax.sharding import PartitionSpec as P

F = 16
VALUE_WIDTH = 128
WIN = 64
EPS = 1e-05

HEADS = 2
ROWS = 512
LANES = 256
FEATURES = 153
KEPT = 144
PACKED = 160
TILE = 128
EDGE = 2 * WIN
OWN = 64
f32 = jnp.float32
bf16 = jnp.bfloat16


def feature_tables():
    pairs = [(a, b) for a in range(F) for b in range(a, F)]
    count = len(pairs)
    choose = np.zeros((2, 2, 128, HEADS * LANES), np.float32)
    lanes = np.zeros((8, HEADS * LANES), np.float32)
    factor = F ** (-0.25)
    for head in range(HEADS):
        at = head * LANES
        for side in range(2):
            for first in (side * HEADS * F, 64, 96):
                row = first + head * F
                for lane, (a, b) in enumerate(pairs):
                    choose[side, 0, row + a, at + lane] = 1.0
                    choose[side, 1, row + b, at + lane] = 1.0
                for a in range(F):
                    choose[side, 0, row + a, at + count + a] = 1.0
        for lane, (a, b) in enumerate(pairs):
            lanes[2, at + lane] = factor * factor / math.sqrt(2.0)
            lanes[3, at + lane] = 1.0 if a == b else 2.0
        lanes[1, at + count : at + count + F + 1] = 1.0
        lanes[0, at + count + F] = 1.0
        lanes[2, at + count : at + count + F] = factor
        lanes[2, at + count + F] = 1.0
        lanes[3, at + count : at + count + F + 1] = 1.0
    lanes[4] = lanes[2] * lanes[3]
    return choose, lanes


def mm(a, b):
    return lax.dot_general(a, b, (((1,), (0,)), ((), ())), preferred_element_type=f32)


def mm_nt(a, b):
    return lax.dot_general(a, b, (((1,), (1,)), ((), ())), preferred_element_type=f32)


def mm_tn(a, b):
    return lax.dot_general(a, b, (((0,), (0,)), ((), ())), preferred_element_type=f32)


def low_pair(part):
    high = part.astype(bf16)
    return high, (part - high.astype(f32)).astype(bf16)


class Place:

    def __init__(self, starts):
        me, seq = lax.axis_index("head"), lax.axis_index("seq")
        self.base = seq * ROWS
        self.x, self.z = lax.shift_right_logical(seq, 2), lax.bitwise_and(seq, 3)
        self.y, self.core = lax.shift_right_logical(me, 1), lax.bitwise_and(me, 1)
        self.loaded = starts

    def starts(self):
        return [self.loaded[0, i] for i in range(4)]

    def rows(self, distance, other=False):
        quarter = lax.bitwise_and(self.y + distance, 3)
        core = 1 - self.core if other else self.core
        return pl.ds(pl.multiple_of(quarter * (2 * OWN) + core * OWN, OWN), OWN)


class Loaded:

    def __init__(self, ref, copies):
        self.ref, self.copies = ref, list(copies)
        self.shape = ref.shape

    def part(self, index):
        if self.copies and self.copies[index] is not None:
            self.copies[index].wait()
            self.copies[index] = None

    def ready(self):
        for index in range(len(self.copies)):
            self.part(index)

    def __getitem__(self, index):
        self.ready()
        return self.ref[index]


class Stored:

    def __init__(self, ref, copies):
        self.ref, self.copies, self.sent = ref, copies, set()
        self.shape, self.dtype = ref.shape, ref.dtype

    def __getitem__(self, index):
        return self.ref[index]

    def __setitem__(self, index, value):
        self.ref[index] = value

    def send(self, part=None):
        for index in range(len(self.copies)) if part is None else (part,):
            if index not in self.sent:
                self.copies[index].start()
                self.sent.add(index)


def doc_of(info, position):
    starts = info.starts()
    count = (position >= starts[0]).astype(jnp.int32)
    for start in starts[1:]:
        count = count + (position >= start).astype(jnp.int32)
    return count


def column_positions(info, first, count):
    return info.base + first + lax.broadcasted_iota(jnp.int32, (count, 1), 0)


def row_positions(info, first, count):
    return info.base + first + lax.broadcasted_iota(jnp.int32, (1, count), 1)


def prefix_mask(info):
    before = doc_of(info, info.base - 1)
    same = doc_of(info, column_positions(info, 0, ROWS)) == before
    return (same & (info.base > 0)).astype(f32)


def tail_mask(info):
    last = doc_of(info, info.base + ROWS - 1)
    return (doc_of(info, column_positions(info, 0, ROWS)) == last).astype(f32)


def factors(raw, side, choose_ref, lanes_ref):
    high, rest = low_pair(raw)
    high, rest = high.astype(f32), rest.astype(f32)
    left = raw - high - rest
    at = side * HEADS * F
    lane = lax.broadcasted_iota(jnp.int32, (1, 128), 1)
    parts = jnp.where(lane < 96, pltpu.roll(rest, 64 - at, 1), pltpu.roll(left, 96 - at, 1))
    parts = jnp.where(lane < 64, high, parts).astype(bf16)
    return [mm(parts, choose_ref[i]) + lanes_ref[i : i + 1, :] for i in range(2)]


def feature_back(gradient, left, right, choose_ref):
    first = mm_nt((gradient * right).astype(bf16), choose_ref[0])
    return first + mm_nt((gradient * left).astype(bf16), choose_ref[1])


def write_packed(packed_ref, head, state, norm):
    packed_ref[head, 0:KEPT, :] = state[:KEPT].astype(bf16)
    row = lax.broadcasted_iota(jnp.int32, (16, 128), 0) + (KEPT - FEATURES)
    high = norm.astype(bf16).astype(f32)
    rest = norm - high
    tile = jnp.where(row == 0, high[:, :128], state[KEPT:PACKED])
    tile = jnp.where(row == 1, high[:, 128:], tile)
    tile = jnp.where(row == 2, rest[:, :128], tile)
    tile = jnp.where(row == 3, rest[:, 128:], tile)
    packed_ref[head, KEPT:PACKED, :] = tile.astype(bf16)


def read_total(before_ref, got_refs, head):
    total = before_ref[head]
    for ref in got_refs:
        total = total + ref[head, 0:PACKED, :].astype(f32)
    state = jnp.concatenate(
        [total, jnp.zeros((LANES - PACKED, VALUE_WIDTH), f32)], axis=0
    ).astype(bf16)
    rows = [total[FEATURES + i : FEATURES + i + 1] for i in range(4)]
    return state, jnp.concatenate([rows[0] + rows[2], rows[1] + rows[3]], axis=1)


def head_lanes(head):
    return slice(head * VALUE_WIDTH, (head + 1) * VALUE_WIDTH)


def window_rows(own_ref, halo_ref, which, head, tile):
    first, lanes = tile * TILE, head_lanes(head)
    if tile == 0:
        after = halo_ref.shape[1] - EDGE + which * WIN
        halo = halo_ref[head, after : after + WIN, :]
        return jnp.concatenate([halo, own_ref[0:TILE, lanes]], axis=0)
    return own_ref[first - WIN : first + TILE, lanes]


def window_tile(info, head, tile, queries, key_rows, value_rows):
    first = tile * TILE
    query_at = column_positions(info, first, TILE)
    key_at = row_positions(info, first - WIN, TILE + WIN)
    near_by = (
        (key_at <= query_at)
        & (query_at - key_at < WIN)
        & (doc_of(info, query_at) == doc_of(info, key_at))
        & (key_at >= 0)
    )
    logits = mm_nt(queries, key_rows) * VALUE_WIDTH ** (-0.5)
    logits = jnp.where(near_by, logits, -1e30)
    exps = jnp.exp(logits - jnp.max(logits, axis=-1, keepdims=True))
    probs = exps / jnp.sum(exps, axis=-1, keepdims=True)
    return probs, mm(probs.astype(bf16), value_rows)


class Near:
    near = True

    def __init__(self, arrays, dims=None, places=None, parts=1):
        self.arrays = [
            a.arrays[0] if isinstance(a, Near) else a
            for a in (arrays if isinstance(arrays, (list, tuple)) else [arrays])
        ]
        self.dims = tuple(dims or self.arrays[0].shape)
        self.dtype = self.arrays[0].dtype
        self.places, self.parts = places, parts

    def copies(self, info, refs, buffer):
        if self.places is None:
            return pieces_of(refs[0], buffer, self.parts)
        return self.places(info, refs, buffer)

    def count(self):
        return self.parts if self.places is None else self.places(None)

    def copied(self):
        return self.places is not None


class Far(Near):
    near = False

    def copied(self):
        return True


class Out:

    def __init__(self, *dims, dtype=bf16, near=False, far=False, parts=1, width=None, first=0, onto=None):
        self.dims, self.dtype, self.parts = dims, dtype, parts
        self.near, self.far = near, far
        self.whole = dims if width is None else (dims[0], width)
        self.first, self.onto = first, onto

    def shapes(self):
        near = [jax.ShapeDtypeStruct(self.dims, self.dtype)] * self.near
        return near + [pltpu.HBM(self.whole, self.dtype)] * self.far

    def spaces(self):
        return [pltpu.VMEM] * self.near + [pltpu.HBM] * self.far

    def copies(self, buffer, target):
        if self.whole != self.dims:
            target = target.at[:, self.first : self.first + self.dims[1]]
        return pieces_of(buffer, target, self.parts)


class Stage:
    near, far, parts, onto = True, False, 1, None

    def __init__(self, source):
        self.source = source if isinstance(source, Far) else Far(source)
        self.dims, self.dtype = self.source.dims, self.source.dtype

    def shapes(self):
        return [jax.ShapeDtypeStruct(self.dims, self.dtype)]

    def spaces(self):
        return [pltpu.VMEM]


class Export:
    near, far, parts, onto = False, True, 1, None

    def __init__(self, source, dims=None, view=None):
        self.source, self.view = source, view
        self.dims, self.dtype = tuple(dims or source.dims), source.dtype

    def shapes(self):
        return [pltpu.HBM(self.dims, self.dtype)]

    def spaces(self):
        return [pltpu.HBM]

    def copies(self, ref, target):
        return [(ref if self.view is None else self.view(ref), target)]


def near(*dims, dtype=bf16):
    return Out(*dims, dtype=dtype, near=True)


def far(*dims, dtype=bf16, parts=1, **columns):
    return Out(*dims, dtype=dtype, far=True, parts=parts, **columns)


def both(*dims, dtype=bf16):
    return Out(*dims, dtype=dtype, near=True, far=True)


def pieces_of(source, target, parts):
    if parts == 1:
        return [(source, target)]
    count = source.shape[0] // parts
    return [
        (source.at[i * count : (i + 1) * count], target.at[i * count : (i + 1) * count])
        for i in range(parts)
    ]


def in_hbm(array):
    return pltpu.with_memory_space_constraint(array, pltpu.HBM)


def call(body, results, operands, starts=None, after=(), flops=0, scratch=(), megabytes=28):
    operands = [o if isinstance(o, Near) else Far(o) for o in operands]
    waits = [pl.ANY if isinstance(o, Near) else pltpu.HBM for o in after]
    after = [o.arrays[0] if isinstance(o, Near) else in_hbm(o) for o in after]
    staged = [o for o in results if isinstance(o, Stage)]
    inputs = operands + [o.source for o in results if isinstance(o, (Stage, Export))]
    arrays = [a for o in inputs for a in o.arrays]
    copied = [o for o in operands if o.copied()]
    held = [o for o in results if not o.near and not isinstance(o, Export)]
    count_out = sum(o.near + o.far for o in results)
    onto = {o: i for i, o in enumerate(results) if o.onto is not None}
    aliases = {len(arrays) + len(after) + i: onto[o] for i, o in enumerate(onto)}
    waits += [pltpu.HBM] * len(onto)
    after += [in_hbm(o.onto) for o in onto]
    moves = sum(o.count() for o in copied) + sum(o.source.count() for o in staged) + sum(o.parts for o in results if o.far)
    named = starts is not None

    def kernel(*refs):
        sources, refs = refs[: len(arrays)], refs[len(arrays) + len(after) :]
        named_ref, refs = (refs[0], refs[1:]) if named else (None, refs)
        targets, rest = list(refs[:count_out]), refs[count_out:]
        buffers, rest = list(rest[: len(copied)]), rest[len(copied) :]
        leaving, rest = list(rest[: len(held)]), rest[len(held) :]
        sems, rest = rest[0], rest[1:]
        marks = None
        if named:
            copy = pltpu.make_async_copy(named_ref, rest[0], sems.at[moves])
            copy.start()
            marks, rest = Loaded(rest[0], [copy]), rest[1:]
        info = Place(marks)
        loaded, at, sem = [], 0, 0

        def copies_of(pairs):
            nonlocal sem
            sem += len(pairs)
            return [
                pltpu.make_async_copy(source, target, sems.at[sem - len(pairs) + i])
                for i, (source, target) in enumerate(pairs)
            ]

        for operand in operands:
            own = sources[at : at + len(operand.arrays)]
            at += len(own)
            if not operand.copied():
                loaded.append(Loaded(own[0], []))
                continue
            buffer = buffers.pop(0)
            loaded.append(Loaded(buffer, copies_of(operand.copies(info, own, buffer))))
            for copy in loaded[-1].copies:
                copy.start()
        stored, staging = [], []
        for result in results:
            if isinstance(result, Export):
                staging += copies_of(result.copies(sources[at], targets.pop(0)))
                at += 1
                continue
            buffer = targets.pop(0) if result.near else leaving.pop(0)
            if isinstance(result, Stage):
                own = sources[at : at + len(result.source.arrays)]
                at += len(own)
                staging += copies_of(result.source.copies(info, own, buffer))
                continue
            target = targets.pop(0) if result.far else None
            pairs = result.copies(buffer, target) if result.far else []
            stored.append(Stored(buffer, copies_of(pairs)))
        for copy in staging:
            copy.start()
        body(info, *loaded, *stored, *rest)
        for copy in staging:
            copy.wait()
        for item in loaded + ([marks] if named else []):
            item.ready()
        for item in stored:
            item.send()
        for item in stored:
            for copy in item.copies:
                copy.wait()

    spaces = [pltpu.VMEM if o.near else pltpu.HBM for o in inputs for _ in o.arrays]
    placed = [a if space is pltpu.VMEM else in_hbm(a) for a, space in zip(arrays, spaces)]
    spaces += waits + [pltpu.HBM] * named
    moved = sum(a.size * a.dtype.itemsize for a in arrays)
    moved += sum(math.prod(o.dims) * jnp.dtype(o.dtype).itemsize for o in results)
    given = pl.pallas_call(
        kernel,
        name=getattr(body, "func", body).__name__,
        out_shape=tuple(s for o in results for s in o.shapes()),
        in_specs=[pl.BlockSpec(memory_space=space) for space in spaces],
        out_specs=tuple(pl.BlockSpec(memory_space=s) for o in results for s in o.spaces()),
        input_output_aliases=aliases,
        scratch_shapes=[pltpu.VMEM(o.dims, o.dtype) for o in copied]
        + [pltpu.VMEM(o.dims, o.dtype) for o in held]
        + [pltpu.SemaphoreType.DMA((max(1, moves + named),))]
        + [pltpu.SMEM((1, 4), jnp.int32)] * named
        + list(scratch),
        compiler_params=pltpu.CompilerParams(vmem_limit_bytes=megabytes * 2**20),
        cost_estimate=pl.CostEstimate(flops=0, bytes_accessed=1024, transcendentals=0),
    )(*placed, *after, *([in_hbm(starts)] if named else []))
    given, answer = list(given), []
    for result in results:
        item = (Near(given.pop(0)),) if result.near else ()
        item += (given.pop(0),) if result.far else ()
        answer.append(item if len(item) == 2 else item[0])
    return answer


def moved_by(array, axis, route):
    array = array.arrays[0] if isinstance(array, Near) else array
    return Near(lax.ppermute(array, axis, route))


def feature_weights(feat_query_t, feat_key_t):
    def places(info, sources=None, buffer=None):
        if info is None:
            return 2
        return [(sources[0], buffer.at[0:32]), (sources[1], buffer.at[32:64])]

    return Far([feat_query_t, feat_key_t], (128, feat_query_t.shape[1]), places)


def own_part(block):
    def places(info, sources=None, buffer=None):
        if info is None:
            return 1
        return [(sources[0].at[info.rows(0)], buffer)]

    return Far(block, (OWN, block.shape[1]), places)


def keys_kernel(
    info, x_ref, gain_ref, key_ref, value_ref, feat_ref, choose_ref, lanes_ref,
    normed_ref, inv_ref, raw_ref, keys_ref, values_ref, km_ref, packed_ref, wide_ref,
):
    gain = gain_ref[...]

    def norm_rows(part):
        for i in range(2):
            rows = slice(part * 128 + i * 64, part * 128 + i * 64 + 64)
            x = x_ref.ref[rows, :].astype(f32)
            inv = lax.rsqrt(jnp.mean(x * x, axis=-1, keepdims=True) + EPS)
            inv_ref[rows, :] = inv
            normed_ref[rows, :] = (x * inv * gain).astype(bf16)

    x_ref.part(0)
    norm_rows(0)
    x_ref.part(1)
    norm_rows(1)
    for ref in (x_ref, feat_ref, key_ref, value_ref, choose_ref, lanes_ref):
        ref.ready()
    feat_ref.ref[64:128, :] = jnp.zeros((64, feat_ref.shape[1]), bf16)
    half = ROWS // 2
    features = []
    for first in (0, half):
        rows = slice(first, first + half)
        normed = normed_ref[rows, :]
        raw = mm_nt(normed, feat_ref[...])
        raw_ref[rows, :] = raw
        if first == 0:
            norm_rows(2)
            norm_rows(3)
        keys_ref[rows, :] = mm(normed, key_ref[...]).astype(bf16)
        values_ref[rows, :] = mm(normed, value_ref[...]).astype(bf16)
        left, right = factors(raw, 1, choose_ref, lanes_ref)
        part = (left * right * lanes_ref[2:3, :]).astype(bf16)
        features.append((part.astype(f32) * lanes_ref[3:4, :]).astype(bf16))
    features = jnp.concatenate(features, axis=0)
    values = values_ref[...]
    for head in range(HEADS):
        km_ref[head] = features[:, head * LANES : (head + 1) * LANES]
    tail = tail_mask(info)
    for head in range(HEADS):
        own = features[:, head * LANES : (head + 1) * LANES]
        lanes = head_lanes(head)
        kept = (values[:, lanes].astype(f32) * tail).astype(bf16)
        state = mm_tn(own, kept)
        norm = jnp.sum(own.astype(f32) * tail, axis=0, keepdims=True)
        write_packed(packed_ref, head, state, norm)
        wide_ref[head, 0:PACKED, :] = packed_ref[head]
        wide_ref[head, PACKED : PACKED + WIN, :] = keys_ref[ROWS - WIN :, lanes]
        wide_ref[head, PACKED + WIN :, :] = values[ROWS - WIN :, lanes]


def local_kernel(
    info, raw_ref, choose_ref, lanes_ref, values_ref, km_ref, normed_ref, query_ref,
    qf_ref, low_ref, num_ref, den_ref, queries_ref,
):
    left, right = factors(raw_ref[...], 0, choose_ref, lanes_ref)
    features = (left * right * lanes_ref[2:3, :]).astype(bf16)
    for head in range(HEADS):
        qf_ref[head] = features[:, head * LANES : (head + 1) * LANES]
    half = ROWS // 2
    causal = []
    for block in range(2):
        query_at = column_positions(info, block * half, half)
        key_at = row_positions(info, 0, (block + 1) * half)
        causal.append((query_at >= key_at) & (doc_of(info, query_at) == doc_of(info, key_at)))
    for head in range(HEADS):
        for block in range(2):
            first, reach = block * half, (block + 1) * half
            own = qf_ref[head, first:reach, :]
            weights = jnp.where(causal[block], mm_nt(own, km_ref[head, :reach, :]), 0.0)
            den_ref[head, first:reach, :] = jnp.sum(weights, axis=-1, keepdims=True)
            weights = weights.astype(bf16)
            low_ref[head, first:reach, 0:reach] = weights
            num_ref[first:reach, head_lanes(head)] = mm(
                weights, values_ref[:reach, head_lanes(head)]
            )
    queries_ref[...] = mm(normed_ref[...], query_ref[...]).astype(bf16)


def window_kernel(
    info, queries_ref, keys_ref, values_ref, probs_ref, window_ref,
):
    queries = queries_ref[...]
    for head in range(HEADS):
        lanes = head_lanes(head)
        for tile in range(1, ROWS // TILE):
            rows = slice(tile * TILE, (tile + 1) * TILE)
            probs, result = window_tile(
                info, head, tile, queries[rows, lanes],
                window_rows(keys_ref, None, 0, head, tile), window_rows(values_ref, None, 1, head, tile),
            )
            probs_ref[head, tile - 1] = probs
            window_ref[rows, lanes] = result


def by_distance(ref, info, other):
    return jnp.concatenate([ref[info.rows(d, other), :] for d in range(4)], axis=0)


def mixed_kernel(
    info, before_ref, got1_ref, got2_ref, got3_ref, qf_ref, num_ref, den_ref, window_ref, out_ref,
    queries_ref, keys_ref, values_ref,
    mixed_ref, linear_ref, total_den_ref, state_ref, norm_ref, probs_ref, other_ref,
):
    use = prefix_mask(info)
    for head in range(HEADS):
        lanes = head_lanes(head)
        state, norm = read_total(before_ref, (got1_ref, got2_ref, got3_ref), head)
        state_ref[head] = state
        norm_ref[head] = jnp.broadcast_to(norm, (8, LANES))
        features = qf_ref[head]
        inter = mm(features, state) * use
        den = jnp.sum(features.astype(f32) * norm, axis=-1, keepdims=True) * use + den_ref[head]
        total_den_ref[head] = den
        linear = (inter + num_ref[:, lanes]) / den
        linear_ref[:, lanes] = linear
        probs, window = window_tile(
            info, head, 0, queries_ref[0:TILE, lanes],
            window_rows(keys_ref, got1_ref, 0, head, 0), window_rows(values_ref, got1_ref, 1, head, 0),
        )
        probs_ref[head] = probs
        mixed_ref[0:TILE, lanes] = (linear[0:TILE] + window).astype(bf16)
        mixed_ref[TILE:, lanes] = (linear[TILE:] + window_ref[TILE:, lanes]).astype(bf16)
    other_ref[...] = mm(by_distance(mixed_ref, info, True), out_ref[...]).astype(bf16)


def mixed_own_kernel(info, mixed_ref, out_ref, own_ref):
    own_ref[...] = mm(by_distance(mixed_ref, info, False), out_ref[...]).astype(bf16)


def quarters_kernel(info, own_ref, got_ref, *out_refs):
    out_refs[4][...] = got_ref[0:16, 0:128]
    for d in (1, 2, 3, 0):
        rows = slice(d * OWN, (d + 1) * OWN)
        total = own_ref[rows, :].astype(f32) + got_ref[rows, :].astype(f32)
        out_refs[d][...] = total.astype(out_refs[d].dtype)
        out_refs[d].send()


def resid_kernel(
    info, mine_ref, x_ref, gain_ref, got1_ref, got2_ref, got3_ref, normed_ref, resid_ref, inv_ref
):
    resid = x_ref[...].astype(f32) + mine_ref[...]
    for ref in (got1_ref, got2_ref, got3_ref):
        resid = resid + ref[...].astype(f32)
    resid_ref[...] = resid
    inv = lax.rsqrt(jnp.mean(resid * resid, axis=-1, keepdims=True) + EPS)
    inv_ref[...] = inv
    normed_ref[...] = (resid * inv * gain_ref[...]).astype(bf16)


def grad_resid_kernel(
    info, mine_ref, resid_ref, inv_ref, top_ref, gain_ref, got1_ref, got2_ref, got3_ref,
    sent_ref, grad_ref, gains_ref,
):
    grad = mine_ref[...]
    for ref in (got1_ref, got2_ref, got3_ref):
        grad = grad + ref[...].astype(f32)
    resid = resid_ref[...]
    inv = inv_ref[...]
    grad_resid = top_ref[...].astype(f32) + norm_back(resid, inv, gain_ref[...], grad)
    sent_ref[...] = grad_resid.astype(bf16)
    sent_ref.send()
    grad_ref[...] = grad_resid
    gains_ref[0:1, :] = jnp.sum(grad * resid * inv, axis=0, keepdims=True)


def grad_x_kernel(
    info, mine_ref, x_ref, grad_resid_ref, gain_ref, resid_ref, out_ref, got1_ref, got2_ref, got3_ref,
    out1_ref, out2_ref, out3_ref, sent_ref,
):
    total = resid_ref[...] + out_ref[...]
    for ref in (out1_ref, out2_ref, out3_ref):
        total = total + ref[...].astype(f32)
    sent_ref[0:OWN, :] = total.astype(bf16)
    grad = mine_ref[...]
    for ref in (got1_ref, got2_ref, got3_ref):
        grad = grad + ref[...].astype(f32)
    x = x_ref[...].astype(f32)
    inv = lax.rsqrt(jnp.mean(x * x, axis=-1, keepdims=True) + EPS)
    sent_ref[OWN:, :] = (grad_resid_ref[...] + norm_back(x, inv, gain_ref[...], grad)).astype(bf16)


def norm_back(in_rows, inv_rms, gain, grad_normed):
    weighted = grad_normed * gain
    return inv_rms * weighted - in_rows * inv_rms**3 * jnp.mean(
        weighted * in_rows, axis=-1, keepdims=True
    )


def by_halves(block):
    def places(info, sources=None, buffer=None):
        if info is None:
            return 8
        return [
            (sources[0].at[info.rows(i % 4, other=i >= 4)], buffer.at[i * OWN : (i + 1) * OWN])
            for i in range(8)
        ]

    return Far(block, block.shape, places)


def grad_act_kernel(info, top_ref, down_ref, own_ref, other_ref):
    top = top_ref[...]
    half = ROWS // 2
    for first in range(0, down_ref.shape[0], 256):
        span = slice(first, min(first + 256, down_ref.shape[0]))
        grad = mm_nt(top, down_ref[span, :])
        own_ref[:, span] = grad[:half]
        other_ref[:, span] = grad[half:]


def ffn_rows(pieces, gate_ref, up_ref, grad_act_ref, normed_ref, act_ref, grad_gate_ref, grad_up_ref):
    normed = jnp.concatenate([piece[...] for piece in pieces], axis=0)
    normed_ref[...] = normed
    hidden = gate_ref.shape[0]
    for first in range(0, hidden, 256):
        span = slice(first, min(first + 256, hidden))
        gate = mm_nt(normed, gate_ref[span, :])
        up_value = mm_nt(normed, up_ref[span, :])
        sigmoid_gate = jax.nn.sigmoid(gate)
        silu_gate = gate * sigmoid_gate
        act_ref[:, span] = (silu_gate * up_value).astype(bf16)
        grad_act = grad_act_ref[:, span]
        grad_gate_ref[:, span] = (
            grad_act * up_value * sigmoid_gate * (1.0 + gate * (1.0 - sigmoid_gate))
        ).astype(bf16)
        grad_up_ref[:, span] = (grad_act * silu_gate).astype(bf16)


def ffn_own_kernel(info, p0, p3, p1, p2, gate_ref, up_ref, grad_act_ref, *out_refs):
    ffn_rows((p0, p3, p2, p1), gate_ref, up_ref, grad_act_ref, *out_refs)


def ffn_other_kernel(info, s0, s3, s1, s2, gate_ref, up_ref, grad_act_ref, back_ref, *out_refs):
    ffn_rows((s0, s3, s2, s1), gate_ref, up_ref, grad_act_ref, *out_refs)
    ffn_back_kernel(info, out_refs[2], out_refs[3], gate_ref, up_ref, back_ref)


def ffn_back_kernel(info, grad_gate_ref, grad_up_ref, gate_ref, up_ref, back_ref):
    grad_gate, grad_up = grad_gate_ref[...], grad_up_ref[...]
    for first in range(0, back_ref.shape[1], 512):
        span = slice(first, first + 512)
        part = mm(grad_gate, gate_ref[:, span]) + mm(grad_up, up_ref[:, span])
        back_ref[:, span] = part.astype(bf16)


def ffn_out_kernel(info, act_own_ref, act_other_ref, down_ref, other_ref, own_ref):
    for target, act_ref in ((other_ref, act_other_ref), (own_ref, act_own_ref)):
        act = act_ref[...]
        for first in range(0, target.shape[1], 512):
            span = slice(first, first + 512)
            target[:, span] = mm(act, down_ref[:, span]).astype(bf16)


def column_grads(pairs, out_ref, last=None):
    count = out_ref.shape[0] // 4
    for part in range(4):
        span = slice(part * count, (part + 1) * count)
        first = 0
        for i, (rows_refs, grads) in enumerate(pairs):
            rows_refs = rows_refs if isinstance(rows_refs, tuple) else (rows_refs,)
            grads = grads if isinstance(grads, tuple) else (grads,)
            total = sum(mm_tn(rows[:, span], grad) for rows, grad in zip(rows_refs, grads))
            if last is not None and i == len(pairs) - 1:
                total = total + last[span, :].astype(f32)
            end = first + total.shape[1]
            out_ref[span, first:end] = total.astype(bf16)
            first = end
        out_ref.send(part)


def gate_grads_kernel(
    info, own_ref, other_ref, gate_own_ref, gate_other_ref, up_own_ref, up_other_ref, out_ref
):
    rows = (own_ref, other_ref)
    gate = (gate_own_ref[...], gate_other_ref[...])
    up = (up_own_ref[...], up_other_ref[...])
    column_grads(((rows, gate), (rows, up)), out_ref)


class Rows:

    def __init__(self, ref, first, count):
        self.ref, self.rows = ref, slice(first, first + count)

    def __getitem__(self, index):
        return self.ref[self.rows, index[1]]


def down_grads_kernel(info, top_ref, act_own_ref, act_other_ref, out_ref, tail_ref):
    half, whole = ROWS // 2, out_ref.shape[1]
    rows = (Rows(top_ref, 0, half), Rows(top_ref, half, half))
    acts = (act_own_ref[...], act_other_ref[...])
    column_grads(((rows, tuple(act[:, :whole] for act in acts)),), out_ref)
    room = jnp.zeros((half, 128 - acts[0].shape[1] % 128), bf16)
    rest = [jnp.concatenate([act[:, whole:], room], axis=1) for act in acts]
    tail_ref[...] = sum(mm_tn(row[:, :], act) for row, act in zip(rows, rest)).astype(bf16)


def grad_x_out_kernel(info, p0, p1, p2, p3, s0, s1, s2, s3, output_ref, grad_ref):
    for i, piece in enumerate((p0, p1, p2, p3, s0, s1, s2, s3)):
        rows = info.rows(4 - i % 4, other=i >= 4)
        output_ref[rows, :] = piece[0:OWN, :]
        grad_ref[rows, :] = piece[OWN : 2 * OWN, :].astype(f32)


def window_tile_back(top, probs, key_rows, value_rows):
    grad_probs = mm_nt(top, value_rows)
    shared = jnp.sum(grad_probs * probs, axis=-1, keepdims=True)
    return (probs * (grad_probs - shared)).astype(bf16)


def mixed_back_kernel(
    info, p0, p3, p1, p2, s0, s3, s1, s2, out_ref, linear_ref, den_ref, qf_ref, probs0_ref, keys_ref,
    values_ref, halo_ref, queries_ref, packed_ref, wide_ref, top_ref, gm_ref, gnum_ref, gden_ref,
):
    for i, piece in enumerate((p0, p1, p2, p3, s0, s1, s2, s3)):
        top_ref[info.rows(4 - i % 4, other=i >= 4), :] = piece[...]
    grad_mixed = mm_nt(top_ref[...], out_ref[...]).astype(bf16)
    gm_ref[...] = grad_mixed
    use = prefix_mask(info)
    for head in range(HEADS):
        lanes = head_lanes(head)
        wide = grad_mixed[:, lanes].astype(f32)
        den = den_ref[head]
        grad_num = (wide / den).astype(bf16)
        gnum_ref[:, lanes] = grad_num
        grad_den = -jnp.sum(wide * linear_ref[:, lanes], axis=-1, keepdims=True) / den
        gden_ref[head] = grad_den
        features = qf_ref[head]
        used = (grad_num.astype(f32) * use).astype(bf16)
        state = mm_tn(features, used)
        norm = jnp.sum(features.astype(f32) * (grad_den * use), axis=0, keepdims=True)
        write_packed(packed_ref, head, state, norm)
        wide_ref[head, 0:PACKED, :] = packed_ref[head]
        top, probs = grad_mixed[0:TILE, lanes], probs0_ref[head]
        grad_logits = window_tile_back(
            top, probs, window_rows(keys_ref, halo_ref, 0, head, 0),
            window_rows(values_ref, halo_ref, 1, head, 0),
        )
        grad_keys = mm_tn(grad_logits, queries_ref[0:TILE, lanes]) * VALUE_WIDTH ** (-0.5)
        wide_ref[head, PACKED : PACKED + WIN, :] = grad_keys[0:WIN].astype(bf16)
        grad_values = mm_tn(probs.astype(bf16), top)
        wide_ref[head, PACKED + WIN :, :] = grad_values[0:WIN].astype(bf16)


def window_back_kernel(
    info, gm_ref, probs0_ref, probs_ref, keys_ref, values_ref, halo_ref, queries_ref,
    top_ref, mixed_ref, gq_ref, gk_ref, gv_ref, out_ref, key_acc, value_acc,
):
    column_grads(((top_ref, mixed_ref[...]),), out_ref)
    scale = VALUE_WIDTH ** (-0.5)
    key_acc[...] = jnp.zeros_like(key_acc)
    value_acc[...] = jnp.zeros_like(value_acc)
    for tile in range(ROWS // TILE):
        first = tile * TILE
        reach = slice(first, first + TILE + WIN)
        for head in range(HEADS):
            lanes = head_lanes(head)
            key_rows = window_rows(keys_ref, halo_ref, 0, head, tile)
            value_rows = window_rows(values_ref, halo_ref, 1, head, tile)
            top = gm_ref[first : first + TILE, lanes]
            probs = probs0_ref[head] if tile == 0 else probs_ref[head, tile - 1]
            grad_logits = window_tile_back(top, probs, key_rows, value_rows)
            gq_ref[first : first + TILE, lanes] = (mm(grad_logits, key_rows) * scale).astype(bf16)
            queries = queries_ref[first : first + TILE, lanes]
            key_acc[reach, lanes] += mm_tn(grad_logits, queries) * scale
            value_acc[reach, lanes] += mm_tn(probs.astype(bf16), top)
    gk_ref[...] = key_acc[WIN:, :]
    gv_ref[...] = value_acc[WIN:, :]


def linear_back_kernel(
    info, gnum_ref, gden_ref, values_ref, low_ref, km_ref, qf_ref, state_ref, norm_ref, raw_ref,
    choose_ref, choose_k_ref, lanes_ref, window_gv_ref, normed_ref, gq_ref,
    gfeat_ref, gv_ref, gkf_ref, left_ref, right_ref, out_ref,
):
    column_grads(((normed_ref, gq_ref[...]),), out_ref)
    use = prefix_mask(info)
    half = ROWS // 2
    grads = [[None, None], [None, None]]
    for head in range(HEADS):
        lanes = head_lanes(head)
        inter = mm_nt((gnum_ref[:, lanes].astype(f32) * use).astype(bf16), state_ref[head])
        inter = inter + (gden_ref[head] * use) * norm_ref[head, 0:1, :]
        for block in range(2):
            first, reach = block * half, (block + 1) * half
            query_at = column_positions(info, first, half)
            key_at = row_positions(info, 0, reach)
            causal = (query_at >= key_at) & (doc_of(info, query_at) == doc_of(info, key_at))
            grad_num = gnum_ref[first:reach, lanes]
            grad = mm_nt(grad_num, values_ref[:reach, lanes]) + gden_ref[head, first:reach, :]
            grad = jnp.where(causal, grad, 0.0).astype(bf16)
            grads[head][block] = mm(grad, km_ref[head, :reach, :]) + inter[first:reach]
            key_part = mm_tn(grad, qf_ref[head, first:reach, :])
            value_part = mm_tn(low_ref[head, first:reach, 0:reach], grad_num)
            if block == 0:
                gkf_ref[head, 0:half] = key_part
                gv_ref[0:half, lanes] = window_gv_ref[0:half, lanes] + value_part
            else:
                gkf_ref[head, 0:half] += key_part[0:half]
                gkf_ref[head, half:] = key_part[half:]
                gv_ref[0:half, lanes] += value_part[0:half]
                gv_ref[half:, lanes] = window_gv_ref[half:, lanes] + value_part[half:]
    left, right = factors(raw_ref[...], 0, choose_ref, lanes_ref)
    gradient = jnp.concatenate([jnp.concatenate(g, axis=0) for g in grads], axis=1)
    gradient = gradient * lanes_ref[2:3, :]
    gfeat_ref[...] = feature_back(gradient, left, right, choose_ref)
    left_ref[...], right_ref[...] = factors(raw_ref[...], 1, choose_k_ref, lanes_ref)


def keys_back_kernel(
    info, before_ref, got1_ref, got2_ref, got3_ref, values_ref, km_ref, gkf_ref, gk_ref, gv_ref,
    left_ref, right_ref, choose_ref, lanes_ref, gfeat_ref, normed_ref, tail_ref,
    gkw_ref, gvw_ref, gf_ref, out_ref,
):
    tail = tail_mask(info)
    inner = ROWS - WIN
    gkw_ref[0:inner, :] = gk_ref[0:inner, :].astype(bf16)
    gradients = []
    for head in range(HEADS):
        lanes = head_lanes(head)
        later, norm = read_total(before_ref, (got1_ref, got2_ref, got3_ref), head)
        kept = (values_ref[:, lanes].astype(f32) * tail).astype(bf16)
        gradients.append(gkf_ref[head] + mm_nt(kept, later) + tail * norm)
        grad_values = gv_ref[:, lanes] + mm(km_ref[head], later) * tail
        gvw_ref[0:inner, lanes] = grad_values[0:inner].astype(bf16)
        right = got1_ref[head, PACKED:, :].astype(f32)
        gkw_ref[inner:, lanes] = (gk_ref[inner:, lanes] + right[0:WIN]).astype(bf16)
        gvw_ref[inner:, lanes] = (grad_values[inner:] + right[WIN:]).astype(bf16)
    gradient = jnp.concatenate(gradients, axis=1) * lanes_ref[4:5, :]
    gradient = feature_back(gradient, left_ref[...], right_ref[...], choose_ref) + gfeat_ref[...]
    gf_ref[...] = gradient.astype(bf16)
    lane = lax.broadcasted_iota(jnp.int32, (1, 128), 1)
    beside = jnp.where(lane < 64, 0.0, pltpu.roll(gradient, 64, 1)).astype(bf16)
    column_grads(
        (
            (normed_ref, gkw_ref[...]), (normed_ref, gvw_ref[...]), (normed_ref, beside),
        ),
        out_ref, last=tail_ref,
    )


def normed_back_kernel(
    info, gq_ref, gkw_ref, gvw_ref, gf_ref, wq_ref, wk_ref, wv_ref, wf_ref, x_ref, inv_ref, gain_ffn_ref,
    other_ref, own_ref, gains_ref,
):
    wf_ref.ready()
    wf_ref.ref[64:128, :] = jnp.zeros((64, wf_ref.shape[1]), bf16)
    for target, other in ((other_ref, True), (own_ref, False)):
        grads = [by_distance(ref, info, other) for ref in (gq_ref, gkw_ref, gvw_ref, gf_ref)]
        scaled_by = by_distance(inv_ref, info, other)
        for piece in range(4):
            span = slice(piece * 512, (piece + 1) * 512)
            part = mm_nt(grads[0], wq_ref[span, :])
            part = part + mm_nt(grads[1], wk_ref[span, :])
            part = part + mm_nt(grads[2], wv_ref[span, :])
            part = part + mm(grads[3], wf_ref[:, span])
            target[:, span] = part.astype(bf16)
            x_rows = jnp.concatenate([x_ref[info.rows(d, other), span] for d in range(4)], axis=0)
            total = jnp.sum(part * (x_rows.astype(f32) * scaled_by), axis=0, keepdims=True)
            gains_ref[0:1, span] = total if other else total + gains_ref[0:1, span]
    gains_ref[1:2, :] = gain_ffn_ref[0:1, :]


def columns(block, first, last):
    def places(info, sources=None, buffer=None):
        return 1 if info is None else [(sources[0].at[:, first:last], buffer)]

    return Far(block, (block.shape[0], last - first), places)


def grads_out_kernel(
    info, both_ref, in_ref, gate_ref, up_ref, down_ref, out_ref, grad_q_ref, grad_k_ref, grad_v_ref,
    feat_query_ref, feat_key_ref,
):
    hidden, width = gate_ref.shape[0], out_ref.shape[0]
    whole = hidden // 128 * 128
    both = both_ref[...].astype(f32).T
    gate_ref[...] = both[0:hidden]
    gate_ref.send()
    up_ref[...] = both[hidden:]
    up_ref.send()
    down_ref[0:whole, :] = in_ref[:, 0:whole].astype(f32).T
    at = whole
    out_ref[...] = in_ref[:, at : at + width].astype(f32).T
    out_ref.send()
    for ref in (grad_q_ref, grad_k_ref, grad_v_ref):
        at += width
        ref[...] = in_ref[:, at : at + width].astype(f32)
        ref.send()
    tail = in_ref[:, at + width :].astype(f32).T
    down_ref[whole:, :] = tail[0 : hidden - whole]
    down_ref.send()
    feat_query_ref[...] = tail[64:96]
    feat_key_ref[...] = tail[96:128]


def total_of(refs):
    total = refs[0][...]
    for ref in refs[1:]:
        total = total + ref[...]
    return total


def gains_kernel(info, *refs):
    refs[-1][...] = total_of(refs[:-1])


def spread_kernel(info, *refs):
    total, out_ref = total_of(refs[:-1]), refs[-1]
    for i in range(out_ref.shape[0]):
        out_ref[i, 0:2, :] = total[:, i * 128 : (i + 1) * 128]
        out_ref[i, 2:, :] = jnp.zeros((6, 128), f32)


def gathered_sum_kernel(info, in_ref, out_ref):
    total = in_ref[0]
    for i in range(1, in_ref.shape[0]):
        total = total + in_ref[i]
    out_ref[...] = total


def along_y(distance):
    return [(i, (i + 2 * distance) % 8) for i in range(8)]


def sibling():
    return [(i, i ^ 1) for i in range(8)]


def along_x(distance):
    return [(i, (i + 4 * distance) % 16) for i in range(16)]


def along_z(distance):
    return [(4 * a + z, 4 * a + (z + distance) % 4) for a in range(4) for z in range(4)]


def head_quarters(own, other, after=()):
    got = moved_by(other, "head", sibling())
    width = own.dims[1]
    with jax.named_scope("quarters"):
        mine, *sent, token = call(
            quarters_kernel,
            [near(OWN, width, dtype=f32)] + [near(OWN, width)] * 3 + [near(16, 128)],
            (own, got), after=after,
        )
    parts = [moved_by(sent[d - 1], "head", along_y(d)) for d in (2, 1, 3)]
    return mine, parts, moved_by(token, "head", sibling())


def head_pieces(own):
    far_piece = moved_by(own, "head", along_y(2))
    pieces = [own, moved_by(own, "head", along_y(1)), far_piece, moved_by(own, "head", along_y(3))]
    return pieces + [moved_by(piece, "head", sibling()) for piece in pieces]


def gains_sum(gains):
    with jax.named_scope("gains"):
        (pair,) = call(
            gains_kernel, [near(*gains.dims, dtype=f32)], (gains, moved_by(gains, "head", sibling()))
        )
        parts = [pair] + [moved_by(pair, "head", along_y(d)) for d in (2, 1, 3)]
        (blocks,) = call(spread_kernel, [far(16, 8, 128, dtype=f32)], parts)
        blocks = lax.all_to_all(blocks, "seq", 0, 0)
        (total,) = call(gathered_sum_kernel, [far(8, 128, dtype=f32)], (blocks,))
    return total


def scan_kernel(reverse, info, own_ref, got1_ref, got2_ref, got3_ref, before_ref, *sent_refs):
    place_x, place_z = (3 - info.x, 3 - info.z) if reverse else (info.x, info.z)
    before = jnp.zeros(before_ref.shape, f32)
    for d, ref in enumerate((got1_ref, got2_ref, got3_ref), 1):
        before = before + ref[:, 0:PACKED, :].astype(f32) * (place_x >= d).astype(f32)
    before_ref[...] = before
    row = lax.broadcasted_iota(jnp.int32, (HEADS, 16, 128), 1) + (KEPT - FEATURES)
    sent = []
    for total in (before, before + own_ref[:, 0:PACKED, :].astype(f32)):
        tile = total[:, KEPT:]
        norm = tile + jnp.roll(tile, -2, axis=1)
        high = norm.astype(bf16).astype(f32)
        rest = jnp.roll(norm - high, 2, axis=1)
        norm = jnp.where(row < 0, tile, jnp.where(row < 2, high, jnp.where(row < 4, rest, 0.0)))
        sent.append((total[:, :KEPT], norm))
    for d, ref in enumerate(sent_refs, 1):
        with_own = (place_z + d < 4).astype(f32)
        for part, rows in ((0, slice(0, KEPT)), (1, slice(KEPT, PACKED))):
            less, more = sent[0][part], sent[1][part]
            ref[:, rows, :] = (more * with_own + less * (1.0 - with_own)).astype(bf16)
        if ref.shape[1] > PACKED:
            own, earlier = own_ref[:, PACKED:, :].astype(f32), got1_ref[:, PACKED:, :].astype(f32)
            ref[:, PACKED:, :] = (own * with_own + earlier * (1.0 - with_own)).astype(bf16)


def exclusive_parts(own, reverse, after=(), wide=None):
    sign = -1 if reverse else 1
    first = own if wide is None else wide
    got = [moved_by(first if d == 1 else own, "seq", along_x(sign * d)) for d in (1, 2, 3)]
    with jax.named_scope("scan"):
        before, *sent = call(
            functools.partial(scan_kernel, reverse),
            [near(*own.dims, dtype=f32), near(*first.dims), near(*own.dims), near(*own.dims)],
            (first, *got), after=after,
        )
    return [before] + [
        moved_by(sent[d - 1], "seq", along_z(sign * d)) for d in (1, 2, 3)
    ]


def shards(
    inputs,
    gain_mix,
    feat_query,
    feat_key,
    win_query,
    win_key,
    value_proj,
    out_proj,
    gain_ffn,
    gate_proj,
    up_proj,
    down_proj,
    document_starts,
    cotangent,
):
    choose, lanes = feature_tables()
    choose = jnp.asarray(choose, bf16)
    lanes = jnp.asarray(lanes, f32)
    choose_q, choose_k = choose[0], choose[1]
    feat = feature_weights(feat_query.T, feat_key.T)
    gain_mix = gain_mix.reshape(1, -1)
    gain_ffn = gain_ffn.reshape(1, -1)
    model = inputs.shape[1]
    width = HEADS * VALUE_WIDTH
    hidden = gate_proj.shape[1]
    half = ROWS // 2
    unit = 2 * ROWS * model
    starts = document_starts

    normed, inv_mix, raw, keys, values, km, packed, wide = call(
        keys_kernel,
        (
            near(ROWS, model), near(ROWS, 1, dtype=f32), near(ROWS, 128, dtype=f32),
            near(ROWS, width), near(ROWS, width), near(HEADS, ROWS, LANES),
            near(HEADS, PACKED, 128), near(HEADS, PACKED + EDGE, 128),
        ),
        (Far(inputs, parts=4), gain_mix, win_key, value_proj, feat, choose_k, lanes),
        starts=starts, flops=unit * 640,
    )
    qf, low, num, den, queries, near_out, normed_far, inv_mix, raw_far, keys_far, values_far, km_far = call(
        local_kernel,
        (
            near(HEADS, ROWS, LANES), near(HEADS, ROWS, ROWS), near(ROWS, width, dtype=f32),
            near(HEADS, ROWS, 1, dtype=f32), near(ROWS, width), Stage(out_proj), Export(normed),
            Export(inv_mix), Export(raw), Export(keys), Export(values), Export(km),
        ),
        (raw, choose_q, lanes, values, km, normed, win_query),
        starts=starts, flops=unit * 300,
    )
    sums = exclusive_parts(packed, False, after=(qf,), wide=wide)
    probs, window, qf_far, low = call(
        window_kernel,
        (
            near(HEADS, 3, TILE, TILE + WIN, dtype=f32),
            near(ROWS, width, dtype=f32), Export(qf), Export(low),
        ),
        (queries, keys, values),
        starts=starts, flops=unit * 400,
    )
    mixed, linear, total_den, state, norm, probs_first, other = call(
        mixed_kernel,
        (
            near(ROWS, width), near(ROWS, width, dtype=f32), near(HEADS, ROWS, 1, dtype=f32),
            near(HEADS, LANES, VALUE_WIDTH), near(HEADS, 8, LANES, dtype=f32),
            near(HEADS, TILE, TILE + WIN, dtype=f32), near(half, model),
        ),
        (*sums, qf, num, den, window, near_out, queries, keys, values),
        starts=starts, flops=unit * 300,
    )
    own, halo, *rest = call(
        mixed_own_kernel,
        (
            near(half, model),
            Export(sums[1], (HEADS, EDGE, 128), lambda ref: ref.at[:, PACKED:, :]),
            *map(Export, (mixed, linear, total_den, state, norm, probs_first, probs, queries)),
        ),
        (mixed, near_out), after=(other,), flops=unit * 100,
    )
    mixed, linear, total_den, state, norm, probs_first, probs, queries_far = rest
    mine, parts, signal = head_quarters(own, other)
    grad_act_own, grad_act_other, x_own, near_gain, near_gate, near_up = call(
        grad_act_kernel,
        (
            near(half, hidden, dtype=f32), near(half, hidden, dtype=f32), Stage(own_part(inputs)), Stage(gain_ffn),
            Stage(gate_proj.T), Stage(up_proj.T),
        ),
        (by_halves(cotangent), down_proj),
        after=(signal,), flops=unit * hidden,
    )
    own_normed, resid, inv_ffn = call(
        resid_kernel,
        (near(OWN, model), near(OWN, model, dtype=f32), near(OWN, 1, dtype=f32)),
        (mine, x_own, near_gain, *parts), after=(grad_act_own,),
    )
    pieces = head_pieces(own_normed)
    def ffn_half(body, pieces, grad_act, *more, after=()):
        order = [pieces[i] for i in (0, 3, 1, 2)]
        return call(
            body,
            (
                *more, near(half, model), near(half, hidden), near(half, hidden), near(half, hidden),
            ),
            (*order, near_gate, near_up, grad_act), after=after, flops=unit * 2 * hidden,
        )

    normed_own, act_own, gate_own, up_own = ffn_half(ffn_own_kernel, pieces[:4], grad_act_own)
    other, normed_other, act_other, gate_other, up_other = ffn_half(
        ffn_other_kernel, pieces[4:], grad_act_other, near(half, model), after=(gate_own,)
    )
    (own,) = call(
        ffn_back_kernel, (near(half, model),), (gate_own, up_own, near_gate, near_up),
        after=(other,), flops=unit * hidden,
    )
    mine, parts, signal = head_quarters(own, other)
    whole = hidden // 128 * 128
    place = dict(parts=4, width=2 * hidden + whole + 4 * width + 128)
    grads, resid_far, near_top, near_gain, *near_mixed = call(
        gate_grads_kernel,
        (
            far(model, 2 * hidden, **place), Export(resid), Stage(own_part(cotangent)),
            Stage(gain_ffn), Stage(out_proj), Stage(linear), Stage(total_den), Stage(qf_far),
            Stage(probs_first), Stage(probs), Stage(keys_far), Stage(values_far), Stage(halo),
            Stage(queries_far),
        ),
        (normed_own, normed_other, gate_own, gate_other, up_own, up_other),
        after=(signal,), flops=unit * 2 * hidden,
    )
    at = 2 * hidden
    *near_mixed, probs_first, probs, keys, values, halo, queries = near_mixed
    grads, tail, *near_back = call(
        down_grads_kernel,
        (
            far(model, whole, first=at, onto=grads, **place), near(model, 128), Stage(low),
            Stage(km_far),
            Stage(state), Stage(norm), Stage(raw_far), Stage(choose_q), Stage(choose_k),
            Stage(lanes), Stage(mixed), Export(act_own), Export(act_other),
        ),
        (by_halves(cotangent), act_own, act_other), after=(signal,), flops=unit * hidden,
    )
    low, km, state, norm, raw, *rest = near_back
    choose_q, choose_k, lanes, mixed, act_own, act_other = rest
    at += whole
    sent, grad_resid, gain_ffn_part = call(
        grad_resid_kernel,
        (near(OWN, model), near(OWN, model, dtype=f32), near(8, model, dtype=f32)),
        (mine, resid, inv_ffn, near_top, near_gain, *parts), after=(grads,),
    )
    pieces = head_pieces(sent)
    packed, wide, top, grad_mixed, grad_num, grad_den = call(
        mixed_back_kernel,
        (
            near(HEADS, PACKED, 128), near(HEADS, PACKED + EDGE, 128), near(ROWS, model), near(ROWS, width), near(ROWS, width),
            near(HEADS, ROWS, 1, dtype=f32),
        ),
        (
            *[pieces[i] for i in (0, 3, 1, 2, 4, 7, 5, 6)], *near_mixed, probs_first, keys, values,
            halo, queries,
        ),
        starts=starts, flops=unit * 300,
    )
    gq, gk, gv, grads, normed = call(
        window_back_kernel,
        (
            near(ROWS, width), near(ROWS, width, dtype=f32),
            near(ROWS, width, dtype=f32), far(model, width, first=at, onto=grads, **place),
            Stage(normed_far),
        ),
        (grad_mixed, probs_first, probs, keys, values, halo, queries, top, mixed),
        flops=unit * 300, scratch=[pltpu.VMEM((ROWS + WIN, width), f32)] * 2,
    )
    sums = exclusive_parts(packed, True, after=(gq,), wide=wide)
    gfeat, gv, gkf, left, right, grads = call(
        linear_back_kernel,
        (
            near(ROWS, 128, dtype=f32), near(ROWS, width, dtype=f32),
            near(HEADS, ROWS, LANES, dtype=f32), near(ROWS, HEADS * LANES, dtype=f32),
            near(ROWS, HEADS * LANES, dtype=f32),
            far(model, width, first=at + width, onto=grads, **place),
        ),
        (
            grad_num, grad_den, values, low, km, near_mixed[3], state, norm, raw, choose_q, choose_k,
            lanes, gv, normed, gq,
        ),
        starts=starts, after=(sums[0],), flops=unit * 300,
    )
    gkw, gvw, gf, grads = call(
        keys_back_kernel,
        (
            near(ROWS, width), near(ROWS, width), near(ROWS, 128),
            far(model, 2 * width + 128, first=at + 2 * width, onto=grads, **place),
        ),
        (
            *sums, values, km, gkf, gk, gv, left, right, choose_k, lanes, gfeat, normed, tail,
        ),
        starts=starts, flops=unit * 1400,
    )
    grads_sum = lax.psum_scatter(grads, "seq", scatter_dimension=0, tiled=True)
    other, own, gains = call(
        normed_back_kernel, (near(half, model), near(half, model), near(2, model, dtype=f32)),
        (
            gq, gkw, gvw, gf, win_query, win_key, value_proj, feat, inputs, inv_mix, gain_ffn_part,
        ),
        after=(grads,),
        flops=unit * 900,
    )
    mine, parts, signal = head_quarters(own, other)
    other, own = call(
        ffn_out_kernel, (near(half, model), near(half, model)), (act_own, act_other, down_proj),
        after=(signal,), flops=unit * hidden,
    )
    out_mine, out_parts, signal = head_quarters(own, other)
    gains = gains_sum(gains)
    (sent,) = call(
        grad_x_kernel, (near(2 * OWN, model),),
        (mine, own_part(inputs), grad_resid, gain_mix, resid_far, out_mine, *parts, *out_parts),
        after=(gains,),
    )
    pieces = head_pieces(sent)
    output, grad_x = call(
        grad_x_out_kernel, (far(ROWS, model), far(ROWS, model, dtype=f32)), pieces,
    )
    grad_gate_t, grad_up_t, grad_down, grad_out, *rest = call(
        grads_out_kernel,
        (far(hidden, 128, dtype=f32),) * 3 + (far(width, 128, dtype=f32),)
        + (far(128, width, dtype=f32),) * 3 + (far(32, 128, dtype=f32),) * 2,
        (columns(grads_sum, 0, 2 * hidden), columns(grads_sum, 2 * hidden, grads_sum.shape[1])),
        after=(grad_x,),
    )
    grad_wq, grad_wk, grad_wv, grad_fq_t, grad_fk_t = rest
    return (
        output,
        grad_x,
        gains[0],
        grad_fq_t.T,
        grad_fk_t.T,
        grad_wq,
        grad_wk,
        grad_wv,
        grad_out,
        gains[1],
        grad_gate_t.T,
        grad_up_t.T,
        grad_down,
    )


def solution(mesh):
    placed = (
        P("seq", None),
        P(),
        P(None, "head"),
        P(None, "head"),
        P(None, "head"),
        P(None, "head"),
        P(None, "head"),
        P("head", None),
        P(),
        P(None, "head"),
        P(None, "head"),
        P("head", None),
        P(),
        P("seq", None),
    )
    return jax.shard_map(
        shards,
        mesh=mesh,
        in_specs=placed,
        out_specs=(
            P("seq", None),
            P("seq", None),
            P("seq"),
            P("seq", "head"),
            P("seq", "head"),
            P("seq", "head"),
            P("seq", "head"),
            P("seq", "head"),
            P("head", "seq"),
            P("seq"),
            P("seq", "head"),
            P("seq", "head"),
            P("head", "seq"),
        ),
        check_vma=False,
    )
```

```python
import functools
import math

import jax
import jax.numpy as jnp
import numpy as np
from jax import lax
from jax.experimental import pallas as pl
from jax.experimental.pallas import tpu as pltpu
from jax.sharding import PartitionSpec as P

F = 16
VALUE_WIDTH = 128
WIN = 64
EPS = 1e-05

HEADS = 2
ROWS = 512
LANES = 256
FEATURES = 153
KEPT = 144
PACKED = 160
TILE = 128
EDGE = 2 * WIN
OWN = 64
f32 = jnp.float32
bf16 = jnp.bfloat16


def feature_tables():
    pairs = [(a, b) for a in range(F) for b in range(a, F)]
    count = len(pairs)
    choose = np.zeros((2, 2, 128, HEADS * LANES), np.float32)
    lanes = np.zeros((8, HEADS * LANES), np.float32)
    factor = F ** (-0.25)
    for head in range(HEADS):
        at = head * LANES
        for side in range(2):
            for first in (side * HEADS * F, 64, 96):
                row = first + head * F
                for lane, (a, b) in enumerate(pairs):
                    choose[side, 0, row + a, at + lane] = 1.0
                    choose[side, 1, row + b, at + lane] = 1.0
                for a in range(F):
                    choose[side, 0, row + a, at + count + a] = 1.0
        for lane, (a, b) in enumerate(pairs):
            lanes[2, at + lane] = factor * factor / math.sqrt(2.0)
            lanes[3, at + lane] = 1.0 if a == b else 2.0
        lanes[1, at + count : at + count + F + 1] = 1.0
        lanes[0, at + count + F] = 1.0
        lanes[2, at + count : at + count + F] = factor
        lanes[2, at + count + F] = 1.0
        lanes[3, at + count : at + count + F + 1] = 1.0
    lanes[4] = lanes[2] * lanes[3]
    return choose, lanes


def mm(a, b):
    return lax.dot_general(a, b, (((1,), (0,)), ((), ())), preferred_element_type=f32)


def mm_nt(a, b):
    return lax.dot_general(a, b, (((1,), (1,)), ((), ())), preferred_element_type=f32)


def mm_tn(a, b):
    return lax.dot_general(a, b, (((0,), (0,)), ((), ())), preferred_element_type=f32)


def low_pair(part):
    high = part.astype(bf16)
    return high, (part - high.astype(f32)).astype(bf16)


class Place:

    def __init__(self, starts):
        me, seq = lax.axis_index("head"), lax.axis_index("seq")
        self.base = seq * ROWS
        self.x, self.z = lax.shift_right_logical(seq, 2), lax.bitwise_and(seq, 3)
        self.y, self.core = lax.shift_right_logical(me, 1), lax.bitwise_and(me, 1)
        self.loaded = starts

    def starts(self):
        return [self.loaded[0, i] for i in range(4)]

    def rows(self, distance, other=False):
        quarter = lax.bitwise_and(self.y + distance, 3)
        core = 1 - self.core if other else self.core
        return pl.ds(pl.multiple_of(quarter * (2 * OWN) + core * OWN, OWN), OWN)


class Loaded:

    def __init__(self, ref, copies):
        self.ref, self.copies = ref, list(copies)
        self.shape = ref.shape

    def part(self, index):
        if self.copies and self.copies[index] is not None:
            self.copies[index].wait()
            self.copies[index] = None

    def ready(self):
        for index in range(len(self.copies)):
            self.part(index)

    def __getitem__(self, index):
        self.ready()
        return self.ref[index]


class Stored:

    def __init__(self, ref, copies):
        self.ref, self.copies, self.sent = ref, copies, set()
        self.shape, self.dtype = ref.shape, ref.dtype

    def __getitem__(self, index):
        return self.ref[index]

    def __setitem__(self, index, value):
        self.ref[index] = value

    def send(self, part=None):
        for index in range(len(self.copies)) if part is None else (part,):
            if index not in self.sent:
                self.copies[index].start()
                self.sent.add(index)


def doc_of(info, position):
    starts = info.starts()
    count = (position >= starts[0]).astype(jnp.int32)
    for start in starts[1:]:
        count = count + (position >= start).astype(jnp.int32)
    return count


def column_positions(info, first, count):
    return info.base + first + lax.broadcasted_iota(jnp.int32, (count, 1), 0)


def row_positions(info, first, count):
    return info.base + first + lax.broadcasted_iota(jnp.int32, (1, count), 1)


def prefix_mask(info):
    before = doc_of(info, info.base - 1)
    same = doc_of(info, column_positions(info, 0, ROWS)) == before
    return (same & (info.base > 0)).astype(f32)


def tail_mask(info):
    last = doc_of(info, info.base + ROWS - 1)
    return (doc_of(info, column_positions(info, 0, ROWS)) == last).astype(f32)


def factors(raw, side, choose_ref, lanes_ref):
    high, rest = low_pair(raw)
    high, rest = high.astype(f32), rest.astype(f32)
    left = raw - high - rest
    at = side * HEADS * F
    lane = lax.broadcasted_iota(jnp.int32, (1, 128), 1)
    parts = jnp.where(lane < 96, pltpu.roll(rest, 64 - at, 1), pltpu.roll(left, 96 - at, 1))
    parts = jnp.where(lane < 64, high, parts).astype(bf16)
    return [mm(parts, choose_ref[i]) + lanes_ref[i : i + 1, :] for i in range(2)]


def feature_back(gradient, left, right, choose_ref):
    first = mm_nt((gradient * right).astype(bf16), choose_ref[0])
    return first + mm_nt((gradient * left).astype(bf16), choose_ref[1])


def write_packed(packed_ref, head, state, norm):
    packed_ref[head, 0:KEPT, :] = state[:KEPT].astype(bf16)
    row = lax.broadcasted_iota(jnp.int32, (16, 128), 0) + (KEPT - FEATURES)
    high = norm.astype(bf16).astype(f32)
    rest = norm - high
    tile = jnp.where(row == 0, high[:, :128], state[KEPT:PACKED])
    tile = jnp.where(row == 1, high[:, 128:], tile)
    tile = jnp.where(row == 2, rest[:, :128], tile)
    tile = jnp.where(row == 3, rest[:, 128:], tile)
    packed_ref[head, KEPT:PACKED, :] = tile.astype(bf16)


def read_total(before_ref, got_refs, head):
    total = before_ref[head]
    for ref in got_refs:
        total = total + ref[head, 0:PACKED, :].astype(f32)
    state = jnp.concatenate(
        [total, jnp.zeros((LANES - PACKED, VALUE_WIDTH), f32)], axis=0
    ).astype(bf16)
    rows = [total[FEATURES + i : FEATURES + i + 1] for i in range(4)]
    return state, jnp.concatenate([rows[0] + rows[2], rows[1] + rows[3]], axis=1)


def head_lanes(head):
    return slice(head * VALUE_WIDTH, (head + 1) * VALUE_WIDTH)


def window_rows(own_ref, halo_ref, which, head, tile):
    first, lanes = tile * TILE, head_lanes(head)
    if tile == 0:
        after = halo_ref.shape[1] - EDGE + which * WIN
        halo = halo_ref[head, after : after + WIN, :]
        return jnp.concatenate([halo, own_ref[0:TILE, lanes]], axis=0)
    return own_ref[first - WIN : first + TILE, lanes]


def window_tile(info, head, tile, queries, key_rows, value_rows):
    first = tile * TILE
    query_at = column_positions(info, first, TILE)
    key_at = row_positions(info, first - WIN, TILE + WIN)
    near_by = (
        (key_at <= query_at)
        & (query_at - key_at < WIN)
        & (doc_of(info, query_at) == doc_of(info, key_at))
        & (key_at >= 0)
    )
    logits = mm_nt(queries, key_rows) * VALUE_WIDTH ** (-0.5)
    logits = jnp.where(near_by, logits, -1e30)
    exps = jnp.exp(logits - jnp.max(logits, axis=-1, keepdims=True))
    probs = exps / jnp.sum(exps, axis=-1, keepdims=True)
    return probs, mm(probs.astype(bf16), value_rows)


class Near:
    near = True

    def __init__(self, arrays, dims=None, places=None, parts=1):
        self.arrays = [
            a.arrays[0] if isinstance(a, Near) else a
            for a in (arrays if isinstance(arrays, (list, tuple)) else [arrays])
        ]
        self.dims = tuple(dims or self.arrays[0].shape)
        self.dtype = self.arrays[0].dtype
        self.places, self.parts = places, parts

    def copies(self, info, refs, buffer):
        if self.places is None:
            return pieces_of(refs[0], buffer, self.parts)
        return self.places(info, refs, buffer)

    def count(self):
        return self.parts if self.places is None else self.places(None)

    def copied(self):
        return self.places is not None


class Far(Near):
    near = False

    def copied(self):
        return True


class Out:

    def __init__(
        self, *dims, dtype=bf16, near=False, far=False, parts=1, width=None, first=0, onto=None, cut=None
    ):
        self.dims, self.dtype, self.parts, self.cut = dims, dtype, parts * (2 if cut else 1), cut
        self.near, self.far = near, far
        self.whole = dims if width is None else (dims[0], width)
        self.first, self.onto = first, onto

    def shapes(self):
        near = [jax.ShapeDtypeStruct(self.dims, self.dtype)] * self.near
        return near + [pltpu.HBM(self.whole, self.dtype)] * self.far

    def spaces(self):
        return [pltpu.VMEM] * self.near + [pltpu.HBM] * self.far

    def copies(self, buffer, target):
        if self.whole != self.dims:
            target = target.at[:, self.first : self.first + self.dims[1]]
        if not self.cut:
            return pieces_of(buffer, target, self.parts)
        sides = slice(0, self.cut), slice(self.cut, self.dims[1])
        return [
            pair
            for side in sides
            for pair in pieces_of(buffer.at[:, side], target.at[:, side], self.parts // 2)
        ]


class Stage:
    near, far, parts, onto = True, False, 1, None

    def __init__(self, source):
        self.source = source if isinstance(source, Far) else Far(source)
        self.dims, self.dtype = self.source.dims, self.source.dtype

    def shapes(self):
        return [jax.ShapeDtypeStruct(self.dims, self.dtype)]

    def spaces(self):
        return [pltpu.VMEM]


class Export:
    near, far, parts, onto = False, True, 1, None

    def __init__(self, source, dims=None, view=None):
        self.source, self.view = source, view
        self.dims, self.dtype = tuple(dims or source.dims), source.dtype

    def shapes(self):
        return [pltpu.HBM(self.dims, self.dtype)]

    def spaces(self):
        return [pltpu.HBM]

    def copies(self, ref, target):
        return [(ref if self.view is None else self.view(ref), target)]


def near(*dims, dtype=bf16):
    return Out(*dims, dtype=dtype, near=True)


def far(*dims, dtype=bf16, parts=1, **columns):
    return Out(*dims, dtype=dtype, far=True, parts=parts, **columns)


def both(*dims, dtype=bf16):
    return Out(*dims, dtype=dtype, near=True, far=True)


def pieces_of(source, target, parts):
    if parts == 1:
        return [(source, target)]
    count = source.shape[0] // parts
    return [
        (source.at[i * count : (i + 1) * count], target.at[i * count : (i + 1) * count])
        for i in range(parts)
    ]


def in_hbm(array):
    return pltpu.with_memory_space_constraint(array, pltpu.HBM)


def call(body, results, operands, starts=None, after=(), flops=0, scratch=(), megabytes=28):
    operands = [o if isinstance(o, Near) else Far(o) for o in operands]
    waits = [pl.ANY if isinstance(o, Near) else pltpu.HBM for o in after]
    after = [o.arrays[0] if isinstance(o, Near) else in_hbm(o) for o in after]
    staged = [o for o in results if isinstance(o, Stage)]
    inputs = operands + [o.source for o in results if isinstance(o, (Stage, Export))]
    arrays = [a for o in inputs for a in o.arrays]
    copied = [o for o in operands if o.copied()]
    held = [o for o in results if not o.near and not isinstance(o, Export)]
    count_out = sum(o.near + o.far for o in results)
    onto = {o: i for i, o in enumerate(results) if o.onto is not None}
    aliases = {len(arrays) + len(after) + i: onto[o] for i, o in enumerate(onto)}
    waits += [pltpu.HBM] * len(onto)
    after += [in_hbm(o.onto) for o in onto]
    moves = sum(o.count() for o in copied) + sum(o.source.count() for o in staged) + sum(o.parts for o in results if o.far)
    named = starts is not None

    def kernel(*refs):
        sources, refs = refs[: len(arrays)], refs[len(arrays) + len(after) :]
        named_ref, refs = (refs[0], refs[1:]) if named else (None, refs)
        targets, rest = list(refs[:count_out]), refs[count_out:]
        buffers, rest = list(rest[: len(copied)]), rest[len(copied) :]
        leaving, rest = list(rest[: len(held)]), rest[len(held) :]
        sems, rest = rest[0], rest[1:]
        marks = None
        if named:
            copy = pltpu.make_async_copy(named_ref, rest[0], sems.at[moves])
            copy.start()
            marks, rest = Loaded(rest[0], [copy]), rest[1:]
        info = Place(marks)
        loaded, at, sem = [], 0, 0

        def copies_of(pairs):
            nonlocal sem
            sem += len(pairs)
            return [
                pltpu.make_async_copy(source, target, sems.at[sem - len(pairs) + i])
                for i, (source, target) in enumerate(pairs)
            ]

        for operand in operands:
            own = sources[at : at + len(operand.arrays)]
            at += len(own)
            if not operand.copied():
                loaded.append(Loaded(own[0], []))
                continue
            buffer = buffers.pop(0)
            loaded.append(Loaded(buffer, copies_of(operand.copies(info, own, buffer))))
            for copy in loaded[-1].copies:
                copy.start()
        stored, staging = [], []
        for result in results:
            if isinstance(result, Export):
                staging += copies_of(result.copies(sources[at], targets.pop(0)))
                at += 1
                continue
            buffer = targets.pop(0) if result.near else leaving.pop(0)
            if isinstance(result, Stage):
                own = sources[at : at + len(result.source.arrays)]
                at += len(own)
                staging += copies_of(result.source.copies(info, own, buffer))
                continue
            target = targets.pop(0) if result.far else None
            pairs = result.copies(buffer, target) if result.far else []
            stored.append(Stored(buffer, copies_of(pairs)))
        for copy in staging:
            copy.start()
        body(info, *loaded, *stored, *rest)
        for copy in staging:
            copy.wait()
        for item in loaded + ([marks] if named else []):
            item.ready()
        for item in stored:
            item.send()
        for item in stored:
            for copy in item.copies:
                copy.wait()

    spaces = [pltpu.VMEM if o.near else pltpu.HBM for o in inputs for _ in o.arrays]
    placed = [a if space is pltpu.VMEM else in_hbm(a) for a, space in zip(arrays, spaces)]
    spaces += waits + [pltpu.HBM] * named
    moved = sum(a.size * a.dtype.itemsize for a in arrays)
    moved += sum(math.prod(o.dims) * jnp.dtype(o.dtype).itemsize for o in results)
    given = pl.pallas_call(
        kernel,
        name=getattr(body, "func", body).__name__,
        out_shape=tuple(s for o in results for s in o.shapes()),
        in_specs=[pl.BlockSpec(memory_space=space) for space in spaces],
        out_specs=tuple(pl.BlockSpec(memory_space=s) for o in results for s in o.spaces()),
        input_output_aliases=aliases,
        scratch_shapes=[pltpu.VMEM(o.dims, o.dtype) for o in copied]
        + [pltpu.VMEM(o.dims, o.dtype) for o in held]
        + [pltpu.SemaphoreType.DMA((max(1, moves + named),))]
        + [pltpu.SMEM((1, 4), jnp.int32)] * named
        + list(scratch),
        compiler_params=pltpu.CompilerParams(vmem_limit_bytes=megabytes * 2**20),
        cost_estimate=pl.CostEstimate(flops=0, bytes_accessed=1024, transcendentals=0),
    )(*placed, *after, *([in_hbm(starts)] if named else []))
    given, answer = list(given), []
    for result in results:
        item = (Near(given.pop(0)),) if result.near else ()
        item += (given.pop(0),) if result.far else ()
        answer.append(item if len(item) == 2 else item[0])
    return answer


def moved_by(array, axis, route):
    array = array.arrays[0] if isinstance(array, Near) else array
    return Near(lax.ppermute(array, axis, route))


def feature_weights(feat_query_t, feat_key_t):
    def places(info, sources=None, buffer=None):
        if info is None:
            return 2
        return [(sources[0], buffer.at[0:32]), (sources[1], buffer.at[32:64])]

    return Far([feat_query_t, feat_key_t], (128, feat_query_t.shape[1]), places)


def own_part(block):
    def places(info, sources=None, buffer=None):
        if info is None:
            return 1
        return [(sources[0].at[info.rows(0)], buffer)]

    return Far(block, (OWN, block.shape[1]), places)


def keys_kernel(
    info, x_ref, gain_ref, key_ref, value_ref, feat_ref, choose_ref, lanes_ref,
    normed_ref, inv_ref, raw_ref, keys_ref, values_ref, km_ref, packed_ref, wide_ref,
):
    gain = gain_ref[...]

    def norm_rows(part):
        for i in range(2):
            rows = slice(part * 128 + i * 64, part * 128 + i * 64 + 64)
            x = x_ref.ref[rows, :].astype(f32)
            inv = lax.rsqrt(jnp.mean(x * x, axis=-1, keepdims=True) + EPS)
            inv_ref[rows, :] = inv
            normed_ref[rows, :] = (x * inv * gain).astype(bf16)

    x_ref.part(0)
    norm_rows(0)
    x_ref.part(1)
    norm_rows(1)
    for ref in (x_ref, feat_ref, key_ref, value_ref, choose_ref, lanes_ref):
        ref.ready()
    feat_ref.ref[64:128, :] = jnp.zeros((64, feat_ref.shape[1]), bf16)
    half = ROWS // 2
    features = []
    for first in (0, half):
        rows = slice(first, first + half)
        normed = normed_ref[rows, :]
        raw = mm_nt(normed, feat_ref[...])
        raw_ref[rows, :] = raw
        if first == 0:
            norm_rows(2)
            norm_rows(3)
        keys_ref[rows, :] = mm(normed, key_ref[...]).astype(bf16)
        values_ref[rows, :] = mm(normed, value_ref[...]).astype(bf16)
        left, right = factors(raw, 1, choose_ref, lanes_ref)
        part = (left * right * lanes_ref[2:3, :]).astype(bf16)
        features.append((part.astype(f32) * lanes_ref[3:4, :]).astype(bf16))
    features = jnp.concatenate(features, axis=0)
    values = values_ref[...]
    for head in range(HEADS):
        km_ref[head] = features[:, head * LANES : (head + 1) * LANES]
    tail = tail_mask(info)
    for head in range(HEADS):
        own = features[:, head * LANES : (head + 1) * LANES]
        lanes = head_lanes(head)
        kept = (values[:, lanes].astype(f32) * tail).astype(bf16)
        state = mm_tn(own, kept)
        norm = jnp.sum(own.astype(f32) * tail, axis=0, keepdims=True)
        write_packed(packed_ref, head, state, norm)
        wide_ref[head, 0:PACKED, :] = packed_ref[head]
        wide_ref[head, PACKED : PACKED + WIN, :] = keys_ref[ROWS - WIN :, lanes]
        wide_ref[head, PACKED + WIN :, :] = values[ROWS - WIN :, lanes]


def local_kernel(
    info, raw_ref, choose_ref, lanes_ref, values_ref, km_ref, normed_ref, query_ref,
    qf_ref, low_ref, num_ref, den_ref, queries_ref,
):
    left, right = factors(raw_ref[...], 0, choose_ref, lanes_ref)
    features = (left * right * lanes_ref[2:3, :]).astype(bf16)
    for head in range(HEADS):
        qf_ref[head] = features[:, head * LANES : (head + 1) * LANES]
    half = ROWS // 2
    causal = []
    for block in range(2):
        query_at = column_positions(info, block * half, half)
        key_at = row_positions(info, 0, (block + 1) * half)
        causal.append((query_at >= key_at) & (doc_of(info, query_at) == doc_of(info, key_at)))
    for head in range(HEADS):
        for block in range(2):
            first, reach = block * half, (block + 1) * half
            own = qf_ref[head, first:reach, :]
            weights = jnp.where(causal[block], mm_nt(own, km_ref[head, :reach, :]), 0.0)
            den_ref[head, first:reach, :] = jnp.sum(weights, axis=-1, keepdims=True)
            weights = weights.astype(bf16)
            low_ref[head, first:reach, 0:reach] = weights
            num_ref[first:reach, head_lanes(head)] = mm(
                weights, values_ref[:reach, head_lanes(head)]
            )
    queries_ref[...] = mm(normed_ref[...], query_ref[...]).astype(bf16)


def window_kernel(
    info, queries_ref, keys_ref, values_ref, probs_ref, window_ref,
):
    queries = queries_ref[...]
    for head in range(HEADS):
        lanes = head_lanes(head)
        for tile in range(1, ROWS // TILE):
            rows = slice(tile * TILE, (tile + 1) * TILE)
            probs, result = window_tile(
                info, head, tile, queries[rows, lanes],
                window_rows(keys_ref, None, 0, head, tile), window_rows(values_ref, None, 1, head, tile),
            )
            probs_ref[head, tile - 1] = probs
            window_ref[rows, lanes] = result


def by_distance(ref, info, other):
    return jnp.concatenate([ref[info.rows(d, other), :] for d in range(4)], axis=0)


def mixed_kernel(
    info, before_ref, got1_ref, got2_ref, got3_ref, qf_ref, num_ref, den_ref, window_ref, out_ref,
    queries_ref, keys_ref, values_ref,
    mixed_ref, linear_ref, total_den_ref, state_ref, norm_ref, probs_ref, other_ref,
):
    use = prefix_mask(info)
    for head in range(HEADS):
        lanes = head_lanes(head)
        state, norm = read_total(before_ref, (got1_ref, got2_ref, got3_ref), head)
        state_ref[head] = state
        norm_ref[head] = jnp.broadcast_to(norm, (8, LANES))
        features = qf_ref[head]
        inter = mm(features, state) * use
        den = jnp.sum(features.astype(f32) * norm, axis=-1, keepdims=True) * use + den_ref[head]
        total_den_ref[head] = den
        linear = (inter + num_ref[:, lanes]) / den
        linear_ref[:, lanes] = linear
        probs, window = window_tile(
            info, head, 0, queries_ref[0:TILE, lanes],
            window_rows(keys_ref, got1_ref, 0, head, 0), window_rows(values_ref, got1_ref, 1, head, 0),
        )
        probs_ref[head] = probs
        mixed_ref[0:TILE, lanes] = (linear[0:TILE] + window).astype(bf16)
        mixed_ref[TILE:, lanes] = (linear[TILE:] + window_ref[TILE:, lanes]).astype(bf16)
    other_ref[...] = mm(by_distance(mixed_ref, info, True), out_ref[...]).astype(bf16)


def mixed_own_kernel(info, mixed_ref, out_ref, own_ref):
    own_ref[...] = mm(by_distance(mixed_ref, info, False), out_ref[...]).astype(bf16)


def quarters_kernel(info, own_ref, got_ref, *out_refs):
    out_refs[4][...] = got_ref[0:16, 0:128]
    for d in (1, 2, 3, 0):
        rows = slice(d * OWN, (d + 1) * OWN)
        total = own_ref[rows, :].astype(f32) + got_ref[rows, :].astype(f32)
        out_refs[d][...] = total.astype(out_refs[d].dtype)
        out_refs[d].send()


def resid_kernel(
    info, mine_ref, x_ref, gain_ref, got1_ref, got2_ref, got3_ref, normed_ref, resid_ref, inv_ref
):
    resid = x_ref[...].astype(f32) + mine_ref[...]
    for ref in (got1_ref, got2_ref, got3_ref):
        resid = resid + ref[...].astype(f32)
    resid_ref[...] = resid
    inv = lax.rsqrt(jnp.mean(resid * resid, axis=-1, keepdims=True) + EPS)
    inv_ref[...] = inv
    normed_ref[...] = (resid * inv * gain_ref[...]).astype(bf16)


def grad_resid_kernel(
    info, mine_ref, resid_ref, inv_ref, top_ref, gain_ref, got1_ref, got2_ref, got3_ref,
    sent_ref, grad_ref, gains_ref,
):
    grad = mine_ref[...]
    for ref in (got1_ref, got2_ref, got3_ref):
        grad = grad + ref[...].astype(f32)
    resid = resid_ref[...]
    inv = inv_ref[...]
    grad_resid = top_ref[...].astype(f32) + norm_back(resid, inv, gain_ref[...], grad)
    sent_ref[...] = grad_resid.astype(bf16)
    sent_ref.send()
    grad_ref[...] = grad_resid
    gains_ref[0:1, :] = jnp.sum(grad * resid * inv, axis=0, keepdims=True)


def grad_x_kernel(
    info, mine_ref, x_ref, grad_resid_ref, gain_ref, resid_ref, out_ref, got1_ref, got2_ref, got3_ref,
    out1_ref, out2_ref, out3_ref, sent_ref,
):
    total = resid_ref[...] + out_ref[...]
    for ref in (out1_ref, out2_ref, out3_ref):
        total = total + ref[...].astype(f32)
    sent_ref[0:OWN, :] = total.astype(bf16)
    grad = mine_ref[...]
    for ref in (got1_ref, got2_ref, got3_ref):
        grad = grad + ref[...].astype(f32)
    x = x_ref[...].astype(f32)
    inv = lax.rsqrt(jnp.mean(x * x, axis=-1, keepdims=True) + EPS)
    sent_ref[OWN:, :] = (grad_resid_ref[...] + norm_back(x, inv, gain_ref[...], grad)).astype(bf16)


def norm_back(in_rows, inv_rms, gain, grad_normed):
    weighted = grad_normed * gain
    return inv_rms * weighted - in_rows * inv_rms**3 * jnp.mean(
        weighted * in_rows, axis=-1, keepdims=True
    )


def by_halves(block):
    def places(info, sources=None, buffer=None):
        if info is None:
            return 8
        return [
            (sources[0].at[info.rows(i % 4, other=i >= 4)], buffer.at[i * OWN : (i + 1) * OWN])
            for i in range(8)
        ]

    return Far(block, block.shape, places)


def grad_act_kernel(info, top_ref, down_ref, own_ref, other_ref):
    top = top_ref[...]
    half = ROWS // 2
    for first in range(0, down_ref.shape[0], 256):
        span = slice(first, min(first + 256, down_ref.shape[0]))
        grad = mm_nt(top, down_ref[span, :])
        own_ref[:, span] = grad[:half]
        other_ref[:, span] = grad[half:]


def ffn_rows(pieces, gate_ref, up_ref, grad_act_ref, normed_ref, act_ref, grad_gate_ref, grad_up_ref):
    normed = jnp.concatenate([piece[...] for piece in pieces], axis=0)
    normed_ref[...] = normed
    hidden = gate_ref.shape[0]
    for first in range(0, hidden, 256):
        span = slice(first, min(first + 256, hidden))
        gate = mm_nt(normed, gate_ref[span, :])
        up_value = mm_nt(normed, up_ref[span, :])
        sigmoid_gate = jax.nn.sigmoid(gate)
        silu_gate = gate * sigmoid_gate
        act_ref[:, span] = (silu_gate * up_value).astype(bf16)
        grad_act = grad_act_ref[:, span]
        grad_gate_ref[:, span] = (
            grad_act * up_value * sigmoid_gate * (1.0 + gate * (1.0 - sigmoid_gate))
        ).astype(bf16)
        grad_up_ref[:, span] = (grad_act * silu_gate).astype(bf16)


def ffn_own_kernel(info, p0, p3, p1, p2, gate_ref, up_ref, grad_act_ref, *out_refs):
    ffn_rows((p0, p3, p2, p1), gate_ref, up_ref, grad_act_ref, *out_refs)


def ffn_other_kernel(info, s0, s3, s1, s2, gate_ref, up_ref, grad_act_ref, back_ref, *out_refs):
    ffn_rows((s0, s3, s2, s1), gate_ref, up_ref, grad_act_ref, *out_refs)
    ffn_back_kernel(info, out_refs[2], out_refs[3], gate_ref, up_ref, back_ref)


def ffn_back_kernel(info, grad_gate_ref, grad_up_ref, gate_ref, up_ref, back_ref):
    grad_gate, grad_up = grad_gate_ref[...], grad_up_ref[...]
    for first in range(0, back_ref.shape[1], 512):
        span = slice(first, first + 512)
        part = mm(grad_gate, gate_ref[:, span]) + mm(grad_up, up_ref[:, span])
        back_ref[:, span] = part.astype(bf16)


def ffn_out_kernel(info, act_own_ref, act_other_ref, down_ref, other_ref, own_ref):
    for target, act_ref in ((other_ref, act_other_ref), (own_ref, act_own_ref)):
        act = act_ref[...]
        for first in range(0, target.shape[1], 512):
            span = slice(first, first + 512)
            target[:, span] = mm(act, down_ref[:, span]).astype(bf16)


def column_grads(pairs, out_ref, last=None, at=0, sent=0):
    count = out_ref.shape[0] // 4
    for part in range(4):
        span = slice(part * count, (part + 1) * count)
        first = at
        for i, (rows_refs, grads) in enumerate(pairs):
            rows_refs = rows_refs if isinstance(rows_refs, tuple) else (rows_refs,)
            grads = grads if isinstance(grads, tuple) else (grads,)
            total = sum(mm_tn(rows[:, span], grad) for rows, grad in zip(rows_refs, grads))
            if last is not None and i == len(pairs) - 1:
                total = total + last[span, :].astype(f32)
            end = first + total.shape[1]
            out_ref[span, first:end] = total.astype(bf16)
            first = end
        out_ref.send(sent + part)


class Rows:

    def __init__(self, ref, first, count):
        self.ref, self.rows = ref, slice(first, first + count)

    def __getitem__(self, index):
        return self.ref[self.rows, index[1]]


def ffn_grads_kernel(
    info, own_ref, other_ref, gate_own_ref, gate_other_ref, up_own_ref, up_other_ref, top_ref, act_own_ref,
    act_other_ref, out_ref, tail_ref,
):
    rows = (own_ref, other_ref)
    gate = (gate_own_ref[...], gate_other_ref[...])
    up = (up_own_ref[...], up_other_ref[...])
    column_grads(((rows, gate), (rows, up)), out_ref)
    half, hidden = ROWS // 2, gate[0].shape[1]
    whole = hidden // 128 * 128
    rows = (Rows(top_ref, 0, half), Rows(top_ref, half, half))
    acts = (act_own_ref[...], act_other_ref[...])
    column_grads(
        ((rows, tuple(act[:, :whole] for act in acts)),), out_ref, at=2 * hidden, sent=4
    )
    room = jnp.zeros((half, 128 - hidden % 128), bf16)
    rest = [jnp.concatenate([act[:, whole:], room], axis=1) for act in acts]
    tail_ref[...] = sum(mm_tn(row[:, :], act) for row, act in zip(rows, rest)).astype(bf16)


def grad_x_out_kernel(info, p0, p1, p2, p3, s0, s1, s2, s3, output_ref, grad_ref):
    for i, piece in enumerate((p0, p1, p2, p3, s0, s1, s2, s3)):
        rows = info.rows(4 - i % 4, other=i >= 4)
        output_ref[rows, :] = piece[0:OWN, :]
        grad_ref[rows, :] = piece[OWN : 2 * OWN, :].astype(f32)


def window_tile_back(top, probs, key_rows, value_rows):
    grad_probs = mm_nt(top, value_rows)
    shared = jnp.sum(grad_probs * probs, axis=-1, keepdims=True)
    return (probs * (grad_probs - shared)).astype(bf16)


def mixed_back_kernel(
    info, p0, p3, p1, p2, s0, s3, s1, s2, out_ref, linear_ref, den_ref, qf_ref, probs0_ref, keys_ref,
    values_ref, halo_ref, queries_ref, packed_ref, wide_ref, top_ref, gm_ref, gnum_ref, gden_ref,
):
    for i, piece in enumerate((p0, p1, p2, p3, s0, s1, s2, s3)):
        top_ref[info.rows(4 - i % 4, other=i >= 4), :] = piece[...]
    grad_mixed = mm_nt(top_ref[...], out_ref[...]).astype(bf16)
    gm_ref[...] = grad_mixed
    use = prefix_mask(info)
    for head in range(HEADS):
        lanes = head_lanes(head)
        wide = grad_mixed[:, lanes].astype(f32)
        den = den_ref[head]
        grad_num = (wide / den).astype(bf16)
        gnum_ref[:, lanes] = grad_num
        grad_den = -jnp.sum(wide * linear_ref[:, lanes], axis=-1, keepdims=True) / den
        gden_ref[head] = grad_den
        features = qf_ref[head]
        used = (grad_num.astype(f32) * use).astype(bf16)
        state = mm_tn(features, used)
        norm = jnp.sum(features.astype(f32) * (grad_den * use), axis=0, keepdims=True)
        write_packed(packed_ref, head, state, norm)
        wide_ref[head, 0:PACKED, :] = packed_ref[head]
        top, probs = grad_mixed[0:TILE, lanes], probs0_ref[head]
        grad_logits = window_tile_back(
            top, probs, window_rows(keys_ref, halo_ref, 0, head, 0),
            window_rows(values_ref, halo_ref, 1, head, 0),
        )
        grad_keys = mm_tn(grad_logits, queries_ref[0:TILE, lanes]) * VALUE_WIDTH ** (-0.5)
        wide_ref[head, PACKED : PACKED + WIN, :] = grad_keys[0:WIN].astype(bf16)
        grad_values = mm_tn(probs.astype(bf16), top)
        wide_ref[head, PACKED + WIN :, :] = grad_values[0:WIN].astype(bf16)


def window_back_kernel(
    info, gm_ref, probs0_ref, probs_ref, keys_ref, values_ref, halo_ref, queries_ref,
    top_ref, mixed_ref, gq_ref, gk_ref, gv_ref, out_ref, key_acc, value_acc,
):
    column_grads(((top_ref, mixed_ref[...]),), out_ref)
    scale = VALUE_WIDTH ** (-0.5)
    key_acc[...] = jnp.zeros_like(key_acc)
    value_acc[...] = jnp.zeros_like(value_acc)
    for tile in range(ROWS // TILE):
        first = tile * TILE
        reach = slice(first, first + TILE + WIN)
        for head in range(HEADS):
            lanes = head_lanes(head)
            key_rows = window_rows(keys_ref, halo_ref, 0, head, tile)
            value_rows = window_rows(values_ref, halo_ref, 1, head, tile)
            top = gm_ref[first : first + TILE, lanes]
            probs = probs0_ref[head] if tile == 0 else probs_ref[head, tile - 1]
            grad_logits = window_tile_back(top, probs, key_rows, value_rows)
            gq_ref[first : first + TILE, lanes] = (mm(grad_logits, key_rows) * scale).astype(bf16)
            queries = queries_ref[first : first + TILE, lanes]
            key_acc[reach, lanes] += mm_tn(grad_logits, queries) * scale
            value_acc[reach, lanes] += mm_tn(probs.astype(bf16), top)
    gk_ref[...] = key_acc[WIN:, :]
    gv_ref[...] = value_acc[WIN:, :]


def linear_back_kernel(
    info, gnum_ref, gden_ref, values_ref, low_ref, km_ref, qf_ref, state_ref, norm_ref, raw_ref,
    choose_ref, choose_k_ref, lanes_ref, window_gv_ref, normed_ref, gq_ref,
    gfeat_ref, gv_ref, gkf_ref, left_ref, right_ref, out_ref,
):
    column_grads(((normed_ref, gq_ref[...]),), out_ref)
    use = prefix_mask(info)
    half = ROWS // 2
    grads = [[None, None], [None, None]]
    for head in range(HEADS):
        lanes = head_lanes(head)
        inter = mm_nt((gnum_ref[:, lanes].astype(f32) * use).astype(bf16), state_ref[head])
        inter = inter + (gden_ref[head] * use) * norm_ref[head, 0:1, :]
        for block in range(2):
            first, reach = block * half, (block + 1) * half
            query_at = column_positions(info, first, half)
            key_at = row_positions(info, 0, reach)
            causal = (query_at >= key_at) & (doc_of(info, query_at) == doc_of(info, key_at))
            grad_num = gnum_ref[first:reach, lanes]
            grad = mm_nt(grad_num, values_ref[:reach, lanes]) + gden_ref[head, first:reach, :]
            grad = jnp.where(causal, grad, 0.0).astype(bf16)
            grads[head][block] = mm(grad, km_ref[head, :reach, :]) + inter[first:reach]
            key_part = mm_tn(grad, qf_ref[head, first:reach, :])
            value_part = mm_tn(low_ref[head, first:reach, 0:reach], grad_num)
            if block == 0:
                gkf_ref[head, 0:half] = key_part
                gv_ref[0:half, lanes] = window_gv_ref[0:half, lanes] + value_part
            else:
                gkf_ref[head, 0:half] += key_part[0:half]
                gkf_ref[head, half:] = key_part[half:]
                gv_ref[0:half, lanes] += value_part[0:half]
                gv_ref[half:, lanes] = window_gv_ref[half:, lanes] + value_part[half:]
    left, right = factors(raw_ref[...], 0, choose_ref, lanes_ref)
    gradient = jnp.concatenate([jnp.concatenate(g, axis=0) for g in grads], axis=1)
    gradient = gradient * lanes_ref[2:3, :]
    gfeat_ref[...] = feature_back(gradient, left, right, choose_ref)
    left_ref[...], right_ref[...] = factors(raw_ref[...], 1, choose_k_ref, lanes_ref)


def keys_back_kernel(
    info, before_ref, got1_ref, got2_ref, got3_ref, values_ref, km_ref, gkf_ref, gk_ref, gv_ref,
    left_ref, right_ref, choose_ref, lanes_ref, gfeat_ref, normed_ref, tail_ref,
    gkw_ref, gvw_ref, gf_ref, out_ref,
):
    tail = tail_mask(info)
    inner = ROWS - WIN
    gkw_ref[0:inner, :] = gk_ref[0:inner, :].astype(bf16)
    gradients = []
    for head in range(HEADS):
        lanes = head_lanes(head)
        later, norm = read_total(before_ref, (got1_ref, got2_ref, got3_ref), head)
        kept = (values_ref[:, lanes].astype(f32) * tail).astype(bf16)
        gradients.append(gkf_ref[head] + mm_nt(kept, later) + tail * norm)
        grad_values = gv_ref[:, lanes] + mm(km_ref[head], later) * tail
        gvw_ref[0:inner, lanes] = grad_values[0:inner].astype(bf16)
        right = got1_ref[head, PACKED:, :].astype(f32)
        gkw_ref[inner:, lanes] = (gk_ref[inner:, lanes] + right[0:WIN]).astype(bf16)
        gvw_ref[inner:, lanes] = (grad_values[inner:] + right[WIN:]).astype(bf16)
    gradient = jnp.concatenate(gradients, axis=1) * lanes_ref[4:5, :]
    gradient = feature_back(gradient, left_ref[...], right_ref[...], choose_ref) + gfeat_ref[...]
    gf_ref[...] = gradient.astype(bf16)
    lane = lax.broadcasted_iota(jnp.int32, (1, 128), 1)
    beside = jnp.where(lane < 64, 0.0, pltpu.roll(gradient, 64, 1)).astype(bf16)
    column_grads(
        (
            (normed_ref, gkw_ref[...]), (normed_ref, gvw_ref[...]), (normed_ref, beside),
        ),
        out_ref, last=tail_ref,
    )


def normed_back_kernel(
    info, gq_ref, gkw_ref, gvw_ref, gf_ref, wq_ref, wk_ref, wv_ref, wf_ref, x_ref, inv_ref, gain_ffn_ref,
    other_ref, own_ref, gains_ref,
):
    wf_ref.ready()
    wf_ref.ref[64:128, :] = jnp.zeros((64, wf_ref.shape[1]), bf16)
    for target, other in ((other_ref, True), (own_ref, False)):
        grads = [by_distance(ref, info, other) for ref in (gq_ref, gkw_ref, gvw_ref, gf_ref)]
        scaled_by = by_distance(inv_ref, info, other)
        for piece in range(4):
            span = slice(piece * 512, (piece + 1) * 512)
            part = mm_nt(grads[0], wq_ref[span, :])
            part = part + mm_nt(grads[1], wk_ref[span, :])
            part = part + mm_nt(grads[2], wv_ref[span, :])
            part = part + mm(grads[3], wf_ref[:, span])
            target[:, span] = part.astype(bf16)
            x_rows = jnp.concatenate([x_ref[info.rows(d, other), span] for d in range(4)], axis=0)
            total = jnp.sum(part * (x_rows.astype(f32) * scaled_by), axis=0, keepdims=True)
            gains_ref[0:1, span] = total if other else total + gains_ref[0:1, span]
    gains_ref[1:2, :] = gain_ffn_ref[0:1, :]


def columns(block, first, last):
    def places(info, sources=None, buffer=None):
        return 1 if info is None else [(sources[0].at[:, first:last], buffer)]

    return Far(block, (block.shape[0], last - first), places)


def grads_out_kernel(
    info, both_ref, in_ref, gate_ref, up_ref, down_ref, out_ref, grad_q_ref, grad_k_ref, grad_v_ref,
    feat_query_ref, feat_key_ref,
):
    hidden, width = gate_ref.shape[0], out_ref.shape[0]
    whole = hidden // 128 * 128
    both = both_ref[...].astype(f32).T
    gate_ref[...] = both[0:hidden]
    gate_ref.send()
    up_ref[...] = both[hidden:]
    up_ref.send()
    down_ref[0:whole, :] = in_ref[:, 0:whole].astype(f32).T
    at = whole
    out_ref[...] = in_ref[:, at : at + width].astype(f32).T
    out_ref.send()
    for ref in (grad_q_ref, grad_k_ref, grad_v_ref):
        at += width
        ref[...] = in_ref[:, at : at + width].astype(f32)
        ref.send()
    tail = in_ref[:, at + width :].astype(f32).T
    down_ref[whole:, :] = tail[0 : hidden - whole]
    down_ref.send()
    feat_query_ref[...] = tail[64:96]
    feat_key_ref[...] = tail[96:128]


def total_of(refs):
    total = refs[0][...]
    for ref in refs[1:]:
        total = total + ref[...]
    return total


def gains_kernel(info, *refs):
    refs[-1][...] = total_of(refs[:-1])


def spread_kernel(info, *refs):
    total, out_ref = total_of(refs[:-1]), refs[-1]
    for i in range(out_ref.shape[0]):
        out_ref[i, 0:2, :] = total[:, i * 128 : (i + 1) * 128]
        out_ref[i, 2:, :] = jnp.zeros((6, 128), f32)


def gathered_sum_kernel(info, in_ref, out_ref):
    total = in_ref[0]
    for i in range(1, in_ref.shape[0]):
        total = total + in_ref[i]
    out_ref[...] = total


def along_y(distance):
    return [(i, (i + 2 * distance) % 8) for i in range(8)]


def sibling():
    return [(i, i ^ 1) for i in range(8)]


def along_x(distance):
    return [(i, (i + 4 * distance) % 16) for i in range(16)]


def along_z(distance):
    return [(4 * a + z, 4 * a + (z + distance) % 4) for a in range(4) for z in range(4)]


def head_quarters(own, other, after=()):
    got = moved_by(other, "head", sibling())
    width = own.dims[1]
    with jax.named_scope("quarters"):
        mine, *sent, token = call(
            quarters_kernel,
            [near(OWN, width, dtype=f32)] + [near(OWN, width)] * 3 + [near(16, 128)],
            (own, got), after=after,
        )
    parts = [moved_by(sent[d - 1], "head", along_y(d)) for d in (2, 1, 3)]
    return mine, parts, moved_by(token, "head", sibling())


def head_pieces(own):
    far_piece = moved_by(own, "head", along_y(2))
    pieces = [own, moved_by(own, "head", along_y(1)), far_piece, moved_by(own, "head", along_y(3))]
    return pieces + [moved_by(piece, "head", sibling()) for piece in pieces]


def gains_sum(gains):
    with jax.named_scope("gains"):
        (pair,) = call(
            gains_kernel, [near(*gains.dims, dtype=f32)], (gains, moved_by(gains, "head", sibling()))
        )
        parts = [pair] + [moved_by(pair, "head", along_y(d)) for d in (2, 1, 3)]
        (blocks,) = call(spread_kernel, [far(16, 8, 128, dtype=f32)], parts)
        blocks = lax.all_to_all(blocks, "seq", 0, 0)
        (total,) = call(gathered_sum_kernel, [far(8, 128, dtype=f32)], (blocks,))
    return total


def scan_kernel(reverse, info, own_ref, got1_ref, got2_ref, got3_ref, before_ref, *sent_refs):
    place_x, place_z = (3 - info.x, 3 - info.z) if reverse else (info.x, info.z)
    before = jnp.zeros(before_ref.shape, f32)
    for d, ref in enumerate((got1_ref, got2_ref, got3_ref), 1):
        before = before + ref[:, 0:PACKED, :].astype(f32) * (place_x >= d).astype(f32)
    before_ref[...] = before
    row = lax.broadcasted_iota(jnp.int32, (HEADS, 16, 128), 1) + (KEPT - FEATURES)
    sent = []
    for total in (before, before + own_ref[:, 0:PACKED, :].astype(f32)):
        tile = total[:, KEPT:]
        norm = tile + jnp.roll(tile, -2, axis=1)
        high = norm.astype(bf16).astype(f32)
        rest = jnp.roll(norm - high, 2, axis=1)
        norm = jnp.where(row < 0, tile, jnp.where(row < 2, high, jnp.where(row < 4, rest, 0.0)))
        sent.append((total[:, :KEPT], norm))
    for d, ref in enumerate(sent_refs, 1):
        with_own = (place_z + d < 4).astype(f32)
        for part, rows in ((0, slice(0, KEPT)), (1, slice(KEPT, PACKED))):
            less, more = sent[0][part], sent[1][part]
            ref[:, rows, :] = (more * with_own + less * (1.0 - with_own)).astype(bf16)
        if ref.shape[1] > PACKED:
            own, earlier = own_ref[:, PACKED:, :].astype(f32), got1_ref[:, PACKED:, :].astype(f32)
            ref[:, PACKED:, :] = (own * with_own + earlier * (1.0 - with_own)).astype(bf16)


def exclusive_parts(own, reverse, after=(), wide=None):
    sign = -1 if reverse else 1
    first = own if wide is None else wide
    got = [moved_by(first if d == 1 else own, "seq", along_x(sign * d)) for d in (1, 2, 3)]
    with jax.named_scope("scan"):
        before, *sent = call(
            functools.partial(scan_kernel, reverse),
            [near(*own.dims, dtype=f32), near(*first.dims), near(*own.dims), near(*own.dims)],
            (first, *got), after=after,
        )
    return [before] + [
        moved_by(sent[d - 1], "seq", along_z(sign * d)) for d in (1, 2, 3)
    ]


def shards(
    inputs,
    gain_mix,
    feat_query,
    feat_key,
    win_query,
    win_key,
    value_proj,
    out_proj,
    gain_ffn,
    gate_proj,
    up_proj,
    down_proj,
    document_starts,
    cotangent,
):
    choose, lanes = feature_tables()
    choose = jnp.asarray(choose, bf16)
    lanes = jnp.asarray(lanes, f32)
    choose_q, choose_k = choose[0], choose[1]
    feat = feature_weights(feat_query.T, feat_key.T)
    gain_mix = gain_mix.reshape(1, -1)
    gain_ffn = gain_ffn.reshape(1, -1)
    model = inputs.shape[1]
    width = HEADS * VALUE_WIDTH
    hidden = gate_proj.shape[1]
    half = ROWS // 2
    unit = 2 * ROWS * model
    starts = document_starts

    normed, inv_mix, raw, keys, values, km, packed, wide = call(
        keys_kernel,
        (
            near(ROWS, model), near(ROWS, 1, dtype=f32), near(ROWS, 128, dtype=f32),
            near(ROWS, width), near(ROWS, width), near(HEADS, ROWS, LANES),
            near(HEADS, PACKED, 128), near(HEADS, PACKED + EDGE, 128),
        ),
        (Far(inputs, parts=4), gain_mix, win_key, value_proj, feat, choose_k, lanes),
        starts=starts, flops=unit * 640,
    )
    qf, low, num, den, queries, near_out, normed_far, inv_mix, raw_far, keys_far, values_far, km_far = call(
        local_kernel,
        (
            near(HEADS, ROWS, LANES), near(HEADS, ROWS, ROWS), near(ROWS, width, dtype=f32),
            near(HEADS, ROWS, 1, dtype=f32), near(ROWS, width), Stage(out_proj), Export(normed),
            Export(inv_mix), Export(raw), Export(keys), Export(values), Export(km),
        ),
        (raw, choose_q, lanes, values, km, normed, win_query),
        starts=starts, flops=unit * 300,
    )
    sums = exclusive_parts(packed, False, after=(qf,), wide=wide)
    probs, window, qf_far, low = call(
        window_kernel,
        (
            near(HEADS, 3, TILE, TILE + WIN, dtype=f32),
            near(ROWS, width, dtype=f32), Export(qf), Export(low),
        ),
        (queries, keys, values),
        starts=starts, flops=unit * 400,
    )
    mixed, linear, total_den, state, norm, probs_first, other = call(
        mixed_kernel,
        (
            near(ROWS, width), near(ROWS, width, dtype=f32), near(HEADS, ROWS, 1, dtype=f32),
            near(HEADS, LANES, VALUE_WIDTH), near(HEADS, 8, LANES, dtype=f32),
            near(HEADS, TILE, TILE + WIN, dtype=f32), near(half, model),
        ),
        (*sums, qf, num, den, window, near_out, queries, keys, values),
        starts=starts, flops=unit * 300,
    )
    own, halo, *rest = call(
        mixed_own_kernel,
        (
            near(half, model),
            Export(sums[1], (HEADS, EDGE, 128), lambda ref: ref.at[:, PACKED:, :]),
            *map(Export, (mixed, linear, total_den, state, norm, probs_first, probs, queries)),
        ),
        (mixed, near_out), after=(other,), flops=unit * 100,
    )
    mixed, linear, total_den, state, norm, probs_first, probs, queries_far = rest
    mine, parts, signal = head_quarters(own, other)
    grad_act_own, grad_act_other, x_own, near_gain, near_gate, near_up = call(
        grad_act_kernel,
        (
            near(half, hidden, dtype=f32), near(half, hidden, dtype=f32), Stage(own_part(inputs)), Stage(gain_ffn),
            Stage(gate_proj.T), Stage(up_proj.T),
        ),
        (by_halves(cotangent), down_proj),
        after=(signal,), flops=unit * hidden,
    )
    own_normed, resid, inv_ffn = call(
        resid_kernel,
        (near(OWN, model), near(OWN, model, dtype=f32), near(OWN, 1, dtype=f32)),
        (mine, x_own, near_gain, *parts), after=(grad_act_own,),
    )
    pieces = head_pieces(own_normed)
    def ffn_half(body, pieces, grad_act, *more, after=()):
        order = [pieces[i] for i in (0, 3, 1, 2)]
        return call(
            body,
            (
                *more, near(half, model), near(half, hidden), near(half, hidden), near(half, hidden),
            ),
            (*order, near_gate, near_up, grad_act), after=after, flops=unit * 2 * hidden,
        )

    normed_own, act_own, gate_own, up_own = ffn_half(ffn_own_kernel, pieces[:4], grad_act_own)
    other, normed_other, act_other, gate_other, up_other = ffn_half(
        ffn_other_kernel, pieces[4:], grad_act_other, near(half, model), after=(gate_own,)
    )
    (own,) = call(
        ffn_back_kernel, (near(half, model),), (gate_own, up_own, near_gate, near_up),
        after=(other,), flops=unit * hidden,
    )
    mine, parts, signal = head_quarters(own, other)
    whole = hidden // 128 * 128
    place = dict(parts=4, width=2 * hidden + whole + 4 * width + 128)
    grads, tail, resid_far, act_own_far, act_other_far, near_top, near_gain, *staged = call(
        ffn_grads_kernel,
        (
            far(model, 2 * hidden + whole, cut=2 * hidden, **place), near(model, 128),
            Export(resid), Export(act_own), Export(act_other), Stage(own_part(cotangent)),
            Stage(gain_ffn), Stage(out_proj), Stage(linear), Stage(total_den), Stage(qf_far),
            Stage(probs_first), Stage(probs), Stage(keys_far), Stage(values_far), Stage(halo),
            Stage(queries_far), Stage(low), Stage(km_far), Stage(state), Stage(norm),
            Stage(raw_far), Stage(choose_q), Stage(choose_k), Stage(lanes), Stage(mixed),
        ),
        (
            normed_own, normed_other, gate_own, gate_other, up_own, up_other, by_halves(cotangent),
            act_own, act_other,
        ),
        after=(signal,), flops=unit * 3 * hidden,
    )
    near_mixed, staged = staged[:4], staged[4:]
    probs_first, probs, keys, values, halo, queries, *near_back = staged
    act_own, act_other = act_own_far, act_other_far
    at = 2 * hidden + whole
    low, km, state, norm, raw, *rest = near_back
    choose_q, choose_k, lanes, mixed = rest
    sent, grad_resid, gain_ffn_part = call(
        grad_resid_kernel,
        (near(OWN, model), near(OWN, model, dtype=f32), near(8, model, dtype=f32)),
        (mine, resid, inv_ffn, near_top, near_gain, *parts), after=(grads,),
    )
    pieces = head_pieces(sent)
    packed, wide, top, grad_mixed, grad_num, grad_den = call(
        mixed_back_kernel,
        (
            near(HEADS, PACKED, 128), near(HEADS, PACKED + EDGE, 128), near(ROWS, model), near(ROWS, width), near(ROWS, width),
            near(HEADS, ROWS, 1, dtype=f32),
        ),
        (
            *[pieces[i] for i in (0, 3, 1, 2, 4, 7, 5, 6)], *near_mixed, probs_first, keys, values,
            halo, queries,
        ),
        starts=starts, flops=unit * 300,
    )
    gq, gk, gv, grads, normed = call(
        window_back_kernel,
        (
            near(ROWS, width), near(ROWS, width, dtype=f32),
            near(ROWS, width, dtype=f32), far(model, width, first=at, onto=grads, **place),
            Stage(normed_far),
        ),
        (grad_mixed, probs_first, probs, keys, values, halo, queries, top, mixed),
        flops=unit * 300, scratch=[pltpu.VMEM((ROWS + WIN, width), f32)] * 2,
    )
    sums = exclusive_parts(packed, True, after=(gq,), wide=wide)
    gfeat, gv, gkf, left, right, grads = call(
        linear_back_kernel,
        (
            near(ROWS, 128, dtype=f32), near(ROWS, width, dtype=f32),
            near(HEADS, ROWS, LANES, dtype=f32), near(ROWS, HEADS * LANES, dtype=f32),
            near(ROWS, HEADS * LANES, dtype=f32),
            far(model, width, first=at + width, onto=grads, **place),
        ),
        (
            grad_num, grad_den, values, low, km, near_mixed[3], state, norm, raw, choose_q, choose_k,
            lanes, gv, normed, gq,
        ),
        starts=starts, after=(sums[0],), flops=unit * 300,
    )
    gkw, gvw, gf, grads = call(
        keys_back_kernel,
        (
            near(ROWS, width), near(ROWS, width), near(ROWS, 128),
            far(model, 2 * width + 128, first=at + 2 * width, onto=grads, **place),
        ),
        (
            *sums, values, km, gkf, gk, gv, left, right, choose_k, lanes, gfeat, normed, tail,
        ),
        starts=starts, flops=unit * 1400,
    )
    grads_sum = lax.psum_scatter(grads, "seq", scatter_dimension=0, tiled=True)
    other, own, gains = call(
        normed_back_kernel, (near(half, model), near(half, model), near(2, model, dtype=f32)),
        (
            gq, gkw, gvw, gf, win_query, win_key, value_proj, feat, inputs, inv_mix, gain_ffn_part,
        ),
        after=(grads,),
        flops=unit * 900,
    )
    mine, parts, signal = head_quarters(own, other)
    other, own = call(
        ffn_out_kernel, (near(half, model), near(half, model)), (act_own, act_other, down_proj),
        after=(signal,), flops=unit * hidden,
    )
    out_mine, out_parts, signal = head_quarters(own, other)
    gains = gains_sum(gains)
    (sent,) = call(
        grad_x_kernel, (near(2 * OWN, model),),
        (mine, own_part(inputs), grad_resid, gain_mix, resid_far, out_mine, *parts, *out_parts),
        after=(gains,),
    )
    pieces = head_pieces(sent)
    output, grad_x = call(
        grad_x_out_kernel, (far(ROWS, model), far(ROWS, model, dtype=f32)), pieces,
    )
    grad_gate_t, grad_up_t, grad_down, grad_out, *rest = call(
        grads_out_kernel,
        (far(hidden, 128, dtype=f32),) * 3 + (far(width, 128, dtype=f32),)
        + (far(128, width, dtype=f32),) * 3 + (far(32, 128, dtype=f32),) * 2,
        (columns(grads_sum, 0, 2 * hidden), columns(grads_sum, 2 * hidden, grads_sum.shape[1])),
        after=(grad_x,),
    )
    grad_wq, grad_wk, grad_wv, grad_fq_t, grad_fk_t = rest
    return (
        output,
        grad_x,
        gains[0],
        grad_fq_t.T,
        grad_fk_t.T,
        grad_wq,
        grad_wk,
        grad_wv,
        grad_out,
        gains[1],
        grad_gate_t.T,
        grad_up_t.T,
        grad_down,
    )


def solution(mesh):
    placed = (
        P("seq", None),
        P(),
        P(None, "head"),
        P(None, "head"),
        P(None, "head"),
        P(None, "head"),
        P(None, "head"),
        P("head", None),
        P(),
        P(None, "head"),
        P(None, "head"),
        P("head", None),
        P(),
        P("seq", None),
    )
    return jax.shard_map(
        shards,
        mesh=mesh,
        in_specs=placed,
        out_specs=(
            P("seq", None),
            P("seq", None),
            P("seq"),
            P("seq", "head"),
            P("seq", "head"),
            P("seq", "head"),
            P("seq", "head"),
            P("seq", "head"),
            P("head", "seq"),
            P("seq"),
            P("seq", "head"),
            P("seq", "head"),
            P("head", "seq"),
        ),
        check_vma=False,
    )
```

```python
import functools
import math

import jax
import jax.numpy as jnp
import numpy as np
from jax import lax
from jax.experimental import pallas as pl
from jax.experimental.pallas import tpu as pltpu
from jax.sharding import PartitionSpec as P

F = 16
VALUE_WIDTH = 128
WIN = 64
EPS = 1e-05

HEADS = 2
ROWS = 512
LANES = 256
FEATURES = 153
KEPT = 144
PACKED = 160
TILE = 128
EDGE = 2 * WIN
OWN = 64
f32 = jnp.float32
bf16 = jnp.bfloat16


def feature_tables():
    pairs = [(a, b) for a in range(F) for b in range(a, F)]
    count = len(pairs)
    choose = np.zeros((2, 2, 128, HEADS * LANES), np.float32)
    lanes = np.zeros((8, HEADS * LANES), np.float32)
    factor = F ** (-0.25)
    for head in range(HEADS):
        at = head * LANES
        for side in range(2):
            for first in (side * HEADS * F, 64, 96):
                row = first + head * F
                for lane, (a, b) in enumerate(pairs):
                    choose[side, 0, row + a, at + lane] = 1.0
                    choose[side, 1, row + b, at + lane] = 1.0
                for a in range(F):
                    choose[side, 0, row + a, at + count + a] = 1.0
        for lane, (a, b) in enumerate(pairs):
            lanes[2, at + lane] = factor * factor / math.sqrt(2.0)
            lanes[3, at + lane] = 1.0 if a == b else 2.0
        lanes[1, at + count : at + count + F + 1] = 1.0
        lanes[0, at + count + F] = 1.0
        lanes[2, at + count : at + count + F] = factor
        lanes[2, at + count + F] = 1.0
        lanes[3, at + count : at + count + F + 1] = 1.0
    lanes[4] = lanes[2] * lanes[3]
    return choose, lanes


def mm(a, b):
    return lax.dot_general(a, b, (((1,), (0,)), ((), ())), preferred_element_type=f32)


def mm_nt(a, b):
    return lax.dot_general(a, b, (((1,), (1,)), ((), ())), preferred_element_type=f32)


def mm_tn(a, b):
    return lax.dot_general(a, b, (((0,), (0,)), ((), ())), preferred_element_type=f32)


def low_pair(part):
    high = part.astype(bf16)
    return high, (part - high.astype(f32)).astype(bf16)


class Place:

    def __init__(self, starts):
        me, seq = lax.axis_index("head"), lax.axis_index("seq")
        self.base = seq * ROWS
        self.x, self.z = lax.shift_right_logical(seq, 2), lax.bitwise_and(seq, 3)
        self.y, self.core = lax.shift_right_logical(me, 1), lax.bitwise_and(me, 1)
        self.loaded = starts

    def starts(self):
        return [self.loaded[0, i] for i in range(4)]

    def rows(self, distance, other=False):
        quarter = lax.bitwise_and(self.y + distance, 3)
        core = 1 - self.core if other else self.core
        return pl.ds(pl.multiple_of(quarter * (2 * OWN) + core * OWN, OWN), OWN)


class Loaded:

    def __init__(self, ref, copies):
        self.ref, self.copies = ref, list(copies)
        self.shape = ref.shape

    def part(self, index):
        if self.copies and self.copies[index] is not None:
            self.copies[index].wait()
            self.copies[index] = None

    def ready(self):
        for index in range(len(self.copies)):
            self.part(index)

    def __getitem__(self, index):
        self.ready()
        return self.ref[index]


class Stored:

    def __init__(self, ref, copies):
        self.ref, self.copies, self.sent = ref, copies, set()
        self.shape, self.dtype = ref.shape, ref.dtype

    def __getitem__(self, index):
        return self.ref[index]

    def __setitem__(self, index, value):
        self.ref[index] = value

    def send(self, part=None):
        for index in range(len(self.copies)) if part is None else (part,):
            if index not in self.sent:
                self.copies[index].start()
                self.sent.add(index)


def doc_of(info, position):
    starts = info.starts()
    count = (position >= starts[0]).astype(jnp.int32)
    for start in starts[1:]:
        count = count + (position >= start).astype(jnp.int32)
    return count


def column_positions(info, first, count):
    return info.base + first + lax.broadcasted_iota(jnp.int32, (count, 1), 0)


def row_positions(info, first, count):
    return info.base + first + lax.broadcasted_iota(jnp.int32, (1, count), 1)


def prefix_mask(info):
    before = doc_of(info, info.base - 1)
    same = doc_of(info, column_positions(info, 0, ROWS)) == before
    return (same & (info.base > 0)).astype(f32)


def tail_mask(info):
    last = doc_of(info, info.base + ROWS - 1)
    return (doc_of(info, column_positions(info, 0, ROWS)) == last).astype(f32)


def factors(raw, side, choose_ref, lanes_ref):
    high, rest = low_pair(raw)
    high, rest = high.astype(f32), rest.astype(f32)
    left = raw - high - rest
    at = side * HEADS * F
    lane = lax.broadcasted_iota(jnp.int32, (1, 128), 1)
    parts = jnp.where(lane < 96, pltpu.roll(rest, 64 - at, 1), pltpu.roll(left, 96 - at, 1))
    parts = jnp.where(lane < 64, high, parts).astype(bf16)
    return [mm(parts, choose_ref[i]) + lanes_ref[i : i + 1, :] for i in range(2)]


def feature_back(gradient, left, right, choose_ref):
    first = mm_nt((gradient * right).astype(bf16), choose_ref[0])
    return first + mm_nt((gradient * left).astype(bf16), choose_ref[1])


def write_packed(packed_ref, head, state, norm):
    packed_ref[head, 0:KEPT, :] = state[:KEPT].astype(bf16)
    row = lax.broadcasted_iota(jnp.int32, (16, 128), 0) + (KEPT - FEATURES)
    high = norm.astype(bf16).astype(f32)
    rest = norm - high
    tile = jnp.where(row == 0, high[:, :128], state[KEPT:PACKED])
    tile = jnp.where(row == 1, high[:, 128:], tile)
    tile = jnp.where(row == 2, rest[:, :128], tile)
    tile = jnp.where(row == 3, rest[:, 128:], tile)
    packed_ref[head, KEPT:PACKED, :] = tile.astype(bf16)


def read_total(before_ref, got_refs, head):
    total = before_ref[head]
    for ref in got_refs:
        total = total + ref[head, 0:PACKED, :].astype(f32)
    state = jnp.concatenate(
        [total, jnp.zeros((LANES - PACKED, VALUE_WIDTH), f32)], axis=0
    ).astype(bf16)
    rows = [total[FEATURES + i : FEATURES + i + 1] for i in range(4)]
    return state, jnp.concatenate([rows[0] + rows[2], rows[1] + rows[3]], axis=1)


def head_lanes(head):
    return slice(head * VALUE_WIDTH, (head + 1) * VALUE_WIDTH)


def window_rows(own_ref, halo_ref, which, head, tile):
    first, lanes = tile * TILE, head_lanes(head)
    if tile == 0:
        after = halo_ref.shape[1] - EDGE + which * WIN
        halo = halo_ref[head, after : after + WIN, :]
        return jnp.concatenate([halo, own_ref[0:TILE, lanes]], axis=0)
    return own_ref[first - WIN : first + TILE, lanes]


def window_tile(info, head, tile, queries, key_rows, value_rows):
    first = tile * TILE
    query_at = column_positions(info, first, TILE)
    key_at = row_positions(info, first - WIN, TILE + WIN)
    near_by = (
        (key_at <= query_at)
        & (query_at - key_at < WIN)
        & (doc_of(info, query_at) == doc_of(info, key_at))
        & (key_at >= 0)
    )
    logits = mm_nt(queries, key_rows) * VALUE_WIDTH ** (-0.5)
    logits = jnp.where(near_by, logits, -1e30)
    exps = jnp.exp(logits - jnp.max(logits, axis=-1, keepdims=True))
    probs = exps / jnp.sum(exps, axis=-1, keepdims=True)
    return probs, mm(probs.astype(bf16), value_rows)


class Near:
    near = True

    def __init__(self, arrays, dims=None, places=None, parts=1):
        self.arrays = [
            a.arrays[0] if isinstance(a, Near) else a
            for a in (arrays if isinstance(arrays, (list, tuple)) else [arrays])
        ]
        self.dims = tuple(dims or self.arrays[0].shape)
        self.dtype = self.arrays[0].dtype
        self.places, self.parts = places, parts

    def copies(self, info, refs, buffer):
        if self.places is None:
            return pieces_of(refs[0], buffer, self.parts)
        return self.places(info, refs, buffer)

    def count(self):
        return self.parts if self.places is None else self.places(None)

    def copied(self):
        return self.places is not None


class Far(Near):
    near = False

    def copied(self):
        return True


class Out:

    def __init__(self, *dims, dtype=bf16, near=False, far=False, parts=1, width=None, first=0, onto=None):
        self.dims, self.dtype, self.parts = dims, dtype, parts
        self.near, self.far = near, far
        self.whole = dims if width is None else (dims[0], width)
        self.first, self.onto = first, onto

    def shapes(self):
        near = [jax.ShapeDtypeStruct(self.dims, self.dtype)] * self.near
        return near + [pltpu.HBM(self.whole, self.dtype)] * self.far

    def spaces(self):
        return [pltpu.VMEM] * self.near + [pltpu.HBM] * self.far

    def copies(self, buffer, target):
        if self.whole != self.dims:
            target = target.at[:, self.first : self.first + self.dims[1]]
        return pieces_of(buffer, target, self.parts)


class Stage:
    near, far, parts, onto = True, False, 1, None

    def __init__(self, source):
        self.source = source if isinstance(source, Far) else Far(source)
        self.dims, self.dtype = self.source.dims, self.source.dtype

    def shapes(self):
        return [jax.ShapeDtypeStruct(self.dims, self.dtype)]

    def spaces(self):
        return [pltpu.VMEM]


class Export:
    near, far, parts, onto = False, True, 1, None

    def __init__(self, source, dims=None, view=None):
        self.source, self.view = source, view
        self.dims, self.dtype = tuple(dims or source.dims), source.dtype

    def shapes(self):
        return [pltpu.HBM(self.dims, self.dtype)]

    def spaces(self):
        return [pltpu.HBM]

    def copies(self, ref, target):
        return [(ref if self.view is None else self.view(ref), target)]


def near(*dims, dtype=bf16):
    return Out(*dims, dtype=dtype, near=True)


def far(*dims, dtype=bf16, parts=1, **columns):
    return Out(*dims, dtype=dtype, far=True, parts=parts, **columns)


def both(*dims, dtype=bf16):
    return Out(*dims, dtype=dtype, near=True, far=True)


def pieces_of(source, target, parts):
    if parts == 1:
        return [(source, target)]
    count = source.shape[0] // parts
    return [
        (source.at[i * count : (i + 1) * count], target.at[i * count : (i + 1) * count])
        for i in range(parts)
    ]


def in_hbm(array):
    return pltpu.with_memory_space_constraint(array, pltpu.HBM)


def call(body, results, operands, starts=None, after=(), flops=0, scratch=(), megabytes=28):
    operands = [o if isinstance(o, Near) else Far(o) for o in operands]
    waits = [pl.ANY if isinstance(o, Near) else pltpu.HBM for o in after]
    after = [o.arrays[0] if isinstance(o, Near) else in_hbm(o) for o in after]
    staged = [o for o in results if isinstance(o, Stage)]
    inputs = operands + [o.source for o in results if isinstance(o, (Stage, Export))]
    arrays = [a for o in inputs for a in o.arrays]
    copied = [o for o in operands if o.copied()]
    held = [o for o in results if not o.near and not isinstance(o, Export)]
    count_out = sum(o.near + o.far for o in results)
    onto = {o: i for i, o in enumerate(results) if o.onto is not None}
    aliases = {len(arrays) + len(after) + i: onto[o] for i, o in enumerate(onto)}
    waits += [pltpu.HBM] * len(onto)
    after += [in_hbm(o.onto) for o in onto]
    moves = sum(o.count() for o in copied) + sum(o.source.count() for o in staged) + sum(o.parts for o in results if o.far)
    named = starts is not None

    def kernel(*refs):
        sources, refs = refs[: len(arrays)], refs[len(arrays) + len(after) :]
        named_ref, refs = (refs[0], refs[1:]) if named else (None, refs)
        targets, rest = list(refs[:count_out]), refs[count_out:]
        buffers, rest = list(rest[: len(copied)]), rest[len(copied) :]
        leaving, rest = list(rest[: len(held)]), rest[len(held) :]
        sems, rest = rest[0], rest[1:]
        marks = None
        if named:
            copy = pltpu.make_async_copy(named_ref, rest[0], sems.at[moves])
            copy.start()
            marks, rest = Loaded(rest[0], [copy]), rest[1:]
        info = Place(marks)
        loaded, at, sem = [], 0, 0

        def copies_of(pairs):
            nonlocal sem
            sem += len(pairs)
            return [
                pltpu.make_async_copy(source, target, sems.at[sem - len(pairs) + i])
                for i, (source, target) in enumerate(pairs)
            ]

        for operand in operands:
            own = sources[at : at + len(operand.arrays)]
            at += len(own)
            if not operand.copied():
                loaded.append(Loaded(own[0], []))
                continue
            buffer = buffers.pop(0)
            loaded.append(Loaded(buffer, copies_of(operand.copies(info, own, buffer))))
            for copy in loaded[-1].copies:
                copy.start()
        stored, staging = [], []
        for result in results:
            if isinstance(result, Export):
                staging += copies_of(result.copies(sources[at], targets.pop(0)))
                at += 1
                continue
            buffer = targets.pop(0) if result.near else leaving.pop(0)
            if isinstance(result, Stage):
                own = sources[at : at + len(result.source.arrays)]
                at += len(own)
                staging += copies_of(result.source.copies(info, own, buffer))
                continue
            target = targets.pop(0) if result.far else None
            pairs = result.copies(buffer, target) if result.far else []
            stored.append(Stored(buffer, copies_of(pairs)))
        for copy in staging:
            copy.start()
        body(info, *loaded, *stored, *rest)
        for copy in staging:
            copy.wait()
        for item in loaded + ([marks] if named else []):
            item.ready()
        for item in stored:
            item.send()
        for item in stored:
            for copy in item.copies:
                copy.wait()

    spaces = [pltpu.VMEM if o.near else pltpu.HBM for o in inputs for _ in o.arrays]
    placed = [a if space is pltpu.VMEM else in_hbm(a) for a, space in zip(arrays, spaces)]
    spaces += waits + [pltpu.HBM] * named
    moved = sum(a.size * a.dtype.itemsize for a in arrays)
    moved += sum(math.prod(o.dims) * jnp.dtype(o.dtype).itemsize for o in results)
    given = pl.pallas_call(
        kernel,
        name=getattr(body, "func", body).__name__,
        out_shape=tuple(s for o in results for s in o.shapes()),
        in_specs=[pl.BlockSpec(memory_space=space) for space in spaces],
        out_specs=tuple(pl.BlockSpec(memory_space=s) for o in results for s in o.spaces()),
        input_output_aliases=aliases,
        scratch_shapes=[pltpu.VMEM(o.dims, o.dtype) for o in copied]
        + [pltpu.VMEM(o.dims, o.dtype) for o in held]
        + [pltpu.SemaphoreType.DMA((max(1, moves + named),))]
        + [pltpu.SMEM((1, 4), jnp.int32)] * named
        + list(scratch),
        compiler_params=pltpu.CompilerParams(vmem_limit_bytes=megabytes * 2**20),
        cost_estimate=pl.CostEstimate(flops=0, bytes_accessed=1024, transcendentals=0),
    )(*placed, *after, *([in_hbm(starts)] if named else []))
    given, answer = list(given), []
    for result in results:
        item = (Near(given.pop(0)),) if result.near else ()
        item += (given.pop(0),) if result.far else ()
        answer.append(item if len(item) == 2 else item[0])
    return answer


def moved_by(array, axis, route):
    array = array.arrays[0] if isinstance(array, Near) else array
    return Near(lax.ppermute(array, axis, route))


def feature_weights(feat_query_t, feat_key_t):
    def places(info, sources=None, buffer=None):
        if info is None:
            return 2
        return [(sources[0], buffer.at[0:32]), (sources[1], buffer.at[32:64])]

    return Far([feat_query_t, feat_key_t], (128, feat_query_t.shape[1]), places)


def own_part(block):
    def places(info, sources=None, buffer=None):
        if info is None:
            return 1
        return [(sources[0].at[info.rows(0)], buffer)]

    return Far(block, (OWN, block.shape[1]), places)


def keys_kernel(
    info, x_ref, gain_ref, key_ref, value_ref, feat_ref, choose_ref, lanes_ref,
    normed_ref, inv_ref, raw_ref, keys_ref, values_ref, km_ref, packed_ref, wide_ref,
):
    gain = gain_ref[...]

    def norm_rows(part):
        for i in range(2):
            rows = slice(part * 128 + i * 64, part * 128 + i * 64 + 64)
            x = x_ref.ref[rows, :].astype(f32)
            inv = lax.rsqrt(jnp.mean(x * x, axis=-1, keepdims=True) + EPS)
            inv_ref[rows, :] = inv
            normed_ref[rows, :] = (x * inv * gain).astype(bf16)

    x_ref.part(0)
    norm_rows(0)
    x_ref.part(1)
    norm_rows(1)
    for ref in (x_ref, feat_ref, key_ref, value_ref, choose_ref, lanes_ref):
        ref.ready()
    feat_ref.ref[64:128, :] = jnp.zeros((64, feat_ref.shape[1]), bf16)
    half = ROWS // 2
    features = []
    for first in (0, half):
        rows = slice(first, first + half)
        normed = normed_ref[rows, :]
        raw = mm_nt(normed, feat_ref[...])
        raw_ref[rows, :] = raw
        if first == 0:
            norm_rows(2)
            norm_rows(3)
        keys_ref[rows, :] = mm(normed, key_ref[...]).astype(bf16)
        values_ref[rows, :] = mm(normed, value_ref[...]).astype(bf16)
        left, right = factors(raw, 1, choose_ref, lanes_ref)
        part = (left * right * lanes_ref[2:3, :]).astype(bf16)
        features.append((part.astype(f32) * lanes_ref[3:4, :]).astype(bf16))
    features = jnp.concatenate(features, axis=0)
    values = values_ref[...]
    for head in range(HEADS):
        km_ref[head] = features[:, head * LANES : (head + 1) * LANES]
    tail = tail_mask(info)
    for head in range(HEADS):
        own = features[:, head * LANES : (head + 1) * LANES]
        lanes = head_lanes(head)
        kept = (values[:, lanes].astype(f32) * tail).astype(bf16)
        state = mm_tn(own, kept)
        norm = jnp.sum(own.astype(f32) * tail, axis=0, keepdims=True)
        write_packed(packed_ref, head, state, norm)
        wide_ref[head, 0:PACKED, :] = packed_ref[head]
        wide_ref[head, PACKED : PACKED + WIN, :] = keys_ref[ROWS - WIN :, lanes]
        wide_ref[head, PACKED + WIN :, :] = values[ROWS - WIN :, lanes]


def local_kernel(
    info, raw_ref, choose_ref, lanes_ref, values_ref, km_ref, normed_ref, query_ref,
    qf_ref, low_ref, num_ref, den_ref, queries_ref,
):
    left, right = factors(raw_ref[...], 0, choose_ref, lanes_ref)
    features = (left * right * lanes_ref[2:3, :]).astype(bf16)
    for head in range(HEADS):
        qf_ref[head] = features[:, head * LANES : (head + 1) * LANES]
    half = ROWS // 2
    causal = []
    for block in range(2):
        query_at = column_positions(info, block * half, half)
        key_at = row_positions(info, 0, (block + 1) * half)
        causal.append((query_at >= key_at) & (doc_of(info, query_at) == doc_of(info, key_at)))
    for head in range(HEADS):
        for block in range(2):
            first, reach = block * half, (block + 1) * half
            own = qf_ref[head, first:reach, :]
            weights = jnp.where(causal[block], mm_nt(own, km_ref[head, :reach, :]), 0.0)
            den_ref[head, first:reach, :] = jnp.sum(weights, axis=-1, keepdims=True)
            weights = weights.astype(bf16)
            low_ref[head, first:reach, 0:reach] = weights
            num_ref[first:reach, head_lanes(head)] = mm(
                weights, values_ref[:reach, head_lanes(head)]
            )
    queries_ref[...] = mm(normed_ref[...], query_ref[...]).astype(bf16)


def window_kernel(
    info, queries_ref, keys_ref, values_ref, probs_ref, window_ref,
):
    queries = queries_ref[...]
    for head in range(HEADS):
        lanes = head_lanes(head)
        for tile in range(1, ROWS // TILE):
            rows = slice(tile * TILE, (tile + 1) * TILE)
            probs, result = window_tile(
                info, head, tile, queries[rows, lanes],
                window_rows(keys_ref, None, 0, head, tile), window_rows(values_ref, None, 1, head, tile),
            )
            probs_ref[head, tile - 1] = probs
            window_ref[rows, lanes] = result


def by_distance(ref, info, other):
    return jnp.concatenate([ref[info.rows(d, other), :] for d in range(4)], axis=0)


def mixed_kernel(
    info, before_ref, got1_ref, got2_ref, got3_ref, qf_ref, num_ref, den_ref, window_ref, out_ref,
    queries_ref, keys_ref, values_ref,
    mixed_ref, linear_ref, total_den_ref, state_ref, norm_ref, probs_ref, other_ref,
):
    use = prefix_mask(info)
    for head in range(HEADS):
        lanes = head_lanes(head)
        state, norm = read_total(before_ref, (got1_ref, got2_ref, got3_ref), head)
        state_ref[head] = state
        norm_ref[head] = jnp.broadcast_to(norm, (8, LANES))
        features = qf_ref[head]
        inter = mm(features, state) * use
        den = jnp.sum(features.astype(f32) * norm, axis=-1, keepdims=True) * use + den_ref[head]
        total_den_ref[head] = den
        linear = (inter + num_ref[:, lanes]) / den
        linear_ref[:, lanes] = linear
        probs, window = window_tile(
            info, head, 0, queries_ref[0:TILE, lanes],
            window_rows(keys_ref, got1_ref, 0, head, 0), window_rows(values_ref, got1_ref, 1, head, 0),
        )
        probs_ref[head] = probs
        mixed_ref[0:TILE, lanes] = (linear[0:TILE] + window).astype(bf16)
        mixed_ref[TILE:, lanes] = (linear[TILE:] + window_ref[TILE:, lanes]).astype(bf16)
    other_ref[...] = mm(by_distance(mixed_ref, info, True), out_ref[...]).astype(bf16)


def mixed_own_kernel(info, mixed_ref, out_ref, own_ref):
    own_ref[...] = mm(by_distance(mixed_ref, info, False), out_ref[...]).astype(bf16)


def quarters_kernel(info, own_ref, got_ref, *out_refs):
    out_refs[4][...] = got_ref[0:16, 0:128]
    for d in (1, 2, 3, 0):
        rows = slice(d * OWN, (d + 1) * OWN)
        total = own_ref[rows, :].astype(f32) + got_ref[rows, :].astype(f32)
        out_refs[d][...] = total.astype(out_refs[d].dtype)
        out_refs[d].send()


def resid_kernel(
    info, mine_ref, x_ref, gain_ref, got1_ref, got2_ref, got3_ref, normed_ref, resid_ref, inv_ref
):
    resid = x_ref[...].astype(f32) + mine_ref[...]
    for ref in (got1_ref, got2_ref, got3_ref):
        resid = resid + ref[...].astype(f32)
    resid_ref[...] = resid
    inv = lax.rsqrt(jnp.mean(resid * resid, axis=-1, keepdims=True) + EPS)
    inv_ref[...] = inv
    normed_ref[...] = (resid * inv * gain_ref[...]).astype(bf16)


def grad_resid_kernel(
    info, mine_ref, resid_ref, inv_ref, top_ref, gain_ref, got1_ref, got2_ref, got3_ref,
    sent_ref, grad_ref, gains_ref,
):
    grad = mine_ref[...]
    for ref in (got1_ref, got2_ref, got3_ref):
        grad = grad + ref[...].astype(f32)
    resid = resid_ref[...]
    inv = inv_ref[...]
    grad_resid = top_ref[...].astype(f32) + norm_back(resid, inv, gain_ref[...], grad)
    sent_ref[...] = grad_resid.astype(bf16)
    sent_ref.send()
    grad_ref[...] = grad_resid
    gains_ref[0:1, :] = jnp.sum(grad * resid * inv, axis=0, keepdims=True)


def grad_x_kernel(
    info, mine_ref, x_ref, grad_resid_ref, gain_ref, resid_ref, out_ref, got1_ref, got2_ref, got3_ref,
    out1_ref, out2_ref, out3_ref, sent_ref,
):
    total = resid_ref[...] + out_ref[...]
    for ref in (out1_ref, out2_ref, out3_ref):
        total = total + ref[...].astype(f32)
    sent_ref[0:OWN, :] = total.astype(bf16)
    grad = mine_ref[...]
    for ref in (got1_ref, got2_ref, got3_ref):
        grad = grad + ref[...].astype(f32)
    x = x_ref[...].astype(f32)
    inv = lax.rsqrt(jnp.mean(x * x, axis=-1, keepdims=True) + EPS)
    sent_ref[OWN:, :] = (grad_resid_ref[...] + norm_back(x, inv, gain_ref[...], grad)).astype(bf16)


def norm_back(in_rows, inv_rms, gain, grad_normed):
    weighted = grad_normed * gain
    return inv_rms * weighted - in_rows * inv_rms**3 * jnp.mean(
        weighted * in_rows, axis=-1, keepdims=True
    )


def by_halves(block):
    def places(info, sources=None, buffer=None):
        if info is None:
            return 8
        return [
            (sources[0].at[info.rows(i % 4, other=i >= 4)], buffer.at[i * OWN : (i + 1) * OWN])
            for i in range(8)
        ]

    return Far(block, block.shape, places)


def grad_act_kernel(info, top_ref, down_ref, own_ref, other_ref):
    top = top_ref[...]
    half = ROWS // 2
    for first in range(0, down_ref.shape[0], 256):
        span = slice(first, min(first + 256, down_ref.shape[0]))
        grad = mm_nt(top, down_ref[span, :])
        own_ref[:, span] = grad[:half]
        other_ref[:, span] = grad[half:]


def ffn_rows(pieces, gate_ref, up_ref, grad_act_ref, normed_ref, act_ref, grad_gate_ref, grad_up_ref):
    normed = jnp.concatenate([piece[...] for piece in pieces], axis=0)
    normed_ref[...] = normed
    hidden = gate_ref.shape[0]
    for first in range(0, hidden, 256):
        span = slice(first, min(first + 256, hidden))
        gate = mm_nt(normed, gate_ref[span, :])
        up_value = mm_nt(normed, up_ref[span, :])
        sigmoid_gate = jax.nn.sigmoid(gate)
        silu_gate = gate * sigmoid_gate
        act_ref[:, span] = (silu_gate * up_value).astype(bf16)
        grad_act = grad_act_ref[:, span]
        grad_gate_ref[:, span] = (
            grad_act * up_value * sigmoid_gate * (1.0 + gate * (1.0 - sigmoid_gate))
        ).astype(bf16)
        grad_up_ref[:, span] = (grad_act * silu_gate).astype(bf16)


def ffn_own_kernel(info, p0, p3, p1, p2, gate_ref, up_ref, grad_act_ref, *out_refs):
    ffn_rows((p0, p3, p2, p1), gate_ref, up_ref, grad_act_ref, *out_refs)


def ffn_other_kernel(info, s0, s3, s1, s2, gate_ref, up_ref, grad_act_ref, back_ref, *out_refs):
    ffn_rows((s0, s3, s2, s1), gate_ref, up_ref, grad_act_ref, *out_refs)
    ffn_back_kernel(info, out_refs[2], out_refs[3], gate_ref, up_ref, back_ref)


def ffn_back_kernel(info, grad_gate_ref, grad_up_ref, gate_ref, up_ref, back_ref):
    grad_gate, grad_up = grad_gate_ref[...], grad_up_ref[...]
    for first in range(0, back_ref.shape[1], 512):
        span = slice(first, first + 512)
        part = mm(grad_gate, gate_ref[:, span]) + mm(grad_up, up_ref[:, span])
        back_ref[:, span] = part.astype(bf16)


def ffn_out_kernel(info, act_own_ref, act_other_ref, down_ref, other_ref, own_ref):
    for target, act_ref in ((other_ref, act_other_ref), (own_ref, act_own_ref)):
        act = act_ref[...]
        for first in range(0, target.shape[1], 512):
            span = slice(first, first + 512)
            target[:, span] = mm(act, down_ref[:, span]).astype(bf16)


def column_grads(pairs, out_ref, last=None):
    count = out_ref.shape[0] // 4
    for part in range(4):
        span = slice(part * count, (part + 1) * count)
        first = 0
        for i, (rows_refs, grads) in enumerate(pairs):
            rows_refs = rows_refs if isinstance(rows_refs, tuple) else (rows_refs,)
            grads = grads if isinstance(grads, tuple) else (grads,)
            total = sum(mm_tn(rows[:, span], grad) for rows, grad in zip(rows_refs, grads))
            if last is not None and i == len(pairs) - 1:
                total = total + last[span, :].astype(f32)
            end = first + total.shape[1]
            out_ref[span, first:end] = total.astype(bf16)
            first = end
        out_ref.send(part)


def gate_grads_kernel(
    info, own_ref, other_ref, gate_own_ref, gate_other_ref, up_own_ref, up_other_ref, out_ref
):
    rows = (own_ref, other_ref)
    gate = (gate_own_ref[...], gate_other_ref[...])
    up = (up_own_ref[...], up_other_ref[...])
    column_grads(((rows, gate), (rows, up)), out_ref)


class Rows:

    def __init__(self, ref, first, count):
        self.ref, self.rows = ref, slice(first, first + count)

    def __getitem__(self, index):
        return self.ref[self.rows, index[1]]


def down_grads_kernel(info, top_ref, act_own_ref, act_other_ref, out_ref, tail_ref):
    half, whole = ROWS // 2, out_ref.shape[1]
    rows = (Rows(top_ref, 0, half), Rows(top_ref, half, half))
    acts = (act_own_ref[...], act_other_ref[...])
    column_grads(((rows, tuple(act[:, :whole] for act in acts)),), out_ref)
    room = jnp.zeros((half, 128 - acts[0].shape[1] % 128), bf16)
    rest = [jnp.concatenate([act[:, whole:], room], axis=1) for act in acts]
    tail_ref[...] = sum(mm_tn(row[:, :], act) for row, act in zip(rows, rest)).astype(bf16)


def grad_x_out_kernel(info, p0, p1, p2, p3, s0, s1, s2, s3, output_ref, grad_ref):
    for i, piece in enumerate((p0, p1, p2, p3, s0, s1, s2, s3)):
        rows = info.rows(4 - i % 4, other=i >= 4)
        output_ref[rows, :] = piece[0:OWN, :]
        grad_ref[rows, :] = piece[OWN : 2 * OWN, :].astype(f32)


def window_tile_back(top, probs, key_rows, value_rows):
    grad_probs = mm_nt(top, value_rows)
    shared = jnp.sum(grad_probs * probs, axis=-1, keepdims=True)
    return (probs * (grad_probs - shared)).astype(bf16)


def mixed_back_kernel(
    info, p0, p3, p1, p2, s0, s3, s1, s2, out_ref, linear_ref, den_ref, qf_ref, probs0_ref, keys_ref,
    values_ref, halo_ref, queries_ref, packed_ref, wide_ref, top_ref, gm_ref, gnum_ref, gden_ref,
):
    for i, piece in enumerate((p0, p1, p2, p3, s0, s1, s2, s3)):
        top_ref[info.rows(4 - i % 4, other=i >= 4), :] = piece[...]
    grad_mixed = mm_nt(top_ref[...], out_ref[...]).astype(bf16)
    gm_ref[...] = grad_mixed
    use = prefix_mask(info)
    for head in range(HEADS):
        lanes = head_lanes(head)
        wide = grad_mixed[:, lanes].astype(f32)
        den = den_ref[head]
        grad_num = (wide / den).astype(bf16)
        gnum_ref[:, lanes] = grad_num
        grad_den = -jnp.sum(wide * linear_ref[:, lanes], axis=-1, keepdims=True) / den
        gden_ref[head] = grad_den
        features = qf_ref[head]
        used = (grad_num.astype(f32) * use).astype(bf16)
        state = mm_tn(features, used)
        norm = jnp.sum(features.astype(f32) * (grad_den * use), axis=0, keepdims=True)
        write_packed(packed_ref, head, state, norm)
        wide_ref[head, 0:PACKED, :] = packed_ref[head]
        top, probs = grad_mixed[0:TILE, lanes], probs0_ref[head]
        grad_logits = window_tile_back(
            top, probs, window_rows(keys_ref, halo_ref, 0, head, 0),
            window_rows(values_ref, halo_ref, 1, head, 0),
        )
        grad_keys = mm_tn(grad_logits, queries_ref[0:TILE, lanes]) * VALUE_WIDTH ** (-0.5)
        wide_ref[head, PACKED : PACKED + WIN, :] = grad_keys[0:WIN].astype(bf16)
        grad_values = mm_tn(probs.astype(bf16), top)
        wide_ref[head, PACKED + WIN :, :] = grad_values[0:WIN].astype(bf16)


def window_back_kernel(
    info, gm_ref, probs0_ref, probs_ref, keys_ref, values_ref, halo_ref, queries_ref,
    top_ref, mixed_ref, gq_ref, gk_ref, gv_ref, out_ref, key_acc, value_acc,
):
    column_grads(((top_ref, mixed_ref[...]),), out_ref)
    scale = VALUE_WIDTH ** (-0.5)
    key_acc[...] = jnp.zeros_like(key_acc)
    value_acc[...] = jnp.zeros_like(value_acc)
    for tile in range(ROWS // TILE):
        first = tile * TILE
        reach = slice(first, first + TILE + WIN)
        for head in range(HEADS):
            lanes = head_lanes(head)
            key_rows = window_rows(keys_ref, halo_ref, 0, head, tile)
            value_rows = window_rows(values_ref, halo_ref, 1, head, tile)
            top = gm_ref[first : first + TILE, lanes]
            probs = probs0_ref[head] if tile == 0 else probs_ref[head, tile - 1]
            grad_logits = window_tile_back(top, probs, key_rows, value_rows)
            gq_ref[first : first + TILE, lanes] = (mm(grad_logits, key_rows) * scale).astype(bf16)
            queries = queries_ref[first : first + TILE, lanes]
            key_acc[reach, lanes] += mm_tn(grad_logits, queries) * scale
            value_acc[reach, lanes] += mm_tn(probs.astype(bf16), top)
    gk_ref[...] = key_acc[WIN:, :]
    gv_ref[...] = value_acc[WIN:, :]


def linear_back_kernel(
    info, gnum_ref, gden_ref, values_ref, low_ref, km_ref, qf_ref, state_ref, norm_ref, raw_ref,
    choose_ref, choose_k_ref, lanes_ref, window_gv_ref, normed_ref, gq_ref,
    gfeat_ref, gv_ref, gkf_ref, left_ref, right_ref, out_ref,
):
    column_grads(((normed_ref, gq_ref[...]),), out_ref)
    use = prefix_mask(info)
    half = ROWS // 2
    grads = [[None, None], [None, None]]
    for head in range(HEADS):
        lanes = head_lanes(head)
        inter = mm_nt((gnum_ref[:, lanes].astype(f32) * use).astype(bf16), state_ref[head])
        inter = inter + (gden_ref[head] * use) * norm_ref[head, 0:1, :]
        for block in range(2):
            first, reach = block * half, (block + 1) * half
            query_at = column_positions(info, first, half)
            key_at = row_positions(info, 0, reach)
            causal = (query_at >= key_at) & (doc_of(info, query_at) == doc_of(info, key_at))
            grad_num = gnum_ref[first:reach, lanes]
            grad = mm_nt(grad_num, values_ref[:reach, lanes]) + gden_ref[head, first:reach, :]
            grad = jnp.where(causal, grad, 0.0).astype(bf16)
            grads[head][block] = mm(grad, km_ref[head, :reach, :]) + inter[first:reach]
            key_part = mm_tn(grad, qf_ref[head, first:reach, :])
            value_part = mm_tn(low_ref[head, first:reach, 0:reach], grad_num)
            if block == 0:
                gkf_ref[head, 0:half] = key_part
                gv_ref[0:half, lanes] = window_gv_ref[0:half, lanes] + value_part
            else:
                gkf_ref[head, 0:half] += key_part[0:half]
                gkf_ref[head, half:] = key_part[half:]
                gv_ref[0:half, lanes] += value_part[0:half]
                gv_ref[half:, lanes] = window_gv_ref[half:, lanes] + value_part[half:]
    left, right = factors(raw_ref[...], 0, choose_ref, lanes_ref)
    gradient = jnp.concatenate([jnp.concatenate(g, axis=0) for g in grads], axis=1)
    gradient = gradient * lanes_ref[2:3, :]
    gfeat_ref[...] = feature_back(gradient, left, right, choose_ref)
    left_ref[...], right_ref[...] = factors(raw_ref[...], 1, choose_k_ref, lanes_ref)


def keys_back_kernel(
    info, before_ref, got1_ref, got2_ref, got3_ref, values_ref, km_ref, gkf_ref, gk_ref, gv_ref,
    left_ref, right_ref, choose_ref, lanes_ref, gfeat_ref, normed_ref, tail_ref,
    gkw_ref, gvw_ref, gf_ref, out_ref,
):
    tail = tail_mask(info)
    inner = ROWS - WIN
    gkw_ref[0:inner, :] = gk_ref[0:inner, :].astype(bf16)
    gradients = []
    for head in range(HEADS):
        lanes = head_lanes(head)
        later, norm = read_total(before_ref, (got1_ref, got2_ref, got3_ref), head)
        kept = (values_ref[:, lanes].astype(f32) * tail).astype(bf16)
        gradients.append(gkf_ref[head] + mm_nt(kept, later) + tail * norm)
        grad_values = gv_ref[:, lanes] + mm(km_ref[head], later) * tail
        gvw_ref[0:inner, lanes] = grad_values[0:inner].astype(bf16)
        right = got1_ref[head, PACKED:, :].astype(f32)
        gkw_ref[inner:, lanes] = (gk_ref[inner:, lanes] + right[0:WIN]).astype(bf16)
        gvw_ref[inner:, lanes] = (grad_values[inner:] + right[WIN:]).astype(bf16)
    gradient = jnp.concatenate(gradients, axis=1) * lanes_ref[4:5, :]
    gradient = feature_back(gradient, left_ref[...], right_ref[...], choose_ref) + gfeat_ref[...]
    gf_ref[...] = gradient.astype(bf16)
    lane = lax.broadcasted_iota(jnp.int32, (1, 128), 1)
    beside = jnp.where(lane < 64, 0.0, pltpu.roll(gradient, 64, 1)).astype(bf16)
    column_grads(
        (
            (normed_ref, gkw_ref[...]), (normed_ref, gvw_ref[...]), (normed_ref, beside),
        ),
        out_ref, last=tail_ref,
    )


def normed_back_kernel(
    info, gq_ref, gkw_ref, gvw_ref, gf_ref, wq_ref, wk_ref, wv_ref, wf_ref, x_ref, inv_ref, gain_ffn_ref,
    other_ref, own_ref, gains_ref,
):
    wf_ref.ready()
    wf_ref.ref[64:128, :] = jnp.zeros((64, wf_ref.shape[1]), bf16)
    for target, other in ((other_ref, True), (own_ref, False)):
        grads = [by_distance(ref, info, other) for ref in (gq_ref, gkw_ref, gvw_ref, gf_ref)]
        scaled_by = by_distance(inv_ref, info, other)
        for piece in range(4):
            span = slice(piece * 512, (piece + 1) * 512)
            part = mm_nt(grads[0], wq_ref[span, :])
            part = part + mm_nt(grads[1], wk_ref[span, :])
            part = part + mm_nt(grads[2], wv_ref[span, :])
            part = part + mm(grads[3], wf_ref[:, span])
            target[:, span] = part.astype(bf16)
            x_rows = jnp.concatenate([x_ref[info.rows(d, other), span] for d in range(4)], axis=0)
            total = jnp.sum(part * (x_rows.astype(f32) * scaled_by), axis=0, keepdims=True)
            gains_ref[0:1, span] = total if other else total + gains_ref[0:1, span]
    gains_ref[1:2, :] = gain_ffn_ref[0:1, :]


def columns(block, first, last):
    def places(info, sources=None, buffer=None):
        return 1 if info is None else [(sources[0].at[:, first:last], buffer)]

    return Far(block, (block.shape[0], last - first), places)


def grads_out_kernel(
    info, both_ref, in_ref, gate_ref, up_ref, down_ref, out_ref, grad_q_ref, grad_k_ref, grad_v_ref,
    feat_query_ref, feat_key_ref,
):
    hidden, width = gate_ref.shape[0], out_ref.shape[0]
    whole = hidden // 128 * 128
    both = both_ref[...].T
    gate_ref[...] = both[0:hidden].astype(f32)
    gate_ref.send()
    up_ref[...] = both[hidden:].astype(f32)
    up_ref.send()
    down_ref[0:whole, :] = in_ref[:, 0:whole].T.astype(f32)
    at = whole
    out_ref[...] = in_ref[:, at : at + width].T.astype(f32)
    out_ref.send()
    for ref in (grad_q_ref, grad_k_ref, grad_v_ref):
        at += width
        ref[...] = in_ref[:, at : at + width].astype(f32)
        ref.send()
    tail = in_ref[:, at + width :].astype(f32).T
    down_ref[whole:, :] = tail[0 : hidden - whole]
    down_ref.send()
    feat_query_ref[...] = tail[64:96]
    feat_key_ref[...] = tail[96:128]


def total_of(refs):
    total = refs[0][...]
    for ref in refs[1:]:
        total = total + ref[...]
    return total


def gains_kernel(info, *refs):
    refs[-1][...] = total_of(refs[:-1])


def spread_kernel(info, *refs):
    total, out_ref = total_of(refs[:-1]), refs[-1]
    for i in range(out_ref.shape[0]):
        out_ref[i, 0:2, :] = total[:, i * 128 : (i + 1) * 128]
        out_ref[i, 2:, :] = jnp.zeros((6, 128), f32)


def gathered_sum_kernel(info, in_ref, out_ref):
    total = in_ref[0]
    for i in range(1, in_ref.shape[0]):
        total = total + in_ref[i]
    out_ref[...] = total


def along_y(distance):
    return [(i, (i + 2 * distance) % 8) for i in range(8)]


def sibling():
    return [(i, i ^ 1) for i in range(8)]


def along_x(distance):
    return [(i, (i + 4 * distance) % 16) for i in range(16)]


def along_z(distance):
    return [(4 * a + z, 4 * a + (z + distance) % 4) for a in range(4) for z in range(4)]


def head_quarters(own, other, after=()):
    got = moved_by(other, "head", sibling())
    width = own.dims[1]
    with jax.named_scope("quarters"):
        mine, *sent, token = call(
            quarters_kernel,
            [near(OWN, width, dtype=f32)] + [near(OWN, width)] * 3 + [near(16, 128)],
            (own, got), after=after,
        )
    parts = [moved_by(sent[d - 1], "head", along_y(d)) for d in (2, 1, 3)]
    return mine, parts, moved_by(token, "head", sibling())


def head_pieces(own):
    far_piece = moved_by(own, "head", along_y(2))
    pieces = [own, moved_by(own, "head", along_y(1)), far_piece, moved_by(own, "head", along_y(3))]
    return pieces + [moved_by(piece, "head", sibling()) for piece in pieces]


def gains_sum(gains):
    with jax.named_scope("gains"):
        (pair,) = call(
            gains_kernel, [near(*gains.dims, dtype=f32)], (gains, moved_by(gains, "head", sibling()))
        )
        parts = [pair] + [moved_by(pair, "head", along_y(d)) for d in (2, 1, 3)]
        (blocks,) = call(spread_kernel, [far(16, 8, 128, dtype=f32)], parts)
        blocks = lax.all_to_all(blocks, "seq", 0, 0)
        (total,) = call(gathered_sum_kernel, [far(8, 128, dtype=f32)], (blocks,))
    return total


def scan_kernel(reverse, info, own_ref, got1_ref, got2_ref, got3_ref, before_ref, *sent_refs):
    place_x, place_z = (3 - info.x, 3 - info.z) if reverse else (info.x, info.z)
    before = jnp.zeros(before_ref.shape, f32)
    for d, ref in enumerate((got1_ref, got2_ref, got3_ref), 1):
        before = before + ref[:, 0:PACKED, :].astype(f32) * (place_x >= d).astype(f32)
    before_ref[...] = before
    row = lax.broadcasted_iota(jnp.int32, (HEADS, 16, 128), 1) + (KEPT - FEATURES)
    sent = []
    for total in (before, before + own_ref[:, 0:PACKED, :].astype(f32)):
        tile = total[:, KEPT:]
        norm = tile + jnp.roll(tile, -2, axis=1)
        high = norm.astype(bf16).astype(f32)
        rest = jnp.roll(norm - high, 2, axis=1)
        norm = jnp.where(row < 0, tile, jnp.where(row < 2, high, jnp.where(row < 4, rest, 0.0)))
        sent.append((total[:, :KEPT], norm))
    for d, ref in enumerate(sent_refs, 1):
        with_own = (place_z + d < 4).astype(f32)
        for part, rows in ((0, slice(0, KEPT)), (1, slice(KEPT, PACKED))):
            less, more = sent[0][part], sent[1][part]
            ref[:, rows, :] = (more * with_own + less * (1.0 - with_own)).astype(bf16)
        if ref.shape[1] > PACKED:
            own, earlier = own_ref[:, PACKED:, :].astype(f32), got1_ref[:, PACKED:, :].astype(f32)
            ref[:, PACKED:, :] = (own * with_own + earlier * (1.0 - with_own)).astype(bf16)


def exclusive_parts(own, reverse, after=(), wide=None):
    sign = -1 if reverse else 1
    first = own if wide is None else wide
    got = [moved_by(first if d == 1 else own, "seq", along_x(sign * d)) for d in (1, 2, 3)]
    with jax.named_scope("scan"):
        before, *sent = call(
            functools.partial(scan_kernel, reverse),
            [near(*own.dims, dtype=f32), near(*first.dims), near(*own.dims), near(*own.dims)],
            (first, *got), after=after,
        )
    return [before] + [
        moved_by(sent[d - 1], "seq", along_z(sign * d)) for d in (1, 2, 3)
    ]


def shards(
    inputs,
    gain_mix,
    feat_query,
    feat_key,
    win_query,
    win_key,
    value_proj,
    out_proj,
    gain_ffn,
    gate_proj,
    up_proj,
    down_proj,
    document_starts,
    cotangent,
):
    choose, lanes = feature_tables()
    choose = jnp.asarray(choose, bf16)
    lanes = jnp.asarray(lanes, f32)
    choose_q, choose_k = choose[0], choose[1]
    feat = feature_weights(feat_query.T, feat_key.T)
    gain_mix = gain_mix.reshape(1, -1)
    gain_ffn = gain_ffn.reshape(1, -1)
    model = inputs.shape[1]
    width = HEADS * VALUE_WIDTH
    hidden = gate_proj.shape[1]
    half = ROWS // 2
    unit = 2 * ROWS * model
    starts = document_starts

    normed, inv_mix, raw, keys, values, km, packed, wide = call(
        keys_kernel,
        (
            near(ROWS, model), near(ROWS, 1, dtype=f32), near(ROWS, 128, dtype=f32),
            near(ROWS, width), near(ROWS, width), near(HEADS, ROWS, LANES),
            near(HEADS, PACKED, 128), near(HEADS, PACKED + EDGE, 128),
        ),
        (Far(inputs, parts=4), gain_mix, win_key, value_proj, feat, choose_k, lanes),
        starts=starts, flops=unit * 640,
    )
    qf, low, num, den, queries, near_out, normed_far, inv_mix, raw_far, keys_far, values_far, km_far = call(
        local_kernel,
        (
            near(HEADS, ROWS, LANES), near(HEADS, ROWS, ROWS), near(ROWS, width, dtype=f32),
            near(HEADS, ROWS, 1, dtype=f32), near(ROWS, width), Stage(out_proj), Export(normed),
            Export(inv_mix), Export(raw), Export(keys), Export(values), Export(km),
        ),
        (raw, choose_q, lanes, values, km, normed, win_query),
        starts=starts, flops=unit * 300,
    )
    sums = exclusive_parts(packed, False, after=(qf,), wide=wide)
    probs, window, qf_far, low = call(
        window_kernel,
        (
            near(HEADS, 3, TILE, TILE + WIN, dtype=f32),
            near(ROWS, width, dtype=f32), Export(qf), Export(low),
        ),
        (queries, keys, values),
        starts=starts, flops=unit * 400,
    )
    mixed, linear, total_den, state, norm, probs_first, other = call(
        mixed_kernel,
        (
            near(ROWS, width), near(ROWS, width, dtype=f32), near(HEADS, ROWS, 1, dtype=f32),
            near(HEADS, LANES, VALUE_WIDTH), near(HEADS, 8, LANES, dtype=f32),
            near(HEADS, TILE, TILE + WIN, dtype=f32), near(half, model),
        ),
        (*sums, qf, num, den, window, near_out, queries, keys, values),
        starts=starts, flops=unit * 300,
    )
    own, halo, *rest = call(
        mixed_own_kernel,
        (
            near(half, model),
            Export(sums[1], (HEADS, EDGE, 128), lambda ref: ref.at[:, PACKED:, :]),
            *map(Export, (mixed, linear, total_den, state, norm, probs_first, probs, queries)),
        ),
        (mixed, near_out), after=(other,), flops=unit * 100,
    )
    mixed, linear, total_den, state, norm, probs_first, probs, queries_far = rest
    mine, parts, signal = head_quarters(own, other)
    grad_act_own, grad_act_other, x_own, near_gain, near_gate, near_up = call(
        grad_act_kernel,
        (
            near(half, hidden, dtype=f32), near(half, hidden, dtype=f32), Stage(own_part(inputs)), Stage(gain_ffn),
            Stage(gate_proj.T), Stage(up_proj.T),
        ),
        (by_halves(cotangent), down_proj),
        after=(signal,), flops=unit * hidden,
    )
    own_normed, resid, inv_ffn = call(
        resid_kernel,
        (near(OWN, model), near(OWN, model, dtype=f32), near(OWN, 1, dtype=f32)),
        (mine, x_own, near_gain, *parts), after=(grad_act_own,),
    )
    pieces = head_pieces(own_normed)
    def ffn_half(body, pieces, grad_act, *more, after=()):
        order = [pieces[i] for i in (0, 3, 1, 2)]
        return call(
            body,
            (
                *more, near(half, model), near(half, hidden), near(half, hidden), near(half, hidden),
            ),
            (*order, near_gate, near_up, grad_act), after=after, flops=unit * 2 * hidden,
        )

    normed_own, act_own, gate_own, up_own = ffn_half(ffn_own_kernel, pieces[:4], grad_act_own)
    other, normed_other, act_other, gate_other, up_other = ffn_half(
        ffn_other_kernel, pieces[4:], grad_act_other, near(half, model), after=(gate_own,)
    )
    (own,) = call(
        ffn_back_kernel, (near(half, model),), (gate_own, up_own, near_gate, near_up),
        after=(other,), flops=unit * hidden,
    )
    mine, parts, signal = head_quarters(own, other)
    whole = hidden // 128 * 128
    place = dict(parts=4, width=2 * hidden + whole + 4 * width + 128)
    grads, resid_far, near_top, near_gain, *near_mixed = call(
        gate_grads_kernel,
        (
            far(model, 2 * hidden, **place), Export(resid), Stage(own_part(cotangent)),
            Stage(gain_ffn), Stage(out_proj), Stage(linear), Stage(total_den), Stage(qf_far),
            Stage(probs_first), Stage(probs), Stage(keys_far), Stage(values_far), Stage(halo),
            Stage(queries_far),
        ),
        (normed_own, normed_other, gate_own, gate_other, up_own, up_other),
        after=(signal,), flops=unit * 2 * hidden,
    )
    at = 2 * hidden
    *near_mixed, probs_first, probs, keys, values, halo, queries = near_mixed
    grads, tail, *near_back = call(
        down_grads_kernel,
        (
            far(model, whole, first=at, onto=grads, **place), near(model, 128), Stage(low),
            Stage(km_far),
            Stage(state), Stage(norm), Stage(raw_far), Stage(choose_q), Stage(choose_k),
            Stage(lanes), Stage(mixed), Export(act_own), Export(act_other),
        ),
        (by_halves(cotangent), act_own, act_other), after=(signal,), flops=unit * hidden,
    )
    low, km, state, norm, raw, *rest = near_back
    choose_q, choose_k, lanes, mixed, act_own, act_other = rest
    at += whole
    sent, grad_resid, gain_ffn_part = call(
        grad_resid_kernel,
        (near(OWN, model), near(OWN, model, dtype=f32), near(8, model, dtype=f32)),
        (mine, resid, inv_ffn, near_top, near_gain, *parts), after=(grads,),
    )
    pieces = head_pieces(sent)
    packed, wide, top, grad_mixed, grad_num, grad_den = call(
        mixed_back_kernel,
        (
            near(HEADS, PACKED, 128), near(HEADS, PACKED + EDGE, 128), near(ROWS, model), near(ROWS, width), near(ROWS, width),
            near(HEADS, ROWS, 1, dtype=f32),
        ),
        (
            *[pieces[i] for i in (0, 3, 1, 2, 4, 7, 5, 6)], *near_mixed, probs_first, keys, values,
            halo, queries,
        ),
        starts=starts, flops=unit * 300,
    )
    gq, gk, gv, grads, normed = call(
        window_back_kernel,
        (
            near(ROWS, width), near(ROWS, width, dtype=f32),
            near(ROWS, width, dtype=f32), far(model, width, first=at, onto=grads, **place),
            Stage(normed_far),
        ),
        (grad_mixed, probs_first, probs, keys, values, halo, queries, top, mixed),
        flops=unit * 300, scratch=[pltpu.VMEM((ROWS + WIN, width), f32)] * 2,
    )
    sums = exclusive_parts(packed, True, after=(gq,), wide=wide)
    gfeat, gv, gkf, left, right, grads = call(
        linear_back_kernel,
        (
            near(ROWS, 128, dtype=f32), near(ROWS, width, dtype=f32),
            near(HEADS, ROWS, LANES, dtype=f32), near(ROWS, HEADS * LANES, dtype=f32),
            near(ROWS, HEADS * LANES, dtype=f32),
            far(model, width, first=at + width, onto=grads, **place),
        ),
        (
            grad_num, grad_den, values, low, km, near_mixed[3], state, norm, raw, choose_q, choose_k,
            lanes, gv, normed, gq,
        ),
        starts=starts, after=(sums[0],), flops=unit * 300,
    )
    gkw, gvw, gf, grads = call(
        keys_back_kernel,
        (
            near(ROWS, width), near(ROWS, width), near(ROWS, 128),
            far(model, 2 * width + 128, first=at + 2 * width, onto=grads, **place),
        ),
        (
            *sums, values, km, gkf, gk, gv, left, right, choose_k, lanes, gfeat, normed, tail,
        ),
        starts=starts, flops=unit * 1400,
    )
    grads_sum = lax.psum_scatter(grads, "seq", scatter_dimension=0, tiled=True)
    other, own, gains = call(
        normed_back_kernel, (near(half, model), near(half, model), near(2, model, dtype=f32)),
        (
            gq, gkw, gvw, gf, win_query, win_key, value_proj, feat, inputs, inv_mix, gain_ffn_part,
        ),
        after=(grads,),
        flops=unit * 900,
    )
    mine, parts, signal = head_quarters(own, other)
    other, own = call(
        ffn_out_kernel, (near(half, model), near(half, model)), (act_own, act_other, down_proj),
        after=(signal,), flops=unit * hidden,
    )
    out_mine, out_parts, signal = head_quarters(own, other)
    gains = gains_sum(gains)
    (sent,) = call(
        grad_x_kernel, (near(2 * OWN, model),),
        (mine, own_part(inputs), grad_resid, gain_mix, resid_far, out_mine, *parts, *out_parts),
        after=(gains,),
    )
    pieces = head_pieces(sent)
    output, grad_x = call(
        grad_x_out_kernel, (far(ROWS, model), far(ROWS, model, dtype=f32)), pieces,
    )
    grad_gate_t, grad_up_t, grad_down, grad_out, *rest = call(
        grads_out_kernel,
        (far(hidden, 128, dtype=f32),) * 3 + (far(width, 128, dtype=f32),)
        + (far(128, width, dtype=f32),) * 3 + (far(32, 128, dtype=f32),) * 2,
        (columns(grads_sum, 0, 2 * hidden), columns(grads_sum, 2 * hidden, grads_sum.shape[1])),
        after=(grad_x,),
    )
    grad_wq, grad_wk, grad_wv, grad_fq_t, grad_fk_t = rest
    return (
        output,
        grad_x,
        gains[0],
        grad_fq_t.T,
        grad_fk_t.T,
        grad_wq,
        grad_wk,
        grad_wv,
        grad_out,
        gains[1],
        grad_gate_t.T,
        grad_up_t.T,
        grad_down,
    )


def solution(mesh):
    placed = (
        P("seq", None),
        P(),
        P(None, "head"),
        P(None, "head"),
        P(None, "head"),
        P(None, "head"),
        P(None, "head"),
        P("head", None),
        P(),
        P(None, "head"),
        P(None, "head"),
        P("head", None),
        P(),
        P("seq", None),
    )
    return jax.shard_map(
        shards,
        mesh=mesh,
        in_specs=placed,
        out_specs=(
            P("seq", None),
            P("seq", None),
            P("seq"),
            P("seq", "head"),
            P("seq", "head"),
            P("seq", "head"),
            P("seq", "head"),
            P("seq", "head"),
            P("head", "seq"),
            P("seq"),
            P("seq", "head"),
            P("seq", "head"),
            P("head", "seq"),
        ),
        check_vma=False,
    )
```

```python
import functools
import math

import jax
import jax.numpy as jnp
import numpy as np
from jax import lax
from jax.experimental import pallas as pl
from jax.experimental.pallas import tpu as pltpu
from jax.sharding import PartitionSpec as P

F = 16
VALUE_WIDTH = 128
WIN = 64
EPS = 1e-05

HEADS = 2
ROWS = 512
LANES = 256
FEATURES = 153
KEPT = 144
PACKED = 160
TILE = 128
EDGE = 2 * WIN
OWN = 64
f32 = jnp.float32
bf16 = jnp.bfloat16


def feature_tables():
    pairs = [(a, b) for a in range(F) for b in range(a, F)]
    count = len(pairs)
    choose = np.zeros((2, 2, 128, HEADS * LANES), np.float32)
    lanes = np.zeros((8, HEADS * LANES), np.float32)
    factor = F ** (-0.25)
    for head in range(HEADS):
        at = head * LANES
        for side in range(2):
            for first in (side * HEADS * F, 64, 96):
                row = first + head * F
                for lane, (a, b) in enumerate(pairs):
                    choose[side, 0, row + a, at + lane] = 1.0
                    choose[side, 1, row + b, at + lane] = 1.0
                for a in range(F):
                    choose[side, 0, row + a, at + count + a] = 1.0
        for lane, (a, b) in enumerate(pairs):
            lanes[2, at + lane] = factor * factor / math.sqrt(2.0)
            lanes[3, at + lane] = 1.0 if a == b else 2.0
        lanes[1, at + count : at + count + F + 1] = 1.0
        lanes[0, at + count + F] = 1.0
        lanes[2, at + count : at + count + F] = factor
        lanes[2, at + count + F] = 1.0
        lanes[3, at + count : at + count + F + 1] = 1.0
    lanes[4] = lanes[2] * lanes[3]
    return choose, lanes


def mm(a, b):
    return lax.dot_general(a, b, (((1,), (0,)), ((), ())), preferred_element_type=f32)


def mm_nt(a, b):
    return lax.dot_general(a, b, (((1,), (1,)), ((), ())), preferred_element_type=f32)


def mm_tn(a, b):
    return lax.dot_general(a, b, (((0,), (0,)), ((), ())), preferred_element_type=f32)


def low_pair(part):
    high = part.astype(bf16)
    return high, (part - high.astype(f32)).astype(bf16)


class Place:

    def __init__(self, starts):
        me, seq = lax.axis_index("head"), lax.axis_index("seq")
        self.base = seq * ROWS
        self.x, self.z = lax.shift_right_logical(seq, 2), lax.bitwise_and(seq, 3)
        self.y, self.core = lax.shift_right_logical(me, 1), lax.bitwise_and(me, 1)
        self.loaded = starts

    def starts(self):
        return [self.loaded[0, i] for i in range(4)]

    def rows(self, distance, other=False):
        quarter = lax.bitwise_and(self.y + distance, 3)
        core = 1 - self.core if other else self.core
        return pl.ds(pl.multiple_of(quarter * (2 * OWN) + core * OWN, OWN), OWN)


class Loaded:

    def __init__(self, ref, copies):
        self.ref, self.copies = ref, list(copies)
        self.shape = ref.shape

    def part(self, index):
        if self.copies and self.copies[index] is not None:
            self.copies[index].wait()
            self.copies[index] = None

    def ready(self):
        for index in range(len(self.copies)):
            self.part(index)

    def __getitem__(self, index):
        self.ready()
        return self.ref[index]


class Stored:

    def __init__(self, ref, copies):
        self.ref, self.copies, self.sent = ref, copies, set()
        self.shape, self.dtype = ref.shape, ref.dtype

    def __getitem__(self, index):
        return self.ref[index]

    def __setitem__(self, index, value):
        self.ref[index] = value

    def send(self, part=None):
        for index in range(len(self.copies)) if part is None else (part,):
            if index not in self.sent:
                self.copies[index].start()
                self.sent.add(index)


def doc_of(info, position):
    starts = info.starts()
    count = (position >= starts[0]).astype(jnp.int32)
    for start in starts[1:]:
        count = count + (position >= start).astype(jnp.int32)
    return count


def column_positions(info, first, count):
    return info.base + first + lax.broadcasted_iota(jnp.int32, (count, 1), 0)


def row_positions(info, first, count):
    return info.base + first + lax.broadcasted_iota(jnp.int32, (1, count), 1)


def prefix_mask(info):
    before = doc_of(info, info.base - 1)
    same = doc_of(info, column_positions(info, 0, ROWS)) == before
    return (same & (info.base > 0)).astype(f32)


def tail_mask(info):
    last = doc_of(info, info.base + ROWS - 1)
    return (doc_of(info, column_positions(info, 0, ROWS)) == last).astype(f32)


def factors(raw, side, choose_ref, lanes_ref):
    high, rest = low_pair(raw)
    high, rest = high.astype(f32), rest.astype(f32)
    left = raw - high - rest
    at = side * HEADS * F
    lane = lax.broadcasted_iota(jnp.int32, (1, 128), 1)
    parts = jnp.where(lane < 96, pltpu.roll(rest, 64 - at, 1), pltpu.roll(left, 96 - at, 1))
    parts = jnp.where(lane < 64, high, parts).astype(bf16)
    return [mm(parts, choose_ref[i]) + lanes_ref[i : i + 1, :] for i in range(2)]


def feature_back(gradient, left, right, choose_ref):
    first = mm_nt((gradient * right).astype(bf16), choose_ref[0])
    return first + mm_nt((gradient * left).astype(bf16), choose_ref[1])


def write_packed(packed_ref, head, state, norm):
    packed_ref[head, 0:KEPT, :] = state[:KEPT].astype(bf16)
    row = lax.broadcasted_iota(jnp.int32, (16, 128), 0) + (KEPT - FEATURES)
    high = norm.astype(bf16).astype(f32)
    rest = norm - high
    tile = jnp.where(row == 0, high[:, :128], state[KEPT:PACKED])
    tile = jnp.where(row == 1, high[:, 128:], tile)
    tile = jnp.where(row == 2, rest[:, :128], tile)
    tile = jnp.where(row == 3, rest[:, 128:], tile)
    packed_ref[head, KEPT:PACKED, :] = tile.astype(bf16)


def read_total(before_ref, got_refs, head):
    total = before_ref[head]
    for ref in got_refs:
        total = total + ref[head, 0:PACKED, :].astype(f32)
    state = jnp.concatenate(
        [total, jnp.zeros((LANES - PACKED, VALUE_WIDTH), f32)], axis=0
    ).astype(bf16)
    rows = [total[FEATURES + i : FEATURES + i + 1] for i in range(4)]
    return state, jnp.concatenate([rows[0] + rows[2], rows[1] + rows[3]], axis=1)


def head_lanes(head):
    return slice(head * VALUE_WIDTH, (head + 1) * VALUE_WIDTH)


def window_rows(own_ref, halo_ref, which, head, tile):
    first, lanes = tile * TILE, head_lanes(head)
    if tile == 0:
        after = halo_ref.shape[1] - EDGE + which * WIN
        halo = halo_ref[head, after : after + WIN, :]
        return jnp.concatenate([halo, own_ref[0:TILE, lanes]], axis=0)
    return own_ref[first - WIN : first + TILE, lanes]


def window_tile(info, head, tile, queries, key_rows, value_rows):
    first = tile * TILE
    query_at = column_positions(info, first, TILE)
    key_at = row_positions(info, first - WIN, TILE + WIN)
    near_by = (
        (key_at <= query_at)
        & (query_at - key_at < WIN)
        & (doc_of(info, query_at) == doc_of(info, key_at))
        & (key_at >= 0)
    )
    logits = mm_nt(queries, key_rows) * VALUE_WIDTH ** (-0.5)
    logits = jnp.where(near_by, logits, -1e30)
    exps = jnp.exp(logits - jnp.max(logits, axis=-1, keepdims=True))
    probs = exps / jnp.sum(exps, axis=-1, keepdims=True)
    return probs, mm(probs.astype(bf16), value_rows)


class Near:
    near = True

    def __init__(self, arrays, dims=None, places=None, parts=1):
        self.arrays = [
            a.arrays[0] if isinstance(a, Near) else a
            for a in (arrays if isinstance(arrays, (list, tuple)) else [arrays])
        ]
        self.dims = tuple(dims or self.arrays[0].shape)
        self.dtype = self.arrays[0].dtype
        self.places, self.parts = places, parts

    def copies(self, info, refs, buffer):
        if self.places is None:
            return pieces_of(refs[0], buffer, self.parts)
        return self.places(info, refs, buffer)

    def count(self):
        return self.parts if self.places is None else self.places(None)

    def copied(self):
        return self.places is not None


class Far(Near):
    near = False

    def copied(self):
        return True


class Out:

    def __init__(self, *dims, dtype=bf16, near=False, far=False, parts=1, width=None, first=0, onto=None):
        self.dims, self.dtype, self.parts = dims, dtype, parts
        self.near, self.far = near, far
        self.whole = dims if width is None else (dims[0], width)
        self.first, self.onto = first, onto

    def shapes(self):
        near = [jax.ShapeDtypeStruct(self.dims, self.dtype)] * self.near
        return near + [pltpu.HBM(self.whole, self.dtype)] * self.far

    def spaces(self):
        return [pltpu.VMEM] * self.near + [pltpu.HBM] * self.far

    def copies(self, buffer, target):
        if self.whole != self.dims:
            target = target.at[:, self.first : self.first + self.dims[1]]
        return pieces_of(buffer, target, self.parts)


class Stage:
    near, far, parts, onto = True, False, 1, None

    def __init__(self, source):
        self.source = source if isinstance(source, Far) else Far(source)
        self.dims, self.dtype = self.source.dims, self.source.dtype

    def shapes(self):
        return [jax.ShapeDtypeStruct(self.dims, self.dtype)]

    def spaces(self):
        return [pltpu.VMEM]


class Export:
    near, far, parts, onto = False, True, 1, None

    def __init__(self, source, dims=None, view=None):
        self.source, self.view = source, view
        self.dims, self.dtype = tuple(dims or source.dims), source.dtype

    def shapes(self):
        return [pltpu.HBM(self.dims, self.dtype)]

    def spaces(self):
        return [pltpu.HBM]

    def copies(self, ref, target):
        return [(ref if self.view is None else self.view(ref), target)]


def near(*dims, dtype=bf16):
    return Out(*dims, dtype=dtype, near=True)


def far(*dims, dtype=bf16, parts=1, **columns):
    return Out(*dims, dtype=dtype, far=True, parts=parts, **columns)


def both(*dims, dtype=bf16):
    return Out(*dims, dtype=dtype, near=True, far=True)


def pieces_of(source, target, parts):
    if parts == 1:
        return [(source, target)]
    count = source.shape[0] // parts
    return [
        (source.at[i * count : (i + 1) * count], target.at[i * count : (i + 1) * count])
        for i in range(parts)
    ]


def in_hbm(array):
    return pltpu.with_memory_space_constraint(array, pltpu.HBM)


def call(body, results, operands, starts=None, after=(), flops=0, scratch=(), megabytes=28):
    operands = [o if isinstance(o, Near) else Far(o) for o in operands]
    waits = [pl.ANY if isinstance(o, Near) else pltpu.HBM for o in after]
    after = [o.arrays[0] if isinstance(o, Near) else in_hbm(o) for o in after]
    staged = [o for o in results if isinstance(o, Stage)]
    inputs = operands + [o.source for o in results if isinstance(o, (Stage, Export))]
    arrays = [a for o in inputs for a in o.arrays]
    copied = [o for o in operands if o.copied()]
    held = [o for o in results if not o.near and not isinstance(o, Export)]
    count_out = sum(o.near + o.far for o in results)
    onto = {o: i for i, o in enumerate(results) if o.onto is not None}
    aliases = {len(arrays) + len(after) + i: onto[o] for i, o in enumerate(onto)}
    waits += [pltpu.HBM] * len(onto)
    after += [in_hbm(o.onto) for o in onto]
    moves = sum(o.count() for o in copied) + sum(o.source.count() for o in staged) + sum(o.parts for o in results if o.far)
    named = starts is not None

    def kernel(*refs):
        sources, refs = refs[: len(arrays)], refs[len(arrays) + len(after) :]
        named_ref, refs = (refs[0], refs[1:]) if named else (None, refs)
        targets, rest = list(refs[:count_out]), refs[count_out:]
        buffers, rest = list(rest[: len(copied)]), rest[len(copied) :]
        leaving, rest = list(rest[: len(held)]), rest[len(held) :]
        sems, rest = rest[0], rest[1:]
        marks = None
        if named:
            copy = pltpu.make_async_copy(named_ref, rest[0], sems.at[moves])
            copy.start()
            marks, rest = Loaded(rest[0], [copy]), rest[1:]
        info = Place(marks)
        loaded, at, sem = [], 0, 0

        def copies_of(pairs):
            nonlocal sem
            sem += len(pairs)
            return [
                pltpu.make_async_copy(source, target, sems.at[sem - len(pairs) + i])
                for i, (source, target) in enumerate(pairs)
            ]

        for operand in operands:
            own = sources[at : at + len(operand.arrays)]
            at += len(own)
            if not operand.copied():
                loaded.append(Loaded(own[0], []))
                continue
            buffer = buffers.pop(0)
            loaded.append(Loaded(buffer, copies_of(operand.copies(info, own, buffer))))
            for copy in loaded[-1].copies:
                copy.start()
        stored, staging = [], []
        for result in results:
            if isinstance(result, Export):
                staging += copies_of(result.copies(sources[at], targets.pop(0)))
                at += 1
                continue
            buffer = targets.pop(0) if result.near else leaving.pop(0)
            if isinstance(result, Stage):
                own = sources[at : at + len(result.source.arrays)]
                at += len(own)
                staging += copies_of(result.source.copies(info, own, buffer))
                continue
            target = targets.pop(0) if result.far else None
            pairs = result.copies(buffer, target) if result.far else []
            stored.append(Stored(buffer, copies_of(pairs)))
        for copy in staging:
            copy.start()
        body(info, *loaded, *stored, *rest)
        for copy in staging:
            copy.wait()
        for item in loaded + ([marks] if named else []):
            item.ready()
        for item in stored:
            item.send()
        for item in stored:
            for copy in item.copies:
                copy.wait()

    spaces = [pltpu.VMEM if o.near else pltpu.HBM for o in inputs for _ in o.arrays]
    placed = [a if space is pltpu.VMEM else in_hbm(a) for a, space in zip(arrays, spaces)]
    spaces += waits + [pltpu.HBM] * named
    moved = sum(a.size * a.dtype.itemsize for a in arrays)
    moved += sum(math.prod(o.dims) * jnp.dtype(o.dtype).itemsize for o in results)
    given = pl.pallas_call(
        kernel,
        name=getattr(body, "func", body).__name__,
        out_shape=tuple(s for o in results for s in o.shapes()),
        in_specs=[pl.BlockSpec(memory_space=space) for space in spaces],
        out_specs=tuple(pl.BlockSpec(memory_space=s) for o in results for s in o.spaces()),
        input_output_aliases=aliases,
        scratch_shapes=[pltpu.VMEM(o.dims, o.dtype) for o in copied]
        + [pltpu.VMEM(o.dims, o.dtype) for o in held]
        + [pltpu.SemaphoreType.DMA((max(1, moves + named),))]
        + [pltpu.SMEM((1, 4), jnp.int32)] * named
        + list(scratch),
        compiler_params=pltpu.CompilerParams(vmem_limit_bytes=megabytes * 2**20),
        cost_estimate=pl.CostEstimate(flops=0, bytes_accessed=1024, transcendentals=0),
    )(*placed, *after, *([in_hbm(starts)] if named else []))
    given, answer = list(given), []
    for result in results:
        item = (Near(given.pop(0)),) if result.near else ()
        item += (given.pop(0),) if result.far else ()
        answer.append(item if len(item) == 2 else item[0])
    return answer


def moved_by(array, axis, route):
    array = array.arrays[0] if isinstance(array, Near) else array
    return Near(lax.ppermute(array, axis, route))


def feature_weights(feat_query_t, feat_key_t):
    def places(info, sources=None, buffer=None):
        if info is None:
            return 2
        return [(sources[0], buffer.at[0:32]), (sources[1], buffer.at[32:64])]

    return Far([feat_query_t, feat_key_t], (128, feat_query_t.shape[1]), places)


def own_part(block):
    def places(info, sources=None, buffer=None):
        if info is None:
            return 1
        return [(sources[0].at[info.rows(0)], buffer)]

    return Far(block, (OWN, block.shape[1]), places)


def keys_kernel(
    info, x_ref, gain_ref, key_ref, value_ref, feat_ref, choose_ref, lanes_ref,
    normed_ref, inv_ref, raw_ref, keys_ref, values_ref, km_ref, packed_ref, wide_ref,
):
    gain = gain_ref[...]

    def norm_rows(part):
        for i in range(2):
            rows = slice(part * 128 + i * 64, part * 128 + i * 64 + 64)
            x = x_ref.ref[rows, :].astype(f32)
            inv = lax.rsqrt(jnp.mean(x * x, axis=-1, keepdims=True) + EPS)
            inv_ref[rows, :] = inv
            normed_ref[rows, :] = (x * inv * gain).astype(bf16)

    x_ref.part(0)
    norm_rows(0)
    x_ref.part(1)
    norm_rows(1)
    for ref in (x_ref, feat_ref, key_ref, value_ref, choose_ref, lanes_ref):
        ref.ready()
    feat_ref.ref[64:128, :] = jnp.zeros((64, feat_ref.shape[1]), bf16)
    half = ROWS // 2
    features = []
    for first in (0, half):
        rows = slice(first, first + half)
        normed = normed_ref[rows, :]
        raw = mm_nt(normed, feat_ref[...])
        raw_ref[rows, :] = raw
        if first == 0:
            norm_rows(2)
            norm_rows(3)
        keys_ref[rows, :] = mm(normed, key_ref[...]).astype(bf16)
        values_ref[rows, :] = mm(normed, value_ref[...]).astype(bf16)
        left, right = factors(raw, 1, choose_ref, lanes_ref)
        part = (left * right * lanes_ref[2:3, :]).astype(bf16)
        features.append((part.astype(f32) * lanes_ref[3:4, :]).astype(bf16))
    features = jnp.concatenate(features, axis=0)
    values = values_ref[...]
    for head in range(HEADS):
        km_ref[head] = features[:, head * LANES : (head + 1) * LANES]
    tail = tail_mask(info)
    for head in range(HEADS):
        own = features[:, head * LANES : (head + 1) * LANES]
        lanes = head_lanes(head)
        kept = (values[:, lanes].astype(f32) * tail).astype(bf16)
        state = mm_tn(own, kept)
        norm = jnp.sum(own.astype(f32) * tail, axis=0, keepdims=True)
        write_packed(packed_ref, head, state, norm)
        wide_ref[head, 0:PACKED, :] = packed_ref[head]
        wide_ref[head, PACKED : PACKED + WIN, :] = keys_ref[ROWS - WIN :, lanes]
        wide_ref[head, PACKED + WIN :, :] = values[ROWS - WIN :, lanes]


def local_kernel(
    info, raw_ref, choose_ref, lanes_ref, values_ref, km_ref, normed_ref, query_ref,
    qf_ref, low_ref, num_ref, den_ref, queries_ref,
):
    left, right = factors(raw_ref[...], 0, choose_ref, lanes_ref)
    features = (left * right * lanes_ref[2:3, :]).astype(bf16)
    for head in range(HEADS):
        qf_ref[head] = features[:, head * LANES : (head + 1) * LANES]
    half = ROWS // 2
    causal = []
    for block in range(2):
        query_at = column_positions(info, block * half, half)
        key_at = row_positions(info, 0, (block + 1) * half)
        causal.append((query_at >= key_at) & (doc_of(info, query_at) == doc_of(info, key_at)))
    for head in range(HEADS):
        for block in range(2):
            first, reach = block * half, (block + 1) * half
            own = qf_ref[head, first:reach, :]
            weights = jnp.where(causal[block], mm_nt(own, km_ref[head, :reach, :]), 0.0)
            den_ref[head, first:reach, :] = jnp.sum(weights, axis=-1, keepdims=True)
            weights = weights.astype(bf16)
            low_ref[head, first:reach, 0:reach] = weights
            num_ref[first:reach, head_lanes(head)] = mm(
                weights, values_ref[:reach, head_lanes(head)]
            )
    queries_ref[...] = mm(normed_ref[...], query_ref[...]).astype(bf16)


def window_kernel(
    info, queries_ref, keys_ref, values_ref, probs_ref, window_ref,
):
    queries = queries_ref[...]
    for head in range(HEADS):
        lanes = head_lanes(head)
        for tile in range(1, ROWS // TILE):
            rows = slice(tile * TILE, (tile + 1) * TILE)
            probs, result = window_tile(
                info, head, tile, queries[rows, lanes],
                window_rows(keys_ref, None, 0, head, tile), window_rows(values_ref, None, 1, head, tile),
            )
            probs_ref[head, tile - 1] = probs
            window_ref[rows, lanes] = result


def by_distance(ref, info, other):
    return jnp.concatenate([ref[info.rows(d, other), :] for d in range(4)], axis=0)


def mixed_kernel(
    info, before_ref, got1_ref, got2_ref, got3_ref, qf_ref, num_ref, den_ref, window_ref, out_ref,
    queries_ref, keys_ref, values_ref,
    mixed_ref, linear_ref, total_den_ref, state_ref, norm_ref, probs_ref, other_ref,
):
    use = prefix_mask(info)
    for head in range(HEADS):
        lanes = head_lanes(head)
        state, norm = read_total(before_ref, (got1_ref, got2_ref, got3_ref), head)
        state_ref[head] = state
        norm_ref[head] = jnp.broadcast_to(norm, (8, LANES))
        features = qf_ref[head]
        inter = mm(features, state) * use
        den = jnp.sum(features.astype(f32) * norm, axis=-1, keepdims=True) * use + den_ref[head]
        total_den_ref[head] = den
        linear = (inter + num_ref[:, lanes]) / den
        linear_ref[:, lanes] = linear
        probs, window = window_tile(
            info, head, 0, queries_ref[0:TILE, lanes],
            window_rows(keys_ref, got1_ref, 0, head, 0), window_rows(values_ref, got1_ref, 1, head, 0),
        )
        probs_ref[head] = probs
        mixed_ref[0:TILE, lanes] = (linear[0:TILE] + window).astype(bf16)
        mixed_ref[TILE:, lanes] = (linear[TILE:] + window_ref[TILE:, lanes]).astype(bf16)
    other_ref[...] = mm(by_distance(mixed_ref, info, True), out_ref[...]).astype(bf16)


def mixed_own_kernel(info, mixed_ref, out_ref, own_ref):
    own_ref[...] = mm(by_distance(mixed_ref, info, False), out_ref[...]).astype(bf16)


def quarters_kernel(info, own_ref, got_ref, *out_refs):
    out_refs[4][...] = got_ref[0:16, 0:128]
    for d in (1, 2, 3, 0):
        rows = slice(d * OWN, (d + 1) * OWN)
        total = own_ref[rows, :].astype(f32) + got_ref[rows, :].astype(f32)
        out_refs[d][...] = total.astype(out_refs[d].dtype)
        out_refs[d].send()


def resid_kernel(
    info, mine_ref, x_ref, gain_ref, got1_ref, got2_ref, got3_ref, normed_ref, resid_ref, inv_ref
):
    resid = x_ref[...].astype(f32) + mine_ref[...]
    for ref in (got1_ref, got2_ref, got3_ref):
        resid = resid + ref[...].astype(f32)
    resid_ref[...] = resid
    inv = lax.rsqrt(jnp.mean(resid * resid, axis=-1, keepdims=True) + EPS)
    inv_ref[...] = inv
    normed_ref[...] = (resid * inv * gain_ref[...]).astype(bf16)


def grad_resid_kernel(
    info, mine_ref, resid_ref, inv_ref, top_ref, gain_ref, got1_ref, got2_ref, got3_ref,
    sent_ref, grad_ref, gains_ref,
):
    grad = mine_ref[...]
    for ref in (got1_ref, got2_ref, got3_ref):
        grad = grad + ref[...].astype(f32)
    resid = resid_ref[...]
    inv = inv_ref[...]
    grad_resid = top_ref[...].astype(f32) + norm_back(resid, inv, gain_ref[...], grad)
    sent_ref[...] = grad_resid.astype(bf16)
    sent_ref.send()
    grad_ref[...] = grad_resid
    gains_ref[0:1, :] = jnp.sum(grad * resid * inv, axis=0, keepdims=True)


def grad_x_kernel(
    info, mine_ref, x_ref, grad_resid_ref, gain_ref, resid_ref, out_ref, got1_ref, got2_ref, got3_ref,
    out1_ref, out2_ref, out3_ref, sent_ref,
):
    total = resid_ref[...] + out_ref[...]
    for ref in (out1_ref, out2_ref, out3_ref):
        total = total + ref[...].astype(f32)
    sent_ref[0:OWN, :] = total.astype(bf16)
    grad = mine_ref[...]
    for ref in (got1_ref, got2_ref, got3_ref):
        grad = grad + ref[...].astype(f32)
    x = x_ref[...].astype(f32)
    inv = lax.rsqrt(jnp.mean(x * x, axis=-1, keepdims=True) + EPS)
    sent_ref[OWN:, :] = (grad_resid_ref[...] + norm_back(x, inv, gain_ref[...], grad)).astype(bf16)


def norm_back(in_rows, inv_rms, gain, grad_normed):
    weighted = grad_normed * gain
    return inv_rms * weighted - in_rows * inv_rms**3 * jnp.mean(
        weighted * in_rows, axis=-1, keepdims=True
    )


def by_halves(block):
    def places(info, sources=None, buffer=None):
        if info is None:
            return 8
        return [
            (sources[0].at[info.rows(i % 4, other=i >= 4)], buffer.at[i * OWN : (i + 1) * OWN])
            for i in range(8)
        ]

    return Far(block, block.shape, places)


def grad_act_kernel(info, top_ref, down_ref, own_ref, other_ref):
    top = top_ref[...]
    half = ROWS // 2
    for first in range(0, down_ref.shape[0], 256):
        span = slice(first, min(first + 256, down_ref.shape[0]))
        grad = mm_nt(top, down_ref[span, :])
        own_ref[:, span] = grad[:half]
        other_ref[:, span] = grad[half:]


def ffn_rows(pieces, gate_ref, up_ref, grad_act_ref, normed_ref, act_ref, grad_gate_ref, grad_up_ref):
    normed = jnp.concatenate([piece[...] for piece in pieces], axis=0)
    normed_ref[...] = normed
    hidden = gate_ref.shape[0]
    for first in range(0, hidden, 256):
        span = slice(first, min(first + 256, hidden))
        gate = mm_nt(normed, gate_ref[span, :])
        up_value = mm_nt(normed, up_ref[span, :])
        sigmoid_gate = jax.nn.sigmoid(gate)
        silu_gate = gate * sigmoid_gate
        act_ref[:, span] = (silu_gate * up_value).astype(bf16)
        grad_act = grad_act_ref[:, span]
        grad_gate_ref[:, span] = (
            grad_act * up_value * sigmoid_gate * (1.0 + gate * (1.0 - sigmoid_gate))
        ).astype(bf16)
        grad_up_ref[:, span] = (grad_act * silu_gate).astype(bf16)


def ffn_own_kernel(info, p0, p3, p1, p2, gate_ref, up_ref, grad_act_ref, *out_refs):
    ffn_rows((p0, p3, p2, p1), gate_ref, up_ref, grad_act_ref, *out_refs)


def ffn_other_kernel(info, s0, s3, s1, s2, gate_ref, up_ref, grad_act_ref, back_ref, *out_refs):
    ffn_rows((s0, s3, s2, s1), gate_ref, up_ref, grad_act_ref, *out_refs)
    ffn_back_kernel(info, out_refs[2], out_refs[3], gate_ref, up_ref, back_ref)


def ffn_back_kernel(info, grad_gate_ref, grad_up_ref, gate_ref, up_ref, back_ref):
    grad_gate, grad_up = grad_gate_ref[...], grad_up_ref[...]
    for first in range(0, back_ref.shape[1], 512):
        span = slice(first, first + 512)
        part = mm(grad_gate, gate_ref[:, span]) + mm(grad_up, up_ref[:, span])
        back_ref[:, span] = part.astype(bf16)


def ffn_out_kernel(info, act_own_ref, act_other_ref, down_ref, other_ref, own_ref):
    for target, act_ref in ((other_ref, act_other_ref), (own_ref, act_own_ref)):
        act = act_ref[...]
        for first in range(0, target.shape[1], 512):
            span = slice(first, first + 512)
            target[:, span] = mm(act, down_ref[:, span]).astype(bf16)


def column_grads(pairs, out_ref, last=None):
    count = out_ref.shape[0] // 4
    for part in range(4):
        span = slice(part * count, (part + 1) * count)
        first = 0
        for i, (rows_refs, grads) in enumerate(pairs):
            rows_refs = rows_refs if isinstance(rows_refs, tuple) else (rows_refs,)
            grads = grads if isinstance(grads, tuple) else (grads,)
            total = sum(mm_tn(rows[:, span], grad) for rows, grad in zip(rows_refs, grads))
            if last is not None and i == len(pairs) - 1:
                total = total + last[span, :].astype(f32)
            end = first + total.shape[1]
            out_ref[span, first:end] = total.astype(bf16)
            first = end
        out_ref.send(part)


def gate_grads_kernel(
    info, own_ref, other_ref, gate_own_ref, gate_other_ref, up_own_ref, up_other_ref, out_ref
):
    rows = (own_ref, other_ref)
    gate = (gate_own_ref[...], gate_other_ref[...])
    up = (up_own_ref[...], up_other_ref[...])
    column_grads(((rows, gate), (rows, up)), out_ref)


class Rows:

    def __init__(self, ref, first, count):
        self.ref, self.rows = ref, slice(first, first + count)

    def __getitem__(self, index):
        return self.ref[self.rows, index[1]]


def down_grads_kernel(info, top_ref, act_own_ref, act_other_ref, out_ref, tail_ref):
    half, whole = ROWS // 2, out_ref.shape[1]
    rows = (Rows(top_ref, 0, half), Rows(top_ref, half, half))
    acts = (act_own_ref[...], act_other_ref[...])
    column_grads(((rows, tuple(act[:, :whole] for act in acts)),), out_ref)
    room = jnp.zeros((half, 128 - acts[0].shape[1] % 128), bf16)
    rest = [jnp.concatenate([act[:, whole:], room], axis=1) for act in acts]
    tail_ref[...] = sum(mm_tn(row[:, :], act) for row, act in zip(rows, rest)).astype(bf16)


def grad_x_out_kernel(info, p0, p1, p2, p3, s0, s1, s2, s3, output_ref, grad_ref):
    for i, piece in enumerate((p0, p1, p2, p3, s0, s1, s2, s3)):
        rows = info.rows(4 - i % 4, other=i >= 4)
        output_ref[rows, :] = piece[0:OWN, :]
        grad_ref[rows, :] = piece[OWN : 2 * OWN, :].astype(f32)


def window_tile_back(top, probs, key_rows, value_rows):
    grad_probs = mm_nt(top, value_rows)
    shared = jnp.sum(grad_probs * probs, axis=-1, keepdims=True)
    return (probs * (grad_probs - shared)).astype(bf16)


def mixed_back_kernel(
    info, p0, p3, p1, p2, s0, s3, s1, s2, out_ref, linear_ref, den_ref, qf_ref, probs0_ref, keys_ref,
    values_ref, halo_ref, queries_ref, packed_ref, wide_ref, top_ref, gm_ref, gnum_ref, gden_ref,
):
    for i, piece in enumerate((p0, p1, p2, p3, s0, s1, s2, s3)):
        top_ref[info.rows(4 - i % 4, other=i >= 4), :] = piece[...]
    grad_mixed = mm_nt(top_ref[...], out_ref[...]).astype(bf16)
    gm_ref[...] = grad_mixed
    use = prefix_mask(info)
    for head in range(HEADS):
        lanes = head_lanes(head)
        wide = grad_mixed[:, lanes].astype(f32)
        den = den_ref[head]
        grad_num = (wide / den).astype(bf16)
        gnum_ref[:, lanes] = grad_num
        grad_den = -jnp.sum(wide * linear_ref[:, lanes], axis=-1, keepdims=True) / den
        gden_ref[head] = grad_den
        features = qf_ref[head]
        used = (grad_num.astype(f32) * use).astype(bf16)
        state = mm_tn(features, used)
        norm = jnp.sum(features.astype(f32) * (grad_den * use), axis=0, keepdims=True)
        write_packed(packed_ref, head, state, norm)
        wide_ref[head, 0:PACKED, :] = packed_ref[head]
        top, probs = grad_mixed[0:TILE, lanes], probs0_ref[head]
        grad_logits = window_tile_back(
            top, probs, window_rows(keys_ref, halo_ref, 0, head, 0),
            window_rows(values_ref, halo_ref, 1, head, 0),
        )
        grad_keys = mm_tn(grad_logits, queries_ref[0:TILE, lanes]) * VALUE_WIDTH ** (-0.5)
        wide_ref[head, PACKED : PACKED + WIN, :] = grad_keys[0:WIN].astype(bf16)
        grad_values = mm_tn(probs.astype(bf16), top)
        wide_ref[head, PACKED + WIN :, :] = grad_values[0:WIN].astype(bf16)


def window_back_kernel(
    info, gm_ref, probs0_ref, probs_ref, keys_ref, values_ref, halo_ref, queries_ref,
    top_ref, mixed_ref, gq_ref, gk_ref, gv_ref, out_ref, key_acc, value_acc,
):
    column_grads(((top_ref, mixed_ref[...]),), out_ref)
    scale = VALUE_WIDTH ** (-0.5)
    key_acc[...] = jnp.zeros_like(key_acc)
    value_acc[...] = jnp.zeros_like(value_acc)
    for tile in range(ROWS // TILE):
        first = tile * TILE
        reach = slice(first, first + TILE + WIN)
        for head in range(HEADS):
            lanes = head_lanes(head)
            key_rows = window_rows(keys_ref, halo_ref, 0, head, tile)
            value_rows = window_rows(values_ref, halo_ref, 1, head, tile)
            top = gm_ref[first : first + TILE, lanes]
            probs = probs0_ref[head] if tile == 0 else probs_ref[head, tile - 1]
            grad_logits = window_tile_back(top, probs, key_rows, value_rows)
            gq_ref[first : first + TILE, lanes] = (mm(grad_logits, key_rows) * scale).astype(bf16)
            queries = queries_ref[first : first + TILE, lanes]
            key_acc[reach, lanes] += mm_tn(grad_logits, queries) * scale
            value_acc[reach, lanes] += mm_tn(probs.astype(bf16), top)
    gk_ref[...] = key_acc[WIN:, :]
    gv_ref[...] = value_acc[WIN:, :]


def linear_back_kernel(
    info, gnum_ref, gden_ref, values_ref, low_ref, km_ref, qf_ref, state_ref, norm_ref, raw_ref,
    choose_ref, choose_k_ref, lanes_ref, window_gv_ref, normed_ref, gq_ref,
    gfeat_ref, gv_ref, gkf_ref, left_ref, right_ref, out_ref,
):
    column_grads(((normed_ref, gq_ref[...]),), out_ref)
    use = prefix_mask(info)
    half = ROWS // 2
    grads = [[None, None], [None, None]]
    for head in range(HEADS):
        lanes = head_lanes(head)
        inter = mm_nt((gnum_ref[:, lanes].astype(f32) * use).astype(bf16), state_ref[head])
        inter = inter + (gden_ref[head] * use) * norm_ref[head, 0:1, :]
        for block in range(2):
            first, reach = block * half, (block + 1) * half
            query_at = column_positions(info, first, half)
            key_at = row_positions(info, 0, reach)
            causal = (query_at >= key_at) & (doc_of(info, query_at) == doc_of(info, key_at))
            grad_num = gnum_ref[first:reach, lanes]
            grad = mm_nt(grad_num, values_ref[:reach, lanes]) + gden_ref[head, first:reach, :]
            grad = jnp.where(causal, grad, 0.0).astype(bf16)
            grads[head][block] = mm(grad, km_ref[head, :reach, :]) + inter[first:reach]
            key_part = mm_tn(grad, qf_ref[head, first:reach, :])
            value_part = mm_tn(low_ref[head, first:reach, 0:reach], grad_num)
            if block == 0:
                gkf_ref[head, 0:half] = key_part
                gv_ref[0:half, lanes] = window_gv_ref[0:half, lanes] + value_part
            else:
                gkf_ref[head, 0:half] += key_part[0:half]
                gkf_ref[head, half:] = key_part[half:]
                gv_ref[0:half, lanes] += value_part[0:half]
                gv_ref[half:, lanes] = window_gv_ref[half:, lanes] + value_part[half:]
    left, right = factors(raw_ref[...], 0, choose_ref, lanes_ref)
    gradient = jnp.concatenate([jnp.concatenate(g, axis=0) for g in grads], axis=1)
    gradient = gradient * lanes_ref[2:3, :]
    gfeat_ref[...] = feature_back(gradient, left, right, choose_ref)
    left_ref[...], right_ref[...] = factors(raw_ref[...], 1, choose_k_ref, lanes_ref)


def keys_back_kernel(
    info, before_ref, got1_ref, got2_ref, got3_ref, values_ref, km_ref, gkf_ref, gk_ref, gv_ref,
    left_ref, right_ref, choose_ref, lanes_ref, gfeat_ref, normed_ref, tail_ref,
    gkw_ref, gvw_ref, gf_ref, out_ref,
):
    tail = tail_mask(info)
    inner = ROWS - WIN
    gkw_ref[0:inner, :] = gk_ref[0:inner, :].astype(bf16)
    gradients = []
    for head in range(HEADS):
        lanes = head_lanes(head)
        later, norm = read_total(before_ref, (got1_ref, got2_ref, got3_ref), head)
        kept = (values_ref[:, lanes].astype(f32) * tail).astype(bf16)
        gradients.append(gkf_ref[head] + mm_nt(kept, later) + tail * norm)
        grad_values = gv_ref[:, lanes] + mm(km_ref[head], later) * tail
        gvw_ref[0:inner, lanes] = grad_values[0:inner].astype(bf16)
        right = got1_ref[head, PACKED:, :].astype(f32)
        gkw_ref[inner:, lanes] = (gk_ref[inner:, lanes] + right[0:WIN]).astype(bf16)
        gvw_ref[inner:, lanes] = (grad_values[inner:] + right[WIN:]).astype(bf16)
    gradient = jnp.concatenate(gradients, axis=1) * lanes_ref[4:5, :]
    gradient = feature_back(gradient, left_ref[...], right_ref[...], choose_ref) + gfeat_ref[...]
    gf_ref[...] = gradient.astype(bf16)
    lane = lax.broadcasted_iota(jnp.int32, (1, 128), 1)
    beside = jnp.where(lane < 64, 0.0, pltpu.roll(gradient, 64, 1)).astype(bf16)
    column_grads(
        (
            (normed_ref, gkw_ref[...]), (normed_ref, gvw_ref[...]), (normed_ref, beside),
        ),
        out_ref, last=tail_ref,
    )


def normed_back_kernel(
    info, gq_ref, gkw_ref, gvw_ref, gf_ref, wq_ref, wk_ref, wv_ref, wf_ref, x_ref, inv_ref, gain_ffn_ref,
    other_ref, own_ref, gains_ref,
):
    wf_ref.ready()
    wf_ref.ref[64:128, :] = jnp.zeros((64, wf_ref.shape[1]), bf16)
    for target, other in ((other_ref, True), (own_ref, False)):
        grads = [by_distance(ref, info, other) for ref in (gq_ref, gkw_ref, gvw_ref, gf_ref)]
        scaled_by = by_distance(inv_ref, info, other)
        for piece in range(4):
            span = slice(piece * 512, (piece + 1) * 512)
            part = mm_nt(grads[0], wq_ref[span, :])
            part = part + mm_nt(grads[1], wk_ref[span, :])
            part = part + mm_nt(grads[2], wv_ref[span, :])
            part = part + mm(grads[3], wf_ref[:, span])
            target[:, span] = part.astype(bf16)
            x_rows = jnp.concatenate([x_ref[info.rows(d, other), span] for d in range(4)], axis=0)
            total = jnp.sum(part * (x_rows.astype(f32) * scaled_by), axis=0, keepdims=True)
            gains_ref[0:1, span] = total if other else total + gains_ref[0:1, span]
    gains_ref[1:2, :] = gain_ffn_ref[0:1, :]


def columns(block, first, last):
    def places(info, sources=None, buffer=None):
        return 1 if info is None else [(sources[0].at[:, first:last], buffer)]

    return Far(block, (block.shape[0], last - first), places)


def grads_out_kernel(
    info, both_ref, in_ref, gate_ref, up_ref, down_ref, out_ref, grad_q_ref, grad_k_ref, grad_v_ref,
    feat_query_ref, feat_key_ref,
):
    hidden, width = gate_ref.shape[0], out_ref.shape[0]
    whole = hidden // 128 * 128
    both = both_ref[...].T
    gate_ref[...] = both[0:hidden].astype(f32)
    gate_ref.send()
    up_ref[...] = both[hidden:].astype(f32)
    up_ref.send()
    down_ref[0:whole, :] = in_ref[:, 0:whole].T.astype(f32)
    at = whole
    out_ref[...] = in_ref[:, at : at + width].T.astype(f32)
    out_ref.send()
    for ref in (grad_q_ref, grad_k_ref, grad_v_ref):
        at += width
        ref[...] = in_ref[:, at : at + width].astype(f32)
        ref.send()
    tail = in_ref[:, at + width :].astype(f32).T
    down_ref[whole:, :] = tail[0 : hidden - whole]
    down_ref.send()
    feat_query_ref[...] = tail[64:96]
    feat_key_ref[...] = tail[96:128]


def total_of(refs):
    total = refs[0][...]
    for ref in refs[1:]:
        total = total + ref[...]
    return total


def gains_kernel(info, *refs):
    refs[-1][...] = total_of(refs[:-1])


def spread_kernel(info, *refs):
    total, out_ref = total_of(refs[:-1]), refs[-1]
    for i in range(out_ref.shape[0]):
        out_ref[i, 0:2, :] = total[:, i * 128 : (i + 1) * 128]
        out_ref[i, 2:, :] = jnp.zeros((6, 128), f32)


def gathered_sum_kernel(info, in_ref, out_ref):
    total = in_ref[0]
    for i in range(1, in_ref.shape[0]):
        total = total + in_ref[i]
    out_ref[...] = total


def along_y(distance):
    return [(i, (i + 2 * distance) % 8) for i in range(8)]


def sibling():
    return [(i, i ^ 1) for i in range(8)]


def along_x(distance):
    return [(i, (i + 4 * distance) % 16) for i in range(16)]


def along_z(distance):
    return [(4 * a + z, 4 * a + (z + distance) % 4) for a in range(4) for z in range(4)]


def head_quarters(own, other, after=()):
    got = moved_by(other, "head", sibling())
    width = own.dims[1]
    with jax.named_scope("quarters"):
        mine, *sent, token = call(
            quarters_kernel,
            [near(OWN, width, dtype=f32)] + [near(OWN, width)] * 3 + [near(16, 128)],
            (own, got), after=after,
        )
    parts = [moved_by(sent[d - 1], "head", along_y(d)) for d in (2, 3, 1)]
    return mine, parts, moved_by(token, "head", sibling())


def head_pieces(own):
    far_piece = moved_by(own, "head", along_y(2))
    pieces = [own, moved_by(own, "head", along_y(1)), far_piece, moved_by(own, "head", along_y(3))]
    return pieces + [moved_by(piece, "head", sibling()) for piece in pieces]


def gains_sum(gains):
    with jax.named_scope("gains"):
        (pair,) = call(
            gains_kernel, [near(*gains.dims, dtype=f32)], (gains, moved_by(gains, "head", sibling()))
        )
        parts = [pair] + [moved_by(pair, "head", along_y(d)) for d in (2, 1, 3)]
        (blocks,) = call(spread_kernel, [far(16, 8, 128, dtype=f32)], parts)
        blocks = lax.all_to_all(blocks, "seq", 0, 0)
        (total,) = call(gathered_sum_kernel, [far(8, 128, dtype=f32)], (blocks,))
    return total


def scan_kernel(reverse, info, own_ref, got1_ref, got2_ref, got3_ref, before_ref, *sent_refs):
    place_x, place_z = (3 - info.x, 3 - info.z) if reverse else (info.x, info.z)
    before = jnp.zeros(before_ref.shape, f32)
    for d, ref in enumerate((got1_ref, got2_ref, got3_ref), 1):
        before = before + ref[:, 0:PACKED, :].astype(f32) * (place_x >= d).astype(f32)
    before_ref[...] = before
    row = lax.broadcasted_iota(jnp.int32, (HEADS, 16, 128), 1) + (KEPT - FEATURES)
    sent = []
    for total in (before, before + own_ref[:, 0:PACKED, :].astype(f32)):
        tile = total[:, KEPT:]
        norm = tile + jnp.roll(tile, -2, axis=1)
        high = norm.astype(bf16).astype(f32)
        rest = jnp.roll(norm - high, 2, axis=1)
        norm = jnp.where(row < 0, tile, jnp.where(row < 2, high, jnp.where(row < 4, rest, 0.0)))
        sent.append((total[:, :KEPT], norm))
    for d, ref in enumerate(sent_refs, 1):
        with_own = (place_z + d < 4).astype(f32)
        for part, rows in ((0, slice(0, KEPT)), (1, slice(KEPT, PACKED))):
            less, more = sent[0][part], sent[1][part]
            ref[:, rows, :] = (more * with_own + less * (1.0 - with_own)).astype(bf16)
        if ref.shape[1] > PACKED:
            own, earlier = own_ref[:, PACKED:, :].astype(f32), got1_ref[:, PACKED:, :].astype(f32)
            ref[:, PACKED:, :] = (own * with_own + earlier * (1.0 - with_own)).astype(bf16)


def exclusive_parts(own, reverse, after=(), wide=None):
    sign = -1 if reverse else 1
    first = own if wide is None else wide
    got = [moved_by(first if d == 1 else own, "seq", along_x(sign * d)) for d in (1, 2, 3)]
    with jax.named_scope("scan"):
        before, *sent = call(
            functools.partial(scan_kernel, reverse),
            [near(*own.dims, dtype=f32), near(*first.dims), near(*own.dims), near(*own.dims)],
            (first, *got), after=after,
        )
    return [before] + [
        moved_by(sent[d - 1], "seq", along_z(sign * d)) for d in (1, 2, 3)
    ]


def shards(
    inputs,
    gain_mix,
    feat_query,
    feat_key,
    win_query,
    win_key,
    value_proj,
    out_proj,
    gain_ffn,
    gate_proj,
    up_proj,
    down_proj,
    document_starts,
    cotangent,
):
    choose, lanes = feature_tables()
    choose = jnp.asarray(choose, bf16)
    lanes = jnp.asarray(lanes, f32)
    choose_q, choose_k = choose[0], choose[1]
    feat = feature_weights(feat_query.T, feat_key.T)
    gain_mix = gain_mix.reshape(1, -1)
    gain_ffn = gain_ffn.reshape(1, -1)
    model = inputs.shape[1]
    width = HEADS * VALUE_WIDTH
    hidden = gate_proj.shape[1]
    half = ROWS // 2
    unit = 2 * ROWS * model
    starts = document_starts

    normed, inv_mix, raw, keys, values, km, packed, wide = call(
        keys_kernel,
        (
            near(ROWS, model), near(ROWS, 1, dtype=f32), near(ROWS, 128, dtype=f32),
            near(ROWS, width), near(ROWS, width), near(HEADS, ROWS, LANES),
            near(HEADS, PACKED, 128), near(HEADS, PACKED + EDGE, 128),
        ),
        (Far(inputs, parts=4), gain_mix, win_key, value_proj, feat, choose_k, lanes),
        starts=starts, flops=unit * 640,
    )
    qf, low, num, den, queries, near_out, normed_far, inv_mix, raw_far, keys_far, values_far, km_far = call(
        local_kernel,
        (
            near(HEADS, ROWS, LANES), near(HEADS, ROWS, ROWS), near(ROWS, width, dtype=f32),
            near(HEADS, ROWS, 1, dtype=f32), near(ROWS, width), Stage(out_proj), Export(normed),
            Export(inv_mix), Export(raw), Export(keys), Export(values), Export(km),
        ),
        (raw, choose_q, lanes, values, km, normed, win_query),
        starts=starts, flops=unit * 300,
    )
    sums = exclusive_parts(packed, False, after=(qf,), wide=wide)
    probs, window, qf_far, low = call(
        window_kernel,
        (
            near(HEADS, 3, TILE, TILE + WIN, dtype=f32),
            near(ROWS, width, dtype=f32), Export(qf), Export(low),
        ),
        (queries, keys, values),
        starts=starts, flops=unit * 400,
    )
    mixed, linear, total_den, state, norm, probs_first, other = call(
        mixed_kernel,
        (
            near(ROWS, width), near(ROWS, width, dtype=f32), near(HEADS, ROWS, 1, dtype=f32),
            near(HEADS, LANES, VALUE_WIDTH), near(HEADS, 8, LANES, dtype=f32),
            near(HEADS, TILE, TILE + WIN, dtype=f32), near(half, model),
        ),
        (*sums, qf, num, den, window, near_out, queries, keys, values),
        starts=starts, flops=unit * 300,
    )
    own, halo, *rest = call(
        mixed_own_kernel,
        (
            near(half, model),
            Export(sums[1], (HEADS, EDGE, 128), lambda ref: ref.at[:, PACKED:, :]),
            *map(Export, (mixed, linear, total_den, state, norm, probs_first, probs, queries)),
        ),
        (mixed, near_out), after=(other,), flops=unit * 100,
    )
    mixed, linear, total_den, state, norm, probs_first, probs, queries_far = rest
    mine, parts, signal = head_quarters(own, other)
    grad_act_own, grad_act_other, x_own, near_gain, near_gate, near_up = call(
        grad_act_kernel,
        (
            near(half, hidden, dtype=f32), near(half, hidden, dtype=f32), Stage(own_part(inputs)), Stage(gain_ffn),
            Stage(gate_proj.T), Stage(up_proj.T),
        ),
        (by_halves(cotangent), down_proj),
        after=(signal,), flops=unit * hidden,
    )
    own_normed, resid, inv_ffn = call(
        resid_kernel,
        (near(OWN, model), near(OWN, model, dtype=f32), near(OWN, 1, dtype=f32)),
        (mine, x_own, near_gain, *parts), after=(grad_act_own,),
    )
    pieces = head_pieces(own_normed)
    def ffn_half(body, pieces, grad_act, *more, after=()):
        order = [pieces[i] for i in (0, 3, 1, 2)]
        return call(
            body,
            (
                *more, near(half, model), near(half, hidden), near(half, hidden), near(half, hidden),
            ),
            (*order, near_gate, near_up, grad_act), after=after, flops=unit * 2 * hidden,
        )

    normed_own, act_own, gate_own, up_own = ffn_half(ffn_own_kernel, pieces[:4], grad_act_own)
    other, normed_other, act_other, gate_other, up_other = ffn_half(
        ffn_other_kernel, pieces[4:], grad_act_other, near(half, model), after=(gate_own,)
    )
    (own,) = call(
        ffn_back_kernel, (near(half, model),), (gate_own, up_own, near_gate, near_up),
        after=(other,), flops=unit * hidden,
    )
    mine, parts, signal = head_quarters(own, other)
    whole = hidden // 128 * 128
    place = dict(parts=4, width=2 * hidden + whole + 4 * width + 128)
    grads, resid_far, near_top, near_gain, *near_mixed = call(
        gate_grads_kernel,
        (
            far(model, 2 * hidden, **place), Export(resid), Stage(own_part(cotangent)),
            Stage(gain_ffn), Stage(out_proj), Stage(linear), Stage(total_den), Stage(qf_far),
            Stage(probs_first), Stage(probs), Stage(keys_far), Stage(values_far), Stage(halo),
            Stage(queries_far),
        ),
        (normed_own, normed_other, gate_own, gate_other, up_own, up_other),
        after=(signal,), flops=unit * 2 * hidden,
    )
    at = 2 * hidden
    *near_mixed, probs_first, probs, keys, values, halo, queries = near_mixed
    grads, tail, *near_back = call(
        down_grads_kernel,
        (
            far(model, whole, first=at, onto=grads, **place), near(model, 128), Stage(low),
            Stage(km_far),
            Stage(state), Stage(norm), Stage(raw_far), Stage(choose_q), Stage(choose_k),
            Stage(lanes), Stage(mixed), Export(act_own), Export(act_other),
        ),
        (by_halves(cotangent), act_own, act_other), after=(signal,), flops=unit * hidden,
    )
    low, km, state, norm, raw, *rest = near_back
    choose_q, choose_k, lanes, mixed, act_own, act_other = rest
    at += whole
    sent, grad_resid, gain_ffn_part = call(
        grad_resid_kernel,
        (near(OWN, model), near(OWN, model, dtype=f32), near(8, model, dtype=f32)),
        (mine, resid, inv_ffn, near_top, near_gain, *parts), after=(grads,),
    )
    pieces = head_pieces(sent)
    packed, wide, top, grad_mixed, grad_num, grad_den = call(
        mixed_back_kernel,
        (
            near(HEADS, PACKED, 128), near(HEADS, PACKED + EDGE, 128), near(ROWS, model), near(ROWS, width), near(ROWS, width),
            near(HEADS, ROWS, 1, dtype=f32),
        ),
        (
            *[pieces[i] for i in (0, 3, 1, 2, 4, 7, 5, 6)], *near_mixed, probs_first, keys, values,
            halo, queries,
        ),
        starts=starts, flops=unit * 300,
    )
    gq, gk, gv, grads, normed = call(
        window_back_kernel,
        (
            near(ROWS, width), near(ROWS, width, dtype=f32),
            near(ROWS, width, dtype=f32), far(model, width, first=at, onto=grads, **place),
            Stage(normed_far),
        ),
        (grad_mixed, probs_first, probs, keys, values, halo, queries, top, mixed),
        flops=unit * 300, scratch=[pltpu.VMEM((ROWS + WIN, width), f32)] * 2,
    )
    sums = exclusive_parts(packed, True, after=(gq,), wide=wide)
    gfeat, gv, gkf, left, right, grads = call(
        linear_back_kernel,
        (
            near(ROWS, 128, dtype=f32), near(ROWS, width, dtype=f32),
            near(HEADS, ROWS, LANES, dtype=f32), near(ROWS, HEADS * LANES, dtype=f32),
            near(ROWS, HEADS * LANES, dtype=f32),
            far(model, width, first=at + width, onto=grads, **place),
        ),
        (
            grad_num, grad_den, values, low, km, near_mixed[3], state, norm, raw, choose_q, choose_k,
            lanes, gv, normed, gq,
        ),
        starts=starts, after=(sums[0],), flops=unit * 300,
    )
    gkw, gvw, gf, grads = call(
        keys_back_kernel,
        (
            near(ROWS, width), near(ROWS, width), near(ROWS, 128),
            far(model, 2 * width + 128, first=at + 2 * width, onto=grads, **place),
        ),
        (
            *sums, values, km, gkf, gk, gv, left, right, choose_k, lanes, gfeat, normed, tail,
        ),
        starts=starts, flops=unit * 1400,
    )
    grads_sum = lax.psum_scatter(grads, "seq", scatter_dimension=0, tiled=True)
    other, own, gains = call(
        normed_back_kernel, (near(half, model), near(half, model), near(2, model, dtype=f32)),
        (
            gq, gkw, gvw, gf, win_query, win_key, value_proj, feat, inputs, inv_mix, gain_ffn_part,
        ),
        after=(grads,),
        flops=unit * 900,
    )
    mine, parts, signal = head_quarters(own, other)
    other, own = call(
        ffn_out_kernel, (near(half, model), near(half, model)), (act_own, act_other, down_proj),
        after=(signal,), flops=unit * hidden,
    )
    out_mine, out_parts, signal = head_quarters(own, other)
    gains = gains_sum(gains)
    (sent,) = call(
        grad_x_kernel, (near(2 * OWN, model),),
        (mine, own_part(inputs), grad_resid, gain_mix, resid_far, out_mine, *parts, *out_parts),
        after=(gains,),
    )
    pieces = head_pieces(sent)
    output, grad_x = call(
        grad_x_out_kernel, (far(ROWS, model), far(ROWS, model, dtype=f32)), pieces,
    )
    grad_gate_t, grad_up_t, grad_down, grad_out, *rest = call(
        grads_out_kernel,
        (far(hidden, 128, dtype=f32),) * 3 + (far(width, 128, dtype=f32),)
        + (far(128, width, dtype=f32),) * 3 + (far(32, 128, dtype=f32),) * 2,
        (columns(grads_sum, 0, 2 * hidden), columns(grads_sum, 2 * hidden, grads_sum.shape[1])),
        after=(grad_x,),
    )
    grad_wq, grad_wk, grad_wv, grad_fq_t, grad_fk_t = rest
    return (
        output,
        grad_x,
        gains[0],
        grad_fq_t.T,
        grad_fk_t.T,
        grad_wq,
        grad_wk,
        grad_wv,
        grad_out,
        gains[1],
        grad_gate_t.T,
        grad_up_t.T,
        grad_down,
    )


def solution(mesh):
    placed = (
        P("seq", None),
        P(),
        P(None, "head"),
        P(None, "head"),
        P(None, "head"),
        P(None, "head"),
        P(None, "head"),
        P("head", None),
        P(),
        P(None, "head"),
        P(None, "head"),
        P("head", None),
        P(),
        P("seq", None),
    )
    return jax.shard_map(
        shards,
        mesh=mesh,
        in_specs=placed,
        out_specs=(
            P("seq", None),
            P("seq", None),
            P("seq"),
            P("seq", "head"),
            P("seq", "head"),
            P("seq", "head"),
            P("seq", "head"),
            P("seq", "head"),
            P("head", "seq"),
            P("seq"),
            P("seq", "head"),
            P("seq", "head"),
            P("head", "seq"),
        ),
        check_vma=False,
    )
```
